32 devices in a mesh: dp: 16 (over z, x, core), chan: 2 (over y).
Axes of the slice: x: 2, y: 2, z: 4, core: 2. Of those that a mesh axis runs over, the one named last changes fastest.
Arguments:
- params: float32 [2, 2, 13696, 128], P('chan', None, 'dp'), may hold values from -6 to 6, as said below
- momentum: float32 [2, 2, 13696, 128], P('chan', None, 'dp'), may hold values from -1.5 to 1.5
- ema_params: float32 [2, 2, 13696, 128], P('chan', None, 'dp'), may hold values from -0.75 to 0.75
- latents: float32 [16, 4, 1024], P('dp'), may hold values from -6 to 6
- noise_eps: float32 [16, 4, 1024], P('dp'), may hold values from -6 to 6
- timesteps: int32 [16], P('dp'), may hold values from 0 to 999
- pixel_mask: int32 [16, 1024], P('dp'), may hold values from 0 to 1
- context: bfloat16 [16, 77, 768], P('dp'), may hold values from -6 to 6
Outputs:
- new_params: float32 [2, 2, 13696, 128], P('chan', None, 'dp')
- new_momentum: float32 [2, 2, 13696, 128], P('chan', None, 'dp')
- new_ema: float32 [2, 2, 13696, 128], P('chan', None, 'dp')
- loss_sum: float32 [], replicated
- pixel_count: float32 [], replicated
The draws below stay inside these ranges and needn't reach their ends.
Inputs may be any that keep to these rules, and one draw needn't show every extreme that they name: `params`: weights about fan_in^-0.5 (self_out 8 times, cross_out 4 times that), gains about 1, biases about 0.1.
All inputs are finite; a program needn't handle non-finite values.
Results may differ from the reference program's by a relative error of at most 0.00096.
Values may be sent and summed in bfloat16 or wider, within the bound.
A program may use at most 448 MiB of HBM per device.

```python
import math
import jax
import jax.numpy as jnp
from jax import lax

D = 320
HEADS = 8
GROUPS = 32
CTX = 768
TXT = 77
LAT_CH = 4
SIDE = 32
PIXELS = 1024
SAMPLES = 16
TOKENS = 16384
RB = 13696
N_CHAN = 2


def layout_drawn(model_width, ctx_width, lat_width, halves):
    chan_width = model_width // halves
    front = [('conv_in', (9 * lat_width, chan_width)), ('conv_in_bias', (chan_width,)), ('norm_one_gain', (chan_width,)), ('norm_one_bias', (chan_width,)), ('conv_one', (9 * model_width, chan_width)), ('conv_one_bias', (chan_width,)), ('time_one', (model_width, 4 * chan_width)), ('time_one_bias', (4 * chan_width,)), ('time_two', (4 * model_width, 4 * chan_width)), ('time_two_bias', (4 * chan_width,)), ('time_three', (4 * model_width, chan_width)), ('time_three_bias', (chan_width,))]
    back = [('norm_two_gain', (chan_width,)), ('norm_two_bias', (chan_width,)), ('conv_two', (9 * model_width, chan_width)), ('conv_two_bias', (chan_width,)), ('norm_tr_gain', (chan_width,)), ('norm_tr_bias', (chan_width,)), ('proj_in', (model_width, chan_width)), ('proj_in_bias', (chan_width,)), ('layer_one_gain', (chan_width,)), ('layer_one_bias', (chan_width,)), ('self_qkv', (model_width, 3 * chan_width)), ('self_out', (model_width, chan_width)), ('self_out_bias', (chan_width,)), ('layer_two_gain', (chan_width,)), ('layer_two_bias', (chan_width,)), ('cross_query', (model_width, chan_width)), ('cross_kv', (ctx_width, 2 * chan_width)), ('cross_out', (model_width, chan_width)), ('cross_out_bias', (chan_width,)), ('layer_three_gain', (chan_width,)), ('layer_three_bias', (chan_width,)), ('geglu_in', (model_width, 8 * chan_width)), ('geglu_in_bias', (8 * chan_width,)), ('geglu_out', (4 * model_width, chan_width)), ('geglu_out_bias', (chan_width,)), ('proj_out', (model_width, chan_width)), ('proj_out_bias', (chan_width,)), ('norm_out_gain', (chan_width,)), ('norm_out_bias', (chan_width,)), ('conv_out', (9 * model_width, lat_width // halves)), ('conv_out_bias', (lat_width // halves,))]
    return (front, back)


def boost_of(entry_name):
    if entry_name == 'self_out':
        return 8.0
    if entry_name == 'cross_out':
        return 4.0
    return 1.0


def draw_params(key, part):
    key = jax.random.fold_in(key, 7)
    segments = layout_drawn(D, CTX, LAT_CH, N_CHAN)
    scale_parts = []
    shift_parts = []
    for part_segments in segments:
        scale_list = []
        shift_list = []
        filled = 0
        for entry_name, entry_shape in part_segments:
            extent = math.prod(entry_shape)
            if entry_name[-5:] == '_gain':
                scale_list.append(jnp.full((extent,), 0.1, jnp.float32))
                shift_list.append(jnp.ones((extent,), jnp.float32))
            elif entry_name[-5:] == '_bias':
                scale_list.append(jnp.full((extent,), 0.1, jnp.float32))
                shift_list.append(jnp.zeros((extent,), jnp.float32))
            else:
                factor = boost_of(entry_name) / math.sqrt(entry_shape[0])
                scale_list.append(jnp.full((extent,), factor, jnp.float32))
                shift_list.append(jnp.zeros((extent,), jnp.float32))
            filled += extent
        rest = RB * 128 - filled
        scale_list.append(jnp.full((rest,), 0.1, jnp.float32))
        shift_list.append(jnp.zeros((rest,), jnp.float32))
        scale_parts.append(jnp.concatenate(scale_list))
        shift_parts.append(jnp.concatenate(shift_list))
    scale_all = jnp.stack(scale_parts)[None]
    shift_all = jnp.stack(shift_parts)[None]
    normal_vals = jax.random.truncated_normal(key, -4.0, 4.0, (N_CHAN, 2, RB * 128), jnp.float32)
    drawn = jnp.clip(normal_vals * scale_all + shift_all, -6.0, 6.0)
    return drawn.reshape(N_CHAN, 2, RB, 128)


def draw_pixel_mask(key, part):
    key = jax.random.fold_in(key, 5)
    sample_ids = jnp.arange(SAMPLES, dtype=jnp.int32)[:, None]
    thresholds = 250 + 500 * sample_ids // max(SAMPLES - 1, 1)
    rolled = jax.random.randint(key, (SAMPLES, PIXELS), 0, 1000, dtype=jnp.int32)
    return (rolled < thresholds).astype(jnp.int32)


def with_ends(entries, own_key, smallest, high):
    place = [jax.random.randint(jax.random.fold_in(own_key, axis), (), 0, length) for axis, length in enumerate(entries.shape)]
    longest = entries.shape.index(max(entries.shape))
    next_to = place[:longest] + [(place[longest] + 1) % entries.shape[longest]] + place[longest + 1:]
    return entries.at[tuple(place)].set(smallest).at[tuple(next_to)].set(high)


def level_of(own_key, shape, cuts, least, high):
    level = 1.0
    for axis_at, shards_of in cuts:
        heights = jax.random.uniform(jax.random.fold_in(jax.random.fold_in(own_key, 6), axis_at), (shards_of,), jnp.float32, least / len(cuts), high / len(cuts))
        level = level * jnp.repeat(jnp.exp(heights), shape[axis_at] // shards_of).reshape((-1,) + (1,) * (len(shape) - 1 - axis_at))
    return level


def centred(rng, dims, deviation, bound, cuts=(), kind=jnp.bfloat16):
    values = deviation * jax.random.normal(rng, dims, jnp.float32)
    if cuts:
        values = values * level_of(rng, dims, cuts, -0.22, 0.18)
    return jnp.clip(values, -bound, bound).astype(kind)


def setup_inputs(seed: int = 0) -> dict:
    streams_of = jax.random.split(jax.random.key(seed), 9)
    params = draw_params(jax.random.fold_in(streams_of[8], 71), 0)
    momentum = centred(streams_of[1], (N_CHAN, 2, RB, 128), (12 * TOKENS ** -0.5), 1.5, ((0, 2), (2, 16)), jnp.float32)
    ema_params = centred(streams_of[2], (N_CHAN, 2, RB, 128), 0.05, 0.75, ((0, 2), (2, 16)), jnp.float32)
    latents = centred(streams_of[3], (SAMPLES, LAT_CH, PIXELS), 1.0, 6.0, ((0, 16),), jnp.float32)
    noise_eps = centred(streams_of[4], (SAMPLES, LAT_CH, PIXELS), 1.0, 6.0, ((0, 16),), jnp.float32)
    timesteps = with_ends(jax.random.randint(streams_of[5], (SAMPLES,), 0, 1000), jax.random.fold_in(streams_of[5], 1), 0, 999).astype(jnp.int32)
    pixel_mask = draw_pixel_mask(jax.random.fold_in(streams_of[8], 71), 0)
    context = centred(streams_of[7], (SAMPLES, TXT, CTX), 1.0, 6.0, ((0, 16),))
    return dict(params=params, momentum=momentum, ema_params=ema_params, latents=latents, noise_eps=noise_eps, timesteps=timesteps, pixel_mask=pixel_mask, context=context)


norm_eps = 1e-05
learn_rate = 0.2
momentum_decay = 0.9
ema_decay = 0.9
split_members = {'self_qkv': 3, 'cross_kv': 2, 'geglu_in': 2, 'geglu_in_bias': 2}

@jax.custom_vjp
def low(v):
    return lax.optimization_barrier(v.astype(jnp.bfloat16)).astype(jnp.float32)

@jax.custom_vjp
def low_back(v):
    return v

def low_keep(v):
    return (low(v), None)

def low_pass(kept, grad):
    return (grad,)

def back_keep(v):
    return (v, None)

def back_low(kept, grad):
    return (low(grad),)
low.defvjp(low_keep, low_pass)
low_back.defvjp(back_keep, back_low)

def layout(model_width, ctx_width, lat_width, halves):
    chan_width = model_width // halves
    front = [('conv_in', (9 * lat_width, chan_width)), ('conv_in_bias', (chan_width,)), ('norm_one_gain', (chan_width,)), ('norm_one_bias', (chan_width,)), ('conv_one', (9 * model_width, chan_width)), ('conv_one_bias', (chan_width,)), ('time_one', (model_width, 4 * chan_width)), ('time_one_bias', (4 * chan_width,)), ('time_two', (4 * model_width, 4 * chan_width)), ('time_two_bias', (4 * chan_width,)), ('time_three', (4 * model_width, chan_width)), ('time_three_bias', (chan_width,))]
    back = [('norm_two_gain', (chan_width,)), ('norm_two_bias', (chan_width,)), ('conv_two', (9 * model_width, chan_width)), ('conv_two_bias', (chan_width,)), ('norm_tr_gain', (chan_width,)), ('norm_tr_bias', (chan_width,)), ('proj_in', (model_width, chan_width)), ('proj_in_bias', (chan_width,)), ('layer_one_gain', (chan_width,)), ('layer_one_bias', (chan_width,)), ('self_qkv', (model_width, 3 * chan_width)), ('self_out', (model_width, chan_width)), ('self_out_bias', (chan_width,)), ('layer_two_gain', (chan_width,)), ('layer_two_bias', (chan_width,)), ('cross_query', (model_width, chan_width)), ('cross_kv', (ctx_width, 2 * chan_width)), ('cross_out', (model_width, chan_width)), ('cross_out_bias', (chan_width,)), ('layer_three_gain', (chan_width,)), ('layer_three_bias', (chan_width,)), ('geglu_in', (model_width, 8 * chan_width)), ('geglu_in_bias', (8 * chan_width,)), ('geglu_out', (4 * model_width, chan_width)), ('geglu_out_bias', (chan_width,)), ('proj_out', (model_width, chan_width)), ('proj_out_bias', (chan_width,)), ('norm_out_gain', (chan_width,)), ('norm_out_bias', (chan_width,)), ('conv_out', (9 * model_width, lat_width // halves)), ('conv_out_bias', (lat_width // halves,))]
    return (front, back)

def unpack(flat_vec, part_segments):
    pieces = {}
    offset = 0
    for entry_name, entry_shape in part_segments:
        extent = math.prod(entry_shape)
        pieces[entry_name] = flat_vec[offset:offset + extent].reshape(entry_shape)
        offset += extent
    return pieces

def full_weights(packed):
    halves = packed.shape[0]
    segments = layout(D, CTX, LAT_CH, halves)
    flat_all = packed.reshape(halves, 2, -1)
    shards = []
    for chan_idx in range(halves):
        pieces = unpack(flat_all[chan_idx, 0], segments[0])
        later = unpack(flat_all[chan_idx, 1], segments[1])
        for entry_name in later:
            pieces[entry_name] = later[entry_name]
        shards.append(pieces)
    merged = {}
    for entry_name in shards[0]:
        members = split_members[entry_name] if entry_name in split_members else 1
        blocks = []
        for member in range(members):
            for pieces in shards:
                blocks.append(jnp.split(pieces[entry_name], members, axis=-1)[member])
        merged[entry_name] = jnp.concatenate(blocks, axis=-1)
    return merged

def alpha_bar(step_ids):
    levels = jnp.arange(1000, dtype=jnp.float32)
    lowest = 0.00085 ** 0.5
    highest = 0.012 ** 0.5
    beta_values = jnp.square(lowest + (highest - lowest) * levels / 999.0)
    cum_table = jnp.cumprod(1.0 - beta_values)
    matches = levels[None, :] == step_ids.astype(jnp.float32)[:, None]
    return lax.optimization_barrier(jnp.sum(jnp.where(matches, cum_table[None, :], 0.0), axis=1))

def time_features(step_ids, model_width):
    half_width = model_width // 2
    ladder = jnp.arange(half_width, dtype=jnp.float32)
    frequencies = jnp.exp(-math.log(10000.0) * ladder / half_width)
    angles = step_ids.astype(jnp.float32)[:, None] * frequencies[None, :]
    return jnp.concatenate([jnp.cos(angles), jnp.sin(angles)], axis=1)

def unfold(image_grid):
    side_len = image_grid.shape[-2]
    padded = jnp.pad(image_grid, [(0, 0)] * (image_grid.ndim - 3) + [(1, 1), (1, 1), (0, 0)])
    tap_list = [padded[..., row_at:row_at + side_len, col_at:col_at + side_len, :] for row_at in range(3) for col_at in range(3)]
    return jnp.concatenate(tap_list, axis=-1)

def group_norm(values, gain_vec, bias_vec, groups):
    grouped = values.reshape(values.shape[:-1] + (groups, values.shape[-1] // groups))
    center = lax.optimization_barrier(jnp.mean(grouped, axis=(-3, -1), keepdims=True))
    spread = lax.optimization_barrier(jnp.mean(jnp.square(grouped - center), axis=(-3, -1), keepdims=True))
    normed = ((grouped - center) * lax.rsqrt(spread + norm_eps)).reshape(values.shape)
    return normed * gain_vec + bias_vec

def layer_norm(values, gain_vec, bias_vec):
    center = lax.optimization_barrier(jnp.mean(values, axis=-1, keepdims=True))
    spread = lax.optimization_barrier(jnp.mean(jnp.square(values), axis=-1, keepdims=True)) - jnp.square(center)
    return (values - center) * lax.rsqrt(spread + norm_eps) * gain_vec + bias_vec

def linear(inputs, weight):
    return low_back(jnp.dot(inputs, weight, precision=lax.Precision.HIGHEST, preferred_element_type=jnp.float32))

def attention(queries, keys_in, values_in):
    head_size = D // HEADS
    q_heads = queries.reshape(queries.shape[0], HEADS, head_size)
    k_heads = keys_in.reshape(keys_in.shape[0], HEADS, head_size)
    v_heads = values_in.reshape(values_in.shape[0], HEADS, head_size)
    scores = low_back(jnp.einsum('qhd,khd->hqk', q_heads, k_heads, precision=lax.Precision.HIGHEST)) * head_size ** (-0.5)
    prob_vals = low(jax.nn.softmax(scores, axis=-1))
    mix_out = low_back(jnp.einsum('hqk,khd->qhd', prob_vals, v_heads, precision=lax.Precision.HIGHEST))
    return mix_out.reshape(queries.shape[0], D)

def sample_sum(weight_map, clean_lat, fresh_noise, step_id, mask_row, context_row):
    alpha_level = alpha_bar(step_id[None])[0]
    noisy_in = jnp.sqrt(alpha_level) * clean_lat.T + jnp.sqrt(1.0 - alpha_level) * fresh_noise.T

    def conv_apply(act_low, weight_label):
        columns = unfold(act_low.reshape(SIDE, SIDE, -1)).reshape(PIXELS, -1)
        return linear(columns, weight_map[weight_label]) + weight_map[weight_label + '_bias']

    def norm_pair(values, prefix):
        return group_norm(values, weight_map[prefix + '_gain'], weight_map[prefix + '_bias'], GROUPS)

    def layer_pair(values, prefix):
        return layer_norm(values, weight_map[prefix + '_gain'], weight_map[prefix + '_bias'])
    h_zero = conv_apply(low(noisy_in), 'conv_in')
    act_one = low(jax.nn.silu(norm_pair(h_zero, 'norm_one')))
    time_embed = low(time_features(step_id[None], D))
    time_a = low(jax.nn.silu(linear(time_embed, weight_map['time_one']) + weight_map['time_one_bias']))
    time_b = low(jax.nn.silu(linear(time_a, weight_map['time_two']) + weight_map['time_two_bias']))
    time_vec = linear(time_b, weight_map['time_three']) + weight_map['time_three_bias']
    h_one = conv_apply(act_one, 'conv_one') + time_vec
    act_two = low(jax.nn.silu(norm_pair(h_one, 'norm_two')))
    h_two = h_zero + conv_apply(act_two, 'conv_two')
    z_zero = linear(low(norm_pair(h_two, 'norm_tr')), weight_map['proj_in']) + weight_map['proj_in_bias']
    qkv_all = linear(low(layer_pair(z_zero, 'layer_one')), weight_map['self_qkv'])
    q_self, k_self, v_self = jnp.split(qkv_all, 3, axis=1)
    self_mix = attention(low(q_self), low(k_self), low(v_self))
    z_one = z_zero + linear(low(self_mix), weight_map['self_out']) + weight_map['self_out_bias']
    q_cross = low(linear(low(layer_pair(z_one, 'layer_two')), weight_map['cross_query']))
    kv_cross = linear(low(context_row), weight_map['cross_kv'])
    k_cross, v_cross = jnp.split(kv_cross, 2, axis=1)
    cross_mix = attention(q_cross, low(k_cross), low(v_cross))
    z_two = z_one + linear(low(cross_mix), weight_map['cross_out']) + weight_map['cross_out_bias']
    geglu_pre = linear(low(layer_pair(z_two, 'layer_three')), weight_map['geglu_in']) + weight_map['geglu_in_bias']
    value_half, gate_half = jnp.split(geglu_pre, 2, axis=1)
    gated_act = low(value_half * jax.nn.gelu(gate_half, approximate=False))
    z_three = z_two + linear(gated_act, weight_map['geglu_out']) + weight_map['geglu_out_bias']
    h_three = h_two + linear(low(z_three), weight_map['proj_out']) + weight_map['proj_out_bias']
    act_three = low(jax.nn.silu(norm_pair(h_three, 'norm_out')))
    predicted = conv_apply(act_three, 'conv_out')
    miss_err = predicted - fresh_noise.T
    return jnp.sum(mask_row.astype(jnp.float32)[:, None] * jnp.square(miss_err))

def reference(params, momentum, ema_params, latents, noise_eps, timesteps, pixel_mask, context):
    context_full = context.astype(jnp.float32)

    def total_sum(packed):
        weight_map = full_weights(low(packed))

        def one_sample(running, inputs):
            return (running + jax.checkpoint(sample_sum)(weight_map, *inputs), None)
        result, unused = lax.scan(one_sample, jnp.zeros((), jnp.float32), (latents, noise_eps, timesteps, pixel_mask, context_full))
        return result
    loss_sum, pullback = jax.vjp(total_sum, params)
    grad_all, = pullback(jnp.ones((), jnp.float32))
    pixel_count = jnp.sum(pixel_mask.astype(jnp.float32))
    scaled = grad_all / (LAT_CH * jnp.maximum(pixel_count, 1.0))
    new_momentum = momentum_decay * momentum + scaled
    new_params = params - learn_rate * (scaled + momentum_decay * new_momentum)
    new_ema = ema_decay * ema_params + (1.0 - ema_decay) * new_params
    return (new_params, new_momentum, new_ema, loss_sum, pixel_count)
```

```python
import math

import jax
import jax.numpy as jnp
from jax import lax
from jax.experimental import pallas as pl
from jax.experimental.pallas import tpu as pltpu
from jax.sharding import PartitionSpec as P

D = 320
W = 160
HEADS = 8
HD = 40
CTX = 768
TXT = 77
LAT = 4
SIDE = 32
N = 1024
T = 256
EPS = 1e-5
LR = 0.2
MU = 0.9
ED = 0.9
CH = "chan"
DP = "dp"
F32 = jnp.float32
BF = jnp.bfloat16
HI = lax.Precision.HIGHEST
SCALE = HD**-0.5
LOG2E = 1.0 / math.log(2.0)

R0 = 4000
FRONT = 3650
T1, T2, T3 = 3650, 5255, 11660
C2 = 2
PI = 2885
QKV = 3208
SO = 4168
CQ = 4491
CKV = 4811
CO = 6347
GI = 6670
GIB = 9230
GO = 9238
PO = 10519
OUT = 10842
OUTB = 10878
R1 = 13600
VEC0 = (36, 37, 38, 2919)
VEC1 = (0, 1, 2882, 2883, 2884, 3205, 3206, 3207, 4488, 4489, 4490, 6667, 6668, 6669, 10518, 10839, 10840, 10841)
(N2G, N2B, C2B, NTG, NTB, PIB, L1G, L1B, SOB, L2G, L2B, COB, L3G, L3B, GOB, POB, NOG, NOB) = range(18)
MPI, MQ, MK, MV, MSO, MCQ, MCO, MGV, MGG, MGO, MPO = 9, 10, 11, 12, 13, 14, 15, 16, 20, 24, 28
NMAT = 29


def kcall(body, outs, ins, scratch=()):
    vm = pl.BlockSpec(memory_space=pltpu.VMEM)
    return pl.pallas_call(
        body,
        out_shape=outs,
        in_specs=[vm] * len(ins),
        out_specs=jax.tree.map(lambda _: vm, outs),
        scratch_shapes=list(scratch),
        compiler_params=pltpu.CompilerParams(vmem_limit_bytes=60 * 2**20),
    )(*ins)


def sds(shape, dtype=F32):
    return jax.ShapeDtypeStruct(shape, dtype)


def tiles(fn, size=T, total=N):
    @pl.loop(0, total // size)
    def _(t):
        fn(pl.ds(pl.multiple_of(t * size, size), size))


def nn(a, b):
    return jnp.dot(a, b, preferred_element_type=F32)


def nt(a, b):
    return lax.dot_general(a, b, (((1,), (1,)), ((), ())), preferred_element_type=F32)


def tn(a, b):
    return lax.dot_general(a, b, (((0,), (0,)), ((), ())), preferred_element_type=F32)


def colsum(v):
    return jnp.sum(v, axis=0, keepdims=True)


def unroll_rows(a_ref, tmp, s_ref, chunks):
    q = 80

    @pl.loop(0, chunks)
    def _(c):
        src = pl.ds(pl.multiple_of(c * 5 * q, 5 * q), 5 * q)
        for b in range(2):
            tmp[b] = a_ref[b, src, :].astype(F32)
        f = [[tmp[b, pl.ds(j, q, stride=5), :] for j in range(5)] for b in range(2)]
        for i in range(4):
            row = []
            for b in range(2):
                lo = 32 * i
                first, second = f[b][i], f[b][i + 1]
                row += [first[:, lo:], second[:, : lo + 32]] if lo else [first, second[:, :32]]
            full = jnp.concatenate(row, axis=1)
            for k, (lo, hi) in enumerate(((0, 128), (128, 256), (256, 320))):
                s_ref[k, pl.ds(c * 4 * q + i, q, stride=4), : hi - lo] = full[:, lo:hi]


def get_rows(s_ref, start, count, step=1):
    ds = pl.ds(start, count) if step == 1 else pl.ds(start, count, stride=step)
    return jnp.concatenate([s_ref[0, ds, :], s_ref[1, ds, :], s_ref[2, ds, :64]], axis=1)


def unpack0_kernel(a_ref, win, w1, vec, tmp, s_ref):
    unroll_rows(a_ref, tmp, s_ref, R0 // 400)
    win[...] = get_rows(s_ref, 0, 36).astype(BF)
    for t in range(9):
        w1[t] = get_rows(s_ref, 39 + D * t, D).astype(BF)
    for i, r in enumerate(VEC0):
        vec[i : i + 1, :] = get_rows(s_ref, r, 1)


def unpack1_kernel(a_ref, mats, kv, vec, gib, wout, outb, tmp, s_ref, o_ref):
    unroll_rows(a_ref, tmp, s_ref, R1 // 400)
    for t in range(9):
        mats[t] = get_rows(s_ref, C2 + D * t, D).astype(BF)
    for m, r in ((MPI, PI), (MSO, SO), (MCQ, CQ), (MCO, CO), (MPO, PO)):
        mats[m] = get_rows(s_ref, r, D).astype(BF)
    for j in range(3):
        mats[MQ + j] = get_rows(s_ref, QKV + j, D, 3).astype(BF)
    for j in range(8):
        mats[MGV + j] = get_rows(s_ref, GI + j, D, 8).astype(BF)
    for j in range(4):
        for b in range(2):
            mats[MGO + j, b * W : (b + 1) * W, :] = get_rows(s_ref, GO + 640 * b + W * j, W).astype(BF)
    for j in range(2):
        kv[j] = get_rows(s_ref, CKV + j, CTX, 2).astype(BF)
    for i, r in enumerate(VEC1):
        vec[i : i + 1, :] = get_rows(s_ref, r, 1)
    gib[...] = get_rows(s_ref, GIB, 8)
    outb[...] = get_rows(s_ref, OUTB, 1)
    lane = lax.broadcasted_iota(jnp.int32, (W, W), 0)
    col = lax.broadcasted_iota(jnp.int32, (W, W), 1)
    pick = ((lane % 2) * 80 + lane // 2 == col).astype(BF)
    raw = get_rows(s_ref, OUT, 36).astype(BF)
    for b in range(2):
        moved = nn(raw[:, W * b : W * (b + 1)], pick)
        o_ref[0, :36, :] = moved[:, :128]
        o_ref[1, :36, :32] = moved[:, 128:]
        for ch in range(2):
            pieces = []
            for m in range(4):
                ds = pl.ds(m, 9, stride=4)
                both = jnp.concatenate([o_ref[0, ds, :], o_ref[1, ds, :32]], axis=1)
                pieces.append(both[:, 80 * ch : 80 * ch + 80])
            at = (2 * b + ch) * 9
            wout[at : at + 9, :] = jnp.concatenate(pieces, axis=1).astype(BF)


def pixel_col(n, axis):
    shape = (n, 1) if axis == 0 else (1, n)
    return lax.broadcasted_iota(jnp.int32, shape, axis)


def shift_lanes(v, tap):
    r, s = tap // 3 - 1, tap % 3 - 1
    pix = pixel_col(N, 1)
    i, j = pix // SIDE + r, pix % SIDE + s
    ok = (i >= 0) & (i < SIDE) & (j >= 0) & (j < SIDE)
    move = -(r * SIDE + s) % N
    moved = pltpu.roll(v, move, 1) if move else v
    return jnp.where(ok, moved, 0.0)


def put_shifts(ref, rows, v):
    n = v.shape[0]
    j = pixel_col(n, 0) % SIDE
    at = pl.ds(pl.multiple_of(rows.start + SIDE, SIDE), n)
    ref[0, at, :] = jnp.where(j == 0, 0.0, pltpu.roll(v, 1, 0)).astype(BF)
    ref[1, at, :] = v.astype(BF)
    ref[2, at, :] = jnp.where(j == SIDE - 1, 0.0, pltpu.roll(v, n - 1, 0)).astype(BF)


def clear_margins(ref):
    for s in range(3):
        zero = jnp.zeros((SIDE, ref.shape[2]), BF)
        ref[s, :SIDE, :] = zero
        ref[s, N + SIDE :, :] = zero


def tap_rows(ref, rows, tap):
    at = pl.ds(pl.multiple_of(rows.start + SIDE * (tap // 3), SIDE), T)
    return ref[tap % 3, at, :]


def conv_rows(ref, rows, w_ref):
    total = nn(tap_rows(ref, rows, 0), w_ref[0])
    for tap in range(1, 9):
        total += nn(tap_rows(ref, rows, tap), w_ref[tap])
    return total


def conv_back_rows(ref, rows, w_ref):
    total = nt(tap_rows(ref, rows, 8), w_ref[0])
    for tap in range(1, 9):
        total += nt(tap_rows(ref, rows, 8 - tap), w_ref[tap])
    return total


def group_mean(sums):
    a = lax.broadcasted_iota(jnp.int32, (D, D), 0) // 10
    b = lax.broadcasted_iota(jnp.int32, (D, D), 1) // 10
    pool = jnp.where(a == b, 1.0, 0.0)
    wide = jnp.broadcast_to(sums, (8, D))
    out = jnp.dot(wide, pool, precision=HI, preferred_element_type=F32)
    return out[:1] * (1.0 / (10 * N))


def group_stats(v_ref, acc, sums):
    mean = group_mean(sums)
    acc[0:1, :] = jnp.zeros((1, D), F32)

    def one(rows):
        acc[0:1, :] += colsum(jnp.square(v_ref[rows, :] - mean))

    tiles(one)
    return mean, lax.rsqrt(group_mean(acc[0:1, :]) + EPS)


def silu(v):
    return v * jax.nn.sigmoid(v)


def silu_slope(v):
    sig = jax.nn.sigmoid(v)
    return sig * (1.0 + v * (1.0 - sig))


def layer(v):
    mean = jnp.sum(v, axis=1, keepdims=True) * (1.0 / D)
    sq = jnp.sum(v * v, axis=1, keepdims=True) * (1.0 / D)
    inv = lax.rsqrt(sq - mean * mean + EPS)
    return (v - mean) * inv, inv


def layer_back(grad, normed, inv, gain):
    ghat = grad * gain
    m1 = jnp.sum(ghat, axis=1, keepdims=True) * (1.0 / D)
    m2 = jnp.sum(ghat * normed, axis=1, keepdims=True) * (1.0 / D)
    return inv * (ghat - m1 - normed * m2)


def head(v, h):
    return v[:, HD * h : HD * (h + 1)]


def front_kernel(noisy, tv, win, w1, vec0, mats, vec1, h0, h1, h2, z0, a1, a2, ntr, x1, q, k, v, stats, sh, acc):
    cols = jnp.concatenate([shift_lanes(noisy[...], t) for t in range(9)], axis=0).astype(BF)
    acc[...] = jnp.zeros_like(acc)
    clear_margins(sh)
    h = tn(cols, win[...]) + vec0[0:1, :]
    h0[...] = h
    mean, inv = group_stats(h0, acc, colsum(h))
    stats[0:1, :], stats[1:2, :] = mean, inv

    def act(src, dst, gain, bias):
        def one(rows):
            y = silu((src[rows, :] - mean) * inv * gain + bias)
            put_shifts(sh, rows, y)
            dst[rows, :] = y.astype(BF)

        tiles(one)

    act(h0, a1, vec0[1:2, :], vec0[2:3, :])
    acc[1:2, :] = jnp.zeros((1, D), F32)

    def conv1(rows):
        y = conv_rows(sh, rows, w1) + vec0[3:4, :] + tv[...]
        h1[rows, :] = y
        acc[1:2, :] += colsum(y)

    tiles(conv1)
    mean, inv = group_stats(h1, acc, acc[1:2, :])
    stats[2:3, :], stats[3:4, :] = mean, inv
    act(h1, a2, vec1[N2G : N2G + 1, :], vec1[N2B : N2B + 1, :])
    acc[1:2, :] = jnp.zeros((1, D), F32)

    def conv2(rows):
        y = h0[rows, :] + conv_rows(sh, rows, mats) + vec1[C2B : C2B + 1, :]
        h2[rows, :] = y
        acc[1:2, :] += colsum(y)

    tiles(conv2)
    mean, inv = group_stats(h2, acc, acc[1:2, :])
    stats[4:5, :], stats[5:6, :] = mean, inv

    def last(rows):
        n = ((h2[rows, :] - mean) * inv * vec1[NTG : NTG + 1, :] + vec1[NTB : NTB + 1, :]).astype(BF)
        ntr[rows, :] = n
        z = nn(n, mats[MPI]) + vec1[PIB : PIB + 1, :]
        z0[rows, :] = z
        normed, _ = layer(z)
        x = (normed * vec1[L1G : L1G + 1, :] + vec1[L1B : L1B + 1, :]).astype(BF)
        x1[rows, :] = x
        for at, dst in ((MQ, q), (MK, k), (MV, v)):
            y = nn(x, mats[at]).astype(BF)
            for hd in range(HEADS):
                dst[hd, rows, :] = head(y, hd)

    tiles(last)


def attend_kernel(q, k, v, o, lse, ot):
    @pl.loop(0, HEADS)
    def _(h):
        kk = k[h]
        vt = v[h].astype(F32).T.astype(BF)
        for t in range(N // T):
            rows = pl.ds(t * T, T)
            s = nt(kk, q[h, rows, :]) * (SCALE * LOG2E)
            top = jnp.max(s, axis=0, keepdims=True)
            e = jnp.exp2(s - top)
            total = jnp.sum(e, axis=0, keepdims=True)
            lse[h, :, rows] = top + jnp.log(total) * LOG2E
            p = (e * (1.0 / total)).astype(BF)
            ot[pl.ds(pl.multiple_of(h * HD, HD), HD), rows] = nn(vt, p)

    o[...] = ot[...].T.astype(BF)


def cross_head(qh, kh, vh):
    s = nt(kh, qh) * (SCALE * LOG2E)
    e = jnp.exp2(s - jnp.max(s, axis=0, keepdims=True))
    return e * (1.0 / jnp.sum(e, axis=0, keepdims=True))


def back_half_kernel(
    o, z0, h2, ctx, noise, mask, mats, kvw, vec, gib, wout, outb,
    z1, z2, h3, x2, x3, oc, z3b, gl, a3, qc, kc, vc, derr, loss, stats, acc, ot,
):
    acc[...] = jnp.zeros_like(acc)
    kk = nn(ctx[...], kvw[0]).astype(BF)
    vv = nn(ctx[...], kvw[1])
    for h in range(HEADS):
        kc[h] = head(kk, h)
        vc[h] = head(vv, h).astype(BF)
    vt = vv.T

    def trunk(rows):
        z = z0[rows, :] + nn(o[rows, :], mats[MSO]) + vec[SOB : SOB + 1, :]
        z1[rows, :] = z
        normed, _ = layer(z)
        x = (normed * vec[L2G : L2G + 1, :] + vec[L2B : L2B + 1, :]).astype(BF)
        x2[rows, :] = x
        qq = nn(x, mats[MCQ]).astype(BF)
        for h in range(HEADS):
            qh = head(qq, h)
            qc[h, rows, :] = qh
            p = cross_head(qh, kc[h], None).astype(BF)
            ot[HD * h : HD * (h + 1), :] = nn(vt[HD * h : HD * (h + 1), :].astype(BF), p)
        c = ot[...].T.astype(BF)
        oc[rows, :] = c
        z = z + nn(c, mats[MCO]) + vec[COB : COB + 1, :]
        z2[rows, :] = z
        normed, _ = layer(z)
        x = (normed * vec[L3G : L3G + 1, :] + vec[L3B : L3B + 1, :]).astype(BF)
        x3[rows, :] = x
        for j in range(4):
            a = nn(x, mats[MGV + j]) + gib[j : j + 1, :]
            g = nn(x, mats[MGG + j]) + gib[4 + j : 5 + j, :]
            y = (a * (0.5 * g * (1.0 + lax.erf(g * math.sqrt(0.5))))).astype(BF)
            gl[j, rows, :] = y
            z = z + nn(y, mats[MGO + j])
        zb = (z + vec[GOB : GOB + 1, :]).astype(BF)
        z3b[rows, :] = zb
        hh = h2[rows, :] + nn(zb, mats[MPO]) + vec[POB : POB + 1, :]
        h3[rows, :] = hh
        acc[1:2, :] += colsum(hh)

    tiles(trunk)
    mean, inv = group_stats(h3, acc, acc[1:2, :])
    stats[0:1, :], stats[1:2, :] = mean, inv

    def act(rows):
        y = silu((h3[rows, :] - mean) * inv * vec[NOG : NOG + 1, :] + vec[NOB : NOB + 1, :])
        a3[rows, :] = y.astype(BF)

    tiles(act)
    taps = nt(wout[...], a3[...])
    total = jnp.zeros((1,), F32)
    for ch in range(LAT):
        pred = jnp.zeros((1, N), F32)
        for t in range(9):
            pred += shift_lanes(taps[9 * ch + t : 9 * ch + t + 1, :], t)
        at = W * (ch // 2) + ch % 2
        err = pred + outb[0:1, at : at + 1] - noise[ch : ch + 1, :]
        weighed = mask[...] * err
        derr[ch : ch + 1, :] = 2.0 * weighed
        acc[2 + ch : 3 + ch, 0:1] = jnp.sum(weighed * err, axis=1, keepdims=True)
    loss[...] = acc[2:3, 0:1] + acc[3:4, 0:1] + acc[4:5, 0:1] + acc[5:6, 0:1]


def group_back(n_of, grads, gain, dgain, dbias):
    return group_mean(gain * dbias), group_mean(gain * dgain)


def back_one_kernel(
    derr, h3, stats, a3, z1, z2, x3, qc, kc, vc, mats, vec, gib, wout,
    dh3, dz1, dh3b, dz3b, dab, dgb, dz2b, dqc, dz1b, dos, dkv, dvec, dgib, dwout, dbout,
    tmp, acc, ot, kacc, pt,
):
    acc[...] = jnp.zeros_like(acc)
    dgib[...] = jnp.zeros_like(dgib)
    dvec[...] = jnp.zeros_like(dvec)
    kacc[...] = jnp.zeros_like(kacc)
    for ch in range(LAT):
        g = derr[ch : ch + 1, :]
        dbout[ch : ch + 1, :] = jnp.broadcast_to(jnp.sum(g, axis=1, keepdims=True), (1, 128))
        for t in range(9):
            pt[9 * ch + t : 9 * ch + t + 1, :] = shift_lanes(g, 8 - t)
    taps = pt[...].astype(BF)
    dwout[...] = nn(taps, a3[...])
    tmp[...] = tn(taps, wout[...])
    mean, inv = stats[0:1, :], stats[1:2, :]
    gain, bias = vec[NOG : NOG + 1, :], vec[NOB : NOB + 1, :]

    def one(rows):
        n = (h3[rows, :] - mean) * inv
        g = tmp[rows, :] * silu_slope(n * gain + bias)
        tmp[rows, :] = g
        dvec[NOG : NOG + 1, :] += colsum(g * n)
        dvec[NOB : NOB + 1, :] += colsum(g)

    tiles(one)
    m1 = group_mean(gain * dvec[NOB : NOB + 1, :])
    m2 = group_mean(gain * dvec[NOG : NOG + 1, :])

    def trunk(rows):
        n = (h3[rows, :] - mean) * inv
        g = inv * (tmp[rows, :] * gain - m1 - n * m2)
        dh3[rows, :] = g
        dvec[POB : POB + 1, :] += colsum(g)
        gb = g.astype(BF)
        dh3b[rows, :] = gb
        dz3 = nt(gb, mats[MPO])
        dvec[GOB : GOB + 1, :] += colsum(dz3)
        zb = dz3.astype(BF)
        dz3b[rows, :] = zb
        x = x3[rows, :]
        dx = jnp.zeros((T, D), F32)
        for j in range(4):
            a = nn(x, mats[MGV + j]) + gib[j : j + 1, :]
            g = nn(x, mats[MGG + j]) + gib[4 + j : 5 + j, :]
            dgl = nt(zb, mats[MGO + j])
            cdf = 0.5 * (1.0 + lax.erf(g * math.sqrt(0.5)))
            da = dgl * (g * cdf)
            dg = dgl * a * (cdf + g * jnp.exp(-0.5 * g * g) * (1.0 / math.sqrt(2.0 * math.pi)))
            dgib[j : j + 1, :] += colsum(da)
            dgib[4 + j : 5 + j, :] += colsum(dg)
            da, dg = da.astype(BF), dg.astype(BF)
            dab[j, rows, :] = da
            dgb[j, rows, :] = dg
            dx += nt(da, mats[MGV + j]) + nt(dg, mats[MGG + j])
        normed, li = layer(z2[rows, :])
        dvec[L3G : L3G + 1, :] += colsum(dx * normed)
        dvec[L3B : L3B + 1, :] += colsum(dx)
        dz2 = dz3 + layer_back(dx, normed, li, vec[L3G : L3G + 1, :])
        dvec[COB : COB + 1, :] += colsum(dz2)
        zb = dz2.astype(BF)
        dz2b[rows, :] = zb
        do = nt(zb, mats[MCO]).astype(BF)
        for h in range(HEADS):
            qh, kh, vh, doh = qc[h, rows, :], kc[h], vc[h], head(do, h)
            p = cross_head(qh, kh, vh)
            dp = nt(vh, doh)
            ds = (p * (dp - jnp.sum(p * dp, axis=0, keepdims=True)) * SCALE).astype(BF)
            kacc[0, h] += nn(ds, qh)
            kacc[1, h] += nn(p.astype(BF), doh)
            ot[HD * h : HD * (h + 1), :] = tn(kh, ds)
        dq = ot[...].T.astype(BF)
        dqc[rows, :] = dq
        dx = nt(dq, mats[MCQ])
        normed, li = layer(z1[rows, :])
        dvec[L2G : L2G + 1, :] += colsum(dx * normed)
        dvec[L2B : L2B + 1, :] += colsum(dx)
        dz = dz2 + layer_back(dx, normed, li, vec[L2G : L2G + 1, :])
        dz1[rows, :] = dz
        dvec[SOB : SOB + 1, :] += colsum(dz)
        zb = dz.astype(BF)
        dz1b[rows, :] = zb
        do = nt(zb, mats[MSO]).astype(BF)
        for h in range(HEADS):
            dos[h, rows, :] = head(do, h)

    tiles(trunk)
    for j in range(2):
        dkv[j] = jnp.concatenate([kacc[j, h] for h in range(HEADS)], axis=1).astype(BF)


def attend_back_kernel(q, k, v, do, lse, dq, dk, dv, qt, kacc, vacc):
    @pl.loop(0, HEADS)
    def _(h):
        kk, vv = k[h], v[h]
        kt = kk.astype(F32).T.astype(BF)
        for t in range(N // T):
            rows = pl.ds(t * T, T)
            qh, doh = q[h, rows, :], do[h, rows, :]
            p = jnp.exp2(nt(kk, qh) * (SCALE * LOG2E) - lse[h, :, rows])
            dp = nt(vv, doh)
            ds = (p * (dp - jnp.sum(p * dp, axis=0, keepdims=True)) * SCALE).astype(BF)
            dkt, dvt = nn(ds, qh), nn(p.astype(BF), doh)
            if t == 0:
                kacc[h], vacc[h] = dkt, dvt
            else:
                kacc[h] += dkt
                vacc[h] += dvt
            qt[pl.ds(pl.multiple_of(h * HD, HD), HD), rows] = nn(kt, ds)

    dq[...] = qt[...].T.astype(BF)

    def one(rows):
        for acc, dst in ((kacc, dk), (vacc, dv)):
            dst[rows, :] = jnp.concatenate([acc[h, rows, :] for h in range(HEADS)], axis=1).astype(BF)

    tiles(one)


def back_two_kernel(
    dq, dk, dv, dz1, dh3, z0, h2, h1, h0, stats, w1, mats, vec0, vec1,
    dz0b, g2, g1, dh0b, dvec0, dvec1, dtv,
    tmp, dh,
):
    dvec0[...] = jnp.zeros_like(dvec0)
    dvec1[...] = jnp.zeros_like(dvec1)
    dtv[...] = jnp.zeros_like(dtv)
    clear_margins(g1)
    clear_margins(g2)

    def trunk(rows):
        dx = nt(dq[rows, :], mats[MQ]) + nt(dk[rows, :], mats[MK]) + nt(dv[rows, :], mats[MV])
        normed, li = layer(z0[rows, :])
        dvec1[L1G : L1G + 1, :] += colsum(dx * normed)
        dvec1[L1B : L1B + 1, :] += colsum(dx)
        dz = dz1[rows, :] + layer_back(dx, normed, li, vec1[L1G : L1G + 1, :])
        dvec1[PIB : PIB + 1, :] += colsum(dz)
        zb = dz.astype(BF)
        dz0b[rows, :] = zb
        g = nt(zb, mats[MPI])
        tmp[rows, :] = g
        n = (h2[rows, :] - stats[4:5, :]) * stats[5:6, :]
        dvec1[NTG : NTG + 1, :] += colsum(g * n)
        dvec1[NTB : NTB + 1, :] += colsum(g)

    tiles(trunk)

    def norm_rows(rows, src, at, gain, m1, m2):
        n = (src[rows, :] - stats[at : at + 1, :]) * stats[at + 1 : at + 2, :]
        return stats[at + 1 : at + 2, :] * (tmp[rows, :] * gain - m1 - n * m2)

    gain = vec1[NTG : NTG + 1, :]
    m1 = group_mean(gain * dvec1[NTB : NTB + 1, :])
    m2 = group_mean(gain * dvec1[NTG : NTG + 1, :])

    def second(rows):
        g = dh3[rows, :] + norm_rows(rows, h2, 4, gain, m1, m2)
        dh[rows, :] = g
        dvec1[C2B : C2B + 1, :] += colsum(g)
        put_shifts(g2, rows, g)

    tiles(second)
    gain2, bias2 = vec1[N2G : N2G + 1, :], vec1[N2B : N2B + 1, :]

    def conv2(rows):
        n = (h1[rows, :] - stats[2:3, :]) * stats[3:4, :]
        g = conv_back_rows(g2, rows, mats) * silu_slope(n * gain2 + bias2)
        tmp[rows, :] = g
        dvec1[N2G : N2G + 1, :] += colsum(g * n)
        dvec1[N2B : N2B + 1, :] += colsum(g)

    tiles(conv2)
    n1 = group_mean(gain2 * dvec1[N2B : N2B + 1, :])
    n2 = group_mean(gain2 * dvec1[N2G : N2G + 1, :])

    def third(rows):
        g = norm_rows(rows, h1, 2, gain2, n1, n2)
        dtv[...] += colsum(g)
        put_shifts(g1, rows, g)

    tiles(third)
    gain1, bias1 = vec0[1:2, :], vec0[2:3, :]

    def conv1(rows):
        n = (h0[rows, :] - stats[0:1, :]) * stats[1:2, :]
        g = conv_back_rows(g1, rows, w1) * silu_slope(n * gain1 + bias1)
        tmp[rows, :] = g
        dvec0[1:2, :] += colsum(g * n)
        dvec0[2:3, :] += colsum(g)

    tiles(conv1)
    dvec0[3:4, :] = dtv[...]
    k1 = group_mean(gain1 * dvec0[2:3, :])
    k2 = group_mean(gain1 * dvec0[1:2, :])

    def last(rows):
        g = dh[rows, :] + norm_rows(rows, h0, 0, gain1, k1, k2)
        dvec0[0:1, :] += colsum(g)
        dh0b[rows, :] = g.astype(BF)

    tiles(last)


def own(c, v):
    return jnp.where(c == 0, v[..., :W], v[..., W:])


def put_rows(s_ref, start, v, step=1):
    n = v.shape[0]
    ds = pl.ds(start, n) if step == 1 else pl.ds(start, n, stride=step)
    s_ref[0, ds, :] = v[:, :128]
    s_ref[1, ds, :32] = v[:, 128:]


def roll_rows(s_ref, tmp, out_ref, chunks):
    q = 80

    @pl.loop(0, chunks)
    def _(c):
        g = []
        for i in range(4):
            ds = pl.ds(c * 4 * q + i, q, stride=4)
            g.append((s_ref[0, ds, :], s_ref[1, ds, :32]))
        tmp[pl.ds(0, q, stride=5), :] = g[0][0]
        for i in range(3):
            lo = 96 - 32 * i
            tmp[pl.ds(i + 1, q, stride=5), :] = jnp.concatenate(
                ([g[i][0][:, 128 - 32 * i :]] if i else []) + [g[i][1], g[i + 1][0][:, :lo]], axis=1
            )
        tmp[pl.ds(4, q, stride=5), :] = jnp.concatenate([g[3][0][:, 32:], g[3][1]], axis=1)
        out_ref[pl.ds(pl.multiple_of(c * 5 * q, 5 * q), 5 * q), :] = tmp[...].astype(BF)


def conv_grads(c, a_ref, g_ref, s_ref, start, gown):
    at = a_ref[...].astype(F32).T.astype(BF)
    for s in range(3):
        gown[s] = own(c, g_ref[s].astype(F32)).astype(BF)
    for t in range(9):
        u = 8 - t
        put_rows(s_ref, start + D * t, nn(at, gown[u % 3, SIDE * (u // 3) : SIDE * (u // 3) + N, :]))


def grads0_kernel(c_ref, noisy, a1, g1, dh0b, dvec, out, s_ref, tmp, gown):
    c = c_ref[0, 0]
    cols = jnp.concatenate([shift_lanes(noisy[...], t) for t in range(9)], axis=0).astype(BF)
    put_rows(s_ref, 0, nn(cols, own(c, dh0b[...].astype(F32)).astype(BF)))
    conv_grads(c, a1, g1, s_ref, 39, gown)
    for i, r in enumerate(VEC0):
        put_rows(s_ref, r, own(c, dvec[i : i + 1, :]))
    roll_rows(s_ref, tmp, out, R0 // 400)


def grads1_kernel(
    c_ref, a2, g2, ntr, dz0b, x1, dq, dk, dv, o, dz1b, x2, dqc, ctx, dkv, oc, dz2b,
    x3, dab, dgb, gl, dz3b, z3b, dh3b, dvec, dgib, dwout, dbout,
    out, s_ref, tmp, gown, o_ref,
):
    c = c_ref[0, 0]
    conv_grads(c, a2, g2, s_ref, C2, gown)

    def pick(v):
        return own(c, v.astype(F32)).astype(BF)

    for x, g, r in ((ntr, dz0b, PI), (o, dz1b, SO), (x2, dqc, CQ), (oc, dz2b, CO), (z3b, dh3b, PO)):
        put_rows(s_ref, r, tn(x[...], pick(g[...])))
    for j, g in enumerate((dq, dk, dv)):
        put_rows(s_ref, QKV + j, tn(x1[...], pick(g[...])), 3)
    for j in range(4):
        put_rows(s_ref, GI + j, tn(x3[...], pick(dab[j])), 8)
        put_rows(s_ref, GI + 4 + j, tn(x3[...], pick(dgb[j])), 8)
        rows = tn(gl[j], pick(dz3b[...]))
        for b in range(2):
            put_rows(s_ref, GO + 640 * b + W * j, rows[W * b : W * (b + 1), :])
    for j in range(2):
        put_rows(s_ref, CKV + j, tn(ctx[...], pick(dkv[j])), 2)
    for i, r in enumerate(VEC1):
        put_rows(s_ref, r, own(c, dvec[i : i + 1, :]))
    put_rows(s_ref, GIB, own(c, dgib[...]))
    wide = jnp.where(c == 0, dwout[:18, :], dwout[18:36, :])
    for ch in range(2):
        for m in range(4):
            piece = wide[9 * ch : 9 * ch + 9, 80 * m : 80 * m + 80]
            o_ref[ch, pl.ds(m, 9, stride=4), :80] = piece
    lane = lax.broadcasted_iota(jnp.int32, (80, W), 0)
    col = lax.broadcasted_iota(jnp.int32, (80, W), 1)
    total = jnp.zeros((36, W), F32)
    for ch in range(2):
        spot = jnp.where(2 * lane + ch == col, 1.0, 0.0)
        total += jnp.dot(o_ref[ch, :36, :80], spot, precision=HI, preferred_element_type=F32)
    put_rows(s_ref, OUT, total)
    b0 = jnp.where(c == 0, dbout[0:1, 0:1], dbout[2:3, 0:1])
    b1 = jnp.where(c == 0, dbout[1:2, 0:1], dbout[3:4, 0:1])
    at = lax.broadcasted_iota(jnp.int32, (1, W), 1)
    put_rows(s_ref, OUTB, jnp.where(at == 0, b0, jnp.where(at == 1, b1, 0.0)))
    s_ref[:, OUTB + 1 :, :] = jnp.zeros((2, 10880 - OUTB - 1, 128), F32)
    roll_rows(s_ref, tmp, out, R1 // 400)


def spread_wide(u, count):
    rep = jnp.repeat(u, 5, axis=1)
    line = jnp.arange(5)[:, None] == (jnp.arange(rep.shape[1]) % 5)[None, :]
    return jnp.where(line[None], rep[:, None, :], 0.0).astype(u.dtype)


FIRST = (0, 0, 1, 2, 3)
SECOND = (0, 1, 2, 3, 3)


def spread_narrow(u):
    s, total = u.shape
    four = u.reshape(s, total // 4, 4)
    out = []
    for picks in (FIRST, SECOND):
        rep = jnp.stack([four[:, :, i] for i in picks], axis=2).reshape(s, -1)
        line = jnp.arange(5)[:, None] == (jnp.arange(rep.shape[1]) % 5)[None, :]
        out.append(jnp.where(line[None], rep[:, None, :], 0.0))
    return jnp.concatenate(out, axis=1).astype(u.dtype)


def lines_wide(g):
    return g.reshape(g.shape[0], 5, 128)


def lines_narrow(g):
    def pad(v, lo, hi):
        return jnp.pad(v, ((0, 0), (lo, hi)))

    a = [g[:, :128], pad(g[:, 128:], 0, 96), pad(g[:, 96:], 0, 64), pad(g[:, 64:], 0, 32), g[:, 32:]]
    b = [jnp.zeros_like(g[:, :128]), pad(g[:, :96], 32, 0), pad(g[:, :64], 64, 0), pad(g[:, :32], 96, 0)]
    return jnp.stack(a + b + [b[0]], axis=1)


def fold_narrow(y):
    def pad(v, lo, hi):
        return jnp.pad(v, (lo, hi))

    return (
        pad(y[0], 0, 32) + pad(y[1, :32], 128, 0) + pad(y[2, :64], 96, 0) + pad(y[3, :96], 64, 0) + pad(y[4], 32, 0)
        + pad(y[6, 32:], 0, 64) + pad(y[7, 64:], 0, 96) + pad(y[8, 96:], 0, 128)
    )


def extend(u, length):
    one = jnp.ones((u.shape[0], 1), u.dtype)
    rest = jnp.zeros((u.shape[0], length - u.shape[1] - 1), u.dtype)
    return jnp.concatenate([u, one, rest], axis=1)


def time_forward(part, steps):
    ladder = jnp.arange(D // 2, dtype=F32)
    freq = jnp.exp(-math.log(10000.0) * ladder / (D // 2))
    angles = steps.astype(F32)[:, None] * freq[None, :]
    e = jnp.concatenate([jnp.cos(angles), jnp.sin(angles)], axis=1).astype(BF)

    def wide(u, start):
        lines = spread_wide(extend(u, u.shape[1] + 1), 5)[0]
        rows = part[:, start : start + lines.shape[1]]
        return jnp.einsum("jr,brl->bjl", lines, rows, preferred_element_type=F32).reshape(1, -1)

    p1 = wide(e, T1)
    u1 = silu(p1).astype(BF)
    p2 = wide(u1, T2)
    u2 = silu(p2).astype(BF)
    lines = spread_narrow(extend(u2, u2.shape[1] + 4))[0]
    y = jnp.einsum("jr,brl->bjl", lines, part[:, T3 : T3 + lines.shape[1]], preferred_element_type=F32)
    tv = jnp.concatenate([fold_narrow(y[0]), fold_narrow(y[1])])[None, :]
    return tv, (e, u1, u2, p1, p2)


def time_backward(part, kept, dtv):
    e, u1, u2, p1, p2 = kept
    count = 4 * D
    g3 = dtv.astype(BF)
    lines = jnp.concatenate([lines_narrow(g3[:, :W]), lines_narrow(g3[:, W:])], axis=0)
    y = jnp.einsum("brl,bjl->rj", part[:, T3 : T3 + 5 * count // 4], lines, preferred_element_type=F32)
    y = y.reshape(count // 4, 5, 10)
    cols = [0.0] * 4
    for j in range(5):
        cols[FIRST[j]] += y[:, j, j]
        cols[SECOND[j]] += y[:, j, 5 + j]
    du2 = jnp.stack(cols, axis=1).reshape(1, count)
    d2 = du2 * silu_slope(p2)
    g2 = d2.astype(BF).reshape(2, 5, 128)
    y = jnp.einsum("brl,bjl->rj", part[:, T2 : T2 + 5 * count], g2, preferred_element_type=F32)
    y = y.reshape(count, 5, 5)
    du1 = jnp.sum(jnp.where(jnp.eye(5, dtype=bool)[None], y, 0.0), axis=(1, 2)).reshape(1, count)
    d1 = du1 * silu_slope(p1)
    return d1, d2, dtv


def time_rows(e, u1, u2, d1, d2, d3, first, count):
    total = jnp.zeros((count, 128), F32)

    def add(total, lines, grads, start):
        room = lines.shape[2]
        flat = lines.reshape(-1, room)
        flat = jnp.pad(flat, ((0, 0), (start, 0)))
        flat = jnp.pad(flat, ((0, 0), (0, max(0, 128 * 112 - flat.shape[1]))))
        mine = lax.dynamic_slice_in_dim(flat, first, count, 1)
        return total + jnp.einsum(
            "kr,kl->rl", mine, grads.reshape(-1, 128), precision=HI, preferred_element_type=F32
        )

    def parts(u, length):
        zero = jnp.zeros_like(u)
        weights = jnp.concatenate([u, jnp.zeros((u.shape[0], length - u.shape[1]), u.dtype)], axis=1)
        biases = jnp.concatenate([zero, jnp.ones((u.shape[0], 1), u.dtype)], axis=1)
        biases = jnp.pad(biases, ((0, 0), (0, length - biases.shape[1])))
        return weights.astype(F32), biases.astype(F32)

    for u, g, start in ((e, d1, T1), (u1, d2, T2)):
        w, b = parts(u, u.shape[1] + 1)
        total = add(total, spread_wide(w, 5), lines_wide(g.astype(BF).astype(F32)), start)
        total = add(total, spread_wide(b, 5), lines_wide(g), start)
    w, b = parts(u2, u2.shape[1] + 4)
    total = add(total, spread_narrow(w), lines_narrow(d3.astype(BF).astype(F32)), T3)
    total = add(total, spread_narrow(b), lines_narrow(d3), T3)
    return total


def alpha_bar(step_ids):
    levels = jnp.arange(1000, dtype=F32)
    lowest, highest = 0.00085**0.5, 0.012**0.5
    beta = jnp.square(lowest + (highest - lowest) * levels / 999.0)
    table = jnp.cumprod(1.0 - beta)
    matches = levels[None, :] == step_ids.astype(F32)[:, None]
    return jnp.sum(jnp.where(matches, table[None, :], 0.0), axis=1)


def shards(params, momentum, ema_params, latents, noise_eps, timesteps, pixel_mask, context):
    c = lax.axis_index(CH)
    d = lax.axis_index(DP)
    n_dp = lax.axis_size(DP)
    rows_dev = params.shape[2]
    rows_all = rows_dev * n_dp
    low = params.astype(BF)
    part0 = lax.all_gather(lax.all_gather(low[:, 0], CH, axis=0, tiled=True), DP, axis=1, tiled=True)
    part1 = lax.all_gather(lax.all_gather(low[:, 1], CH, axis=0, tiled=True), DP, axis=1, tiled=True)

    alpha = alpha_bar(timesteps)[:, None]
    noise = noise_eps[0]
    noisy = jnp.sqrt(alpha) * latents[0] + jnp.sqrt(1.0 - alpha) * noise
    mask = pixel_mask.astype(F32)

    px = (N, D)
    hx = (HEADS, N, HD)
    sh = (3, N + 2 * SIDE, D)
    win, w1, vec0 = kcall(
        unpack0_kernel,
        (sds((36, D), BF), sds((9, D, D), BF), sds((8, D))),
        (part0[:, :R0],),
        (pltpu.VMEM((2, 400, 128), F32), pltpu.VMEM((3, 4 * R0 // 5, 128), F32)),
    )
    mats, kvw, vec1, gib, wout, outb = kcall(
        unpack1_kernel,
        (sds((NMAT, D, D), BF), sds((2, CTX, D), BF), sds((24, D)), sds((8, D)), sds((36, D), BF), sds((1, D))),
        (part1[:, :R1],),
        (pltpu.VMEM((2, 400, 128), F32), pltpu.VMEM((3, 4 * R1 // 5, 128), F32), pltpu.VMEM((2, 40, 128), F32)),
    )
    tv, kept = time_forward(part0, timesteps)
    h0, h1, h2, z0, a1, a2, ntr, x1, q, k, v, stats = kcall(
        front_kernel,
        (sds(px),) * 4 + (sds(px, BF),) * 4 + (sds(hx, BF),) * 3 + (sds((8, D)),),
        (noisy, tv, win, w1, vec0, mats, vec1),
        (pltpu.VMEM(sh, BF), pltpu.VMEM((8, D), F32)),
    )
    o, lse = kcall(
        attend_kernel, (sds(px, BF), sds((HEADS, 1, N))), (q, k, v), (pltpu.VMEM((D, N), F32),)
    )
    z1, z2, h3, x2, x3, oc, z3b, gl, a3, qc, kc, vc, derr, loss, stats_out = kcall(
        back_half_kernel,
        (sds(px),) * 3 + (sds(px, BF),) * 4
        + (sds((4, N, D), BF), sds(px, BF), sds(hx, BF), sds((HEADS, TXT, HD), BF), sds((HEADS, TXT, HD), BF))
        + (sds((LAT, N)), sds((1, 1)), sds((8, D))),
        (o, z0, h2, context[0], noise, mask, mats, kvw, vec1, gib, wout, outb),
        (pltpu.VMEM((8, D), F32), pltpu.VMEM((D, T), F32)),
    )
    dh3, dz1, dh3b, dz3b, dab, dgb, dz2b, dqc, dz1b, dos, dkv, dvec_a, dgib, dwout, dbout = kcall(
        back_one_kernel,
        (sds(px),) * 2 + (sds(px, BF),) * 2 + (sds((4, N, D), BF),) * 2 + (sds(px, BF),) * 3
        + (sds(hx, BF), sds((2, TXT, D), BF), sds((24, D)), sds((8, D)), sds((36, D)), sds((8, 128))),
        (derr, h3, stats_out, a3, z1, z2, x3, qc, kc, vc, mats, vec1, gib, wout),
        (
            pltpu.VMEM(px, F32),
            pltpu.VMEM((8, D), F32),
            pltpu.VMEM((D, T), F32),
            pltpu.VMEM((2, HEADS, TXT, HD), F32),
            pltpu.VMEM((36, N), F32),
        ),
    )
    dq, dk, dv = kcall(
        attend_back_kernel,
        (sds(px, BF),) * 3,
        (q, k, v, dos, lse),
        (pltpu.VMEM((D, N), F32), pltpu.VMEM(hx, F32), pltpu.VMEM(hx, F32)),
    )
    dz0b, g2, g1, dh0b, dvec0, dvec_b, dtv = kcall(
        back_two_kernel,
        (sds(px, BF), sds(sh, BF), sds(sh, BF), sds(px, BF), sds((8, D)), sds((24, D)), sds((1, D))),
        (dq, dk, dv, dz1, dh3, z0, h2, h1, h0, stats, w1, mats, vec0, vec1),
        (pltpu.VMEM(px, F32), pltpu.VMEM(px, F32)),
    )
    which = jnp.full((1, 1), c, jnp.int32)
    flat1 = kcall(
        grads1_kernel,
        sds((R1, 128), BF),
        (which, a2, g2, ntr, dz0b, x1, dq, dk, dv, o, dz1b, x2, dqc, context[0], dkv, oc, dz2b,
         x3, dab, dgb, gl, dz3b, z3b, dh3b, dvec_a + dvec_b, dgib, dwout, dbout),
        (
            pltpu.VMEM((2, 4 * R1 // 5, 128), F32),
            pltpu.VMEM((400, 128), F32),
            pltpu.VMEM((3, N + 2 * SIDE, W), BF),
            pltpu.VMEM((2, 40, 128), F32),
        ),
    )
    flat0 = kcall(
        grads0_kernel,
        sds((R0, 128), BF),
        (which, noisy, a1, g1, dh0b, dvec0),
        (
            pltpu.VMEM((2, 4 * R0 // 5, 128), F32),
            pltpu.VMEM((400, 128), F32),
            pltpu.VMEM((3, N + 2 * SIDE, W), BF),
        ),
    )
    d1, d2, d3 = time_backward(part0, kept, dtv)
    mine = [lax.dynamic_slice_in_dim(g, c * (g.shape[1] // 2), g.shape[1] // 2, 1) for g in (d1, d2, d3)]
    facts = [f.astype(F32) for f in kept[:3]] + mine
    sizes = [f.shape[1] for f in facts]
    everyone = lax.all_gather(jnp.concatenate(facts, axis=1), DP, axis=0, tiled=True)
    facts = []
    at = 0
    for size in sizes:
        facts.append(everyone[:, at : at + size])
        at += size
    grad0 = time_rows(*facts, d * rows_dev, rows_dev)

    step = 16 * n_dp
    front = -(-FRONT // step) * step
    flat1 = jnp.pad(flat1, ((0, rows_all - R1), (0, 0)))
    keep = jnp.arange(front)[:, None] < FRONT
    flat0 = jnp.pad(flat0, ((0, max(0, front - R0)), (0, 0)))[:front]
    flat0 = jnp.where(keep, flat0, 0.0).astype(BF)
    sum1 = lax.psum_scatter(flat1, DP, scatter_dimension=0, tiled=True).astype(F32)
    some0 = lax.psum_scatter(flat0, DP, scatter_dimension=0, tiled=True)
    sum0 = lax.all_gather(some0, DP, axis=0, tiled=True)
    sum0 = jnp.pad(sum0, ((0, rows_all - front), (0, 0)))
    sum0 = lax.dynamic_slice_in_dim(sum0, d * rows_dev, rows_dev, 0).astype(F32)
    grad = jnp.stack([grad0 + sum0, sum1])[None]

    loss_sum, pixel_count = lax.psum((loss[0, 0], jnp.sum(mask)), DP)
    scaled = grad / (LAT * jnp.maximum(pixel_count, 1.0))
    new_momentum = MU * momentum + scaled
    new_params = params - LR * (scaled + MU * new_momentum)
    new_ema = ED * ema_params + (1.0 - ED) * new_params
    return (new_params, new_momentum, new_ema, loss_sum, pixel_count)


def solution(mesh):
    packed = P(CH, None, DP, None)
    row = P(DP, None, None)
    return jax.shard_map(
        shards,
        mesh=mesh,
        in_specs=(packed, packed, packed, row, row, P(DP), P(DP, None), row),
        out_specs=(packed, packed, packed, P(), P()),
        check_vma=False,
    )
```

```python
import math
from functools import partial

import jax
import jax.numpy as jnp
from jax import lax
from jax.experimental import pallas as pl
from jax.experimental.pallas import tpu as pltpu
from jax.sharding import PartitionSpec as P

D = 320
W = 160
HEADS = 8
HD = 40
CTX = 768
TXT = 77
LAT = 4
SIDE = 32
N = 1024
T = 256
EPS = 1e-5
LR = 0.2
MU = 0.9
ED = 0.9
CH = "chan"
DP = "dp"
F32 = jnp.float32
BF = jnp.bfloat16
HI = lax.Precision.HIGHEST
SCALE = HD**-0.5
LOG2E = 1.0 / math.log(2.0)

R0 = 4000
U1, U2, U3 = 2920, 4204, 9328
FRONT = 3650
T1, T2, T3 = 3650, 5255, 11660
C2 = 2
PI = 2885
QKV = 3208
SO = 4168
CQ = 4491
CKV = 4811
CO = 6347
GI = 6670
GIB = 9230
GO = 9238
PO = 10519
OUT = 10842
OUTB = 10878
R1 = 13600
VEC0 = (36, 37, 38, 2919)
VEC1 = (0, 1, 2882, 2883, 2884, 3205, 3206, 3207, 4488, 4489, 4490, 6667, 6668, 6669, 10518, 10839, 10840, 10841)
(N2G, N2B, C2B, NTG, NTB, PIB, L1G, L1B, SOB, L2G, L2B, COB, L3G, L3B, GOB, POB, NOG, NOB) = range(18)
MPI, MQ, MK, MV, MSO, MCQ, MCO, MGV, MGG, MGO, MPO = 9, 10, 11, 12, 13, 14, 15, 16, 20, 24, 28
NMAT = 29


def kcall(body, outs, ins, scratch=()):
    vm = pl.BlockSpec(memory_space=pltpu.VMEM)
    return pl.pallas_call(
        body,
        out_shape=outs,
        in_specs=[vm] * len(ins),
        out_specs=jax.tree.map(lambda _: vm, outs),
        scratch_shapes=list(scratch),
        compiler_params=pltpu.CompilerParams(vmem_limit_bytes=63 * 2**20),
    )(*ins)


def sds(shape, dtype=F32):
    return jax.ShapeDtypeStruct(shape, dtype)


def tiles(fn, size=T, total=N):
    @pl.loop(0, total // size)
    def _(t):
        fn(pl.ds(pl.multiple_of(t * size, size), size))


def nn(a, b):
    return jnp.dot(a, b, preferred_element_type=F32)


def nt(a, b):
    return lax.dot_general(a, b, (((1,), (1,)), ((), ())), preferred_element_type=F32)


def tn(a, b):
    return lax.dot_general(a, b, (((0,), (0,)), ((), ())), preferred_element_type=F32)


def colsum(v):
    return jnp.sum(v, axis=0, keepdims=True)


def unroll_rows(a_ref, flat, s_ref, chunks, rows):
    q = 80
    for b in range(2):
        for t in range(a_ref.shape[1]):
            flat[b, t * rows : (t + 1) * rows, :] = a_ref[b, t, :rows, :].astype(F32)

    @pl.loop(0, chunks)
    def _(c):
        f = [[flat[b, pl.ds(c * 5 * q + j, q, stride=5), :] for j in range(5)] for b in range(2)]
        for i in range(4):
            row = []
            for b in range(2):
                lo = 32 * i
                first, second = f[b][i], f[b][i + 1]
                row += [first[:, lo:], second[:, : lo + 32]] if lo else [first, second[:, :32]]
            full = jnp.concatenate(row, axis=1)
            for k, (lo, hi) in enumerate(((0, 128), (128, 256), (256, 320))):
                s_ref[k, pl.ds(c * 4 * q + i, q, stride=4), : hi - lo] = full[:, lo:hi]


def get_rows(s_ref, start, count, step=1):
    ds = pl.ds(start, count) if step == 1 else pl.ds(start, count, stride=step)
    return jnp.concatenate([s_ref[0, ds, :], s_ref[1, ds, :], s_ref[2, ds, :64]], axis=1)


def unit_row(parts):
    out = [p[:, W * b : W * (b + 1)] for b in range(2) for p in parts]
    return jnp.broadcast_to(jnp.concatenate(out, axis=1), (8, 4 * D))


def unit_parts(row):
    return [
        jnp.concatenate([row[:, W * i : W * (i + 1)], row[:, 640 + W * i : 640 + W * (i + 1)]], axis=1)
        for i in range(4)
    ]


def unpack0_kernel(rows, a_ref, e, win, w1, vec, tw2, tw3, tv, p1, p2, flat, s_ref):
    unroll_rows(a_ref, flat, s_ref, R1 // 400, rows)
    win[...] = get_rows(s_ref, 0, 36).astype(BF)
    for t in range(9):
        w1[t] = get_rows(s_ref, 39 + D * t, D).astype(BF)
    for i, r in enumerate(VEC0):
        vec[i : i + 1, :] = get_rows(s_ref, r, 1)
    for i in range(4):
        tw2[i] = get_rows(s_ref, U2 + i, 4 * D, 4).astype(BF)
    tw3[...] = get_rows(s_ref, U3, 4 * D).astype(BF)
    u = e[...].astype(BF)
    p1[...] = unit_row(
        [nn(u, get_rows(s_ref, U1 + i, D, 4).astype(BF))[:1] + get_rows(s_ref, U1 + 4 * D + i, 1) for i in range(4)]
    )
    u = silu(p1[...]).astype(BF)
    p2[...] = unit_row([nn(u, tw2[i])[:1] + get_rows(s_ref, U2 + 16 * D + i, 1) for i in range(4)])
    u = silu(p2[...]).astype(BF)
    tv[...] = nn(u, tw3[...])[:1] + get_rows(s_ref, U3 + 4 * D, 1)


def time_back_kernel(dtv, tw2, tw3, p1, p2, d1, d2):
    g = jnp.broadcast_to(dtv[...], (8, D)).astype(BF)
    d2[...] = nt(g, tw3[...]) * silu_slope(p2[...])
    total = jnp.zeros((8, 4 * D), F32)
    for i, part in enumerate(unit_parts(d2[...])):
        total += nt(part.astype(BF), tw2[i])
    d1[...] = total * silu_slope(p1[...])


def unpack1_kernel(rows, a_ref, mats, kv, vec, gib, wout, outb, flat, s_ref, o_ref):
    unroll_rows(a_ref, flat, s_ref, R1 // 400, rows)
    for t in range(9):
        mats[t] = get_rows(s_ref, C2 + D * t, D).astype(BF)
    for m, r in ((MPI, PI), (MSO, SO), (MCQ, CQ), (MCO, CO), (MPO, PO)):
        mats[m] = get_rows(s_ref, r, D).astype(BF)
    for j in range(3):
        mats[MQ + j] = get_rows(s_ref, QKV + j, D, 3).astype(BF)
    for j in range(8):
        mats[MGV + j] = get_rows(s_ref, GI + j, D, 8).astype(BF)
    for j in range(4):
        for b in range(2):
            mats[MGO + j, b * W : (b + 1) * W, :] = get_rows(s_ref, GO + 640 * b + W * j, W).astype(BF)
    for j in range(2):
        kv[j] = get_rows(s_ref, CKV + j, CTX, 2).astype(BF)
    for i, r in enumerate(VEC1):
        vec[i : i + 1, :] = get_rows(s_ref, r, 1)
    gib[...] = get_rows(s_ref, GIB, 8)
    outb[...] = get_rows(s_ref, OUTB, 1)
    lane = lax.broadcasted_iota(jnp.int32, (W, W), 0)
    col = lax.broadcasted_iota(jnp.int32, (W, W), 1)
    pick = ((lane % 2) * 80 + lane // 2 == col).astype(BF)
    raw = get_rows(s_ref, OUT, 36).astype(BF)
    for b in range(2):
        moved = nn(raw[:, W * b : W * (b + 1)], pick)
        o_ref[0, :36, :] = moved[:, :128]
        o_ref[1, :36, :32] = moved[:, 128:]
        for ch in range(2):
            pieces = []
            for m in range(4):
                ds = pl.ds(m, 9, stride=4)
                both = jnp.concatenate([o_ref[0, ds, :], o_ref[1, ds, :32]], axis=1)
                pieces.append(both[:, 80 * ch : 80 * ch + 80])
            at = (2 * b + ch) * 9
            wout[at : at + 9, :] = jnp.concatenate(pieces, axis=1).astype(BF)


def pixel_col(n, axis):
    shape = (n, 1) if axis == 0 else (1, n)
    return lax.broadcasted_iota(jnp.int32, shape, axis)


def shift_lanes(v, tap):
    r, s = tap // 3 - 1, tap % 3 - 1
    pix = pixel_col(N, 1)
    i, j = pix // SIDE + r, pix % SIDE + s
    ok = (i >= 0) & (i < SIDE) & (j >= 0) & (j < SIDE)
    move = -(r * SIDE + s) % N
    moved = pltpu.roll(v, move, 1) if move else v
    return jnp.where(ok, moved, 0.0)


def put_shifts(ref, rows, v):
    n = v.shape[0]
    j = pixel_col(n, 0) % SIDE
    at = pl.ds(pl.multiple_of(rows.start + SIDE, SIDE), n)
    ref[0, at, :] = jnp.where(j == 0, 0.0, pltpu.roll(v, 1, 0)).astype(BF)
    ref[1, at, :] = v.astype(BF)
    ref[2, at, :] = jnp.where(j == SIDE - 1, 0.0, pltpu.roll(v, n - 1, 0)).astype(BF)


def clear_margins(ref):
    for s in range(3):
        zero = jnp.zeros((SIDE, ref.shape[2]), BF)
        ref[s, :SIDE, :] = zero
        ref[s, N + SIDE :, :] = zero


def tap_rows(ref, rows, tap):
    at = pl.ds(pl.multiple_of(rows.start + SIDE * (tap // 3), SIDE), T)
    return ref[tap % 3, at, :]


def conv_rows(ref, rows, w_ref):
    total = nn(tap_rows(ref, rows, 0), w_ref[0])
    for tap in range(1, 9):
        total += nn(tap_rows(ref, rows, tap), w_ref[tap])
    return total


def conv_back_rows(ref, rows, w_ref):
    total = nt(tap_rows(ref, rows, 8), w_ref[0])
    for tap in range(1, 9):
        total += nt(tap_rows(ref, rows, 8 - tap), w_ref[tap])
    return total


def group_mean(sums):
    a = lax.broadcasted_iota(jnp.int32, (D, D), 0) // 10
    b = lax.broadcasted_iota(jnp.int32, (D, D), 1) // 10
    pool = jnp.where(a == b, 1.0, 0.0)
    wide = jnp.broadcast_to(sums, (8, D))
    out = jnp.dot(wide, pool, precision=HI, preferred_element_type=F32)
    return out[:1] * (1.0 / (10 * N))


def group_stats(v_ref, acc, sums):
    mean = group_mean(sums)
    acc[0:1, :] = jnp.zeros((1, D), F32)

    def one(rows):
        acc[0:1, :] += colsum(jnp.square(v_ref[rows, :] - mean))

    tiles(one)
    return mean, lax.rsqrt(group_mean(acc[0:1, :]) + EPS)


def silu(v):
    return v * jax.nn.sigmoid(v)


def silu_slope(v):
    sig = jax.nn.sigmoid(v)
    return sig * (1.0 + v * (1.0 - sig))


def layer(v):
    mean = jnp.sum(v, axis=1, keepdims=True) * (1.0 / D)
    sq = jnp.sum(v * v, axis=1, keepdims=True) * (1.0 / D)
    inv = lax.rsqrt(sq - mean * mean + EPS)
    return (v - mean) * inv, inv


def layer_back(grad, normed, inv, gain):
    ghat = grad * gain
    m1 = jnp.sum(ghat, axis=1, keepdims=True) * (1.0 / D)
    m2 = jnp.sum(ghat * normed, axis=1, keepdims=True) * (1.0 / D)
    return inv * (ghat - m1 - normed * m2)


def own(v):
    return jnp.where(lax.axis_index(CH) == 0, v[..., :W], v[..., W:])


def head(v, h):
    return v[:, HD * h : HD * (h + 1)]


def front_kernel(noisy, tv, win, w1, vec0, mats, vec1, h0, h1, h2, z0, a1, a2, ntr, x1, q, k, v, stats, sh, acc):
    cols = jnp.concatenate([shift_lanes(noisy[...], t) for t in range(9)], axis=0).astype(BF)
    acc[...] = jnp.zeros_like(acc)
    clear_margins(sh)
    h = tn(cols, win[...]) + vec0[0:1, :]
    h0[...] = h
    mean, inv = group_stats(h0, acc, colsum(h))
    stats[0:1, :], stats[1:2, :] = mean, inv

    def act(src, dst, gain, bias):
        def one(rows):
            y = silu((src[rows, :] - mean) * inv * gain + bias)
            put_shifts(sh, rows, y)
            dst[rows, :] = y.astype(BF)

        tiles(one)

    act(h0, a1, vec0[1:2, :], vec0[2:3, :])
    acc[1:2, :] = jnp.zeros((1, D), F32)

    def conv1(rows):
        y = conv_rows(sh, rows, w1) + vec0[3:4, :] + tv[...]
        h1[rows, :] = y
        acc[1:2, :] += colsum(y)

    tiles(conv1)
    mean, inv = group_stats(h1, acc, acc[1:2, :])
    stats[2:3, :], stats[3:4, :] = mean, inv
    act(h1, a2, vec1[N2G : N2G + 1, :], vec1[N2B : N2B + 1, :])
    acc[1:2, :] = jnp.zeros((1, D), F32)

    def conv2(rows):
        y = h0[rows, :] + conv_rows(sh, rows, mats) + vec1[C2B : C2B + 1, :]
        h2[rows, :] = y
        acc[1:2, :] += colsum(y)

    tiles(conv2)
    mean, inv = group_stats(h2, acc, acc[1:2, :])
    stats[4:5, :], stats[5:6, :] = mean, inv

    def last(rows):
        n = ((h2[rows, :] - mean) * inv * vec1[NTG : NTG + 1, :] + vec1[NTB : NTB + 1, :]).astype(BF)
        ntr[rows, :] = n
        z = nn(n, mats[MPI]) + vec1[PIB : PIB + 1, :]
        z0[rows, :] = z
        normed, _ = layer(z)
        x = (normed * vec1[L1G : L1G + 1, :] + vec1[L1B : L1B + 1, :]).astype(BF)
        x1[rows, :] = x
        for at, dst in ((MQ, q), (MK, k), (MV, v)):
            y = nn(x, mats[at]).astype(BF)
            for hd in range(HEADS):
                dst[hd, rows, :] = head(y, hd)

    tiles(last)


def attend_kernel(q, k, v, o, lse, ot):
    @pl.loop(0, HEADS)
    def _(h):
        kk = k[h]
        vt = v[h].astype(F32).T.astype(BF)
        for t in range(N // T):
            rows = pl.ds(t * T, T)
            s = nt(kk, q[h, rows, :]) * (SCALE * LOG2E)
            top = jnp.max(s, axis=0, keepdims=True)
            e = jnp.exp2(s - top)
            total = jnp.sum(e, axis=0, keepdims=True)
            lse[h, :, rows] = top + jnp.log(total) * LOG2E
            p = (e * (1.0 / total)).astype(BF)
            ot[pl.ds(pl.multiple_of(h * HD, HD), HD), rows] = nn(vt, p)

    o[...] = ot[...].T.astype(BF)


def cross_head(qh, kh, vh):
    s = nt(kh, qh) * (SCALE * LOG2E)
    e = jnp.exp2(s - jnp.max(s, axis=0, keepdims=True))
    return e * (1.0 / jnp.sum(e, axis=0, keepdims=True))


def back_half_kernel(
    o, z0, h2, ctx, noise, mask, mats, kvw, vec, gib, wout, outb,
    z1, z2, h3, x2, x3, oc, z3b, gl, a3, qc, kc, vc, derr, loss, stats, acc, ot,
):
    acc[...] = jnp.zeros_like(acc)
    kk = nn(ctx[...], kvw[0]).astype(BF)
    vv = nn(ctx[...], kvw[1])
    for h in range(HEADS):
        kc[h] = head(kk, h)
        vc[h] = head(vv, h).astype(BF)
    vt = vv.T

    def trunk(rows):
        z = z0[rows, :] + nn(o[rows, :], mats[MSO]) + vec[SOB : SOB + 1, :]
        z1[rows, :] = z
        normed, _ = layer(z)
        x = (normed * vec[L2G : L2G + 1, :] + vec[L2B : L2B + 1, :]).astype(BF)
        x2[rows, :] = x
        qq = nn(x, mats[MCQ]).astype(BF)
        for h in range(HEADS):
            qh = head(qq, h)
            qc[h, rows, :] = qh
            p = cross_head(qh, kc[h], None).astype(BF)
            ot[HD * h : HD * (h + 1), :] = nn(vt[HD * h : HD * (h + 1), :].astype(BF), p)
        c = ot[...].T.astype(BF)
        oc[rows, :] = c
        z = z + nn(c, mats[MCO]) + vec[COB : COB + 1, :]
        z2[rows, :] = z
        normed, _ = layer(z)
        x = (normed * vec[L3G : L3G + 1, :] + vec[L3B : L3B + 1, :]).astype(BF)
        x3[rows, :] = x
        for j in range(4):
            a = nn(x, mats[MGV + j]) + gib[j : j + 1, :]
            g = nn(x, mats[MGG + j]) + gib[4 + j : 5 + j, :]
            y = (a * (0.5 * g * (1.0 + lax.erf(g * math.sqrt(0.5))))).astype(BF)
            gl[j, rows, :] = y
            z = z + nn(y, mats[MGO + j])
        zb = (z + vec[GOB : GOB + 1, :]).astype(BF)
        z3b[rows, :] = zb
        hh = h2[rows, :] + nn(zb, mats[MPO]) + vec[POB : POB + 1, :]
        h3[rows, :] = hh
        acc[1:2, :] += colsum(hh)

    tiles(trunk)
    mean, inv = group_stats(h3, acc, acc[1:2, :])
    stats[0:1, :], stats[1:2, :] = mean, inv

    def act(rows):
        y = silu((h3[rows, :] - mean) * inv * vec[NOG : NOG + 1, :] + vec[NOB : NOB + 1, :])
        a3[rows, :] = y.astype(BF)

    tiles(act)
    taps = nt(wout[...], a3[...])
    total = jnp.zeros((1,), F32)
    for ch in range(LAT):
        pred = jnp.zeros((1, N), F32)
        for t in range(9):
            pred += shift_lanes(taps[9 * ch + t : 9 * ch + t + 1, :], t)
        at = W * (ch // 2) + ch % 2
        err = pred + outb[0:1, at : at + 1] - noise[ch : ch + 1, :]
        weighed = mask[...] * err
        derr[ch : ch + 1, :] = 2.0 * weighed
        acc[2 + ch : 3 + ch, 0:1] = jnp.sum(weighed * err, axis=1, keepdims=True)
    loss[...] = acc[2:3, 0:1] + acc[3:4, 0:1] + acc[4:5, 0:1] + acc[5:6, 0:1]


def group_back(n_of, grads, gain, dgain, dbias):
    return group_mean(gain * dbias), group_mean(gain * dgain)


def back_one_kernel(
    derr, h3, stats, a3, z1, z2, x3, qc, kc, vc, mats, vec, gib, wout,
    dh3, dz1, dh3b, dz3b, dab, dgb, dz2b, dqc, dz1b, dos, dkv, dvec, dgib, dwout, dbout,
    tmp, acc, ot, kacc, pt,
):
    acc[...] = jnp.zeros_like(acc)
    dgib[...] = jnp.zeros_like(dgib)
    dvec[...] = jnp.zeros_like(dvec)
    kacc[...] = jnp.zeros_like(kacc)
    for ch in range(LAT):
        g = derr[ch : ch + 1, :]
        dbout[ch : ch + 1, :] = jnp.broadcast_to(jnp.sum(g, axis=1, keepdims=True), (1, 128))
        for t in range(9):
            pt[9 * ch + t : 9 * ch + t + 1, :] = shift_lanes(g, 8 - t)
    taps = pt[...].astype(BF)
    dwout[...] = nn(taps, a3[...])
    tmp[...] = tn(taps, wout[...])
    mean, inv = stats[0:1, :], stats[1:2, :]
    gain, bias = vec[NOG : NOG + 1, :], vec[NOB : NOB + 1, :]

    def one(rows):
        n = (h3[rows, :] - mean) * inv
        g = tmp[rows, :] * silu_slope(n * gain + bias)
        tmp[rows, :] = g
        dvec[NOG : NOG + 1, :] += colsum(g * n)
        dvec[NOB : NOB + 1, :] += colsum(g)

    tiles(one)
    m1 = group_mean(gain * dvec[NOB : NOB + 1, :])
    m2 = group_mean(gain * dvec[NOG : NOG + 1, :])

    def trunk(rows):
        n = (h3[rows, :] - mean) * inv
        g = inv * (tmp[rows, :] * gain - m1 - n * m2)
        dh3[rows, :] = g
        dvec[POB : POB + 1, :] += colsum(g)
        gb = g.astype(BF)
        dh3b[rows, :] = own(g).astype(BF)
        dz3 = nt(gb, mats[MPO])
        dvec[GOB : GOB + 1, :] += colsum(dz3)
        zb = dz3.astype(BF)
        dz3b[rows, :] = own(dz3).astype(BF)
        x = x3[rows, :]
        dx = jnp.zeros((T, D), F32)
        for j in range(4):
            a = nn(x, mats[MGV + j]) + gib[j : j + 1, :]
            g = nn(x, mats[MGG + j]) + gib[4 + j : 5 + j, :]
            dgl = nt(zb, mats[MGO + j])
            cdf = 0.5 * (1.0 + lax.erf(g * math.sqrt(0.5)))
            da = dgl * (g * cdf)
            dg = dgl * a * (cdf + g * jnp.exp(-0.5 * g * g) * (1.0 / math.sqrt(2.0 * math.pi)))
            dgib[j : j + 1, :] += colsum(da)
            dgib[4 + j : 5 + j, :] += colsum(dg)
            dab[j, rows, :] = own(da).astype(BF)
            dgb[j, rows, :] = own(dg).astype(BF)
            da, dg = da.astype(BF), dg.astype(BF)
            dx += nt(da, mats[MGV + j]) + nt(dg, mats[MGG + j])
        normed, li = layer(z2[rows, :])
        dvec[L3G : L3G + 1, :] += colsum(dx * normed)
        dvec[L3B : L3B + 1, :] += colsum(dx)
        dz2 = dz3 + layer_back(dx, normed, li, vec[L3G : L3G + 1, :])
        dvec[COB : COB + 1, :] += colsum(dz2)
        zb = dz2.astype(BF)
        dz2b[rows, :] = own(dz2).astype(BF)
        do = nt(zb, mats[MCO]).astype(BF)
        for h in range(HEADS):
            qh, kh, vh, doh = qc[h, rows, :], kc[h], vc[h], head(do, h)
            p = cross_head(qh, kh, vh)
            dp = nt(vh, doh)
            ds = (p * (dp - jnp.sum(p * dp, axis=0, keepdims=True)) * SCALE).astype(BF)
            kacc[0, h] += nn(ds, qh)
            kacc[1, h] += nn(p.astype(BF), doh)
            ot[HD * h : HD * (h + 1), :] = tn(kh, ds)
        dq = ot[...].T
        dqc[rows, :] = own(dq).astype(BF)
        dq = dq.astype(BF)
        dx = nt(dq, mats[MCQ])
        normed, li = layer(z1[rows, :])
        dvec[L2G : L2G + 1, :] += colsum(dx * normed)
        dvec[L2B : L2B + 1, :] += colsum(dx)
        dz = dz2 + layer_back(dx, normed, li, vec[L2G : L2G + 1, :])
        dz1[rows, :] = dz
        dvec[SOB : SOB + 1, :] += colsum(dz)
        zb = dz.astype(BF)
        dz1b[rows, :] = own(dz).astype(BF)
        do = nt(zb, mats[MSO]).astype(BF)
        for h in range(HEADS):
            dos[h, rows, :] = head(do, h)

    tiles(trunk)
    for j in range(2):
        dkv[j] = own(jnp.concatenate([kacc[j, h] for h in range(HEADS)], axis=1)).astype(BF)


def attend_back_kernel(q, k, v, do, lse, dq, dk, dv, qt, kacc, vacc):
    @pl.loop(0, HEADS)
    def _(h):
        kk, vv = k[h], v[h]
        kt = kk.astype(F32).T.astype(BF)
        for t in range(N // T):
            rows = pl.ds(t * T, T)
            qh, doh = q[h, rows, :], do[h, rows, :]
            p = jnp.exp2(nt(kk, qh) * (SCALE * LOG2E) - lse[h, :, rows])
            dp = nt(vv, doh)
            ds = (p * (dp - jnp.sum(p * dp, axis=0, keepdims=True)) * SCALE).astype(BF)
            dkt, dvt = nn(ds, qh), nn(p.astype(BF), doh)
            if t == 0:
                kacc[h], vacc[h] = dkt, dvt
            else:
                kacc[h] += dkt
                vacc[h] += dvt
            qt[pl.ds(pl.multiple_of(h * HD, HD), HD), rows] = nn(kt, ds)

    dq[...] = qt[...].T.astype(BF)

    def one(rows):
        for acc, dst in ((kacc, dk), (vacc, dv)):
            dst[rows, :] = jnp.concatenate([acc[h, rows, :] for h in range(HEADS)], axis=1).astype(BF)

    tiles(one)


def back_two_kernel(
    dq, dk, dv, dz1, dh3, z0, h2, h1, h0, stats, w1, mats, vec0, vec1,
    dz0b, g2o, g1o, dh0b, dvec0, dvec1, dtv,
    tmp, dh, g2, g1,
):
    dvec0[...] = jnp.zeros_like(dvec0)
    dvec1[...] = jnp.zeros_like(dvec1)
    dtv[...] = jnp.zeros_like(dtv)
    for ref in (g1, g2, g1o, g2o):
        clear_margins(ref)

    def trunk(rows):
        dx = nt(dq[rows, :], mats[MQ]) + nt(dk[rows, :], mats[MK]) + nt(dv[rows, :], mats[MV])
        normed, li = layer(z0[rows, :])
        dvec1[L1G : L1G + 1, :] += colsum(dx * normed)
        dvec1[L1B : L1B + 1, :] += colsum(dx)
        dz = dz1[rows, :] + layer_back(dx, normed, li, vec1[L1G : L1G + 1, :])
        dvec1[PIB : PIB + 1, :] += colsum(dz)
        zb = dz.astype(BF)
        dz0b[rows, :] = own(dz).astype(BF)
        g = nt(zb, mats[MPI])
        tmp[rows, :] = g
        n = (h2[rows, :] - stats[4:5, :]) * stats[5:6, :]
        dvec1[NTG : NTG + 1, :] += colsum(g * n)
        dvec1[NTB : NTB + 1, :] += colsum(g)

    tiles(trunk)

    def norm_rows(rows, src, at, gain, m1, m2):
        n = (src[rows, :] - stats[at : at + 1, :]) * stats[at + 1 : at + 2, :]
        return stats[at + 1 : at + 2, :] * (tmp[rows, :] * gain - m1 - n * m2)

    gain = vec1[NTG : NTG + 1, :]
    m1 = group_mean(gain * dvec1[NTB : NTB + 1, :])
    m2 = group_mean(gain * dvec1[NTG : NTG + 1, :])

    def second(rows):
        g = dh3[rows, :] + norm_rows(rows, h2, 4, gain, m1, m2)
        dh[rows, :] = g
        dvec1[C2B : C2B + 1, :] += colsum(g)
        put_shifts(g2, rows, g)
        put_shifts(g2o, rows, own(g))

    tiles(second)
    gain2, bias2 = vec1[N2G : N2G + 1, :], vec1[N2B : N2B + 1, :]

    def conv2(rows):
        n = (h1[rows, :] - stats[2:3, :]) * stats[3:4, :]
        g = conv_back_rows(g2, rows, mats) * silu_slope(n * gain2 + bias2)
        tmp[rows, :] = g
        dvec1[N2G : N2G + 1, :] += colsum(g * n)
        dvec1[N2B : N2B + 1, :] += colsum(g)

    tiles(conv2)
    n1 = group_mean(gain2 * dvec1[N2B : N2B + 1, :])
    n2 = group_mean(gain2 * dvec1[N2G : N2G + 1, :])

    def third(rows):
        g = norm_rows(rows, h1, 2, gain2, n1, n2)
        dtv[...] += colsum(g)
        put_shifts(g1, rows, g)
        put_shifts(g1o, rows, own(g))

    tiles(third)
    gain1, bias1 = vec0[1:2, :], vec0[2:3, :]

    def conv1(rows):
        n = (h0[rows, :] - stats[0:1, :]) * stats[1:2, :]
        g = conv_back_rows(g1, rows, w1) * silu_slope(n * gain1 + bias1)
        tmp[rows, :] = g
        dvec0[1:2, :] += colsum(g * n)
        dvec0[2:3, :] += colsum(g)

    tiles(conv1)
    dvec0[3:4, :] = dtv[...]
    k1 = group_mean(gain1 * dvec0[2:3, :])
    k2 = group_mean(gain1 * dvec0[1:2, :])

    def last(rows):
        g = dh[rows, :] + norm_rows(rows, h0, 0, gain1, k1, k2)
        dvec0[0:1, :] += colsum(g)
        dh0b[rows, :] = own(g).astype(BF)

    tiles(last)


def put_rows(s_ref, start, v, step=1):
    n = v.shape[0]
    ds = pl.ds(start, n) if step == 1 else pl.ds(start, n, stride=step)
    s_ref[0, ds, :] = v[:, :128]
    s_ref[1, ds, :32] = v[:, 128:]


def roll_rows(s_ref, out_ref, lo_chunk, hi_chunk):
    q = 80

    @pl.loop(lo_chunk, hi_chunk)
    def _(c):
        g = []
        for i in range(4):
            ds = pl.ds(c * 4 * q + i, q, stride=4)
            g.append((s_ref[0, ds, :], s_ref[1, ds, :32]))
        base = (c - lo_chunk) * 5 * q
        out_ref[pl.ds(base, q, stride=5), :] = g[0][0]
        for i in range(3):
            lo = 96 - 32 * i
            out_ref[pl.ds(base + i + 1, q, stride=5), :] = jnp.concatenate(
                ([g[i][0][:, 128 - 32 * i :]] if i else []) + [g[i][1], g[i + 1][0][:, :lo]], axis=1
            )
        out_ref[pl.ds(base + 4, q, stride=5), :] = jnp.concatenate([g[3][0][:, 32:], g[3][1]], axis=1)


def by_owner(s_ref, flat, out, total):
    owners, room = math.prod(out.shape[:-2]), out.shape[-2]
    size = room if total < owners * room and len(out.shape) == 3 else min(room, ROWS)
    half = owners // 2 * size
    for lo, hi, first in ((0, min(-(-half // 400), total // 400), 0), (half // 400, total // 400, owners // 2)):
        if hi > lo:
            roll_rows(s_ref, flat, lo, hi)
        at = 400 * max(hi - lo, 0)
        if at < flat.shape[0]:
            flat[at:, :] = jnp.zeros((flat.shape[0] - at, 128), F32)
        for t in range(first, first + owners // 2):
            spot = (t % 2, t // 2) if len(out.shape) == 4 else (t,)
            row = t * size - 400 * lo
            out[(*spot, slice(0, size))] = flat[row : row + size, :].astype(BF)
            if room > size:
                out[(*spot, slice(size, room))] = jnp.zeros((room - size, 128), BF)


def conv_grads(a_ref, g_ref, s_ref, start):
    at = a_ref[...].astype(F32).T.astype(BF)
    for t in range(9):
        u = 8 - t
        put_rows(s_ref, start + D * t, nn(at, g_ref[u % 3, SIDE * (u // 3) : SIDE * (u // 3) + N, :]))


def grads0_kernel(noisy, a1, g1, dh0b, dvec, out, s_ref, flat):
    cols = jnp.concatenate([shift_lanes(noisy[...], t) for t in range(9)], axis=0).astype(BF)
    put_rows(s_ref, 0, nn(cols, dh0b[...]))
    conv_grads(a1, g1, s_ref, 39)
    for i, r in enumerate(VEC0):
        put_rows(s_ref, r, own(dvec[i : i + 1, :]))
    s_ref[:, 4 * FRONT // 5 :, :] = jnp.zeros((2, s_ref.shape[1] - 4 * FRONT // 5, 128), F32)
    by_owner(s_ref, flat, out, R0)


def grads1_kernel(
    a2, g2, ntr, dz0b, x1, dq, dk, dv, o, dz1b, x2, dqc, ctx, dkv, oc, dz2b,
    x3, dab, dgb, gl, dz3b, z3b, dh3b, dvec, dgib, dwout, dbout,
    out, s_ref, flat, o_ref,
):
    c = lax.axis_index(CH)
    conv_grads(a2, g2, s_ref, C2)

    for x, g, r in ((ntr, dz0b, PI), (o, dz1b, SO), (x2, dqc, CQ), (oc, dz2b, CO), (z3b, dh3b, PO)):
        put_rows(s_ref, r, tn(x[...], g[...]))
    for j, g in enumerate((dq, dk, dv)):
        put_rows(s_ref, QKV + j, tn(x1[...], own(g[...].astype(F32)).astype(BF)), 3)
    for j in range(4):
        put_rows(s_ref, GI + j, tn(x3[...], dab[j]), 8)
        put_rows(s_ref, GI + 4 + j, tn(x3[...], dgb[j]), 8)
        rows = tn(gl[j], dz3b[...])
        for b in range(2):
            put_rows(s_ref, GO + 640 * b + W * j, rows[W * b : W * (b + 1), :])
    for j in range(2):
        put_rows(s_ref, CKV + j, tn(ctx[...], dkv[j]), 2)
    for i, r in enumerate(VEC1):
        put_rows(s_ref, r, own(dvec[i : i + 1, :]))
    put_rows(s_ref, GIB, own(dgib[...]))
    wide = jnp.where(c == 0, dwout[:18, :], dwout[18:36, :])
    for ch in range(2):
        for m in range(4):
            piece = wide[9 * ch : 9 * ch + 9, 80 * m : 80 * m + 80]
            o_ref[ch, pl.ds(m, 9, stride=4), :80] = piece
    lane = lax.broadcasted_iota(jnp.int32, (80, W), 0)
    col = lax.broadcasted_iota(jnp.int32, (80, W), 1)
    total = jnp.zeros((36, W), F32)
    for ch in range(2):
        spot = jnp.where(2 * lane + ch == col, 1.0, 0.0)
        total += jnp.dot(o_ref[ch, :36, :80], spot, precision=HI, preferred_element_type=F32)
    put_rows(s_ref, OUT, total)
    b0 = jnp.where(c == 0, dbout[0:1, 0:1], dbout[2:3, 0:1])
    b1 = jnp.where(c == 0, dbout[1:2, 0:1], dbout[3:4, 0:1])
    at = lax.broadcasted_iota(jnp.int32, (1, W), 1)
    put_rows(s_ref, OUTB, jnp.where(at == 0, b0, jnp.where(at == 1, b1, 0.0)))
    s_ref[:, OUTB + 1 :, :] = jnp.zeros((2, 10880 - OUTB - 1, 128), F32)
    by_owner(s_ref, flat, out, R1)


FIRST = (0, 0, 1, 2, 3)
SECOND = (0, 1, 2, 3, 3)


FE, FU1, FU2, FD1, FD2, FD3, FL = 0, 3, 13, 23, 28, 33, 35
FACTS = 40


def time_rows_kernel(first, facts, out):
    count = out.shape[0]
    row = first[0, 0] + lax.broadcasted_iota(jnp.int32, (count, 1), 0)

    def wide(at, n):
        return jnp.concatenate([facts[:, at + i, :] for i in range(n)], axis=1)

    def meets(u, k):
        spot = jnp.where(k == lax.broadcasted_iota(jnp.int32, (1, u.shape[1]), 1), 1.0, 0.0).astype(BF)
        return nt(spot, u.astype(BF))

    total = jnp.zeros((count, 128), F32)
    for u, at, start, size in ((wide(FE, 3)[:, :D], FD1, T1, D), (wide(FU1, 10), FD2, T2, 4 * D)):
        rel = row - start
        k, line = rel // 5, rel % 5
        met = meets(u, jnp.where(rel < 0, -1, k))
        for j in range(5):
            g = facts[:, at + j, :]
            total += nn(jnp.where(line == j, met, 0.0).astype(BF), g.astype(BF))
            total += jnp.where((rel >= 0) & (k == size) & (line == j), colsum(g), 0.0)
    rel = row - T3
    group, line = rel // 5, rel % 5
    d3 = wide(FD3, 2)[:, :W]
    zero = jnp.zeros((d3.shape[0], 128), F32)
    u = wide(FU2, 10)
    for picks, shift in ((FIRST, 0), (SECOND, 1)):
        k = jnp.full_like(rel, -1)
        for j in range(5):
            k = jnp.where((rel >= 0) & (line == j), 4 * group + picks[j], k)
        met = meets(u, k)
        for j in range(5):
            if shift == 0:
                lo = (0, 128, 96, 64, 32)[j]
                g = d3[:, lo : min(lo + 128, W)]
                g = jnp.concatenate([g, zero[:, : 128 - g.shape[1]]], axis=1) if g.shape[1] < 128 else g
            else:
                if j in (0, 4):
                    continue
                g = jnp.concatenate([zero[:, : 32 * j], d3[:, : 128 - 32 * j]], axis=1)
            total += nn(jnp.where(line == j, met, 0.0).astype(BF), g.astype(BF))
            total += jnp.where((k == 4 * D) & (line == j), colsum(g), 0.0)
    out[...] = total


ROWS = 856
SLAB = 864
SOME = 240
CUT = 736


def send(src, dst, sems, i, j, target):
    copy = pltpu.make_async_remote_copy(
        src_ref=src, dst_ref=dst, send_sem=sems[0].at[i], recv_sem=sems[1].at[j],
        device_id={DP: target}, device_id_type=pl.DeviceIdType.MESH,
    )
    copy.start()
    return copy


PIECES = tuple(slice(16 * a, 16 * b) for a, b in ((0, 7), (7, 14), (14, 21), (21, 28), (28, 35), (35, 42), (42, 48), (48, 54)))


def gather_kernel(low, g0, g1, send_sem, recv_sem, keep_sem):
    me, y = lax.axis_index(DP), lax.axis_index(CH)
    k, x, z = me % 2, (me // 2) % 2, me // 4
    core = {DP: me + 1 - 2 * k}
    side = {DP: me + 2 - 4 * x}
    other = {CH: 1 - y}
    ring = [{DP: (me + 4 * o) % 16} for o in range(4)]
    barrier = pltpu.get_barrier_semaphore()
    for target in [core, side, other] + ring[1:]:
        pl.semaphore_signal(barrier, inc=1, device_id=target, device_id_type=pl.DeviceIdType.MESH)
    pl.semaphore_wait(barrier, 6)
    count = [0]
    started = []

    def push(ref, target):
        i = count[0]
        count[0] += 1
        return [start(ref, ref, i, i, target)]

    def start(src, dst, i, j, target):
        copy = pltpu.make_async_remote_copy(
            src_ref=src, dst_ref=dst, send_sem=send_sem.at[i], recv_sem=recv_sem.at[j],
            device_id=target, device_id_type=pl.DeviceIdType.MESH,
        )
        copy.start()
        started.append(copy)
        return copy

    def push_ring(ref):
        i = count[0]
        count[0] += 3
        return [start(ref, ref, i + o - 1, i + 3 - o, ring[o]) for o in (2, 1, 3)]

    def arrive(copies):
        for copy in copies:
            copy.wait_recv()

    keeps = []
    for p, g in enumerate((g0, g1)):
        keep = pltpu.make_async_copy(low.at[p], g.at[y, z, x, k], keep_sem.at[p])
        keep.start()
        keeps.append(keep)
    work = [(p, g, rows, i % 2) for p, g in enumerate((g0, g1)) for i, rows in enumerate(PIECES)]
    first, second, third, last = {}, {}, {}, []

    def begin(i):
        p, g, rows, _ = work[i]
        if i % len(PIECES) == 0:
            keeps[p].wait()
        first[i] = push_ring(g.at[y, z, x, k, rows])

    def middle(i):
        _, g, rows, turn = work[i]
        arrive(first[i])
        second[i] = push(g.at[y, :, x, k, rows], other if turn else side)
        last.extend(push(g.at[y, :, x, k, rows], core))

    def finish(i):
        _, g, rows, turn = work[i]
        arrive(second[i])
        if turn:
            third[i] = push(g.at[:, :, x, k, rows], side)
            last.extend(push(g.at[1 - y, :, x, k, rows], core))
        else:
            third[i] = push(g.at[y, :, :, k, rows], other)
            last.extend(push(g.at[y, :, 1 - x, k, rows], core))

    def pass_on(i):
        _, g, rows, turn = work[i]
        arrive(third[i])
        last.extend(push(g.at[:, :, 1 - x, k, rows] if turn else g.at[1 - y, :, :, k, rows], core))

    ahead = 4
    for i in range(ahead):
        begin(i)
    for i in range(len(work) + 2):
        if i < len(work):
            middle(i)
            if i + ahead < len(work):
                begin(i + ahead)
        if 0 <= i - 1 < len(work):
            finish(i - 1)
        if 0 <= i - 3 < len(work):
            pass_on(i - 3)
    pass_on(len(work) - 1)
    arrive(last)
    for copy in started:
        copy.wait_send()


def gather_weights(low):
    hbm = pl.BlockSpec(memory_space=pl.ANY)
    whole = sds((2, 4, 2, 2, SLAB, 128), BF)
    dma = pltpu.SemaphoreType.DMA
    return pl.pallas_call(
        gather_kernel,
        out_shape=(whole, whole),
        in_specs=[hbm],
        out_specs=(hbm, hbm),
        scratch_shapes=[dma((128,)), dma((128,)), dma((2,))],
        compiler_params=pltpu.CompilerParams(collective_id=2, has_side_effects=True),
    )(low)


def add_up(*terms):
    total = terms[0].astype(F32)
    for term in terms[1:]:
        total += term.astype(F32)
    return total


def reduce_kernel(
    p1, p0, facts, sum1, sum0, all_facts,
    r1, sa, sb, rax, rbz, ta, raz, tb, rbx, some, land, fx, send_sem, recv_sem, fsend, frecv, gsend, grecv,
):
    me = lax.axis_index(DP)
    k, x, z = me % 2, (me // 2) % 2, me // 4
    barrier = pltpu.get_barrier_semaphore()
    for o in range(1, 16):
        pl.semaphore_signal(barrier, inc=1, device_id={DP: (me + o) % 16}, device_id_type=pl.DeviceIdType.MESH)
    pl.semaphore_wait(barrier, 15)
    sems = (send_sem, recv_sem)
    core = me + 1 - 2 * k
    side = me + 2 - 4 * x
    other = 1 - k
    first = [
        send(p1.at[other, :, :CUT], r1.at[:, :CUT], sems, 0, 0, core),
        send(p1.at[other, :, CUT:], r1.at[:, CUT:SLAB], sems, 1, 1, core),
        send(p0.at[other], r1.at[:, SLAB:], sems, 2, 2, core),
    ]
    fact_copies = [send(facts, fx.at[me], (fsend, frecv), o - 1, o - 1, (me + o) % 16) for o in range(1, 16)]
    first[0].wait_recv()
    for m in range(8):
        sa[m % 2, m // 2] = add_up(p1[k, m, :CUT], r1[m, :CUT]).astype(BF)
    ax = send(sa.at[1 - x], rax, sems, 3, 3, side)
    first[1].wait_recv()
    first[2].wait_recv()
    for m in range(8):
        sb[m // 2, m % 2, : SLAB - CUT] = add_up(p1[k, m, CUT:], r1[m, CUT:SLAB]).astype(BF)
        sb[m // 2, m % 2, SLAB - CUT :] = add_up(p0[k, m], r1[m, SLAB:]).astype(BF)
    bz = [send(sb.at[(z + o) % 4], rbz.at[3 - o], sems, 3 + o, 7 - o, (me + 4 * o) % 16) for o in (2, 1, 3)]
    ax.wait_recv()
    for m in range(4):
        ta[m] = add_up(sa[x, m], rax[m]).astype(BF)
    az = [send(ta.at[(z + o) % 4], raz.at[3 - o], sems, 6 + o, 10 - o, (me + 4 * o) % 16) for o in (2, 1, 3)]
    for copy in bz:
        copy.wait_recv()
    for m in range(2):
        tb[m] = add_up(sb[z, m], rbz[0, m], rbz[1, m], rbz[2, m]).astype(BF)
    bx = send(tb.at[1 - x], rbx, sems, 10, 10, side)
    bx.wait_recv()
    last = add_up(tb[x], rbx[...])
    sum1[CUT:, :] = last[: 856 - CUT]
    some[...] = last[SLAB - CUT :]
    fx[me] = facts[...]

    @pl.when(me > 0)
    def _():
        @pl.loop(0, SOME // 8)
        def _(g):
            row = SOME * me + 8 * g
            owner = row // ROWS
            at = pl.multiple_of(row - ROWS * owner, 8)
            pltpu.make_async_remote_copy(
                src_ref=some.at[pl.ds(pl.multiple_of(8 * g, 8), 8)], dst_ref=land.at[pl.ds(at, 8)],
                send_sem=gsend, recv_sem=grecv, device_id={DP: owner}, device_id_type=pl.DeviceIdType.MESH,
            ).start()

    for copy in az:
        copy.wait_recv()
    sum1[:CUT, :] = add_up(ta[z], raz[0], raz[1], raz[2])
    for copy in fact_copies:
        copy.wait_recv()
    all_facts[...] = fx[...]

    def landed(lo, hi):
        part = land.at[lo:hi]
        pltpu.make_async_remote_copy(
            src_ref=part, dst_ref=part, send_sem=gsend, recv_sem=grecv,
            device_id={DP: me}, device_id_type=pl.DeviceIdType.MESH,
        ).wait_recv()
        sum0[lo:hi, :] = land[lo:hi, :]

    @pl.when(me == 0)
    def _():
        landed(SOME, ROWS)
        sum0[:SOME, :] = some[...]

    @pl.when((me > 0) & (me < 4))
    def _():
        landed(0, ROWS)

    @pl.when(me == 4)
    def _():
        landed(0, 16 * SOME - 4 * ROWS)
        sum0[16 * SOME - 4 * ROWS :, :] = jnp.zeros((5 * ROWS - 16 * SOME, 128), F32)

    @pl.when(me > 4)
    def _():
        sum0[...] = jnp.zeros_like(sum0)

    @pl.when(me > 0)
    def _():
        pltpu.make_async_remote_copy(
            src_ref=some, dst_ref=some, send_sem=gsend, recv_sem=grecv,
            device_id={DP: me}, device_id_type=pl.DeviceIdType.MESH,
        ).wait_send()

    for copy in first + [ax] + bz + az + [bx] + fact_copies:
        copy.wait_send()


def sum_over_samples(p1, p0, facts):
    vm = pl.BlockSpec(memory_space=pltpu.VMEM)
    dma = pltpu.SemaphoreType.DMA
    return pl.pallas_call(
        reduce_kernel,
        out_shape=(sds((ROWS, 128)), sds((ROWS, 128)), sds((16, FACTS, 128))),
        in_specs=[vm] * 3,
        out_specs=(vm,) * 3,
        scratch_shapes=[
            pltpu.VMEM((8, SLAB + SOME, 128), BF),
            pltpu.VMEM((2, 4, CUT, 128), BF),
            pltpu.VMEM((4, 2, SLAB + SOME - CUT, 128), BF),
            pltpu.VMEM((4, CUT, 128), BF),
            pltpu.VMEM((3, 2, SLAB + SOME - CUT, 128), BF),
            pltpu.VMEM((4, CUT, 128), BF),
            pltpu.VMEM((3, CUT, 128), BF),
            pltpu.VMEM((2, SLAB + SOME - CUT, 128), BF),
            pltpu.VMEM((SLAB + SOME - CUT, 128), BF),
            pltpu.VMEM((SOME, 128), F32),
            pltpu.VMEM((ROWS, 128), F32),
            pltpu.VMEM((16, FACTS, 128), F32),
            dma((11,)),
            dma((11,)),
            dma((15,)),
            dma((15,)),
            dma,
            dma,
        ],
        compiler_params=pltpu.CompilerParams(
            collective_id=1, has_side_effects=True, vmem_limit_bytes=40 * 2**20
        ),
    )(p1, p0, facts)


def time_features(steps):
    ladder = jnp.arange(D // 2, dtype=F32)
    freq = jnp.exp(-math.log(10000.0) * ladder / (D // 2))
    angles = steps.astype(F32)[:, None] * freq[None, :]
    return jnp.concatenate([jnp.cos(angles), jnp.sin(angles)], axis=1)


def rounded_silu(v):
    return silu(v).astype(BF).astype(F32)


def alpha_bar(step_ids):
    levels = jnp.arange(1000, dtype=F32)
    lowest, highest = 0.00085**0.5, 0.012**0.5
    beta = jnp.square(lowest + (highest - lowest) * levels / 999.0)
    table = jnp.cumprod(1.0 - beta)
    matches = levels[None, :] == step_ids.astype(F32)[:, None]
    return jnp.sum(jnp.where(matches, table[None, :], 0.0), axis=1)


def shards(params, momentum, ema_params, latents, noise_eps, timesteps, pixel_mask, context):
    c = lax.axis_index(CH)
    d = lax.axis_index(DP)
    n_dp = lax.axis_size(DP)
    rows_dev = params.shape[2]
    rows_all = rows_dev * n_dp
    quick = n_dp == 16 and rows_dev == ROWS
    low = params[0].astype(BF)
    if quick:
        part0, part1 = gather_weights(jnp.pad(low, ((0, 0), (0, SLAB - ROWS), (0, 0))))
        part0, part1 = part0.reshape(2, 16, SLAB, 128), part1.reshape(2, 16, SLAB, 128)
    else:
        part0, part1 = (lax.all_gather(lax.all_gather(low[i], CH, axis=0), DP, axis=1) for i in range(2))

    alpha = alpha_bar(timesteps)[:, None]
    noise = noise_eps[0]
    noisy = jnp.sqrt(alpha) * latents[0] + jnp.sqrt(1.0 - alpha) * noise
    mask = pixel_mask.astype(F32)

    px = (N, D)
    hp = (N, W)
    hx = (HEADS, N, HD)
    sh = (3, N + 2 * SIDE, D)
    e = time_features(timesteps)
    flat = pltpu.VMEM((2, rows_all, 128), F32)
    unrolled = pltpu.VMEM((3, 4 * R1 // 5, 128), F32)
    units = sds((8, 4 * D))
    win, w1, vec0, tw2, tw3, tv, p1, p2 = kcall(
        partial(unpack0_kernel, rows_dev),
        (sds((36, D), BF), sds((9, D, D), BF), sds((8, D)), sds((4, 4 * D, D), BF), sds((4 * D, D), BF), sds((1, D)))
        + (units, units),
        (part0, jnp.broadcast_to(e, (8, D))),
        (flat, unrolled),
    )
    mats, kvw, vec1, gib, wout, outb = kcall(
        partial(unpack1_kernel, rows_dev),
        (sds((NMAT, D, D), BF), sds((2, CTX, D), BF), sds((24, D)), sds((8, D)), sds((36, D), BF), sds((1, D))),
        (part1,),
        (flat, unrolled, pltpu.VMEM((2, 40, 128), F32)),
    )
    h0, h1, h2, z0, a1, a2, ntr, x1, q, k, v, stats = kcall(
        front_kernel,
        (sds(px),) * 4 + (sds(px, BF),) * 4 + (sds(hx, BF),) * 3 + (sds((8, D)),),
        (noisy, tv, win, w1, vec0, mats, vec1),
        (pltpu.VMEM(sh, BF), pltpu.VMEM((8, D), F32)),
    )
    o, lse = kcall(
        attend_kernel, (sds(px, BF), sds((HEADS, 1, N))), (q, k, v), (pltpu.VMEM((D, N), F32),)
    )
    z1, z2, h3, x2, x3, oc, z3b, gl, a3, qc, kc, vc, derr, loss, stats_out = kcall(
        back_half_kernel,
        (sds(px),) * 3 + (sds(px, BF),) * 4
        + (sds((4, N, D), BF), sds(px, BF), sds(hx, BF), sds((HEADS, TXT, HD), BF), sds((HEADS, TXT, HD), BF))
        + (sds((LAT, N)), sds((1, 1)), sds((8, D))),
        (o, z0, h2, context[0], noise, mask, mats, kvw, vec1, gib, wout, outb),
        (pltpu.VMEM((8, D), F32), pltpu.VMEM((D, T), F32)),
    )
    dh3, dz1, dh3b, dz3b, dab, dgb, dz2b, dqc, dz1b, dos, dkv, dvec_a, dgib, dwout, dbout = kcall(
        back_one_kernel,
        (sds(px),) * 2 + (sds(hp, BF),) * 2 + (sds((4, N, W), BF),) * 2 + (sds(hp, BF),) * 3
        + (sds(hx, BF), sds((2, TXT, W), BF), sds((24, D)), sds((8, D)), sds((36, D)), sds((8, 128))),
        (derr, h3, stats_out, a3, z1, z2, x3, qc, kc, vc, mats, vec1, gib, wout),
        (
            pltpu.VMEM(px, F32),
            pltpu.VMEM((8, D), F32),
            pltpu.VMEM((D, T), F32),
            pltpu.VMEM((2, HEADS, TXT, HD), F32),
            pltpu.VMEM((36, N), F32),
        ),
    )
    dq, dk, dv = kcall(
        attend_back_kernel,
        (sds(px, BF),) * 3,
        (q, k, v, dos, lse),
        (pltpu.VMEM((D, N), F32), pltpu.VMEM(hx, F32), pltpu.VMEM(hx, F32)),
    )
    dz0b, g2, g1, dh0b, dvec0, dvec_b, dtv = kcall(
        back_two_kernel,
        (sds(hp, BF), sds(sh[:2] + (W,), BF), sds(sh[:2] + (W,), BF), sds(hp, BF), sds((8, D)), sds((24, D)), sds((1, D))),
        (dq, dk, dv, dz1, dh3, z0, h2, h1, h0, stats, w1, mats, vec0, vec1),
        (pltpu.VMEM(px, F32), pltpu.VMEM(px, F32), pltpu.VMEM(sh, BF), pltpu.VMEM(sh, BF)),
    )
    step = 16 * n_dp
    front = -(-FRONT // step) * step
    lead = (2, 8) if quick else (n_dp,)
    own1 = kcall(
        grads1_kernel,
        sds(lead + (SLAB if quick else rows_dev, 128), BF),
        (a2, g2, ntr, dz0b, x1, dq, dk, dv, o, dz1b, x2, dqc, context[0], dkv, oc, dz2b,
         x3, dab, dgb, gl, dz3b, z3b, dh3b, dvec_a + dvec_b, dgib, dwout, dbout),
        (
            pltpu.VMEM((2, 4 * R1 // 5, 128), F32),
            pltpu.VMEM((7600, 128), F32),
            pltpu.VMEM((2, 40, 128), F32),
        ),
    )
    own0 = kcall(
        grads0_kernel,
        sds(lead + (front // n_dp, 128), BF),
        (noisy, a1, g1, dh0b, dvec0),
        (
            pltpu.VMEM((2, 4 * R0 // 5, 128), F32),
            pltpu.VMEM((2600, 128), F32),
        ),
    )
    d1, d2 = kcall(time_back_kernel, (units, units), (dtv, tw2, tw3, p1, p2))
    mine = [lax.dynamic_slice_in_dim(g[0], c * (g.shape[1] // 2), g.shape[1] // 2, 0) for g in (d1, d2, dtv)]
    e, u1, u2 = e[0].astype(BF).astype(F32), rounded_silu(p1[0]), rounded_silu(p2[0])
    facts = jnp.concatenate(
        [e, jnp.zeros((64,), F32), u1, u2, *mine, jnp.zeros((96,), F32), loss[0], jnp.sum(mask, axis=1)]
    )
    facts = jnp.pad(facts, (0, FACTS * 128 - facts.shape[0])).reshape(FACTS, 128)
    if quick:
        sum1, sum0, all_facts = sum_over_samples(own1, own0, facts)
    else:
        sum1 = lax.psum_scatter(own1, DP, scatter_dimension=0).astype(F32)
        sum0 = lax.all_gather(lax.psum_scatter(own0, DP, scatter_dimension=0), DP, axis=0, tiled=True)
        sum0 = jnp.pad(sum0, ((0, rows_all - front), (0, 0)))
        sum0 = lax.dynamic_slice_in_dim(sum0, d * rows_dev, rows_dev, 0).astype(F32)
        all_facts = lax.all_gather(facts, DP, axis=0)
    grad0 = kcall(
        time_rows_kernel, sds((rows_dev, 128)), (jnp.full((1, 1), d * rows_dev, jnp.int32), all_facts)
    )
    grad = jnp.stack([grad0 + sum0, sum1])[None]
    loss_sum = jnp.sum(all_facts[:, FL, 0])
    pixel_count = jnp.sum(all_facts[:, FL, 1])
    scaled = grad / (LAT * jnp.maximum(pixel_count, 1.0))
    new_momentum = MU * momentum + scaled
    new_params = params - LR * (scaled + MU * new_momentum)
    new_ema = ED * ema_params + (1.0 - ED) * new_params
    return (new_params, new_momentum, new_ema, loss_sum, pixel_count)


def solution(mesh):
    packed = P(CH, None, DP, None)
    row = P(DP, None, None)
    return jax.shard_map(
        shards,
        mesh=mesh,
        in_specs=(packed, packed, packed, row, row, P(DP), P(DP, None), row),
        out_specs=(packed, packed, packed, P(), P()),
        check_vma=False,
    )
```

```python
import math
from functools import partial

import jax
import jax.numpy as jnp
from jax import lax
from jax.experimental import pallas as pl
from jax.experimental.pallas import tpu as pltpu
from jax.sharding import PartitionSpec as P

D = 320
W = 160
HEADS = 8
HD = 40
CTX = 768
TXT = 77
LAT = 4
SIDE = 32
N = 1024
EPS = 1e-5
LR = 0.2
MU = 0.9
ED = 0.9
CH = "chan"
DP = "dp"
F32 = jnp.float32
BF = jnp.bfloat16
HI = lax.Precision.HIGHEST
SCALE = HD**-0.5
LOG2E = 1.0 / math.log(2.0)

R0 = 4000
U1, U2, U3 = 2920, 4204, 9328
FRONT = 3650
T1, T2, T3 = 3650, 5255, 11660
C2 = 2
PI = 2885
QKV = 3208
SO = 4168
CQ = 4491
CKV = 4811
CO = 6347
GI = 6670
GIB = 9230
GO = 9238
PO = 10519
OUT = 10842
OUTB = 10878
R1 = 13600
VEC0 = (36, 37, 38, 2919)
VEC1 = (0, 1, 2882, 2883, 2884, 3205, 3206, 3207, 4488, 4489, 4490, 6667, 6668, 6669, 10518, 10839, 10840, 10841)
(N2G, N2B, C2B, NTG, NTB, PIB, L1G, L1B, SOB, L2G, L2B, COB, L3G, L3B, GOB, POB, NOG, NOB) = range(18)
MPI, MQ, MK, MV = range(4)
MSO, MCQ, MCO, MPO, MGV, MGG, MGO = 0, 1, 2, 3, 4, 8, 12


def kcall(body, outs, ins, scratch=()):
    vm = pl.BlockSpec(memory_space=pltpu.VMEM)
    return pl.pallas_call(
        body,
        out_shape=outs,
        in_specs=[vm] * len(ins),
        out_specs=jax.tree.map(lambda _: vm, outs),
        scratch_shapes=list(scratch),
        compiler_params=pltpu.CompilerParams(vmem_limit_bytes=63 * 2**20),
    )(*ins)


def sds(shape, dtype=F32):
    return jax.ShapeDtypeStruct(shape, dtype)


def tiles(fn, size=256, total=N):
    for t in range(total // size):
        fn(pl.ds(t * size, size))


def nn(a, b):
    return jnp.dot(a, b, preferred_element_type=F32)


def nt(a, b):
    return lax.dot_general(a, b, (((1,), (1,)), ((), ())), preferred_element_type=F32)


def tn(a, b):
    return lax.dot_general(a, b, (((0,), (0,)), ((), ())), preferred_element_type=F32)


def colsum(v):
    return jnp.sum(v, axis=0, keepdims=True)


def unroll_rows(a_ref, flat, s_ref, chunks, rows):
    q = 80
    for b in range(2):
        for t in range(a_ref.shape[1]):
            flat[b, t * rows : (t + 1) * rows, :] = a_ref[b, t, :rows, :].astype(F32)

    @pl.loop(0, chunks)
    def _(c):
        f = [[flat[b, pl.ds(c * 5 * q + j, q, stride=5), :] for j in range(5)] for b in range(2)]
        for i in range(4):
            row = []
            for b in range(2):
                lo = 32 * i
                first, second = f[b][i], f[b][i + 1]
                row += [first[:, lo:], second[:, : lo + 32]] if lo else [first, second[:, :32]]
            full = jnp.concatenate(row, axis=1)
            for k, (lo, hi) in enumerate(((0, 128), (128, 256), (256, 320))):
                s_ref[k, pl.ds(c * 4 * q + i, q, stride=4), : hi - lo] = full[:, lo:hi]


def get_rows(s_ref, start, count, step=1):
    ds = pl.ds(start, count) if step == 1 else pl.ds(start, count, stride=step)
    return jnp.concatenate([s_ref[0, ds, :], s_ref[1, ds, :], s_ref[2, ds, :64]], axis=1)


def put_taps(s_ref, start, w, back):
    for r in range(3):
        taps = [get_rows(s_ref, start + D * (3 * r + i), D).astype(BF) for i in range(3)]
        for i in range(3):
            w[r, D * i : D * (i + 1), :] = taps[i]
        back[r] = jnp.concatenate(taps[::-1], axis=1)


def unit_row(parts):
    out = [p[:, W * b : W * (b + 1)] for b in range(2) for p in parts]
    return jnp.broadcast_to(jnp.concatenate(out, axis=1), (8, 4 * D))


def unit_parts(row):
    return [
        jnp.concatenate([row[:, W * i : W * (i + 1)], row[:, 640 + W * i : 640 + W * (i + 1)]], axis=1)
        for i in range(4)
    ]


def unpack0_kernel(rows, a_ref, e, win, w1, w1b, vec, tw2, tw3, tv, p1, p2, flat, s_ref):
    unroll_rows(a_ref, flat, s_ref, R1 // 400, rows)
    win[...] = get_rows(s_ref, 0, 36).astype(BF)
    put_taps(s_ref, 39, w1, w1b)
    for i, r in enumerate(VEC0):
        vec[i : i + 1, :] = get_rows(s_ref, r, 1)
    for i in range(4):
        tw2[i] = get_rows(s_ref, U2 + i, 4 * D, 4).astype(BF)
    tw3[...] = get_rows(s_ref, U3, 4 * D).astype(BF)
    u = e[...].astype(BF)
    p1[...] = unit_row(
        [nn(u, get_rows(s_ref, U1 + i, D, 4).astype(BF))[:1] + get_rows(s_ref, U1 + 4 * D + i, 1) for i in range(4)]
    )
    u = silu(p1[...]).astype(BF)
    p2[...] = unit_row([nn(u, tw2[i])[:1] + get_rows(s_ref, U2 + 16 * D + i, 1) for i in range(4)])
    u = silu(p2[...]).astype(BF)
    tv[...] = nn(u, tw3[...])[:1] + get_rows(s_ref, U3 + 4 * D, 1)


FE, FU1, FU2, FD1, FD2, FD3, FL = 0, 3, 13, 23, 28, 33, 35
FACTS = 40


def time_back_kernel(dtv, tw2, tw3, p1, p2, e, mask, loss, facts):
    first = lax.axis_index(CH) == 0
    g = jnp.broadcast_to(dtv[...], (8, D)).astype(BF)
    d2 = nt(g, tw3[...]) * silu_slope(p2[...])
    total = jnp.zeros((8, 4 * D), F32)
    for i, part in enumerate(unit_parts(d2)):
        total += nt(part.astype(BF), tw2[i])
    d1 = total * silu_slope(p1[...])
    facts[...] = jnp.zeros_like(facts)

    def put(at, v):
        for i in range(0, v.shape[1], 128):
            n = min(128, v.shape[1] - i)
            facts[at + i // 128 : at + i // 128 + 1, :n] = v[:1, i : i + n]

    put(FE, e[...].astype(BF).astype(F32))
    put(FU1, silu(p1[...]).astype(BF).astype(F32))
    put(FU2, silu(p2[...]).astype(BF).astype(F32))
    put(FD1, jnp.where(first, d1[:, : 2 * D], d1[:, 2 * D :]))
    put(FD2, jnp.where(first, d2[:, : 2 * D], d2[:, 2 * D :]))
    put(FD3, own(dtv[...]))
    facts[FL : FL + 1, 0:1] = loss[...]
    facts[FL : FL + 1, 1:2] = jnp.sum(mask[...].astype(F32), axis=1, keepdims=True)


def unpack1_kernel(rows, a_ref, c2, c2b, tr, mats, kv, vec, gib, wout, outb, flat, s_ref, o_ref):
    unroll_rows(a_ref, flat, s_ref, R1 // 400, rows)
    put_taps(s_ref, C2, c2, c2b)
    tr[MPI] = get_rows(s_ref, PI, D).astype(BF)
    for m, r in ((MSO, SO), (MCQ, CQ), (MCO, CO), (MPO, PO)):
        mats[m] = get_rows(s_ref, r, D).astype(BF)
    for j in range(3):
        tr[MQ + j] = get_rows(s_ref, QKV + j, D, 3).astype(BF)
    for j in range(8):
        mats[MGV + j] = get_rows(s_ref, GI + j, D, 8).astype(BF)
    for j in range(4):
        for b in range(2):
            mats[MGO + j, b * W : (b + 1) * W, :] = get_rows(s_ref, GO + 640 * b + W * j, W).astype(BF)
    for j in range(2):
        kv[j] = get_rows(s_ref, CKV + j, CTX, 2).astype(BF)
    for i, r in enumerate(VEC1):
        vec[i : i + 1, :] = get_rows(s_ref, r, 1)
    gib[...] = get_rows(s_ref, GIB, 8)
    outb[...] = get_rows(s_ref, OUTB, 1)
    lane = lax.broadcasted_iota(jnp.int32, (W, W), 0)
    col = lax.broadcasted_iota(jnp.int32, (W, W), 1)
    pick = ((lane % 2) * 80 + lane // 2 == col).astype(BF)
    raw = get_rows(s_ref, OUT, 36).astype(BF)
    for b in range(2):
        moved = nn(raw[:, W * b : W * (b + 1)], pick)
        o_ref[0, :36, :] = moved[:, :128]
        o_ref[1, :36, :32] = moved[:, 128:]
        for ch in range(2):
            pieces = []
            for m in range(4):
                ds = pl.ds(m, 9, stride=4)
                both = jnp.concatenate([o_ref[0, ds, :], o_ref[1, ds, :32]], axis=1)
                pieces.append(both[:, 80 * ch : 80 * ch + 80])
            at = (2 * b + ch) * 9
            wout[at : at + 9, :] = jnp.concatenate(pieces, axis=1).astype(BF)


def pixel_col(n, axis):
    shape = (n, 1) if axis == 0 else (1, n)
    return lax.broadcasted_iota(jnp.int32, shape, axis)


def shift_lanes(v, tap):
    r, s = tap // 3 - 1, tap % 3 - 1
    pix = pixel_col(N, 1)
    i, j = pix // SIDE + r, pix % SIDE + s
    ok = (i >= 0) & (i < SIDE) & (j >= 0) & (j < SIDE)
    move = -(r * SIDE + s) % N
    moved = pltpu.roll(v, move, 1) if move else v
    return jnp.where(ok, moved, 0.0)


def put_shifts(ref, v):
    j = pixel_col(N, 0) % SIDE
    left = jnp.where(j == 0, 0.0, pltpu.roll(v, 1, 0)).astype(BF)
    right = jnp.where(j == SIDE - 1, 0.0, pltpu.roll(v, N - 1, 0)).astype(BF)
    ref[SIDE : SIDE + N, :] = jnp.concatenate([left, v.astype(BF), right], axis=1)


def clear_margins(ref):
    zero = jnp.zeros((SIDE, ref.shape[1]), BF)
    ref[:SIDE, :] = zero
    ref[SIDE + N :, :] = zero


def conv_rows(ref, w_ref):
    return sum(nn(ref[SIDE * r : SIDE * r + N, :], w_ref[r]) for r in range(3))


def conv_back_rows(ref, w_ref):
    return sum(nt(ref[SIDE * (2 - r) : SIDE * (2 - r) + N, :], w_ref[r]) for r in range(3))


def group_mean(sums):
    a = lax.broadcasted_iota(jnp.int32, (D, D), 0) // 10
    b = lax.broadcasted_iota(jnp.int32, (D, D), 1) // 10
    pool = jnp.where(a == b, 1.0, 0.0)
    wide = jnp.broadcast_to(sums, (8, D))
    out = jnp.dot(wide, pool, precision=HI, preferred_element_type=F32)
    return out[:1] * (1.0 / (10 * N))


def group_stats(v_ref, acc, sums):
    mean = group_mean(sums)
    acc[0:1, :] = colsum(jnp.square(v_ref[...] - mean))
    return mean, lax.rsqrt(group_mean(acc[0:1, :]) + EPS)


def silu(v):
    return v * jax.nn.sigmoid(v)


def silu_slope(v):
    sig = jax.nn.sigmoid(v)
    return sig * (1.0 + v * (1.0 - sig))


def layer(v):
    mean = jnp.sum(v, axis=1, keepdims=True) * (1.0 / D)
    sq = jnp.sum(v * v, axis=1, keepdims=True) * (1.0 / D)
    inv = lax.rsqrt(sq - mean * mean + EPS)
    return (v - mean) * inv, inv


def layer_back(grad, normed, inv, gain):
    ghat = grad * gain
    m1 = jnp.sum(ghat, axis=1, keepdims=True) * (1.0 / D)
    m2 = jnp.sum(ghat * normed, axis=1, keepdims=True) * (1.0 / D)
    return inv * (ghat - m1 - normed * m2)


def own(v):
    return jnp.where(lax.axis_index(CH) == 0, v[..., :W], v[..., W:])


def head(v, h):
    return v[:, HD * h : HD * (h + 1)]


def front_kernel(noisy, tv, win, w1, vec0, c2, tr, vec1, h0, h1, h2, z0, a1, a2, ntr, x1, q, k, v, stats, sh, acc):
    cols = jnp.concatenate([shift_lanes(noisy[...], t) for t in range(9)], axis=0).astype(BF)
    clear_margins(sh)

    def norm(src, total, at):
        mean, inv = group_stats(src, acc, total)
        stats[at : at + 1, :], stats[at + 1 : at + 2, :] = mean, inv
        return (src[...] - mean) * inv

    h = tn(cols, win[...]) + vec0[0:1, :]
    h0[...] = h
    y = silu(norm(h0, colsum(h), 0) * vec0[1:2, :] + vec0[2:3, :])
    put_shifts(sh, y)
    a1[...] = y.astype(BF)
    h = conv_rows(sh, w1) + (vec0[3:4, :] + tv[...])
    h1[...] = h
    y = silu(norm(h1, colsum(h), 2) * vec1[N2G : N2G + 1, :] + vec1[N2B : N2B + 1, :])
    put_shifts(sh, y)
    a2[...] = y.astype(BF)
    h = h0[...] + conv_rows(sh, c2) + vec1[C2B : C2B + 1, :]
    h2[...] = h
    n = (norm(h2, colsum(h), 4) * vec1[NTG : NTG + 1, :] + vec1[NTB : NTB + 1, :]).astype(BF)
    ntr[...] = n
    z = nn(n, tr[MPI]) + vec1[PIB : PIB + 1, :]
    z0[...] = z
    normed, _ = layer(z)
    x = (normed * vec1[L1G : L1G + 1, :] + vec1[L1B : L1B + 1, :]).astype(BF)
    x1[...] = x
    for at, dst in ((MQ, q), (MK, k), (MV, v)):
        y = nn(x, tr[at]).astype(BF)
        for hd in range(HEADS):
            dst[hd] = head(y, hd)


AT = 512


def attend_kernel(q, k, v, o, lse, ot):
    steps = [(h, pl.ds(t * AT, AT)) for h in range(HEADS) for t in range(N // AT)]

    def scores(h, rows):
        return nt(k[h], q[h, rows, :])

    now = scores(*steps[0])
    for i, (h, rows) in enumerate(steps):
        later = scores(*steps[i + 1]) if i + 1 < len(steps) else None
        if i % (N // AT) == 0:
            vt = v[h].astype(F32).T.astype(BF)
        s = now * (SCALE * LOG2E)
        top = jnp.max(s, axis=0, keepdims=True)
        e = jnp.exp2(s - top)
        total = jnp.sum(e, axis=0, keepdims=True)
        lse[h, :, rows] = top + jnp.log(total) * LOG2E
        ot[h * HD : (h + 1) * HD, rows] = nn(vt, (e * (1.0 / total)).astype(BF))
        now = later
    o[...] = ot[...].T.astype(BF)


def cross_head(qh, kh):
    s = nt(kh, qh) * (SCALE * LOG2E)
    e = jnp.exp2(s - jnp.max(s, axis=0, keepdims=True))
    return e * (1.0 / jnp.sum(e, axis=0, keepdims=True))


def transposed(v):
    return v.astype(F32).T.astype(BF)


def middle_kernel(
    o, z0, h2, ctx, noise, mask, mats, kvw, vec, gib, wout, outb,
    dz1, dh3, dos, loss, gd, ggi, ggo, gkv, dvec, dgib, dwout, dbout,
    z1, z2, h3, x2, x3, oc, z3b, gl, a3, qc, kc, vc, derr, acc, ot, pt,
):
    def row(i):
        return vec[i : i + 1, :]

    def put(i, v):
        dvec[i : i + 1, :] = v

    kk = nn(ctx[...], kvw[0]).astype(BF)
    vv = nn(ctx[...], kvw[1])
    for h in range(HEADS):
        kc[h] = head(kk, h)
        vc[h] = head(vv, h).astype(BF)
    vt = vv.T
    z = z0[...] + nn(o[...], mats[MSO]) + row(SOB)
    z1[...] = z
    normed, _ = layer(z)
    x = (normed * row(L2G) + row(L2B)).astype(BF)
    x2[...] = x
    qq = nn(x, mats[MCQ]).astype(BF)
    for h in range(HEADS):
        qh = head(qq, h)
        qc[h] = qh
        p = cross_head(qh, kc[h]).astype(BF)
        ot[HD * h : HD * (h + 1), :] = nn(vt[HD * h : HD * (h + 1), :].astype(BF), p)
    c = ot[...].T.astype(BF)
    oc[...] = c
    z = z1[...] + nn(c, mats[MCO]) + row(COB)
    z2[...] = z
    normed, _ = layer(z)
    x = (normed * row(L3G) + row(L3B)).astype(BF)
    x3[...] = x
    for j in range(4):
        a = nn(x, mats[MGV + j]) + gib[j : j + 1, :]
        g = nn(x, mats[MGG + j]) + gib[4 + j : 5 + j, :]
        y = (a * (0.5 * g * (1.0 + lax.erf(g * math.sqrt(0.5))))).astype(BF)
        gl[j] = y
        z = z + nn(y, mats[MGO + j])
    zb = (z + row(GOB)).astype(BF)
    z3b[...] = zb
    h = h2[...] + nn(zb, mats[MPO]) + row(POB)
    h3[...] = h
    mean, inv = group_stats(h3, acc, colsum(h))
    gain, bias = row(NOG), row(NOB)
    a3[...] = silu((h3[...] - mean) * inv * gain + bias).astype(BF)
    taps = nt(wout[...], a3[...])
    for ch in range(LAT):
        pred = jnp.zeros((1, N), F32)
        for t in range(9):
            pred += shift_lanes(taps[9 * ch + t : 9 * ch + t + 1, :], t)
        at = W * (ch // 2) + ch % 2
        err = pred + outb[0:1, at : at + 1] - noise[ch : ch + 1, :]
        weighed = mask[...].astype(F32) * err
        g = 2.0 * weighed
        acc[2 + ch : 3 + ch, 0:1] = jnp.sum(weighed * err, axis=1, keepdims=True)
        dbout[ch : ch + 1, :] = jnp.broadcast_to(jnp.sum(g, axis=1, keepdims=True), (1, 128))
        for t in range(9):
            pt[9 * ch + t : 9 * ch + t + 1, :] = shift_lanes(g, 8 - t)
    loss[...] = acc[2:3, 0:1] + acc[3:4, 0:1] + acc[4:5, 0:1] + acc[5:6, 0:1]

    dvec[...] = jnp.zeros_like(dvec)
    taps = pt[...].astype(BF)
    dwout[...] = nn(taps, a3[...])
    n = (h3[...] - mean) * inv
    g = tn(taps, wout[...]) * silu_slope(n * gain + bias)
    dgain, dbias = colsum(g * n), colsum(g)
    put(NOG, dgain)
    put(NOB, dbias)
    g = inv * (g * gain - group_mean(gain * dbias) - n * group_mean(gain * dgain))
    dh3[...] = g
    put(POB, colsum(g))
    gd[0] = nn(transposed(z3b[...]), own(g).astype(BF)).astype(BF)
    dz3 = nt(g.astype(BF), mats[MPO])
    z1b = dz3.astype(BF)
    put(GOB, colsum(dz3))
    mine = own(dz3).astype(BF)
    x = x3[...]
    xt = transposed(x)
    dx = jnp.zeros((N, D), F32)
    for j in range(4):
        a = nn(x, mats[MGV + j]) + gib[j : j + 1, :]
        g = nn(x, mats[MGG + j]) + gib[4 + j : 5 + j, :]
        dgl = nt(z1b, mats[MGO + j])
        ggo[j] = tn(gl[j], mine).astype(BF)
        cdf = 0.5 * (1.0 + lax.erf(g * math.sqrt(0.5)))
        da = dgl * (g * cdf)
        dg = dgl * a * (cdf + g * jnp.exp(-0.5 * g * g) * (1.0 / math.sqrt(2.0 * math.pi)))
        dgib[j : j + 1, :] = colsum(da)
        dgib[4 + j : 5 + j, :] = colsum(dg)
        ggi[j] = nn(xt, own(da).astype(BF)).astype(BF)
        ggi[4 + j] = nn(xt, own(dg).astype(BF)).astype(BF)
        dx += nt(da.astype(BF), mats[MGV + j]) + nt(dg.astype(BF), mats[MGG + j])
    normed, li = layer(z2[...])
    put(L3G, colsum(dx * normed))
    put(L3B, colsum(dx))
    dz = dz3 + layer_back(dx, normed, li, row(L3G))
    z2[...] = dz
    put(COB, colsum(dz))
    gd[1] = tn(oc[...], own(dz).astype(BF)).astype(BF)
    do = nt(dz.astype(BF), mats[MCO]).astype(BF)
    dks, dvs = [], []
    for h in range(HEADS):
        qh, kh, vh, doh = qc[h], kc[h], vc[h], head(do, h)
        p = cross_head(qh, kh)
        dp = nt(vh, doh)
        ds = (p * (dp - jnp.sum(p * dp, axis=0, keepdims=True)) * SCALE).astype(BF)
        dks.append(nn(ds, qh))
        dvs.append(nn(p.astype(BF), doh))
        ot[HD * h : HD * (h + 1), :] = tn(kh, ds)
    for j, g in enumerate((dks, dvs)):
        gkv[j] = tn(ctx[...], own(jnp.concatenate(g, axis=1)).astype(BF)).astype(BF)
    dq = ot[...].T
    gd[2] = tn(x2[...], own(dq).astype(BF)).astype(BF)
    dx = nt(dq.astype(BF), mats[MCQ])
    normed, li = layer(z1[...])
    put(L2G, colsum(dx * normed))
    put(L2B, colsum(dx))
    dz = z2[...] + layer_back(dx, normed, li, row(L2G))
    dz1[...] = dz
    put(SOB, colsum(dz))
    gd[3] = tn(o[...], own(dz).astype(BF)).astype(BF)
    do = nt(dz.astype(BF), mats[MSO]).astype(BF)
    for h in range(HEADS):
        dos[h] = head(do, h)


ABT = 256


def attend_back_kernel(q, k, v, do, lse, dq, dk, dv, qt, kacc, vacc):
    steps = [(h, pl.ds(t * ABT, ABT)) for h in range(HEADS) for t in range(N // ABT)]

    def scores(h, rows):
        return nt(k[h], q[h, rows, :]), nt(v[h], do[h, rows, :])

    now = scores(*steps[0])
    for i, (h, rows) in enumerate(steps):
        later = scores(*steps[i + 1]) if i + 1 < len(steps) else None
        s, dp = now
        p = jnp.exp2(s * (SCALE * LOG2E) - lse[h, :, rows])
        ds = (p * (dp - jnp.sum(p * dp, axis=0, keepdims=True)) * SCALE).astype(BF)
        dkt, dvt = nn(ds, q[h, rows, :]), nn(p.astype(BF), do[h, rows, :])
        if i % (N // ABT) == 0:
            kt = k[h].astype(F32).T.astype(BF)
            kacc[h], vacc[h] = dkt, dvt
        else:
            kacc[h] += dkt
            vacc[h] += dvt
        qt[h * HD : (h + 1) * HD, rows] = nn(kt, ds)
        now = later

    dq[...] = qt[...].T.astype(BF)

    def one(rows):
        for acc, dst in ((kacc, dk), (vacc, dv)):
            dst[rows, :] = jnp.concatenate([acc[h, rows, :] for h in range(HEADS)], axis=1).astype(BF)

    tiles(one)


def put_rows(s_ref, start, v, step=1):
    n = v.shape[0]
    ds = pl.ds(start, n) if step == 1 else pl.ds(start, n, stride=step)
    s_ref[0, ds, :] = v[:, :128]
    s_ref[1, ds, :32] = v[:, 128:]


def roll_rows(s_ref, out_ref, lo_chunk, hi_chunk):
    q = 80

    @pl.loop(lo_chunk, hi_chunk)
    def _(c):
        g = []
        for i in range(4):
            ds = pl.ds(c * 4 * q + i, q, stride=4)
            g.append((s_ref[0, ds, :], s_ref[1, ds, :32]))
        base = (c - lo_chunk) * 5 * q
        out_ref[pl.ds(base, q, stride=5), :] = g[0][0]
        for i in range(3):
            lo = 96 - 32 * i
            out_ref[pl.ds(base + i + 1, q, stride=5), :] = jnp.concatenate(
                ([g[i][0][:, 128 - 32 * i :]] if i else []) + [g[i][1], g[i + 1][0][:, :lo]], axis=1
            )
        out_ref[pl.ds(base + 4, q, stride=5), :] = jnp.concatenate([g[3][0][:, 32:], g[3][1]], axis=1)


def by_owner(s_ref, flat, out, total):
    owners, room = math.prod(out.shape[:-2]), out.shape[-2]
    size = room if total < owners * room and len(out.shape) == 3 else min(room, ROWS)
    half = owners // 2 * size
    for lo, hi, first in ((0, min(-(-half // 400), total // 400), 0), (half // 400, total // 400, owners // 2)):
        if hi > lo:
            roll_rows(s_ref, flat, lo, hi)
        at = 400 * max(hi - lo, 0)
        if at < flat.shape[0]:
            flat[at:, :] = jnp.zeros((flat.shape[0] - at, 128), F32)
        for t in range(first, first + owners // 2):
            spot = (t % 2, t // 2) if len(out.shape) == 4 else (t,)
            row = t * size - 400 * lo
            out[(*spot, slice(0, size))] = flat[row : row + size, :].astype(BF)
            if room > size:
                out[(*spot, slice(size, room))] = jnp.zeros((room - size, 128), BF)


def conv_grads(a_ref, g_ref, s_ref, start):
    at = transposed(a_ref[...])
    for r in range(3):
        rows = SIDE * (2 - r)
        three = nn(at, g_ref[rows : rows + N, :])
        for i in range(3):
            put_rows(s_ref, start + D * (3 * r + i), three[:, W * (2 - i) : W * (3 - i)])


def back_kernel(
    dq, dk, dv, dz1, dh3, z0, h2, h1, h0, stats, w1, c2, tr, vec0, vec1, a1, a2, ntr, x1, noisy,
    gd, ggi, ggo, gkv, dvec_in, dgib, dwout, dbout,
    out1, out0, dtv,
    dh, g_ref, go_ref, dvec, s_ref, flat, o_ref,
):
    c = lax.axis_index(CH)
    clear_margins(g_ref)
    clear_margins(go_ref)
    dvec[...] = dvec_in[...]

    def row(i):
        return vec1[i : i + 1, :]

    def put(i, v):
        dvec[i : i + 1, :] = v

    dx = nt(dq[...], tr[MQ]) + nt(dk[...], tr[MK]) + nt(dv[...], tr[MV])
    xt = transposed(x1[...])
    for j, g in enumerate((dq, dk, dv)):
        put_rows(s_ref, QKV + j, nn(xt, own(g[...].astype(F32)).astype(BF)), 3)
    normed, li = layer(z0[...])
    put(L1G, colsum(dx * normed))
    put(L1B, colsum(dx))
    dz = dz1[...] + layer_back(dx, normed, li, row(L1G))
    put(PIB, colsum(dz))
    put_rows(s_ref, PI, tn(ntr[...], own(dz).astype(BF)))
    g = nt(dz.astype(BF), tr[MPI])

    def norm_back(g, n, at, gain):
        dgain, dbias = colsum(g * n), colsum(g)
        back = stats[at + 1 : at + 2, :] * (g * gain - group_mean(gain * dbias) - n * group_mean(gain * dgain))
        return back, dgain, dbias

    def normed_of(src, at):
        return (src[...] - stats[at : at + 1, :]) * stats[at + 1 : at + 2, :]

    g, dgain, dbias = norm_back(g, normed_of(h2, 4), 4, row(NTG))
    put(NTG, dgain)
    put(NTB, dbias)
    g = dh3[...] + g
    dh[...] = g
    put(C2B, colsum(g))
    put_shifts(g_ref, g)
    put_shifts(go_ref, own(g))
    conv_grads(a2, go_ref, s_ref, C2)
    n = normed_of(h1, 2)
    g = conv_back_rows(g_ref, c2) * silu_slope(n * row(N2G) + row(N2B))
    g, dgain, dbias = norm_back(g, n, 2, row(N2G))
    put(N2G, dgain)
    put(N2B, dbias)
    total = colsum(g)
    dtv[...] = total
    put_shifts(g_ref, g)
    put_shifts(go_ref, own(g))

    for i, r in enumerate((PO, CO, CQ, SO)):
        put_rows(s_ref, r, gd[i].astype(F32))
    for j in range(8):
        put_rows(s_ref, GI + j, ggi[j].astype(F32), 8)
    for j in range(4):
        rows = ggo[j].astype(F32)
        for b in range(2):
            put_rows(s_ref, GO + 640 * b + W * j, rows[W * b : W * (b + 1), :])
    for j in range(2):
        put_rows(s_ref, CKV + j, gkv[j].astype(F32), 2)
    for i, r in enumerate(VEC1):
        put_rows(s_ref, r, own(dvec[i : i + 1, :]))
    put_rows(s_ref, GIB, own(dgib[...]))
    wide = jnp.where(c == 0, dwout[:18, :], dwout[18:36, :])
    for ch in range(2):
        for m in range(4):
            o_ref[ch, pl.ds(m, 9, stride=4), :80] = wide[9 * ch : 9 * ch + 9, 80 * m : 80 * m + 80]
    lane = lax.broadcasted_iota(jnp.int32, (80, W), 0)
    col = lax.broadcasted_iota(jnp.int32, (80, W), 1)
    moved = jnp.zeros((36, W), F32)
    for ch in range(2):
        spot = jnp.where(2 * lane + ch == col, 1.0, 0.0)
        moved += jnp.dot(o_ref[ch, :36, :80], spot, precision=HI, preferred_element_type=F32)
    put_rows(s_ref, OUT, moved)
    b0 = jnp.where(c == 0, dbout[0:1, 0:1], dbout[2:3, 0:1])
    b1 = jnp.where(c == 0, dbout[1:2, 0:1], dbout[3:4, 0:1])
    at = lax.broadcasted_iota(jnp.int32, (1, W), 1)
    put_rows(s_ref, OUTB, jnp.where(at == 0, b0, jnp.where(at == 1, b1, 0.0)))
    s_ref[:, OUTB + 1 :, :] = jnp.zeros((2, 4 * R1 // 5 - OUTB - 1, 128), F32)
    by_owner(s_ref, flat, out1, R1)

    conv_grads(a1, go_ref, s_ref, 39)
    n = normed_of(h0, 0)
    g = conv_back_rows(g_ref, w1) * silu_slope(n * vec0[1:2, :] + vec0[2:3, :])
    g, dgain, dbias = norm_back(g, n, 0, vec0[1:2, :])
    g = dh[...] + g
    cols = jnp.concatenate([shift_lanes(noisy[...], t) for t in range(9)], axis=0).astype(BF)
    put_rows(s_ref, 0, nn(cols, own(g).astype(BF)))
    for r, v in zip(VEC0, (colsum(g), dgain, dbias, total)):
        put_rows(s_ref, r, own(v))
    s_ref[:, 4 * FRONT // 5 : 4 * R0 // 5, :] = jnp.zeros((2, 4 * (R0 - FRONT) // 5, 128), F32)
    by_owner(s_ref, flat, out0, R0)


FIRST = (0, 0, 1, 2, 3)
SECOND = (0, 1, 2, 3, 3)


def time_rows(facts, count):
    row = lax.axis_index(DP) * count + lax.broadcasted_iota(jnp.int32, (count, 1), 0)

    def wide(at, n):
        return jnp.concatenate([facts[:, at + i, :] for i in range(n)], axis=1)

    def meets(u, k):
        spot = jnp.where(k == lax.broadcasted_iota(jnp.int32, (1, u.shape[1]), 1), 1.0, 0.0).astype(BF)
        return nt(spot, u.astype(BF))

    total = jnp.zeros((count, 128), F32)
    for u, at, start, size in ((wide(FE, 3)[:, :D], FD1, T1, D), (wide(FU1, 10), FD2, T2, 4 * D)):
        rel = row - start
        k, line = rel // 5, rel % 5
        met = meets(u, jnp.where(rel < 0, -1, k))
        for j in range(5):
            g = facts[:, at + j, :]
            total += nn(jnp.where(line == j, met, 0.0).astype(BF), g.astype(BF))
            total += jnp.where((rel >= 0) & (k == size) & (line == j), colsum(g), 0.0)
    rel = row - T3
    group, line = rel // 5, rel % 5
    d3 = wide(FD3, 2)[:, :W]
    zero = jnp.zeros((d3.shape[0], 128), F32)
    u = wide(FU2, 10)
    for picks, shift in ((FIRST, 0), (SECOND, 1)):
        k = jnp.full_like(rel, -1)
        for j in range(5):
            k = jnp.where((rel >= 0) & (line == j), 4 * group + picks[j], k)
        met = meets(u, k)
        for j in range(5):
            if shift == 0:
                lo = (0, 128, 96, 64, 32)[j]
                g = d3[:, lo : min(lo + 128, W)]
                g = jnp.concatenate([g, zero[:, : 128 - g.shape[1]]], axis=1) if g.shape[1] < 128 else g
            else:
                if j in (0, 4):
                    continue
                g = jnp.concatenate([zero[:, : 32 * j], d3[:, : 128 - 32 * j]], axis=1)
            total += nn(jnp.where(line == j, met, 0.0).astype(BF), g.astype(BF))
            total += jnp.where((k == 4 * D) & (line == j), colsum(g), 0.0)
    return total


def update_kernel(with_time, params, momentum, ema, sum1, sum0, facts, new_params, new_momentum, new_ema, sums):
    total = facts[0, FL : FL + 1, :]
    for i in range(1, facts.shape[0]):
        total += facts[i, FL : FL + 1, :]
    sums[...] = total
    scale = 1.0 / (LAT * jnp.maximum(total[:, 1:2], 1.0))
    first = sum0[...]
    if with_time:
        first += time_rows(facts, sum0.shape[0])
    for p, g in enumerate((first, sum1[...])):
        g = g * scale
        m = MU * momentum[p] + g
        new_momentum[p] = m
        w = params[p] - LR * (g + MU * m)
        new_params[p] = w
        new_ema[p] = ED * ema[p] + (1.0 - ED) * w


ROWS = 856
SLAB = 864
SOME = 240
REST = SLAB - 3 * SOME


def send(src, dst, sems, i, j, target):
    copy = pltpu.make_async_remote_copy(
        src_ref=src, dst_ref=dst, send_sem=sems[0].at[i], recv_sem=sems[1].at[j],
        device_id={DP: target}, device_id_type=pl.DeviceIdType.MESH,
    )
    copy.start()
    return copy


PIECES = tuple(slice(16 * a, 16 * b) for a, b in ((0, 7), (7, 14), (14, 21), (21, 28), (28, 35), (35, 42), (42, 48), (48, 54)))


def gather_kernel(params, g0, g1, low, send_sem, recv_sem, keep_sem):
    low[:, :ROWS, :] = params[...].astype(BF)
    low[:, ROWS:, :] = jnp.zeros((2, SLAB - ROWS, 128), BF)
    me, y = lax.axis_index(DP), lax.axis_index(CH)
    k, x, z = me % 2, (me // 2) % 2, me // 4
    core = {DP: me + 1 - 2 * k}
    side = {DP: me + 2 - 4 * x}
    other = {CH: 1 - y}
    ring = [{DP: (me + 4 * o) % 16} for o in range(4)]
    barrier = pltpu.get_barrier_semaphore()
    for target in [core, side, other] + ring[1:]:
        pl.semaphore_signal(barrier, inc=1, device_id=target, device_id_type=pl.DeviceIdType.MESH)
    pl.semaphore_wait(barrier, 6)
    count = [0]
    started = []

    def push(ref, target):
        i = count[0]
        count[0] += 1
        return [start(ref, ref, i, i, target)]

    def start(src, dst, i, j, target):
        copy = pltpu.make_async_remote_copy(
            src_ref=src, dst_ref=dst, send_sem=send_sem.at[i], recv_sem=recv_sem.at[j],
            device_id=target, device_id_type=pl.DeviceIdType.MESH,
        )
        copy.start()
        started.append(copy)
        return copy

    def push_ring(ref):
        i = count[0]
        count[0] += 3
        return [start(ref, ref, i + o - 1, i + 3 - o, ring[o]) for o in (2, 1, 3)]

    def arrive(copies):
        for copy in copies:
            copy.wait_recv()

    keeps = []
    for p, g in enumerate((g0, g1)):
        keep = pltpu.make_async_copy(low.at[p], g.at[y, z, x, k], keep_sem.at[p])
        keep.start()
        keeps.append(keep)
    work = [(p, g, rows, i % 2) for p, g in enumerate((g0, g1)) for i, rows in enumerate(PIECES)]
    first, second, third, last = {}, {}, {}, []

    def begin(i):
        p, g, rows, _ = work[i]
        if i % len(PIECES) == 0:
            keeps[p].wait()
        first[i] = push_ring(g.at[y, z, x, k, rows])

    def middle(i):
        _, g, rows, turn = work[i]
        arrive(first[i])
        second[i] = push(g.at[y, :, x, k, rows], other if turn else side)
        last.extend(push(g.at[y, :, x, k, rows], core))

    def finish(i):
        _, g, rows, turn = work[i]
        arrive(second[i])
        if turn:
            third[i] = push(g.at[:, :, x, k, rows], side)
            last.extend(push(g.at[1 - y, :, x, k, rows], core))
        else:
            third[i] = push(g.at[y, :, :, k, rows], other)
            last.extend(push(g.at[y, :, 1 - x, k, rows], core))

    def pass_on(i):
        _, g, rows, turn = work[i]
        arrive(third[i])
        last.extend(push(g.at[:, :, 1 - x, k, rows] if turn else g.at[1 - y, :, :, k, rows], core))

    ahead = 4
    for i in range(ahead):
        begin(i)
    for i in range(len(work) + 2):
        if i < len(work):
            middle(i)
            if i + ahead < len(work):
                begin(i + ahead)
        if 0 <= i - 1 < len(work):
            finish(i - 1)
        if 0 <= i - 3 < len(work):
            pass_on(i - 3)
    pass_on(len(work) - 1)
    arrive(last)
    for copy in started:
        copy.wait_send()


def gather_weights(params):
    hbm = pl.BlockSpec(memory_space=pl.ANY)
    whole = sds((2, 4, 2, 2, SLAB, 128), BF)
    dma = pltpu.SemaphoreType.DMA
    return pl.pallas_call(
        gather_kernel,
        out_shape=(whole, whole),
        in_specs=[pl.BlockSpec(memory_space=pltpu.VMEM)],
        out_specs=(hbm, hbm),
        scratch_shapes=[pltpu.VMEM((2, SLAB, 128), BF), dma((128,)), dma((128,)), dma((2,))],
        compiler_params=pltpu.CompilerParams(collective_id=2, has_side_effects=True),
    )(params)


def add_up(*terms):
    total = terms[0].astype(F32)
    for term in terms[1:]:
        total += term.astype(F32)
    return total


def reduce_kernel(
    p1, p0, facts, sum1, sum0, all_facts,
    r1, sa, rx, ta, rz, r1b, sb, rbz, tb, rbx, some, land, fx, send_sem, recv_sem, fsend, frecv, gsend, grecv,
):
    me = lax.axis_index(DP)
    k, x, z = me % 2, (me // 2) % 2, me // 4
    barrier = pltpu.get_barrier_semaphore()
    for o in range(1, 16):
        pl.semaphore_signal(barrier, inc=1, device_id={DP: (me + o) % 16}, device_id_type=pl.DeviceIdType.MESH)
    pl.semaphore_wait(barrier, 15)
    sems = (send_sem, recv_sem)
    core = me + 1 - 2 * k
    side = me + 2 - 4 * x
    chunks = [p0] + [p1.at[:, :, SOME * i : SOME * (i + 1)] for i in range(3)]
    rest = p1.at[:, :, 3 * SOME :]

    def over_z(src, dst, base):
        return [
            send(src.at[(z + o) % 4], dst.at[3 - o], sems, base + o - 1, base + 3 - o, (me + 4 * o) % 16)
            for o in (2, 1, 3)
        ]

    over_core_b = send(rest.at[1 - k], r1b, sems, 20, 20, core)
    over_core = [send(ref.at[1 - k], r1.at[i], sems, i, i, core) for i, ref in enumerate(chunks)]
    fact_copies = [send(facts, fx.at[me], (fsend, frecv), o - 1, o - 1, (me + o) % 16) for o in range(1, 16)]
    over_core_b.wait_recv()
    for m in range(8):
        sb[m // 2, m % 2] = add_up(rest[k, m], r1b[m]).astype(BF)
    over_z_b = over_z(sb, rbz, 21)
    over_x = []
    for i, ref in enumerate(chunks):
        over_core[i].wait_recv()
        for m in range(8):
            sa[i, m % 2, m // 2] = add_up(ref[k, m], r1[i, m]).astype(BF)
        over_x.append(send(sa.at[i, 1 - x], rx.at[i], sems, 4 + i, 4 + i, side))
    along = []
    for i in range(4):
        over_x[i].wait_recv()
        for m in range(4):
            ta[i, m] = add_up(sa[i, x, m], rx[i, m]).astype(BF)
        along.append(over_z(ta.at[i], rz.at[i], 8 + 3 * i))
    for copy in over_z_b:
        copy.wait_recv()
    for m in range(2):
        tb[m] = add_up(sb[z, m], rbz[0, m], rbz[1, m], rbz[2, m]).astype(BF)
    over_x_b = send(tb.at[1 - x], rbx, sems, 24, 24, side)

    def done(i):
        for copy in along[i]:
            copy.wait_recv()
        return add_up(ta[i, z], rz[i, 0], rz[i, 1], rz[i, 2])

    some[...] = done(0)
    fx[me] = facts[...]

    @pl.when(me > 0)
    def _():
        @pl.loop(0, SOME // 8)
        def _(g):
            row = SOME * me + 8 * g
            owner = row // ROWS
            at = pl.multiple_of(row - ROWS * owner, 8)
            pltpu.make_async_remote_copy(
                src_ref=some.at[pl.ds(pl.multiple_of(8 * g, 8), 8)], dst_ref=land.at[pl.ds(at, 8)],
                send_sem=gsend, recv_sem=grecv, device_id={DP: owner}, device_id_type=pl.DeviceIdType.MESH,
            ).start()

    for copy in fact_copies:
        copy.wait_recv()
    all_facts[...] = fx[...]
    for i in range(3):
        sum1[SOME * i : SOME * (i + 1), :] = done(i + 1)
    over_x_b.wait_recv()
    sum1[3 * SOME :, :] = add_up(tb[x, : ROWS - 3 * SOME], rbx[: ROWS - 3 * SOME])

    def landed(lo, hi):
        part = land.at[lo:hi]
        pltpu.make_async_remote_copy(
            src_ref=part, dst_ref=part, send_sem=gsend, recv_sem=grecv,
            device_id={DP: me}, device_id_type=pl.DeviceIdType.MESH,
        ).wait_recv()
        sum0[lo:hi, :] = land[lo:hi, :]

    @pl.when(me == 0)
    def _():
        landed(SOME, ROWS)
        sum0[:SOME, :] = some[...]

    @pl.when((me > 0) & (me < 4))
    def _():
        landed(0, ROWS)

    @pl.when(me == 4)
    def _():
        landed(0, 16 * SOME - 4 * ROWS)
        sum0[16 * SOME - 4 * ROWS :, :] = jnp.zeros((5 * ROWS - 16 * SOME, 128), F32)

    @pl.when(me > 4)
    def _():
        sum0[...] = jnp.zeros_like(sum0)

    @pl.when(me > 0)
    def _():
        pltpu.make_async_remote_copy(
            src_ref=some, dst_ref=some, send_sem=gsend, recv_sem=grecv,
            device_id={DP: me}, device_id_type=pl.DeviceIdType.MESH,
        ).wait_send()

    for copy in [over_core_b, over_x_b] + over_core + over_z_b + over_x + sum(along, []) + fact_copies:
        copy.wait_send()


def sum_over_samples(p1, p0, facts):
    vm = pl.BlockSpec(memory_space=pltpu.VMEM)
    dma = pltpu.SemaphoreType.DMA
    return pl.pallas_call(
        reduce_kernel,
        out_shape=(sds((ROWS, 128)), sds((ROWS, 128)), sds((16, FACTS, 128))),
        in_specs=[vm] * 3,
        out_specs=(vm,) * 3,
        scratch_shapes=[
            pltpu.VMEM((4, 8, SOME, 128), BF),
            pltpu.VMEM((4, 2, 4, SOME, 128), BF),
            pltpu.VMEM((4, 4, SOME, 128), BF),
            pltpu.VMEM((4, 4, SOME, 128), BF),
            pltpu.VMEM((4, 3, SOME, 128), BF),
            pltpu.VMEM((8, REST, 128), BF),
            pltpu.VMEM((4, 2, REST, 128), BF),
            pltpu.VMEM((3, 2, REST, 128), BF),
            pltpu.VMEM((2, REST, 128), BF),
            pltpu.VMEM((REST, 128), BF),
            pltpu.VMEM((SOME, 128), F32),
            pltpu.VMEM((ROWS, 128), F32),
            pltpu.VMEM((16, FACTS, 128), F32),
            dma((25,)),
            dma((25,)),
            dma((15,)),
            dma((15,)),
            dma,
            dma,
        ],
        compiler_params=pltpu.CompilerParams(
            collective_id=1, has_side_effects=True, vmem_limit_bytes=40 * 2**20
        ),
    )(p1, p0, facts)


def time_features(steps):
    ladder = jnp.arange(D // 2, dtype=F32)
    freq = jnp.exp(-math.log(10000.0) * ladder / (D // 2))
    angles = steps.astype(F32)[:, None] * freq[None, :]
    return jnp.concatenate([jnp.cos(angles), jnp.sin(angles)], axis=1)


def alpha_bar(step_ids):
    levels = jnp.arange(1000, dtype=F32)
    lowest, highest = 0.00085**0.5, 0.012**0.5
    beta = jnp.square(lowest + (highest - lowest) * levels / 999.0)
    table = jnp.cumprod(1.0 - beta)
    matches = levels[None, :] == step_ids.astype(F32)[:, None]
    return jnp.sum(jnp.where(matches, table[None, :], 0.0), axis=1)


def shards(params, momentum, ema_params, latents, noise_eps, timesteps, pixel_mask, context):
    c = lax.axis_index(CH)
    d = lax.axis_index(DP)
    n_dp = lax.axis_size(DP)
    rows_dev = params.shape[2]
    rows_all = rows_dev * n_dp
    quick = n_dp == 16 and rows_dev == ROWS
    if quick:
        part0, part1 = gather_weights(params[0])
        part0, part1 = part0.reshape(2, 16, SLAB, 128), part1.reshape(2, 16, SLAB, 128)
    else:
        low = params[0].astype(BF)
        part0, part1 = (lax.all_gather(lax.all_gather(low[i], CH, axis=0), DP, axis=1) for i in range(2))

    alpha = alpha_bar(timesteps)[:, None]
    noise = noise_eps[0]
    noisy = jnp.sqrt(alpha) * latents[0] + jnp.sqrt(1.0 - alpha) * noise

    px = (N, D)
    hx = (HEADS, N, HD)
    sh = (N + 2 * SIDE, 3 * D)
    taps, back = sds((3, 3 * D, D), BF), sds((3, D, 3 * D), BF)
    e = time_features(timesteps)
    flat = pltpu.VMEM((2, rows_all, 128), F32)
    unrolled = pltpu.VMEM((3, 4 * R1 // 5, 128), F32)
    units = sds((8, 4 * D))
    win, w1, w1b, vec0, tw2, tw3, tv, p1, p2 = kcall(
        partial(unpack0_kernel, rows_dev),
        (sds((36, D), BF), taps, back, sds((8, D)), sds((4, 4 * D, D), BF), sds((4 * D, D), BF), sds((1, D)))
        + (units, units),
        (part0, jnp.broadcast_to(e, (8, D))),
        (flat, unrolled),
    )
    c2, c2b, tr, mats, kvw, vec1, gib, wout, outb = kcall(
        partial(unpack1_kernel, rows_dev),
        (taps, back, sds((4, D, D), BF), sds((16, D, D), BF), sds((2, CTX, D), BF))
        + (sds((24, D)), sds((8, D)), sds((36, D), BF), sds((1, D))),
        (part1,),
        (flat, unrolled, pltpu.VMEM((2, 40, 128), F32)),
    )
    h0, h1, h2, z0, a1, a2, ntr, x1, q, k, v, stats = kcall(
        front_kernel,
        (sds(px),) * 4 + (sds(px, BF),) * 4 + (sds(hx, BF),) * 3 + (sds((8, D)),),
        (noisy, tv, win, w1, vec0, c2, tr, vec1),
        (pltpu.VMEM(sh, BF), pltpu.VMEM((8, D), F32)),
    )
    o, lse = kcall(
        attend_kernel, (sds(px, BF), sds((HEADS, 1, N))), (q, k, v), (pltpu.VMEM((D, N), F32),)
    )
    square = (D, W)
    dz1, dh3, dos, loss, gd, ggi, ggo, gkv, dvec, dgib, dwout, dbout = kcall(
        middle_kernel,
        (sds(px), sds(px), sds(hx, BF), sds((1, 1)))
        + (sds((4,) + square, BF), sds((8,) + square, BF), sds((4,) + square, BF), sds((2, CTX, W), BF))
        + (sds((24, D)), sds((8, D)), sds((36, D)), sds((8, 128))),
        (o, z0, h2, context[0], noise, pixel_mask, mats, kvw, vec1, gib, wout, outb),
        [pltpu.VMEM(px, F32)] * 3
        + [pltpu.VMEM(px, BF)] * 4
        + [
            pltpu.VMEM((4, N, D), BF),
            pltpu.VMEM(px, BF),
            pltpu.VMEM(hx, BF),
            pltpu.VMEM((HEADS, TXT, HD), BF),
            pltpu.VMEM((HEADS, TXT, HD), BF),
            pltpu.VMEM((LAT, N), F32),
            pltpu.VMEM((8, D), F32),
            pltpu.VMEM((D, N), F32),
            pltpu.VMEM((36, N), F32),
        ],
    )
    dq, dk, dv = kcall(
        attend_back_kernel,
        (sds(px, BF),) * 3,
        (q, k, v, dos, lse),
        (pltpu.VMEM((D, N), F32), pltpu.VMEM(hx, F32), pltpu.VMEM(hx, F32)),
    )
    step = 16 * n_dp
    front = -(-FRONT // step) * step
    lead = (2, 8) if quick else (n_dp,)
    own1, own0, dtv = kcall(
        back_kernel,
        (
            sds(lead + (SLAB if quick else rows_dev, 128), BF),
            sds(lead + (front // n_dp, 128), BF),
            sds((1, D)),
        ),
        (dq, dk, dv, dz1, dh3, z0, h2, h1, h0, stats, w1b, c2b, tr, vec0, vec1, a1, a2, ntr, x1, noisy,
         gd, ggi, ggo, gkv, dvec, dgib, dwout, dbout),
        (
            pltpu.VMEM(px, F32),
            pltpu.VMEM(sh, BF),
            pltpu.VMEM((sh[0], 3 * W), BF),
            pltpu.VMEM((24, D), F32),
            pltpu.VMEM((2, 4 * R1 // 5, 128), F32),
            pltpu.VMEM((7600, 128), F32),
            pltpu.VMEM((2, 40, 128), F32),
        ),
    )
    facts = kcall(
        time_back_kernel, sds((FACTS, 128)), (dtv, tw2, tw3, p1, p2, jnp.broadcast_to(e, (8, D)), pixel_mask, loss)
    )
    if quick:
        sum1, sum0, all_facts = sum_over_samples(own1, own0, facts)
    else:
        sum1 = lax.psum_scatter(own1, DP, scatter_dimension=0).astype(F32)
        sum0 = lax.all_gather(lax.psum_scatter(own0, DP, scatter_dimension=0), DP, axis=0, tiled=True)
        sum0 = jnp.pad(sum0, ((0, rows_all - front), (0, 0)))
        sum0 = lax.dynamic_slice_in_dim(sum0, d * rows_dev, rows_dev, 0).astype(F32)
        all_facts = lax.all_gather(facts, DP, axis=0)
    state = sds((2, rows_dev, 128))
    new_params, new_momentum, new_ema, sums = kcall(
        partial(update_kernel, True),
        (state, state, state, sds((1, 128))),
        (params[0], momentum[0], ema_params[0], sum1, sum0, all_facts),
    )
    return (new_params[None], new_momentum[None], new_ema[None], sums[0, 0], sums[0, 1])


def solution(mesh):
    packed = P(CH, None, DP, None)
    row = P(DP, None, None)
    return jax.shard_map(
        shards,
        mesh=mesh,
        in_specs=(packed, packed, packed, row, row, P(DP), P(DP, None), row),
        out_specs=(packed, packed, packed, P(), P()),
        check_vma=False,
    )
```

```python
import math
from functools import partial

import jax
import jax.numpy as jnp
from jax import lax
from jax.experimental import pallas as pl
from jax.experimental.pallas import tpu as pltpu
from jax.sharding import PartitionSpec as P

D = 320
W = 160
HEADS = 8
HD = 40
CTX = 768
TXT = 77
LAT = 4
SIDE = 32
N = 1024
EPS = 1e-5
LR = 0.2
MU = 0.9
ED = 0.9
CH = "chan"
DP = "dp"
F32 = jnp.float32
BF = jnp.bfloat16
HI = lax.Precision.HIGHEST
SCALE = HD**-0.5
LOG2E = 1.0 / math.log(2.0)

R0 = 4000
U1, U2, U3 = 2920, 4204, 9328
FRONT = 3650
T1, T2, T3 = 3650, 5255, 11660
C2 = 2
PI = 2885
QKV = 3208
SO = 4168
CQ = 4491
CKV = 4811
CO = 6347
GI = 6670
GIB = 9230
GO = 9238
PO = 10519
OUT = 10842
OUTB = 10878
R1 = 13600
VEC0 = (36, 37, 38, 2919)
VEC1 = (0, 1, 2882, 2883, 2884, 3205, 3206, 3207, 4488, 4489, 4490, 6667, 6668, 6669, 10518, 10839, 10840, 10841)
(N2G, N2B, C2B, NTG, NTB, PIB, L1G, L1B, SOB, L2G, L2B, COB, L3G, L3B, GOB, POB, NOG, NOB) = range(18)
MPI, MQ, MK, MV = range(4)
MSO, MCQ, MCO, MPO, MGV, MGG, MGO = 0, 1, 2, 3, 4, 8, 12


class Flow:
    def __init__(self, ins, outs, sems):
        self.ins = {i: pltpu.make_async_copy(src, dst, sems.at[j]) for j, (i, src, dst) in enumerate(ins)}
        n = len(ins)
        self.outs = {i: pltpu.make_async_copy(src, dst, sems.at[n + j]) for j, (i, dst, src) in enumerate(outs)}
        self.waiting = set(self.ins)
        self.going = []
        for copy in self.ins.values():
            copy.start()

    def need(self, *which):
        for i in which:
            self.ins[i].wait()
            self.waiting.discard(i)

    def ready(self, *which):
        for i in which:
            self.outs[i].start()
            self.going.append(i)

    def end(self):
        self.need(*sorted(self.waiting))
        self.ready(*(i for i in self.outs if i not in self.going))
        for copy in self.outs.values():
            copy.wait()


def kcall(body, outs, ins, scratch=(), late=(), early=()):
    vm, hbm = pl.BlockSpec(memory_space=pltpu.VMEM), pl.BlockSpec(memory_space=pl.ANY)
    single = not isinstance(outs, tuple)
    outs = (outs,) if single else outs
    n, m = len(ins), len(outs)
    late, early = tuple(late), tuple(early)
    scratch = list(scratch)
    count = len(scratch)
    if late or early:
        scratch += [pltpu.VMEM(ins[i].shape, ins[i].dtype) for i in late]
        scratch += [pltpu.VMEM(outs[i].shape, outs[i].dtype) for i in early]
        scratch.append(pltpu.SemaphoreType.DMA((len(late) + len(early),)))

    def whole(*refs):
        if not (late or early):
            return body(*refs)
        given, made, rest = list(refs[:n]), list(refs[n : n + m]), refs[n + m :]
        kept = rest[count:-1]
        inward = [(i, given[i], kept[j]) for j, i in enumerate(late)]
        outward = [(i, made[i], kept[len(late) + j]) for j, i in enumerate(early)]
        for i, _, ref in inward:
            given[i] = ref
        for i, _, ref in outward:
            made[i] = ref
        flow = Flow(inward, outward, rest[-1])
        body(flow, *given, *made, *rest[:count])
        flow.end()

    done = pl.pallas_call(
        whole,
        out_shape=outs,
        in_specs=[hbm if i in late else vm for i in range(n)],
        out_specs=tuple(hbm if i in early else vm for i in range(m)),
        scratch_shapes=scratch,
        compiler_params=pltpu.CompilerParams(vmem_limit_bytes=63 * 2**20),
    )(*ins)
    return done[0] if single else done


def sds(shape, dtype=F32):
    return jax.ShapeDtypeStruct(shape, dtype)


def tiles(fn, size=256, total=N):
    for t in range(total // size):
        fn(pl.ds(t * size, size))


def nn(a, b):
    return jnp.dot(a, b, preferred_element_type=F32)


def nt(a, b):
    return lax.dot_general(a, b, (((1,), (1,)), ((), ())), preferred_element_type=F32)


def tn(a, b):
    return lax.dot_general(a, b, (((0,), (0,)), ((), ())), preferred_element_type=F32)


def colsum(v):
    return jnp.sum(v, axis=0, keepdims=True)


def flatten(a_ref, flat, rows):
    for b in range(2):
        for t in range(a_ref.shape[1]):
            flat[b, t * rows : (t + 1) * rows, :] = a_ref[b, t, :rows, :].astype(F32)


def unroll(flat, s_ref, lo_chunk, hi_chunk):
    q = 80

    @pl.loop(lo_chunk, hi_chunk)
    def _(c):
        f = [[flat[b, pl.ds(c * 5 * q + j, q, stride=5), :] for j in range(5)] for b in range(2)]
        for i in range(4):
            row = []
            for b in range(2):
                lo = 32 * i
                first, second = f[b][i], f[b][i + 1]
                row += [first[:, lo:], second[:, : lo + 32]] if lo else [first, second[:, :32]]
            full = jnp.concatenate(row, axis=1)
            for k, (lo, hi) in enumerate(((0, 128), (128, 256), (256, 320))):
                s_ref[k, pl.ds(c * 4 * q + i, q, stride=4), : hi - lo] = full[:, lo:hi]


def get_rows(s_ref, start, count, step=1):
    ds = pl.ds(start, count) if step == 1 else pl.ds(start, count, stride=step)
    return jnp.concatenate([s_ref[0, ds, :], s_ref[1, ds, :], s_ref[2, ds, :64]], axis=1)


def put_taps(s_ref, start, w, back):
    for r in range(3):
        taps = [get_rows(s_ref, start + D * (3 * r + i), D).astype(BF) for i in range(3)]
        for i in range(3):
            w[r, D * i : D * (i + 1), :] = taps[i]
        back[r] = jnp.concatenate(taps[::-1], axis=1)


def unit_row(parts):
    out = [p[:, W * b : W * (b + 1)] for b in range(2) for p in parts]
    return jnp.broadcast_to(jnp.concatenate(out, axis=1), (8, 4 * D))


def unit_parts(row):
    return [
        jnp.concatenate([row[:, W * i : W * (i + 1)], row[:, 640 + W * i : 640 + W * (i + 1)]], axis=1)
        for i in range(4)
    ]


def take_front(s_ref, win, w1, w1b, vec):
    win[...] = get_rows(s_ref, 0, 36).astype(BF)
    put_taps(s_ref, 39, w1, w1b)
    for i, r in enumerate(VEC0):
        vec[i : i + 1, :] = get_rows(s_ref, r, 1)


def take_time(s_ref, tw2, tw3):
    for i in range(4):
        tw2[i] = get_rows(s_ref, U2 + i, 4 * D, 4).astype(BF)
    tw3[...] = get_rows(s_ref, U3, 4 * D).astype(BF)


def time_forward(s_ref, e, tw2, tw3, tv, p1, p2):
    u = e[...].astype(BF)
    p1[...] = unit_row(
        [nn(u, get_rows(s_ref, U1 + i, D, 4).astype(BF))[:1] + get_rows(s_ref, U1 + 4 * D + i, 1) for i in range(4)]
    )
    u = silu(p1[...]).astype(BF)
    p2[...] = unit_row([nn(u, tw2[i])[:1] + get_rows(s_ref, U2 + 16 * D + i, 1) for i in range(4)])
    u = silu(p2[...]).astype(BF)
    tv[...] = nn(u, tw3[...])[:1] + get_rows(s_ref, U3 + 4 * D, 1)


def unpack0_kernel(rows, a_ref, e, win, w1, w1b, vec, tw2, tw3, tv, p1, p2, flat, s_ref):
    flatten(a_ref, flat, rows)
    unroll(flat, s_ref, 0, R1 // 400)
    take_front(s_ref, win, w1, w1b, vec)
    take_time(s_ref, tw2, tw3)
    time_forward(s_ref, e, tw2, tw3, tv, p1, p2)


FE, FU1, FU2, FD1, FD2, FD3, FL = 0, 3, 13, 23, 28, 33, 35
FACTS = 40


def time_back_kernel(dtv, tw2, tw3, p1, p2, e, mask, loss, facts):
    first = lax.axis_index(CH) == 0
    g = jnp.broadcast_to(dtv[...], (8, D)).astype(BF)
    d2 = nt(g, tw3[...]) * silu_slope(p2[...])
    total = jnp.zeros((8, 4 * D), F32)
    for i, part in enumerate(unit_parts(d2)):
        total += nt(part.astype(BF), tw2[i])
    d1 = total * silu_slope(p1[...])
    facts[...] = jnp.zeros_like(facts)

    def put(at, v):
        for i in range(0, v.shape[1], 128):
            n = min(128, v.shape[1] - i)
            facts[at + i // 128 : at + i // 128 + 1, :n] = v[:1, i : i + n]

    put(FE, e[...].astype(BF).astype(F32))
    put(FU1, silu(p1[...]).astype(BF).astype(F32))
    put(FU2, silu(p2[...]).astype(BF).astype(F32))
    put(FD1, jnp.where(first, d1[:, : 2 * D], d1[:, 2 * D :]))
    put(FD2, jnp.where(first, d2[:, : 2 * D], d2[:, 2 * D :]))
    put(FD3, own(dtv[...]))
    facts[FL : FL + 1, 0:1] = loss[...]
    facts[FL : FL + 1, 1:2] = jnp.sum(mask[...].astype(F32), axis=1, keepdims=True)


def unpack1_kernel(rows, a_ref, c2, c2b, tr, mats, kv, vec, gib, wout, outb, flat, s_ref, o_ref):
    flatten(a_ref, flat, rows)
    unroll(flat, s_ref, 0, R1 // 400)
    put_taps(s_ref, C2, c2, c2b)
    tr[MPI] = get_rows(s_ref, PI, D).astype(BF)
    for m, r in ((MSO, SO), (MCQ, CQ), (MCO, CO), (MPO, PO)):
        mats[m] = get_rows(s_ref, r, D).astype(BF)
    for j in range(3):
        tr[MQ + j] = get_rows(s_ref, QKV + j, D, 3).astype(BF)
    for j in range(8):
        mats[MGV + j] = get_rows(s_ref, GI + j, D, 8).astype(BF)
    for j in range(4):
        for b in range(2):
            mats[MGO + j, b * W : (b + 1) * W, :] = get_rows(s_ref, GO + 640 * b + W * j, W).astype(BF)
    for j in range(2):
        kv[j] = get_rows(s_ref, CKV + j, CTX, 2).astype(BF)
    for i, r in enumerate(VEC1):
        vec[i : i + 1, :] = get_rows(s_ref, r, 1)
    gib[...] = get_rows(s_ref, GIB, 8)
    outb[...] = get_rows(s_ref, OUTB, 1)
    lane = lax.broadcasted_iota(jnp.int32, (W, W), 0)
    col = lax.broadcasted_iota(jnp.int32, (W, W), 1)
    pick = ((lane % 2) * 80 + lane // 2 == col).astype(BF)
    raw = get_rows(s_ref, OUT, 36).astype(BF)
    for b in range(2):
        moved = nn(raw[:, W * b : W * (b + 1)], pick)
        o_ref[0, :36, :] = moved[:, :128]
        o_ref[1, :36, :32] = moved[:, 128:]
        for ch in range(2):
            pieces = []
            for m in range(4):
                ds = pl.ds(m, 9, stride=4)
                both = jnp.concatenate([o_ref[0, ds, :], o_ref[1, ds, :32]], axis=1)
                pieces.append(both[:, 80 * ch : 80 * ch + 80])
            at = (2 * b + ch) * 9
            wout[at : at + 9, :] = jnp.concatenate(pieces, axis=1).astype(BF)


def pixel_col(n, axis):
    shape = (n, 1) if axis == 0 else (1, n)
    return lax.broadcasted_iota(jnp.int32, shape, axis)


def shift_lanes(v, tap):
    r, s = tap // 3 - 1, tap % 3 - 1
    pix = pixel_col(N, 1)
    i, j = pix // SIDE + r, pix % SIDE + s
    ok = (i >= 0) & (i < SIDE) & (j >= 0) & (j < SIDE)
    move = -(r * SIDE + s) % N
    moved = pltpu.roll(v, move, 1) if move else v
    return jnp.where(ok, moved, 0.0)


def put_shifts(ref, v):
    j = pixel_col(N, 0) % SIDE
    left = jnp.where(j == 0, 0.0, pltpu.roll(v, 1, 0)).astype(BF)
    right = jnp.where(j == SIDE - 1, 0.0, pltpu.roll(v, N - 1, 0)).astype(BF)
    ref[SIDE : SIDE + N, :] = jnp.concatenate([left, v.astype(BF), right], axis=1)


def clear_margins(ref):
    zero = jnp.zeros((SIDE, ref.shape[1]), BF)
    ref[:SIDE, :] = zero
    ref[SIDE + N :, :] = zero


def conv_rows(ref, w_ref):
    return sum(nn(ref[SIDE * r : SIDE * r + N, :], w_ref[r]) for r in range(3))


def conv_back_rows(ref, w_ref):
    return sum(nt(ref[SIDE * (2 - r) : SIDE * (2 - r) + N, :], w_ref[r]) for r in range(3))


def group_mean(sums):
    a = lax.broadcasted_iota(jnp.int32, (D, D), 0) // 10
    b = lax.broadcasted_iota(jnp.int32, (D, D), 1) // 10
    pool = jnp.where(a == b, 1.0, 0.0)
    wide = jnp.broadcast_to(sums, (8, D))
    out = jnp.dot(wide, pool, precision=HI, preferred_element_type=F32)
    return out[:1] * (1.0 / (10 * N))


def group_stats(v_ref, acc, sums):
    mean = group_mean(sums)
    acc[0:1, :] = colsum(jnp.square(v_ref[...] - mean))
    return mean, lax.rsqrt(group_mean(acc[0:1, :]) + EPS)


def silu(v):
    return v * jax.nn.sigmoid(v)


def silu_slope(v):
    sig = jax.nn.sigmoid(v)
    return sig * (1.0 + v * (1.0 - sig))


def layer(v):
    mean = jnp.sum(v, axis=1, keepdims=True) * (1.0 / D)
    sq = jnp.sum(v * v, axis=1, keepdims=True) * (1.0 / D)
    inv = lax.rsqrt(sq - mean * mean + EPS)
    return (v - mean) * inv, inv


def layer_back(grad, normed, inv, gain):
    ghat = grad * gain
    m1 = jnp.sum(ghat, axis=1, keepdims=True) * (1.0 / D)
    m2 = jnp.sum(ghat * normed, axis=1, keepdims=True) * (1.0 / D)
    return inv * (ghat - m1 - normed * m2)


def own(v):
    return jnp.where(lax.axis_index(CH) == 0, v[..., :W], v[..., W:])


def head(v, h):
    return v[:, HD * h : HD * (h + 1)]


def group_norm(src, acc, total, stats, at):
    mean, inv = group_stats(src, acc, total)
    stats[at : at + 1, :], stats[at + 1 : at + 2, :] = mean, inv
    return (src[...] - mean) * inv


def start_steps(noisy, tv, win, w1, vec0, h0, h1, a1, stats, sh, acc):
    def first():
        cols = jnp.concatenate([shift_lanes(noisy[...], t) for t in range(9)], axis=0).astype(BF)
        clear_margins(sh)
        stats[...] = jnp.zeros_like(stats)
        h = tn(cols, win[...]) + vec0[0:1, :]
        h0[...] = h
        y = silu(group_norm(h0, acc, colsum(h), stats, 0) * vec0[1:2, :] + vec0[2:3, :])
        put_shifts(sh, y)
        a1[...] = y.astype(BF)

    def taps(r):
        def one():
            part = nn(sh[SIDE * r : SIDE * r + N, :], w1[r])
            h1[...] = (h1[...] if r else vec0[3:4, :] + tv[...]) + part

        return one

    return [first, taps(0), taps(1), taps(2)]


def start_kernel(noisy, tv, win, w1, vec0, h0, h1, a1, stats, sh, acc):
    for step in start_steps(noisy, tv, win, w1, vec0, h0, h1, a1, stats, sh, acc):
        step()


def front_kernel(flow, h0, h1, stats_in, c2, tr, vec1, h2, z0, a2, ntr, x1, q, k, v, stats, sh, acc):
    clear_margins(sh)
    stats[...] = stats_in[...]
    y = silu(group_norm(h1, acc, colsum(h1[...]), stats, 2) * vec1[N2G : N2G + 1, :] + vec1[N2B : N2B + 1, :])
    put_shifts(sh, y)
    a2[...] = y.astype(BF)
    flow.ready(2)
    flow.need(0, 3)
    h = h0[...] + conv_rows(sh, c2) + vec1[C2B : C2B + 1, :]
    h2[...] = h
    flow.ready(0)
    n = group_norm(h2, acc, colsum(h), stats, 4)
    n = (n * vec1[NTG : NTG + 1, :] + vec1[NTB : NTB + 1, :]).astype(BF)
    ntr[...] = n
    flow.ready(3)
    flow.need(4)
    z = nn(n, tr[MPI]) + vec1[PIB : PIB + 1, :]
    z0[...] = z
    flow.ready(1)
    normed, _ = layer(z)
    x = (normed * vec1[L1G : L1G + 1, :] + vec1[L1B : L1B + 1, :]).astype(BF)
    x1[...] = x
    flow.ready(4)
    for i, (at, dst) in enumerate(((MQ, q), (MK, k), (MV, v))):
        y = nn(x, tr[at]).astype(BF)
        for hd in range(HEADS):
            dst[hd] = head(y, hd)
        flow.ready(5 + i)


AT = 512


def attend_kernel(q, k, v, o, lse, ot):
    steps = [(h, pl.ds(t * AT, AT)) for h in range(HEADS) for t in range(N // AT)]

    def scores(h, rows):
        return nt(k[h], q[h, rows, :])

    now = scores(*steps[0])
    for i, (h, rows) in enumerate(steps):
        later = scores(*steps[i + 1]) if i + 1 < len(steps) else None
        if i % (N // AT) == 0:
            vt = v[h].astype(F32).T.astype(BF)
        s = now * (SCALE * LOG2E)
        top = jnp.max(s, axis=0, keepdims=True)
        e = jnp.exp2(s - top)
        total = jnp.sum(e, axis=0, keepdims=True)
        lse[h, :, rows] = top + jnp.log(total) * LOG2E
        ot[h * HD : (h + 1) * HD, rows] = nn(vt, (e * (1.0 / total)).astype(BF))
        now = later
    o[...] = ot[...].T.astype(BF)


KEYS = 128


def by_head(v):
    wide = jnp.concatenate([v, jnp.zeros((KEYS - TXT, D), v.dtype)], axis=0)
    col = lax.broadcasted_iota(jnp.int32, (KEYS, D), 1) // HD
    return jnp.concatenate([jnp.where(col == h, wide, 0.0) for h in range(HEADS)], axis=0)


def from_heads(vt):
    row = lax.broadcasted_iota(jnp.int32, (D, KEYS), 0) // HD
    total = jnp.zeros((D, KEYS), F32)
    for h in range(HEADS):
        total += jnp.where(row == h, vt[:, KEYS * h : KEYS * (h + 1)], 0.0)
    return total.T[:TXT]


def transposed(v):
    return v.astype(F32).T.astype(BF)


def middle_kernel(
    flow, o, z0, h2, ctx, noise, mask, mats, kvw, vec, gib, wout, outb,
    dz1, dh3, dos, loss, gd, ggi, ggo, gkv, dvec, dgib, dwout, dbout,
    z1, z2, h3, x2, x3, oc, z3b, gl, by_a, by_g, a3, qc, kb, vb, prob, dsc, acc, pt,
):
    def row(i):
        return vec[i : i + 1, :]

    def put(i, v):
        dvec[i : i + 1, :] = v

    flow.need(7)
    kb[...] = by_head(nn(ctx[...], kvw[0])).astype(BF)
    vb[...] = by_head(nn(ctx[...], kvw[1])).astype(BF)
    flow.need(6, 1)
    z = z0[...] + nn(o[...], mats[MSO]) + row(SOB)
    z1[...] = z
    normed, _ = layer(z)
    x = (normed * row(L2G) + row(L2B)).astype(BF)
    x2[...] = x
    qq = nn(x, mats[MCQ]).astype(BF)
    qc[...] = qq
    s = nt(qq, kb[...]) * (SCALE * LOG2E)
    there = lax.broadcasted_iota(jnp.int32, (1, KEYS), 1) < TXT
    for h in range(HEADS):
        at = slice(KEYS * h, KEYS * (h + 1))
        sh = jnp.where(there, s[:, at], -jnp.inf)
        e = jnp.exp2(sh - jnp.max(sh, axis=1, keepdims=True))
        prob[:, at] = e * (1.0 / jnp.sum(e, axis=1, keepdims=True))
    c = nn(prob[...].astype(BF), vb[...]).astype(BF)
    oc[...] = c
    z = z1[...] + nn(c, mats[MCO]) + row(COB)
    z2[...] = z
    normed, _ = layer(z)
    x = (normed * row(L3G) + row(L3B)).astype(BF)
    x3[...] = x
    for j in range(4):
        a = nn(x, mats[MGV + j]) + gib[j : j + 1, :]
        g = nn(x, mats[MGG + j]) + gib[4 + j : 5 + j, :]
        cdf = 0.5 * (1.0 + lax.erf(g * math.sqrt(0.5)))
        gelu = g * cdf
        by_a[j] = gelu
        by_g[j] = a * (cdf + g * jnp.exp(-0.5 * g * g) * (1.0 / math.sqrt(2.0 * math.pi)))
        y = (a * gelu).astype(BF)
        gl[j] = y
        z = z + nn(y, mats[MGO + j])
    zb = (z + row(GOB)).astype(BF)
    z3b[...] = zb
    flow.need(2)
    h = h2[...] + nn(zb, mats[MPO]) + row(POB)
    h3[...] = h
    mean, inv = group_stats(h3, acc, colsum(h))
    gain, bias = row(NOG), row(NOB)
    a3[...] = silu((h3[...] - mean) * inv * gain + bias).astype(BF)
    taps = nt(wout[...], a3[...])
    for ch in range(LAT):
        pred = jnp.zeros((1, N), F32)
        for t in range(9):
            pred += shift_lanes(taps[9 * ch + t : 9 * ch + t + 1, :], t)
        at = W * (ch // 2) + ch % 2
        err = pred + outb[0:1, at : at + 1] - noise[ch : ch + 1, :]
        weighed = mask[...].astype(F32) * err
        g = 2.0 * weighed
        acc[2 + ch : 3 + ch, 0:1] = jnp.sum(weighed * err, axis=1, keepdims=True)
        dbout[ch : ch + 1, :] = jnp.broadcast_to(jnp.sum(g, axis=1, keepdims=True), (1, 128))
        for t in range(9):
            pt[9 * ch + t : 9 * ch + t + 1, :] = shift_lanes(g, 8 - t)
    loss[...] = acc[2:3, 0:1] + acc[3:4, 0:1] + acc[4:5, 0:1] + acc[5:6, 0:1]

    dvec[...] = jnp.zeros_like(dvec)
    taps = pt[...].astype(BF)
    dwout[...] = nn(taps, a3[...])
    n = (h3[...] - mean) * inv
    g = tn(taps, wout[...]) * silu_slope(n * gain + bias)
    dgain, dbias = colsum(g * n), colsum(g)
    put(NOG, dgain)
    put(NOB, dbias)
    g = inv * (g * gain - group_mean(gain * dbias) - n * group_mean(gain * dgain))
    dh3[...] = g
    flow.ready(1)
    put(POB, colsum(g))
    gd[0] = nn(transposed(z3b[...]), own(g).astype(BF)).astype(BF)
    dz3 = nt(g.astype(BF), mats[MPO])
    z1b = dz3.astype(BF)
    put(GOB, colsum(dz3))
    mine = own(dz3).astype(BF)
    xt = transposed(x3[...])
    dx = jnp.zeros((N, D), F32)
    for j in range(4):
        dgl = nt(z1b, mats[MGO + j])
        ggo[j] = tn(gl[j], mine).astype(BF)
        da = dgl * by_a[j]
        dg = dgl * by_g[j]
        dgib[j : j + 1, :] = colsum(da)
        dgib[4 + j : 5 + j, :] = colsum(dg)
        ggi[j] = nn(xt, own(da).astype(BF)).astype(BF)
        ggi[4 + j] = nn(xt, own(dg).astype(BF)).astype(BF)
        dx += nt(da.astype(BF), mats[MGV + j]) + nt(dg.astype(BF), mats[MGG + j])
    flow.ready(5, 6)
    normed, li = layer(z2[...])
    put(L3G, colsum(dx * normed))
    put(L3B, colsum(dx))
    dz = dz3 + layer_back(dx, normed, li, row(L3G))
    z2[...] = dz
    put(COB, colsum(dz))
    gd[1] = tn(oc[...], own(dz).astype(BF)).astype(BF)
    do = nt(dz.astype(BF), mats[MCO]).astype(BF)
    dp = nt(do, vb[...])
    dot = transposed(do)
    qt = transposed(qc[...])
    gkv[1] = tn(ctx[...], own(from_heads(nn(dot, prob[...].astype(BF)))).astype(BF)).astype(BF)
    for h in range(HEADS):
        at = slice(KEYS * h, KEYS * (h + 1))
        p, d = prob[:, at], dp[:, at]
        dsc[:, at] = (p * (d - jnp.sum(p * d, axis=1, keepdims=True)) * SCALE).astype(BF)
    gkv[0] = tn(ctx[...], own(from_heads(nn(qt, dsc[...]))).astype(BF)).astype(BF)
    flow.ready(7)
    dq = nn(dsc[...], kb[...])
    gd[2] = tn(x2[...], own(dq).astype(BF)).astype(BF)
    dx = nt(dq.astype(BF), mats[MCQ])
    normed, li = layer(z1[...])
    put(L2G, colsum(dx * normed))
    put(L2B, colsum(dx))
    dz = z2[...] + layer_back(dx, normed, li, row(L2G))
    dz1[...] = dz
    flow.ready(0)
    put(SOB, colsum(dz))
    gd[3] = tn(o[...], own(dz).astype(BF)).astype(BF)
    do = nt(dz.astype(BF), mats[MSO]).astype(BF)
    for h in range(HEADS):
        dos[h] = head(do, h)


ABT = 256


def attend_back_kernel(q, k, v, do, lse, dq, dk, dv, qt, kacc, vacc):
    steps = [(h, pl.ds(t * ABT, ABT)) for h in range(HEADS) for t in range(N // ABT)]

    def scores(h, rows):
        return nt(k[h], q[h, rows, :]), nt(v[h], do[h, rows, :])

    now = scores(*steps[0])
    for i, (h, rows) in enumerate(steps):
        later = scores(*steps[i + 1]) if i + 1 < len(steps) else None
        s, dp = now
        p = jnp.exp2(s * (SCALE * LOG2E) - lse[h, :, rows])
        ds = (p * (dp - jnp.sum(p * dp, axis=0, keepdims=True)) * SCALE).astype(BF)
        dkt, dvt = nn(ds, q[h, rows, :]), nn(p.astype(BF), do[h, rows, :])
        if i % (N // ABT) == 0:
            kt = k[h].astype(F32).T.astype(BF)
            kacc[h], vacc[h] = dkt, dvt
        else:
            kacc[h] += dkt
            vacc[h] += dvt
        qt[h * HD : (h + 1) * HD, rows] = nn(kt, ds)
        now = later

    dq[...] = qt[...].T.astype(BF)

    def one(rows):
        for acc, dst in ((kacc, dk), (vacc, dv)):
            dst[rows, :] = jnp.concatenate([acc[h, rows, :] for h in range(HEADS)], axis=1).astype(BF)

    tiles(one)


def put_rows(s_ref, start, v, step=1):
    n = v.shape[0]
    ds = pl.ds(start, n) if step == 1 else pl.ds(start, n, stride=step)
    s_ref[0, ds, :] = v[:, :128]
    s_ref[1, ds, :32] = v[:, 128:]


def roll_rows(s_ref, out_ref, lo_chunk, hi_chunk):
    q = 80

    @pl.loop(lo_chunk, hi_chunk)
    def _(c):
        g = []
        for i in range(4):
            ds = pl.ds(c * 4 * q + i, q, stride=4)
            g.append((s_ref[0, ds, :], s_ref[1, ds, :32]))
        base = (c - lo_chunk) * 5 * q
        out_ref[pl.ds(base, q, stride=5), :] = g[0][0]
        for i in range(3):
            lo = 96 - 32 * i
            out_ref[pl.ds(base + i + 1, q, stride=5), :] = jnp.concatenate(
                ([g[i][0][:, 128 - 32 * i :]] if i else []) + [g[i][1], g[i + 1][0][:, :lo]], axis=1
            )
        out_ref[pl.ds(base + 4, q, stride=5), :] = jnp.concatenate([g[3][0][:, 32:], g[3][1]], axis=1)


def by_owner(s_ref, flat, out, total):
    owners, room = math.prod(out.shape[:-2]), out.shape[-2]
    size = room if total < owners * room and len(out.shape) == 3 else min(room, ROWS)
    half = owners // 2 * size
    for lo, hi, first in ((0, min(-(-half // 400), total // 400), 0), (half // 400, total // 400, owners // 2)):
        if hi > lo:
            roll_rows(s_ref, flat, lo, hi)
        at = 400 * max(hi - lo, 0)
        if at < flat.shape[0]:
            flat[at:, :] = jnp.zeros((flat.shape[0] - at, 128), F32)
        for t in range(first, first + owners // 2):
            spot = (t % 2, t // 2) if len(out.shape) == 4 else (t,)
            row = t * size - 400 * lo
            out[(*spot, slice(0, size))] = flat[row : row + size, :].astype(BF)
            if room > size:
                out[(*spot, slice(size, room))] = jnp.zeros((room - size, 128), BF)


def conv_grads(a_ref, g_ref, s_ref, start):
    at = transposed(a_ref[...])
    for r in range(3):
        rows = SIDE * (2 - r)
        three = nn(at, g_ref[rows : rows + N, :])
        for i in range(3):
            put_rows(s_ref, start + D * (3 * r + i), three[:, W * (2 - i) : W * (3 - i)])


def back_kernel(
    flow, dq, dk, dv, dz1, dh3, z0, h2, h1, h0, stats, w1, c2, tr, vec0, vec1, a1, a2, ntr, x1, noisy,
    gd, ggi, ggo, gkv, dvec_in, dgib, dwout, dbout,
    out1, out0, dtv,
    dh, g_ref, go_ref, dvec, s_ref, flat, o_ref,
):
    c = lax.axis_index(CH)
    clear_margins(g_ref)
    clear_margins(go_ref)
    dvec[...] = dvec_in[...]

    def row(i):
        return vec1[i : i + 1, :]

    def put(i, v):
        dvec[i : i + 1, :] = v

    dx = nt(dq[...], tr[MQ]) + nt(dk[...], tr[MK]) + nt(dv[...], tr[MV])
    xt = transposed(x1[...])
    for j, g in enumerate((dq, dk, dv)):
        put_rows(s_ref, QKV + j, nn(xt, own(g[...].astype(F32)).astype(BF)), 3)
    flow.need(5, 3)
    normed, li = layer(z0[...])
    put(L1G, colsum(dx * normed))
    put(L1B, colsum(dx))
    dz = dz1[...] + layer_back(dx, normed, li, row(L1G))
    put(PIB, colsum(dz))
    flow.need(17)
    put_rows(s_ref, PI, tn(ntr[...], own(dz).astype(BF)))
    g = nt(dz.astype(BF), tr[MPI])

    def norm_back(g, n, at, gain):
        dgain, dbias = colsum(g * n), colsum(g)
        back = stats[at + 1 : at + 2, :] * (g * gain - group_mean(gain * dbias) - n * group_mean(gain * dgain))
        return back, dgain, dbias

    def normed_of(src, at):
        return (src[...] - stats[at : at + 1, :]) * stats[at + 1 : at + 2, :]

    flow.need(6, 4)
    g, dgain, dbias = norm_back(g, normed_of(h2, 4), 4, row(NTG))
    put(NTG, dgain)
    put(NTB, dbias)
    g = dh3[...] + g
    dh[...] = g
    put(C2B, colsum(g))
    put_shifts(g_ref, g)
    put_shifts(go_ref, own(g))
    flow.need(16)
    conv_grads(a2, go_ref, s_ref, C2)
    flow.need(7, 11)
    n = normed_of(h1, 2)
    g = conv_back_rows(g_ref, c2) * silu_slope(n * row(N2G) + row(N2B))
    g, dgain, dbias = norm_back(g, n, 2, row(N2G))
    put(N2G, dgain)
    put(N2B, dbias)
    total = colsum(g)
    dtv[...] = total
    put_shifts(g_ref, g)
    put_shifts(go_ref, own(g))

    flow.need(20, 21, 22, 23)
    for i, r in enumerate((PO, CO, CQ, SO)):
        put_rows(s_ref, r, gd[i].astype(F32))
    for j in range(8):
        put_rows(s_ref, GI + j, ggi[j].astype(F32), 8)
    for j in range(4):
        rows = ggo[j].astype(F32)
        for b in range(2):
            put_rows(s_ref, GO + 640 * b + W * j, rows[W * b : W * (b + 1), :])
    for j in range(2):
        put_rows(s_ref, CKV + j, gkv[j].astype(F32), 2)
    for i, r in enumerate(VEC1):
        put_rows(s_ref, r, own(dvec[i : i + 1, :]))
    put_rows(s_ref, GIB, own(dgib[...]))
    wide = jnp.where(c == 0, dwout[:18, :], dwout[18:36, :])
    for ch in range(2):
        for m in range(4):
            o_ref[ch, pl.ds(m, 9, stride=4), :80] = wide[9 * ch : 9 * ch + 9, 80 * m : 80 * m + 80]
    lane = lax.broadcasted_iota(jnp.int32, (80, W), 0)
    col = lax.broadcasted_iota(jnp.int32, (80, W), 1)
    moved = jnp.zeros((36, W), F32)
    for ch in range(2):
        spot = jnp.where(2 * lane + ch == col, 1.0, 0.0)
        moved += jnp.dot(o_ref[ch, :36, :80], spot, precision=HI, preferred_element_type=F32)
    put_rows(s_ref, OUT, moved)
    b0 = jnp.where(c == 0, dbout[0:1, 0:1], dbout[2:3, 0:1])
    b1 = jnp.where(c == 0, dbout[1:2, 0:1], dbout[3:4, 0:1])
    at = lax.broadcasted_iota(jnp.int32, (1, W), 1)
    put_rows(s_ref, OUTB, jnp.where(at == 0, b0, jnp.where(at == 1, b1, 0.0)))
    s_ref[:, OUTB + 1 :, :] = jnp.zeros((2, 4 * R1 // 5 - OUTB - 1, 128), F32)
    by_owner(s_ref, flat, out1, R1)
    flow.ready(0)

    flow.need(15, 8, 10)
    conv_grads(a1, go_ref, s_ref, 39)
    n = normed_of(h0, 0)
    g = conv_back_rows(g_ref, w1) * silu_slope(n * vec0[1:2, :] + vec0[2:3, :])
    g, dgain, dbias = norm_back(g, n, 0, vec0[1:2, :])
    g = dh[...] + g
    cols = jnp.concatenate([shift_lanes(noisy[...], t) for t in range(9)], axis=0).astype(BF)
    put_rows(s_ref, 0, nn(cols, own(g).astype(BF)))
    for r, v in zip(VEC0, (colsum(g), dgain, dbias, total)):
        put_rows(s_ref, r, own(v))
    s_ref[:, 4 * FRONT // 5 : 4 * R0 // 5, :] = jnp.zeros((2, 4 * (R0 - FRONT) // 5, 128), F32)
    by_owner(s_ref, flat, out0, R0)


FIRST = (0, 0, 1, 2, 3)
SECOND = (0, 1, 2, 3, 3)


def time_rows(facts, count):
    row = lax.axis_index(DP) * count + lax.broadcasted_iota(jnp.int32, (count, 1), 0)

    def wide(at, n):
        return jnp.concatenate([facts[:, at + i, :] for i in range(n)], axis=1)

    def meets(u, k):
        spot = jnp.where(k == lax.broadcasted_iota(jnp.int32, (1, u.shape[1]), 1), 1.0, 0.0).astype(BF)
        return nt(spot, u.astype(BF))

    total = jnp.zeros((count, 128), F32)
    for u, at, start, size in ((wide(FE, 3)[:, :D], FD1, T1, D), (wide(FU1, 10), FD2, T2, 4 * D)):
        rel = row - start
        k, line = rel // 5, rel % 5
        met = meets(u, jnp.where(rel < 0, -1, k))
        for j in range(5):
            g = facts[:, at + j, :]
            total += nn(jnp.where(line == j, met, 0.0).astype(BF), g.astype(BF))
            total += jnp.where((rel >= 0) & (k == size) & (line == j), colsum(g), 0.0)
    rel = row - T3
    group, line = rel // 5, rel % 5
    d3 = wide(FD3, 2)[:, :W]
    zero = jnp.zeros((d3.shape[0], 128), F32)
    u = wide(FU2, 10)
    for picks, shift in ((FIRST, 0), (SECOND, 1)):
        k = jnp.full_like(rel, -1)
        for j in range(5):
            k = jnp.where((rel >= 0) & (line == j), 4 * group + picks[j], k)
        met = meets(u, k)
        for j in range(5):
            if shift == 0:
                lo = (0, 128, 96, 64, 32)[j]
                g = d3[:, lo : min(lo + 128, W)]
                g = jnp.concatenate([g, zero[:, : 128 - g.shape[1]]], axis=1) if g.shape[1] < 128 else g
            else:
                if j in (0, 4):
                    continue
                g = jnp.concatenate([zero[:, : 32 * j], d3[:, : 128 - 32 * j]], axis=1)
            total += nn(jnp.where(line == j, met, 0.0).astype(BF), g.astype(BF))
            total += jnp.where((k == 4 * D) & (line == j), colsum(g), 0.0)
    return total


def update_kernel(with_time, params, momentum, ema, sum1, sum0, facts, new_params, new_momentum, new_ema, sums):
    total = facts[0, FL : FL + 1, :]
    for i in range(1, facts.shape[0]):
        total += facts[i, FL : FL + 1, :]
    sums[...] = total
    scale = 1.0 / (LAT * jnp.maximum(total[:, 1:2], 1.0))
    first = sum0[...]
    if with_time:
        first += time_rows(facts, sum0.shape[0])
    for p, g in enumerate((first, sum1[...])):
        g = g * scale
        m = MU * momentum[p] + g
        new_momentum[p] = m
        w = params[p] - LR * (g + MU * m)
        new_params[p] = w
        new_ema[p] = ED * ema[p] + (1.0 - ED) * w


ROWS = 856
SLAB = 864
SOME = 240
REST = SLAB - 3 * SOME


def send(src, dst, sems, i, j, target):
    copy = pltpu.make_async_remote_copy(
        src_ref=src, dst_ref=dst, send_sem=sems[0].at[i], recv_sem=sems[1].at[j],
        device_id={DP: target}, device_id_type=pl.DeviceIdType.MESH,
    )
    copy.start()
    return copy


PIECES = tuple(slice(16 * a, 16 * b) for a, b in ((0, 7), (7, 14), (14, 21), (21, 28), (28, 35), (35, 42), (42, 48), (48, 54)))


def gather_kernel(
    params, e, noisy, g0, g1, vec, p1, p2, stats, w1b_out, tw2_out, tw3_out, h0_out, h1_out, a1_out,
    low, slabs, flat, s_ref, w1b, tw2, tw3, h0, h1, a1, w1, win, tv, sh, acc,
    send_sem, recv_sem, keep_sem, slab_sem, out_sem,
):
    low[:, :ROWS, :] = params[...].astype(BF)
    low[:, ROWS:, :] = jnp.zeros((2, SLAB - ROWS, 128), BF)
    me, y = lax.axis_index(DP), lax.axis_index(CH)
    k, x, z = me % 2, (me // 2) % 2, me // 4
    core = {DP: me + 1 - 2 * k}
    side = {DP: me + 2 - 4 * x}
    other = {CH: 1 - y}
    ring = [{DP: (me + 4 * o) % 16} for o in range(4)]
    barrier = pltpu.get_barrier_semaphore()
    for target in [core, side, other] + ring[1:]:
        pl.semaphore_signal(barrier, inc=1, device_id=target, device_id_type=pl.DeviceIdType.MESH)
    pl.semaphore_wait(barrier, 6)
    count = [0]
    started = []

    def push(ref, target):
        i = count[0]
        count[0] += 1
        return [start(ref, ref, i, i, target)]

    def start(src, dst, i, j, target):
        copy = pltpu.make_async_remote_copy(
            src_ref=src, dst_ref=dst, send_sem=send_sem.at[i], recv_sem=recv_sem.at[j],
            device_id=target, device_id_type=pl.DeviceIdType.MESH,
        )
        copy.start()
        started.append(copy)
        return copy

    def push_ring(ref):
        i = count[0]
        count[0] += 3
        return [start(ref, ref, i + o - 1, i + 3 - o, ring[o]) for o in (2, 1, 3)]

    def arrive(copies):
        for copy in copies:
            copy.wait_recv()

    keeps = []
    for p, g in enumerate((g0, g1)):
        keep = pltpu.make_async_copy(low.at[p], g.at[y, z, x, k], keep_sem.at[p])
        keep.start()
        keeps.append(keep)
    work = [(p, g, rows, i % 2) for p, g in enumerate((g0, g1)) for i, rows in enumerate(PIECES)]
    first, second, third, last = {}, {}, {}, []

    def begin(i):
        p, g, rows, _ = work[i]
        if i % len(PIECES) == 0:
            keeps[p].wait()
        first[i] = push_ring(g.at[y, z, x, k, rows])

    def middle(i):
        _, g, rows, turn = work[i]
        arrive(first[i])
        second[i] = push(g.at[y, :, x, k, rows], other if turn else side)
        last.extend(push(g.at[y, :, x, k, rows], core))

    def finish(i):
        _, g, rows, turn = work[i]
        arrive(second[i])
        if turn:
            third[i] = push(g.at[:, :, x, k, rows], side)
            last.extend(push(g.at[1 - y, :, x, k, rows], core))
        else:
            third[i] = push(g.at[y, :, :, k, rows], other)
            last.extend(push(g.at[y, :, 1 - x, k, rows], core))

    def pass_on(i):
        _, g, rows, turn = work[i]
        arrive(third[i])
        last.extend(push(g.at[:, :, 1 - x, k, rows] if turn else g.at[1 - y, :, :, k, rows], core))

    outs = [
        pltpu.make_async_copy(src, dst, out_sem.at[i])
        for i, (src, dst) in enumerate(
            ((w1b, w1b_out), (tw2, tw2_out), (tw3, tw3_out), (h0, h0_out), (h1, h1_out), (a1, a1_out))
        )
    ]
    fetches = [
        pltpu.make_async_copy(g0.at[a, b], slabs.at[a, b], slab_sem.at[4 * a + b]) for a in range(2) for b in range(4)
    ]

    def fetch():
        arrive(last)
        last.clear()
        for copy in fetches:
            copy.start()

    def flat_half(a):
        for copy in fetches[4 * a : 4 * a + 4]:
            copy.wait()
        for t in range(16):
            flat[a, t * ROWS : (t + 1) * ROWS, :] = slabs[a, t // 4, t // 2 % 2, t % 2, :ROWS, :].astype(F32)

    def front():
        take_front(s_ref, win, w1, w1b, vec)
        outs[0].start()

    def times():
        take_time(s_ref, tw2, tw3)
        outs[1].start()
        outs[2].start()

    def both(*steps):
        def one():
            for step in steps:
                step()

        return one

    opening, *rows_of_taps = start_steps(noisy, tv, win, w1, vec, h0, h1, a1, stats, sh, acc)
    todo = [
        fetch,
        both(lambda: flat_half(0), lambda: flat_half(1)),
        lambda: unroll(flat, s_ref, 0, 17),
        lambda: unroll(flat, s_ref, 17, R1 // 400),
        both(front, times),
        both(lambda: time_forward(s_ref, e, tw2, tw3, tv, p1, p2), opening),
        both(outs[3].start, outs[5].start, *rows_of_taps[:2]),
        both(rows_of_taps[2], outs[4].start),
    ]
    ahead = 4
    for i in range(ahead):
        begin(i)
    for i in range(len(work) + 2):
        if i < len(work):
            middle(i)
            if i + ahead < len(work):
                begin(i + ahead)
        if 0 <= i - 1 < len(work):
            finish(i - 1)
        if 0 <= i - 3 < len(work):
            pass_on(i - 3)
        if i - 3 >= len(PIECES) - 1:
            todo.pop(0)()
    pass_on(len(work) - 1)
    for step in todo:
        step()
    for copy in outs:
        copy.wait()
    arrive(last)
    for copy in started:
        copy.wait_send()


def gather_weights(params, e, noisy):
    hbm, vm = pl.BlockSpec(memory_space=pl.ANY), pl.BlockSpec(memory_space=pltpu.VMEM)
    gathered = sds((2, 4, 2, 2, SLAB, 128), BF)
    large = (sds((3, D, 3 * D), BF), sds((4, 4 * D, D), BF), sds((4 * D, D), BF))
    large += (sds((N, D)), sds((N, D)), sds((N, D), BF))
    small = (sds((8, D)), sds((8, 4 * D)), sds((8, 4 * D)), sds((8, D)))
    dma = pltpu.SemaphoreType.DMA
    return pl.pallas_call(
        gather_kernel,
        out_shape=(gathered, gathered) + small + large,
        in_specs=[vm, vm, vm],
        out_specs=(hbm, hbm) + (vm,) * len(small) + (hbm,) * len(large),
        scratch_shapes=[
            pltpu.VMEM((2, SLAB, 128), BF),
            pltpu.VMEM(gathered.shape, BF),
            pltpu.VMEM((2, 16 * ROWS, 128), F32),
            pltpu.VMEM((3, 4 * R1 // 5, 128), F32),
            *(pltpu.VMEM(v.shape, v.dtype) for v in large),
            pltpu.VMEM((3, 3 * D, D), BF),
            pltpu.VMEM((36, D), BF),
            pltpu.VMEM((1, D), F32),
            pltpu.VMEM((N + 2 * SIDE, 3 * D), BF),
            pltpu.VMEM((8, D), F32),
            dma((128,)),
            dma((128,)),
            dma((2,)),
            dma((8,)),
            dma((6,)),
        ],
        compiler_params=pltpu.CompilerParams(collective_id=2, has_side_effects=True, vmem_limit_bytes=63 * 2**20),
    )(params, e, noisy)


def add_up(*terms):
    total = terms[0].astype(F32)
    for term in terms[1:]:
        total += term.astype(F32)
    return total


def reduce_kernel(
    p1, p0, facts, sum1, sum0, all_facts,
    r1, sa, rx, ta, rz, r1b, sb, rbz, tb, rbx, some, land, fx, timed, send_sem, recv_sem, fsend, frecv, gsend, grecv,
):
    me = lax.axis_index(DP)
    k, x, z = me % 2, (me // 2) % 2, me // 4
    barrier = pltpu.get_barrier_semaphore()
    for o in range(1, 16):
        pl.semaphore_signal(barrier, inc=1, device_id={DP: (me + o) % 16}, device_id_type=pl.DeviceIdType.MESH)
    pl.semaphore_wait(barrier, 15)
    sems = (send_sem, recv_sem)
    core = me + 1 - 2 * k
    side = me + 2 - 4 * x
    chunks = [p0] + [p1.at[:, :, SOME * i : SOME * (i + 1)] for i in range(3)]
    rest = p1.at[:, :, 3 * SOME :]

    def over_z(src, dst, base):
        return [
            send(src.at[(z + o) % 4], dst.at[3 - o], sems, base + o - 1, base + 3 - o, (me + 4 * o) % 16)
            for o in (2, 1, 3)
        ]

    over_core_b = send(rest.at[1 - k], r1b, sems, 20, 20, core)
    over_core = [send(ref.at[1 - k], r1.at[i], sems, i, i, core) for i, ref in enumerate(chunks)]
    fact_copies = [send(facts, fx.at[me], (fsend, frecv), o - 1, o - 1, (me + o) % 16) for o in range(1, 16)]
    over_core_b.wait_recv()
    for m in range(8):
        sb[m // 2, m % 2] = add_up(rest[k, m], r1b[m]).astype(BF)
    over_z_b = over_z(sb, rbz, 21)
    over_x = []
    for i, ref in enumerate(chunks):
        over_core[i].wait_recv()
        for m in range(8):
            sa[i, m % 2, m // 2] = add_up(ref[k, m], r1[i, m]).astype(BF)
        over_x.append(send(sa.at[i, 1 - x], rx.at[i], sems, 4 + i, 4 + i, side))
    along = []
    for i in range(4):
        over_x[i].wait_recv()
        for m in range(4):
            ta[i, m] = add_up(sa[i, x, m], rx[i, m]).astype(BF)
        along.append(over_z(ta.at[i], rz.at[i], 8 + 3 * i))
    for copy in over_z_b:
        copy.wait_recv()
    for m in range(2):
        tb[m] = add_up(sb[z, m], rbz[0, m], rbz[1, m], rbz[2, m]).astype(BF)
    over_x_b = send(tb.at[1 - x], rbx, sems, 24, 24, side)

    def done(i):
        for copy in along[i]:
            copy.wait_recv()
        return add_up(ta[i, z], rz[i, 0], rz[i, 1], rz[i, 2])

    fx[me] = facts[...]
    for copy in fact_copies:
        copy.wait_recv()
    all_facts[...] = fx[...]
    timed[...] = time_rows(fx, ROWS)
    some[...] = done(0)

    @pl.when(me > 0)
    def _():
        @pl.loop(0, SOME // 8)
        def _(g):
            row = SOME * me + 8 * g
            owner = row // ROWS
            at = pl.multiple_of(row - ROWS * owner, 8)
            pltpu.make_async_remote_copy(
                src_ref=some.at[pl.ds(pl.multiple_of(8 * g, 8), 8)], dst_ref=land.at[pl.ds(at, 8)],
                send_sem=gsend, recv_sem=grecv, device_id={DP: owner}, device_id_type=pl.DeviceIdType.MESH,
            ).start()

    for i in range(3):
        sum1[SOME * i : SOME * (i + 1), :] = done(i + 1)
    over_x_b.wait_recv()
    sum1[3 * SOME :, :] = add_up(tb[x, : ROWS - 3 * SOME], rbx[: ROWS - 3 * SOME])

    def landed(lo, hi):
        part = land.at[lo:hi]
        pltpu.make_async_remote_copy(
            src_ref=part, dst_ref=part, send_sem=gsend, recv_sem=grecv,
            device_id={DP: me}, device_id_type=pl.DeviceIdType.MESH,
        ).wait_recv()
        sum0[lo:hi, :] = land[lo:hi, :] + timed[lo:hi, :]

    @pl.when(me == 0)
    def _():
        landed(SOME, ROWS)
        sum0[:SOME, :] = some[...] + timed[:SOME, :]

    @pl.when((me > 0) & (me < 4))
    def _():
        landed(0, ROWS)

    @pl.when(me == 4)
    def _():
        landed(0, 16 * SOME - 4 * ROWS)
        sum0[16 * SOME - 4 * ROWS :, :] = timed[16 * SOME - 4 * ROWS :, :]

    @pl.when(me > 4)
    def _():
        sum0[...] = timed[...]

    @pl.when(me > 0)
    def _():
        pltpu.make_async_remote_copy(
            src_ref=some, dst_ref=some, send_sem=gsend, recv_sem=grecv,
            device_id={DP: me}, device_id_type=pl.DeviceIdType.MESH,
        ).wait_send()

    for copy in [over_core_b, over_x_b] + over_core + over_z_b + over_x + sum(along, []) + fact_copies:
        copy.wait_send()


def sum_over_samples(p1, p0, facts):
    vm = pl.BlockSpec(memory_space=pltpu.VMEM)
    dma = pltpu.SemaphoreType.DMA
    return pl.pallas_call(
        reduce_kernel,
        out_shape=(sds((ROWS, 128)), sds((ROWS, 128)), sds((16, FACTS, 128))),
        in_specs=[vm] * 3,
        out_specs=(vm,) * 3,
        scratch_shapes=[
            pltpu.VMEM((4, 8, SOME, 128), BF),
            pltpu.VMEM((4, 2, 4, SOME, 128), BF),
            pltpu.VMEM((4, 4, SOME, 128), BF),
            pltpu.VMEM((4, 4, SOME, 128), BF),
            pltpu.VMEM((4, 3, SOME, 128), BF),
            pltpu.VMEM((8, REST, 128), BF),
            pltpu.VMEM((4, 2, REST, 128), BF),
            pltpu.VMEM((3, 2, REST, 128), BF),
            pltpu.VMEM((2, REST, 128), BF),
            pltpu.VMEM((REST, 128), BF),
            pltpu.VMEM((SOME, 128), F32),
            pltpu.VMEM((ROWS, 128), F32),
            pltpu.VMEM((16, FACTS, 128), F32),
            pltpu.VMEM((ROWS, 128), F32),
            dma((25,)),
            dma((25,)),
            dma((15,)),
            dma((15,)),
            dma,
            dma,
        ],
        compiler_params=pltpu.CompilerParams(
            collective_id=1, has_side_effects=True, vmem_limit_bytes=40 * 2**20
        ),
    )(p1, p0, facts)


def time_features(steps):
    ladder = jnp.arange(D // 2, dtype=F32)
    freq = jnp.exp(-math.log(10000.0) * ladder / (D // 2))
    angles = steps.astype(F32)[:, None] * freq[None, :]
    return jnp.concatenate([jnp.cos(angles), jnp.sin(angles)], axis=1)


def alpha_bar(step_ids):
    levels = jnp.arange(1000, dtype=F32)
    lowest, highest = 0.00085**0.5, 0.012**0.5
    beta = jnp.square(lowest + (highest - lowest) * levels / 999.0)
    table = jnp.cumprod(1.0 - beta)
    matches = levels[None, :] == step_ids.astype(F32)[:, None]
    return jnp.sum(jnp.where(matches, table[None, :], 0.0), axis=1)


def shards(params, momentum, ema_params, latents, noise_eps, timesteps, pixel_mask, context):
    c = lax.axis_index(CH)
    d = lax.axis_index(DP)
    n_dp = lax.axis_size(DP)
    rows_dev = params.shape[2]
    rows_all = rows_dev * n_dp
    quick = n_dp == 16 and rows_dev == ROWS
    e = jnp.broadcast_to(time_features(timesteps), (8, D))
    alpha = alpha_bar(timesteps)[:, None]
    noise = noise_eps[0]
    noisy = jnp.sqrt(alpha) * latents[0] + jnp.sqrt(1.0 - alpha) * noise

    if quick:
        _, part1, vec0, p1, p2, stats, w1b, tw2, tw3, h0, h1, a1 = gather_weights(params[0], e, noisy)
        part1 = part1.reshape(2, 16, SLAB, 128)
    else:
        low = params[0].astype(BF)
        part0, part1 = (lax.all_gather(lax.all_gather(low[i], CH, axis=0), DP, axis=1) for i in range(2))

    px = (N, D)
    hx = (HEADS, N, HD)
    sh = (N + 2 * SIDE, 3 * D)
    taps, back = sds((3, 3 * D, D), BF), sds((3, D, 3 * D), BF)
    flat = pltpu.VMEM((2, rows_all, 128), F32)
    unrolled = pltpu.VMEM((3, 4 * R1 // 5, 128), F32)
    units = sds((8, 4 * D))
    if not quick:
        win, w1, w1b, vec0, tw2, tw3, tv, p1, p2 = kcall(
            partial(unpack0_kernel, rows_dev),
            (sds((36, D), BF), taps, back, sds((8, D)), sds((4, 4 * D, D), BF), sds((4 * D, D), BF), sds((1, D)))
            + (units, units),
            (part0, e),
            (flat, unrolled),
        )
        h0, h1, a1, stats = kcall(
            start_kernel,
            (sds(px), sds(px), sds(px, BF), sds((8, D))),
            (noisy, tv, win, w1, vec0),
            (pltpu.VMEM(sh, BF), pltpu.VMEM((8, D), F32)),
        )
    c2, c2b, tr, mats, kvw, vec1, gib, wout, outb = kcall(
        partial(unpack1_kernel, rows_dev),
        (taps, back, sds((4, D, D), BF), sds((16, D, D), BF), sds((2, CTX, D), BF))
        + (sds((24, D)), sds((8, D)), sds((36, D), BF), sds((1, D))),
        (part1,),
        (flat, unrolled, pltpu.VMEM((2, 40, 128), F32)),
    )
    h2, z0, a2, ntr, x1, q, k, v, stats = kcall(
        front_kernel,
        (sds(px),) * 2 + (sds(px, BF),) * 3 + (sds(hx, BF),) * 3 + (sds((8, D)),),
        (h0, h1, stats, c2, tr, vec1),
        (pltpu.VMEM(sh, BF), pltpu.VMEM((8, D), F32)),
        late=(0, 3, 4),
        early=range(8),
    )
    o, lse = kcall(
        attend_kernel, (sds(px, BF), sds((HEADS, 1, N))), (q, k, v), (pltpu.VMEM((D, N), F32),)
    )
    square = (D, W)
    dz1, dh3, dos, loss, gd, ggi, ggo, gkv, dvec, dgib, dwout, dbout = kcall(
        middle_kernel,
        (sds(px), sds(px), sds(hx, BF), sds((1, 1)))
        + (sds((4,) + square, BF), sds((8,) + square, BF), sds((4,) + square, BF), sds((2, CTX, W), BF))
        + (sds((24, D)), sds((8, D)), sds((36, D)), sds((8, 128))),
        (o, z0, h2, context[0], noise, pixel_mask, mats, kvw, vec1, gib, wout, outb),
        [pltpu.VMEM(px, F32)] * 3
        + [pltpu.VMEM(px, BF)] * 4
        + [
            pltpu.VMEM((4, N, D), BF),
            pltpu.VMEM((4, N, D), F32),
            pltpu.VMEM((4, N, D), F32),
            pltpu.VMEM(px, BF),
            pltpu.VMEM(px, BF),
            pltpu.VMEM((HEADS * KEYS, D), BF),
            pltpu.VMEM((HEADS * KEYS, D), BF),
            pltpu.VMEM((N, HEADS * KEYS), F32),
            pltpu.VMEM((N, HEADS * KEYS), BF),
            pltpu.VMEM((8, D), F32),
            pltpu.VMEM((36, N), F32),
        ],
        late=(7, 6, 1, 2),
        early=(0, 1, 2, 4, 5, 6, 7),
    )
    dq, dk, dv = kcall(
        attend_back_kernel,
        (sds(px, BF),) * 3,
        (q, k, v, dos, lse),
        (pltpu.VMEM((D, N), F32), pltpu.VMEM(hx, F32), pltpu.VMEM(hx, F32)),
    )
    step = 16 * n_dp
    front = -(-FRONT // step) * step
    lead = (2, 8) if quick else (n_dp,)
    own1, own0, dtv = kcall(
        back_kernel,
        (
            sds(lead + (SLAB if quick else rows_dev, 128), BF),
            sds(lead + (front // n_dp, 128), BF),
            sds((1, D)),
        ),
        (dq, dk, dv, dz1, dh3, z0, h2, h1, h0, stats, w1b, c2b, tr, vec0, vec1, a1, a2, ntr, x1, noisy,
         gd, ggi, ggo, gkv, dvec, dgib, dwout, dbout),
        (
            pltpu.VMEM(px, F32),
            pltpu.VMEM(sh, BF),
            pltpu.VMEM((sh[0], 3 * W), BF),
            pltpu.VMEM((24, D), F32),
            pltpu.VMEM((2, 4 * R1 // 5, 128), F32),
            pltpu.VMEM((7600, 128), F32),
            pltpu.VMEM((2, 40, 128), F32),
        ),
        late=(5, 3, 17, 6, 4, 16, 7, 11, 20, 21, 22, 23, 15, 8, 10),
        early=(0,),
    )
    facts = kcall(
        time_back_kernel, sds((FACTS, 128)), (dtv, tw2, tw3, p1, p2, e, pixel_mask, loss)
    )
    if quick:
        sum1, sum0, all_facts = sum_over_samples(own1, own0, facts)
    else:
        sum1 = lax.psum_scatter(own1, DP, scatter_dimension=0).astype(F32)
        sum0 = lax.all_gather(lax.psum_scatter(own0, DP, scatter_dimension=0), DP, axis=0, tiled=True)
        sum0 = jnp.pad(sum0, ((0, rows_all - front), (0, 0)))
        sum0 = lax.dynamic_slice_in_dim(sum0, d * rows_dev, rows_dev, 0).astype(F32)
        all_facts = lax.all_gather(facts, DP, axis=0)
    state = sds((2, rows_dev, 128))
    new_params, new_momentum, new_ema, sums = kcall(
        partial(update_kernel, not quick),
        (state, state, state, sds((1, 128))),
        (params[0], momentum[0], ema_params[0], sum1, sum0, all_facts),
    )
    return (new_params[None], new_momentum[None], new_ema[None], sums[0, 0], sums[0, 1])


def solution(mesh):
    packed = P(CH, None, DP, None)
    row = P(DP, None, None)
    return jax.shard_map(
        shards,
        mesh=mesh,
        in_specs=(packed, packed, packed, row, row, P(DP), P(DP, None), row),
        out_specs=(packed, packed, packed, P(), P()),
        check_vma=False,
    )
```

```python
import math
from functools import partial

import jax
import jax.numpy as jnp
from jax import lax
from jax.experimental import pallas as pl
from jax.experimental.pallas import tpu as pltpu
from jax.sharding import PartitionSpec as P

D = 320
W = 160
HEADS = 8
HD = 40
CTX = 768
TXT = 77
LAT = 4
SIDE = 32
N = 1024
EPS = 1e-5
LR = 0.2
MU = 0.9
ED = 0.9
CH = "chan"
DP = "dp"
F32 = jnp.float32
BF = jnp.bfloat16
HI = lax.Precision.HIGHEST
SCALE = HD**-0.5
LOG2E = 1.0 / math.log(2.0)

R0 = 4000
U1, U2, U3 = 2920, 4204, 9328
FRONT = 3650
T1, T2, T3 = 3650, 5255, 11660
C2 = 2
PI = 2885
QKV = 3208
SO = 4168
CQ = 4491
CKV = 4811
CO = 6347
GI = 6670
GIB = 9230
GO = 9238
PO = 10519
OUT = 10842
OUTB = 10878
R1 = 13600
VEC0 = (36, 37, 38, 2919)
VEC1 = (0, 1, 2882, 2883, 2884, 3205, 3206, 3207, 4488, 4489, 4490, 6667, 6668, 6669, 10518, 10839, 10840, 10841)
(N2G, N2B, C2B, NTG, NTB, PIB, L1G, L1B, SOB, L2G, L2B, COB, L3G, L3B, GOB, POB, NOG, NOB) = range(18)
MPI, MQ, MK, MV = range(4)
MSO, MCQ, MCO, MPO, MGV, MGG, MGO = 0, 1, 2, 3, 4, 8, 12


class Flow:
    def __init__(self, ins, outs, sems):
        self.ins = {i: pltpu.make_async_copy(src, dst, sems.at[j]) for j, (i, src, dst) in enumerate(ins)}
        n = len(ins)
        self.outs = {i: pltpu.make_async_copy(src, dst, sems.at[n + j]) for j, (i, dst, src) in enumerate(outs)}
        self.waiting = set(self.ins)
        self.going = []
        for copy in self.ins.values():
            copy.start()

    def need(self, *which):
        for i in which:
            self.ins[i].wait()
            self.waiting.discard(i)

    def ready(self, *which):
        for i in which:
            self.outs[i].start()
            self.going.append(i)

    def end(self):
        self.need(*sorted(self.waiting))
        self.ready(*(i for i in self.outs if i not in self.going))
        for copy in self.outs.values():
            copy.wait()


def kcall(body, outs, ins, scratch=(), late=(), early=()):
    vm, hbm = pl.BlockSpec(memory_space=pltpu.VMEM), pl.BlockSpec(memory_space=pl.ANY)
    single = not isinstance(outs, tuple)
    outs = (outs,) if single else outs
    n, m = len(ins), len(outs)
    late, early = tuple(late), tuple(early)
    scratch = list(scratch)
    count = len(scratch)
    if late or early:
        scratch += [pltpu.VMEM(ins[i].shape, ins[i].dtype) for i in late]
        scratch += [pltpu.VMEM(outs[i].shape, outs[i].dtype) for i in early]
        scratch.append(pltpu.SemaphoreType.DMA((len(late) + len(early),)))

    def whole(*refs):
        if not (late or early):
            return body(*refs)
        given, made, rest = list(refs[:n]), list(refs[n : n + m]), refs[n + m :]
        kept = rest[count:-1]
        inward = [(i, given[i], kept[j]) for j, i in enumerate(late)]
        outward = [(i, made[i], kept[len(late) + j]) for j, i in enumerate(early)]
        for i, _, ref in inward:
            given[i] = ref
        for i, _, ref in outward:
            made[i] = ref
        flow = Flow(inward, outward, rest[-1])
        body(flow, *given, *made, *rest[:count])
        flow.end()

    done = pl.pallas_call(
        whole,
        out_shape=outs,
        in_specs=[hbm if i in late else vm for i in range(n)],
        out_specs=tuple(hbm if i in early else vm for i in range(m)),
        scratch_shapes=scratch,
        compiler_params=pltpu.CompilerParams(vmem_limit_bytes=63 * 2**20),
    )(*ins)
    return done[0] if single else done


def sds(shape, dtype=F32):
    return jax.ShapeDtypeStruct(shape, dtype)


def tiles(fn, size=256, total=N):
    for t in range(total // size):
        fn(pl.ds(t * size, size))


def nn(a, b):
    return jnp.dot(a, b, preferred_element_type=F32)


def nt(a, b):
    return lax.dot_general(a, b, (((1,), (1,)), ((), ())), preferred_element_type=F32)


def tn(a, b):
    return lax.dot_general(a, b, (((0,), (0,)), ((), ())), preferred_element_type=F32)


def colsum(v):
    return jnp.sum(v, axis=0, keepdims=True)


def flatten(a_ref, flat, rows):
    for b in range(2):
        for t in range(a_ref.shape[1]):
            flat[b, t * rows : (t + 1) * rows, :] = a_ref[b, t, :rows, :].astype(F32)


def unroll(flat, s_ref, lo_chunk, hi_chunk):
    q = 80

    @pl.loop(lo_chunk, hi_chunk)
    def _(c):
        f = [[flat[b, pl.ds(c * 5 * q + j, q, stride=5), :] for j in range(5)] for b in range(2)]
        for i in range(4):
            row = []
            for b in range(2):
                lo = 32 * i
                first, second = f[b][i], f[b][i + 1]
                row += [first[:, lo:], second[:, : lo + 32]] if lo else [first, second[:, :32]]
            full = jnp.concatenate(row, axis=1)
            for k, (lo, hi) in enumerate(((0, 128), (128, 256), (256, 320))):
                s_ref[k, pl.ds(c * 4 * q + i, q, stride=4), : hi - lo] = full[:, lo:hi]


def get_rows(s_ref, start, count, step=1):
    ds = pl.ds(start, count) if step == 1 else pl.ds(start, count, stride=step)
    return jnp.concatenate([s_ref[0, ds, :], s_ref[1, ds, :], s_ref[2, ds, :64]], axis=1)


def put_taps(s_ref, start, w, back):
    for r in range(3):
        taps = [get_rows(s_ref, start + D * (3 * r + i), D).astype(BF) for i in range(3)]
        for i in range(3):
            w[r, D * i : D * (i + 1), :] = taps[i]
        back[r] = jnp.concatenate(taps[::-1], axis=1)


def unit_row(parts):
    out = [p[:, W * b : W * (b + 1)] for b in range(2) for p in parts]
    return jnp.broadcast_to(jnp.concatenate(out, axis=1), (8, 4 * D))


def unit_parts(row):
    return [
        jnp.concatenate([row[:, W * i : W * (i + 1)], row[:, 640 + W * i : 640 + W * (i + 1)]], axis=1)
        for i in range(4)
    ]


def take_front(s_ref, win, w1, w1b, vec):
    win[...] = get_rows(s_ref, 0, 36).astype(BF)
    put_taps(s_ref, 39, w1, w1b)
    for i, r in enumerate(VEC0):
        vec[i : i + 1, :] = get_rows(s_ref, r, 1)


def take_time(s_ref, tw2, tw3):
    for i in range(4):
        tw2[i] = get_rows(s_ref, U2 + i, 4 * D, 4).astype(BF)
    tw3[...] = get_rows(s_ref, U3, 4 * D).astype(BF)


def time_forward(s_ref, e, tw2, tw3, tv, p1, p2):
    u = e[...].astype(BF)
    p1[...] = unit_row(
        [nn(u, get_rows(s_ref, U1 + i, D, 4).astype(BF))[:1] + get_rows(s_ref, U1 + 4 * D + i, 1) for i in range(4)]
    )
    u = silu(p1[...]).astype(BF)
    p2[...] = unit_row([nn(u, tw2[i])[:1] + get_rows(s_ref, U2 + 16 * D + i, 1) for i in range(4)])
    u = silu(p2[...]).astype(BF)
    tv[...] = nn(u, tw3[...])[:1] + get_rows(s_ref, U3 + 4 * D, 1)


def unpack0_kernel(rows, a_ref, e, win, w1, w1b, vec, tw2, tw3, tv, p1, p2, flat, s_ref):
    flatten(a_ref, flat, rows)
    unroll(flat, s_ref, 0, R1 // 400)
    take_front(s_ref, win, w1, w1b, vec)
    take_time(s_ref, tw2, tw3)
    time_forward(s_ref, e, tw2, tw3, tv, p1, p2)


FE, FU1, FU2, FD1, FD2, FD3, FL = 0, 3, 13, 23, 28, 33, 35
FACTS = 40


def time_back(dtv, tw2, tw3, p1, p2, e, mask, loss, facts):
    first = lax.axis_index(CH) == 0
    g = jnp.broadcast_to(dtv[...], (8, D)).astype(BF)
    d2 = nt(g, tw3[...]) * silu_slope(p2[...])
    total = jnp.zeros((8, 4 * D), F32)
    for i, part in enumerate(unit_parts(d2)):
        total += nt(part.astype(BF), tw2[i])
    d1 = total * silu_slope(p1[...])
    facts[...] = jnp.zeros_like(facts)

    def put(at, v):
        for i in range(0, v.shape[1], 128):
            n = min(128, v.shape[1] - i)
            facts[at + i // 128 : at + i // 128 + 1, :n] = v[:1, i : i + n]

    put(FE, e[...].astype(BF).astype(F32))
    put(FU1, silu(p1[...]).astype(BF).astype(F32))
    put(FU2, silu(p2[...]).astype(BF).astype(F32))
    put(FD1, jnp.where(first, d1[:, : 2 * D], d1[:, 2 * D :]))
    put(FD2, jnp.where(first, d2[:, : 2 * D], d2[:, 2 * D :]))
    put(FD3, own(dtv[...]))
    facts[FL : FL + 1, 0:1] = loss[...]
    facts[FL : FL + 1, 1:2] = jnp.sum(mask[...].astype(F32), axis=1, keepdims=True)


def unpack1_kernel(rows, a_ref, c2, c2b, tr, mats, kv, vec, gib, wout, outb, flat, s_ref, o_ref):
    flatten(a_ref, flat, rows)
    unroll(flat, s_ref, 0, R1 // 400)
    put_taps(s_ref, C2, c2, c2b)
    tr[MPI] = get_rows(s_ref, PI, D).astype(BF)
    for m, r in ((MSO, SO), (MCQ, CQ), (MCO, CO), (MPO, PO)):
        mats[m] = get_rows(s_ref, r, D).astype(BF)
    for j in range(3):
        tr[MQ + j] = get_rows(s_ref, QKV + j, D, 3).astype(BF)
    for j in range(8):
        mats[MGV + j] = get_rows(s_ref, GI + j, D, 8).astype(BF)
    for j in range(4):
        for b in range(2):
            mats[MGO + j, b * W : (b + 1) * W, :] = get_rows(s_ref, GO + 640 * b + W * j, W).astype(BF)
    for j in range(2):
        kv[j] = get_rows(s_ref, CKV + j, CTX, 2).astype(BF)
    for i, r in enumerate(VEC1):
        vec[i : i + 1, :] = get_rows(s_ref, r, 1)
    gib[...] = get_rows(s_ref, GIB, 8)
    outb[...] = get_rows(s_ref, OUTB, 1)
    lane = lax.broadcasted_iota(jnp.int32, (W, W), 0)
    col = lax.broadcasted_iota(jnp.int32, (W, W), 1)
    pick = ((lane % 2) * 80 + lane // 2 == col).astype(BF)
    raw = get_rows(s_ref, OUT, 36).astype(BF)
    for b in range(2):
        moved = nn(raw[:, W * b : W * (b + 1)], pick)
        o_ref[0, :36, :] = moved[:, :128]
        o_ref[1, :36, :32] = moved[:, 128:]
        for ch in range(2):
            pieces = []
            for m in range(4):
                ds = pl.ds(m, 9, stride=4)
                both = jnp.concatenate([o_ref[0, ds, :], o_ref[1, ds, :32]], axis=1)
                pieces.append(both[:, 80 * ch : 80 * ch + 80])
            at = (2 * b + ch) * 9
            wout[at : at + 9, :] = jnp.concatenate(pieces, axis=1).astype(BF)


def pixel_col(n, axis):
    shape = (n, 1) if axis == 0 else (1, n)
    return lax.broadcasted_iota(jnp.int32, shape, axis)


def shift_lanes(v, tap):
    r, s = tap // 3 - 1, tap % 3 - 1
    pix = pixel_col(N, 1)
    i, j = pix // SIDE + r, pix % SIDE + s
    ok = (i >= 0) & (i < SIDE) & (j >= 0) & (j < SIDE)
    move = -(r * SIDE + s) % N
    moved = pltpu.roll(v, move, 1) if move else v
    return jnp.where(ok, moved, 0.0)


def put_shifts(ref, v):
    j = pixel_col(N, 0) % SIDE
    left = jnp.where(j == 0, 0.0, pltpu.roll(v, 1, 0)).astype(BF)
    right = jnp.where(j == SIDE - 1, 0.0, pltpu.roll(v, N - 1, 0)).astype(BF)
    ref[SIDE : SIDE + N, :] = jnp.concatenate([left, v.astype(BF), right], axis=1)


def clear_margins(ref):
    zero = jnp.zeros((SIDE, ref.shape[1]), BF)
    ref[:SIDE, :] = zero
    ref[SIDE + N :, :] = zero


def conv_rows(ref, w_ref):
    return sum(nn(ref[SIDE * r : SIDE * r + N, :], w_ref[r]) for r in range(3))


def conv_back_rows(ref, w_ref):
    return sum(nt(ref[SIDE * (2 - r) : SIDE * (2 - r) + N, :], w_ref[r]) for r in range(3))


def group_mean(sums):
    a = lax.broadcasted_iota(jnp.int32, (D, D), 0) // 10
    b = lax.broadcasted_iota(jnp.int32, (D, D), 1) // 10
    pool = jnp.where(a == b, 1.0, 0.0)
    wide = jnp.broadcast_to(sums, (8, D))
    out = jnp.dot(wide, pool, precision=HI, preferred_element_type=F32)
    return out[:1] * (1.0 / (10 * N))


def group_stats(v_ref, acc, sums):
    mean = group_mean(sums)
    acc[0:1, :] = colsum(jnp.square(v_ref[...] - mean))
    return mean, lax.rsqrt(group_mean(acc[0:1, :]) + EPS)


def silu(v):
    return v * jax.nn.sigmoid(v)


def silu_slope(v):
    sig = jax.nn.sigmoid(v)
    return sig * (1.0 + v * (1.0 - sig))


def layer(v):
    mean = jnp.sum(v, axis=1, keepdims=True) * (1.0 / D)
    sq = jnp.sum(v * v, axis=1, keepdims=True) * (1.0 / D)
    inv = lax.rsqrt(sq - mean * mean + EPS)
    return (v - mean) * inv, inv


def layer_back(grad, normed, inv, gain):
    ghat = grad * gain
    m1 = jnp.sum(ghat, axis=1, keepdims=True) * (1.0 / D)
    m2 = jnp.sum(ghat * normed, axis=1, keepdims=True) * (1.0 / D)
    return inv * (ghat - m1 - normed * m2)


def own(v):
    return jnp.where(lax.axis_index(CH) == 0, v[..., :W], v[..., W:])


def head(v, h):
    return v[:, HD * h : HD * (h + 1)]


def group_norm(src, acc, total, stats, at):
    mean, inv = group_stats(src, acc, total)
    stats[at : at + 1, :], stats[at + 1 : at + 2, :] = mean, inv
    return (src[...] - mean) * inv


def start_steps(noisy, tv, win, w1, vec0, h0, h1, a1, stats, sh, acc):
    def first():
        cols = jnp.concatenate([shift_lanes(noisy[...], t) for t in range(9)], axis=0).astype(BF)
        clear_margins(sh)
        stats[...] = jnp.zeros_like(stats)
        h = tn(cols, win[...]) + vec0[0:1, :]
        h0[...] = h
        y = silu(group_norm(h0, acc, colsum(h), stats, 0) * vec0[1:2, :] + vec0[2:3, :])
        put_shifts(sh, y)
        a1[...] = y.astype(BF)

    def taps(r):
        def one():
            part = nn(sh[SIDE * r : SIDE * r + N, :], w1[r])
            h1[...] = (h1[...] if r else vec0[3:4, :] + tv[...]) + part

        return one

    return [first, taps(0), taps(1), taps(2)]


def start_kernel(noisy, tv, win, w1, vec0, h0, h1, a1, stats, sh, acc):
    for step in start_steps(noisy, tv, win, w1, vec0, h0, h1, a1, stats, sh, acc):
        step()


def front_kernel(flow, h0, h1, stats_in, c2, tr, vec1, h2, z0, a2, ntr, x1, q, k, v, stats, sh, acc):
    clear_margins(sh)
    stats[...] = stats_in[...]
    y = silu(group_norm(h1, acc, colsum(h1[...]), stats, 2) * vec1[N2G : N2G + 1, :] + vec1[N2B : N2B + 1, :])
    put_shifts(sh, y)
    a2[...] = y.astype(BF)
    flow.ready(2)
    flow.need(0, 3)
    h = h0[...] + conv_rows(sh, c2) + vec1[C2B : C2B + 1, :]
    h2[...] = h
    flow.ready(0)
    n = group_norm(h2, acc, colsum(h), stats, 4)
    n = (n * vec1[NTG : NTG + 1, :] + vec1[NTB : NTB + 1, :]).astype(BF)
    ntr[...] = n
    flow.ready(3)
    flow.need(4)
    z = nn(n, tr[MPI]) + vec1[PIB : PIB + 1, :]
    z0[...] = z
    flow.ready(1)
    normed, _ = layer(z)
    x = (normed * vec1[L1G : L1G + 1, :] + vec1[L1B : L1B + 1, :]).astype(BF)
    x1[...] = x
    flow.ready(4)
    for i, (at, dst) in enumerate(((MQ, q), (MK, k), (MV, v))):
        y = nn(x, tr[at]).astype(BF)
        for hd in range(HEADS):
            dst[hd] = head(y, hd)
        flow.ready(5 + i)


AT = 512


def attend_kernel(q, k, v, o, lse, ot):
    steps = [(h, pl.ds(t * AT, AT)) for h in range(HEADS) for t in range(N // AT)]

    def scores(h, rows):
        return nt(k[h], q[h, rows, :])

    now = scores(*steps[0])
    for i, (h, rows) in enumerate(steps):
        later = scores(*steps[i + 1]) if i + 1 < len(steps) else None
        if i % (N // AT) == 0:
            vt = v[h].astype(F32).T.astype(BF)
        s = now * (SCALE * LOG2E)
        top = jnp.max(s, axis=0, keepdims=True)
        e = jnp.exp2(s - top)
        total = jnp.sum(e, axis=0, keepdims=True)
        lse[h, :, rows] = top + jnp.log(total) * LOG2E
        ot[h * HD : (h + 1) * HD, rows] = nn(vt, (e * (1.0 / total)).astype(BF))
        now = later
    o[...] = ot[...].T.astype(BF)


KEYS = 128


def by_head(v):
    wide = jnp.concatenate([v, jnp.zeros((KEYS - TXT, D), v.dtype)], axis=0)
    col = lax.broadcasted_iota(jnp.int32, (KEYS, D), 1) // HD
    return jnp.concatenate([jnp.where(col == h, wide, 0.0) for h in range(HEADS)], axis=0)


def from_heads(vt):
    row = lax.broadcasted_iota(jnp.int32, (D, KEYS), 0) // HD
    total = jnp.zeros((D, KEYS), F32)
    for h in range(HEADS):
        total += jnp.where(row == h, vt[:, KEYS * h : KEYS * (h + 1)], 0.0)
    return total.T[:TXT]


def transposed(v):
    return v.T


def middle_kernel(
    flow, o, z0, h2, ctx, noise, mask, mats, kvw, vec, gib, wout, outb,
    dz1, dh3, dos, loss, gd, ggi, ggo, gkv, dvec, dgib, dwout, dbout,
    z1, z2, h3, x2, x3, oc, z3b, gl, by_a, by_g, a3, qc, kb, vb, prob, dsc, acc, pt, oct_, x2t, ot, x3t,
):
    def row(i):
        return vec[i : i + 1, :]

    def put(i, v):
        dvec[i : i + 1, :] = v

    flow.need(7)
    kb[...] = by_head(nn(ctx[...], kvw[0])).astype(BF)
    vb[...] = by_head(nn(ctx[...], kvw[1])).astype(BF)
    flow.need(6, 1)
    z = z0[...] + nn(o[...], mats[MSO]) + row(SOB)
    z1[...] = z
    normed, _ = layer(z)
    x = (normed * row(L2G) + row(L2B)).astype(BF)
    x2[...] = x
    qq = nn(x, mats[MCQ]).astype(BF)
    qc[...] = qq
    s = nt(qq, kb[...]) * (SCALE * LOG2E)
    there = lax.broadcasted_iota(jnp.int32, (1, KEYS), 1) < TXT
    for h in range(HEADS):
        at = slice(KEYS * h, KEYS * (h + 1))
        sh = jnp.where(there, s[:, at], -jnp.inf)
        e = jnp.exp2(sh - jnp.max(sh, axis=1, keepdims=True))
        prob[:, at] = e * (1.0 / jnp.sum(e, axis=1, keepdims=True))
    c = nn(prob[...].astype(BF), vb[...]).astype(BF)
    oc[...] = c
    z = z1[...] + nn(c, mats[MCO]) + row(COB)
    z2[...] = z
    normed, _ = layer(z)
    x = (normed * row(L3G) + row(L3B)).astype(BF)
    x3[...] = x
    moving = ((oc, oct_), (x2, x2t), (o, ot), (x3, x3t))
    for j in range(4):
        moving[j][1][...] = transposed(moving[j][0][...])
        a = nn(x, mats[MGV + j]) + gib[j : j + 1, :]
        g = nn(x, mats[MGG + j]) + gib[4 + j : 5 + j, :]
        cdf = 0.5 * (1.0 + lax.erf(g * math.sqrt(0.5)))
        gelu = g * cdf
        by_a[j] = gelu
        by_g[j] = a * (cdf + g * jnp.exp(-0.5 * g * g) * (1.0 / math.sqrt(2.0 * math.pi)))
        y = (a * gelu).astype(BF)
        gl[j] = y
        z = z + nn(y, mats[MGO + j])
    zb = (z + row(GOB)).astype(BF)
    z3b[...] = zb
    flow.need(2)
    h = h2[...] + nn(zb, mats[MPO]) + row(POB)
    h3[...] = h
    mean, inv = group_stats(h3, acc, colsum(h))
    gain, bias = row(NOG), row(NOB)
    a3[...] = silu((h3[...] - mean) * inv * gain + bias).astype(BF)
    taps = nt(wout[...], a3[...])
    for ch in range(LAT):
        pred = jnp.zeros((1, N), F32)
        for t in range(9):
            pred += shift_lanes(taps[9 * ch + t : 9 * ch + t + 1, :], t)
        at = W * (ch // 2) + ch % 2
        err = pred + outb[0:1, at : at + 1] - noise[ch : ch + 1, :]
        weighed = mask[...].astype(F32) * err
        g = 2.0 * weighed
        acc[2 + ch : 3 + ch, 0:1] = jnp.sum(weighed * err, axis=1, keepdims=True)
        dbout[ch : ch + 1, :] = jnp.broadcast_to(jnp.sum(g, axis=1, keepdims=True), (1, 128))
        for t in range(9):
            pt[9 * ch + t : 9 * ch + t + 1, :] = shift_lanes(g, 8 - t)
    loss[...] = acc[2:3, 0:1] + acc[3:4, 0:1] + acc[4:5, 0:1] + acc[5:6, 0:1]

    dvec[...] = jnp.zeros_like(dvec)
    taps = pt[...].astype(BF)
    dwout[...] = nn(taps, a3[...])
    n = (h3[...] - mean) * inv
    g = tn(taps, wout[...]) * silu_slope(n * gain + bias)
    dgain, dbias = colsum(g * n), colsum(g)
    put(NOG, dgain)
    put(NOB, dbias)
    g = inv * (g * gain - group_mean(gain * dbias) - n * group_mean(gain * dgain))
    dh3[...] = g
    flow.ready(1)
    put(POB, colsum(g))
    gd[0] = nn(transposed(z3b[...]), own(g).astype(BF)).astype(BF)
    dz3 = nt(g.astype(BF), mats[MPO])
    z1b = dz3.astype(BF)
    put(GOB, colsum(dz3))
    mine_t = transposed(own(dz3).astype(BF))
    xt = x3t[...]
    dx = jnp.zeros((N, D), F32)
    for j in range(4):
        dgl = nt(z1b, mats[MGO + j])
        ggo[j] = nn(mine_t, gl[j]).T.astype(BF)
        da = dgl * by_a[j]
        dg = dgl * by_g[j]
        dgib[j : j + 1, :] = colsum(da)
        dgib[4 + j : 5 + j, :] = colsum(dg)
        ggi[j] = nn(xt, own(da).astype(BF)).astype(BF)
        ggi[4 + j] = nn(xt, own(dg).astype(BF)).astype(BF)
        dx += nt(da.astype(BF), mats[MGV + j]) + nt(dg.astype(BF), mats[MGG + j])
    flow.ready(5, 6)
    normed, li = layer(z2[...])
    put(L3G, colsum(dx * normed))
    put(L3B, colsum(dx))
    dz = dz3 + layer_back(dx, normed, li, row(L3G))
    z2[...] = dz
    put(COB, colsum(dz))
    gd[1] = nn(oct_[...], own(dz).astype(BF)).astype(BF)
    do = nt(dz.astype(BF), mats[MCO]).astype(BF)
    dp = nt(do, vb[...])
    dot = transposed(do)
    qt = transposed(qc[...])
    gkv[1] = tn(ctx[...], own(from_heads(nn(dot, prob[...].astype(BF)))).astype(BF)).astype(BF)
    for h in range(HEADS):
        at = slice(KEYS * h, KEYS * (h + 1))
        p, d = prob[:, at], dp[:, at]
        dsc[:, at] = (p * (d - jnp.sum(p * d, axis=1, keepdims=True)) * SCALE).astype(BF)
    gkv[0] = tn(ctx[...], own(from_heads(nn(qt, dsc[...]))).astype(BF)).astype(BF)
    flow.ready(7)
    dq = nn(dsc[...], kb[...])
    gd[2] = nn(x2t[...], own(dq).astype(BF)).astype(BF)
    dx = nt(dq.astype(BF), mats[MCQ])
    normed, li = layer(z1[...])
    put(L2G, colsum(dx * normed))
    put(L2B, colsum(dx))
    dz = z2[...] + layer_back(dx, normed, li, row(L2G))
    dz1[...] = dz
    flow.ready(0)
    put(SOB, colsum(dz))
    gd[3] = nn(ot[...], own(dz).astype(BF)).astype(BF)
    do = nt(dz.astype(BF), mats[MSO]).astype(BF)
    for h in range(HEADS):
        dos[h] = head(do, h)


ABT = 256


def attend_back_kernel(q, k, v, do, lse, dq, dk, dv, qt, kacc, vacc):
    steps = [(h, pl.ds(t * ABT, ABT)) for h in range(HEADS) for t in range(N // ABT)]

    def scores(h, rows):
        return nt(k[h], q[h, rows, :]), nt(v[h], do[h, rows, :])

    now = scores(*steps[0])
    for i, (h, rows) in enumerate(steps):
        later = scores(*steps[i + 1]) if i + 1 < len(steps) else None
        s, dp = now
        p = jnp.exp2(s * (SCALE * LOG2E) - lse[h, :, rows])
        ds = (p * (dp - jnp.sum(p * dp, axis=0, keepdims=True)) * SCALE).astype(BF)
        dkt, dvt = nn(ds, q[h, rows, :]), nn(p.astype(BF), do[h, rows, :])
        if i % (N // ABT) == 0:
            kt = k[h].astype(F32).T.astype(BF)
            kacc[h], vacc[h] = dkt, dvt
        else:
            kacc[h] += dkt
            vacc[h] += dvt
        qt[h * HD : (h + 1) * HD, rows] = nn(kt, ds)
        now = later

    dq[...] = qt[...].T.astype(BF)

    def one(rows):
        for acc, dst in ((kacc, dk), (vacc, dv)):
            dst[rows, :] = jnp.concatenate([acc[h, rows, :] for h in range(HEADS)], axis=1).astype(BF)

    tiles(one)


def put_rows(s_ref, start, v, step=1):
    n = v.shape[0]
    ds = pl.ds(start, n) if step == 1 else pl.ds(start, n, stride=step)
    s_ref[0, ds, :] = v[:, :128]
    s_ref[1, ds, :32] = v[:, 128:]


def roll_rows(s_ref, out_ref, lo_chunk, hi_chunk):
    q = 80

    @pl.loop(lo_chunk, hi_chunk)
    def _(c):
        g = []
        for i in range(4):
            ds = pl.ds(c * 4 * q + i, q, stride=4)
            g.append((s_ref[0, ds, :], s_ref[1, ds, :32]))
        base = (c - lo_chunk) * 5 * q
        out_ref[pl.ds(base, q, stride=5), :] = g[0][0]
        for i in range(3):
            lo = 96 - 32 * i
            out_ref[pl.ds(base + i + 1, q, stride=5), :] = jnp.concatenate(
                ([g[i][0][:, 128 - 32 * i :]] if i else []) + [g[i][1], g[i + 1][0][:, :lo]], axis=1
            )
        out_ref[pl.ds(base + 4, q, stride=5), :] = jnp.concatenate([g[3][0][:, 32:], g[3][1]], axis=1)


def by_owner(s_ref, flat, out, total):
    owners, room = math.prod(out.shape[:-2]), out.shape[-2]
    size = room if total < owners * room and len(out.shape) == 3 else min(room, ROWS)
    half = owners // 2 * size
    for lo, hi, first in ((0, min(-(-half // 400), total // 400), 0), (half // 400, total // 400, owners // 2)):
        if hi > lo:
            roll_rows(s_ref, flat, lo, hi)
        at = 400 * max(hi - lo, 0)
        if at < flat.shape[0]:
            flat[at:, :] = jnp.zeros((flat.shape[0] - at, 128), F32)
        for t in range(first, first + owners // 2):
            spot = (t % 2, t // 2) if len(out.shape) == 4 else (t,)
            row = t * size - 400 * lo
            out[(*spot, slice(0, size))] = flat[row : row + size, :].astype(BF)
            if room > size:
                out[(*spot, slice(size, room))] = jnp.zeros((room - size, 128), BF)


def conv_grads(a_ref, g_ref, s_ref, start):
    at = transposed(a_ref[...])
    for r in range(3):
        rows = SIDE * (2 - r)
        three = nn(at, g_ref[rows : rows + N, :])
        for i in range(3):
            put_rows(s_ref, start + D * (3 * r + i), three[:, W * (2 - i) : W * (3 - i)])


def back_kernel(
    flow, dq, dk, dv, dz1, dh3, z0, h2, h1, h0, stats, w1, c2, tr, vec0, vec1, a1, a2, ntr, x1, noisy,
    gd, ggi, ggo, gkv, dvec_in, dgib, dwout, dbout,
    out1, out0, dtv,
    dh, g_ref, go_ref, dvec, s_ref, flat, o_ref,
):
    c = lax.axis_index(CH)
    clear_margins(g_ref)
    clear_margins(go_ref)
    dvec[...] = dvec_in[...]

    def row(i):
        return vec1[i : i + 1, :]

    def put(i, v):
        dvec[i : i + 1, :] = v

    dx = nt(dq[...], tr[MQ]) + nt(dk[...], tr[MK]) + nt(dv[...], tr[MV])
    xt = transposed(x1[...])
    for j, g in enumerate((dq, dk, dv)):
        put_rows(s_ref, QKV + j, nn(xt, own(g[...].astype(F32)).astype(BF)), 3)
    flow.need(5, 3)
    normed, li = layer(z0[...])
    put(L1G, colsum(dx * normed))
    put(L1B, colsum(dx))
    dz = dz1[...] + layer_back(dx, normed, li, row(L1G))
    put(PIB, colsum(dz))
    flow.need(17)
    put_rows(s_ref, PI, tn(ntr[...], own(dz).astype(BF)))
    g = nt(dz.astype(BF), tr[MPI])

    def norm_back(g, n, at, gain):
        dgain, dbias = colsum(g * n), colsum(g)
        back = stats[at + 1 : at + 2, :] * (g * gain - group_mean(gain * dbias) - n * group_mean(gain * dgain))
        return back, dgain, dbias

    def normed_of(src, at):
        return (src[...] - stats[at : at + 1, :]) * stats[at + 1 : at + 2, :]

    flow.need(6, 4)
    g, dgain, dbias = norm_back(g, normed_of(h2, 4), 4, row(NTG))
    put(NTG, dgain)
    put(NTB, dbias)
    g = dh3[...] + g
    dh[...] = g
    put(C2B, colsum(g))
    put_shifts(g_ref, g)
    put_shifts(go_ref, own(g))
    flow.need(16)
    conv_grads(a2, go_ref, s_ref, C2)
    flow.need(7, 11)
    n = normed_of(h1, 2)
    g = conv_back_rows(g_ref, c2) * silu_slope(n * row(N2G) + row(N2B))
    g, dgain, dbias = norm_back(g, n, 2, row(N2G))
    put(N2G, dgain)
    put(N2B, dbias)
    total = colsum(g)
    dtv[...] = total
    put_shifts(g_ref, g)
    put_shifts(go_ref, own(g))

    flow.need(20, 21, 22, 23)
    for i, r in enumerate((PO, CO, CQ, SO)):
        put_rows(s_ref, r, gd[i].astype(F32))
    for j in range(8):
        put_rows(s_ref, GI + j, ggi[j].astype(F32), 8)
    for j in range(4):
        rows = ggo[j].astype(F32)
        for b in range(2):
            put_rows(s_ref, GO + 640 * b + W * j, rows[W * b : W * (b + 1), :])
    for j in range(2):
        put_rows(s_ref, CKV + j, gkv[j].astype(F32), 2)
    for i, r in enumerate(VEC1):
        put_rows(s_ref, r, own(dvec[i : i + 1, :]))
    put_rows(s_ref, GIB, own(dgib[...]))
    wide = jnp.where(c == 0, dwout[:18, :], dwout[18:36, :])
    for ch in range(2):
        for m in range(4):
            o_ref[ch, pl.ds(m, 9, stride=4), :80] = wide[9 * ch : 9 * ch + 9, 80 * m : 80 * m + 80]
    lane = lax.broadcasted_iota(jnp.int32, (80, W), 0)
    col = lax.broadcasted_iota(jnp.int32, (80, W), 1)
    moved = jnp.zeros((36, W), F32)
    for ch in range(2):
        spot = jnp.where(2 * lane + ch == col, 1.0, 0.0)
        moved += jnp.dot(o_ref[ch, :36, :80], spot, precision=HI, preferred_element_type=F32)
    put_rows(s_ref, OUT, moved)
    b0 = jnp.where(c == 0, dbout[0:1, 0:1], dbout[2:3, 0:1])
    b1 = jnp.where(c == 0, dbout[1:2, 0:1], dbout[3:4, 0:1])
    at = lax.broadcasted_iota(jnp.int32, (1, W), 1)
    put_rows(s_ref, OUTB, jnp.where(at == 0, b0, jnp.where(at == 1, b1, 0.0)))
    s_ref[:, OUTB + 1 :, :] = jnp.zeros((2, 4 * R1 // 5 - OUTB - 1, 128), F32)
    by_owner(s_ref, flat, out1, R1)
    flow.ready(0)

    flow.need(15, 8, 10)
    conv_grads(a1, go_ref, s_ref, 39)
    n = normed_of(h0, 0)
    g = conv_back_rows(g_ref, w1) * silu_slope(n * vec0[1:2, :] + vec0[2:3, :])
    g, dgain, dbias = norm_back(g, n, 0, vec0[1:2, :])
    g = dh[...] + g
    cols = jnp.concatenate([shift_lanes(noisy[...], t) for t in range(9)], axis=0).astype(BF)
    put_rows(s_ref, 0, nn(cols, own(g).astype(BF)))
    for r, v in zip(VEC0, (colsum(g), dgain, dbias, total)):
        put_rows(s_ref, r, own(v))
    s_ref[:, 4 * FRONT // 5 : 4 * R0 // 5, :] = jnp.zeros((2, 4 * (R0 - FRONT) // 5, 128), F32)
    by_owner(s_ref, flat, out0, R0)


FIRST = (0, 0, 1, 2, 3)
SECOND = (0, 1, 2, 3, 3)


def time_rows(facts, count):
    row = lax.axis_index(DP) * count + lax.broadcasted_iota(jnp.int32, (count, 1), 0)

    def wide(at, n):
        return jnp.concatenate([facts[:, at + i, :] for i in range(n)], axis=1)

    def meets(u, k):
        spot = jnp.where(k == lax.broadcasted_iota(jnp.int32, (1, u.shape[1]), 1), 1.0, 0.0).astype(BF)
        return nt(spot, u.astype(BF))

    total = jnp.zeros((count, 128), F32)
    for u, at, start, size in ((wide(FE, 3)[:, :D], FD1, T1, D), (wide(FU1, 10), FD2, T2, 4 * D)):
        rel = row - start
        k, line = rel // 5, rel % 5
        met = meets(u, jnp.where(rel < 0, -1, k))
        for j in range(5):
            g = facts[:, at + j, :]
            total += nn(jnp.where(line == j, met, 0.0).astype(BF), g.astype(BF))
            total += jnp.where((rel >= 0) & (k == size) & (line == j), colsum(g), 0.0)
    rel = row - T3
    group, line = rel // 5, rel % 5
    d3 = wide(FD3, 2)[:, :W]
    zero = jnp.zeros((d3.shape[0], 128), F32)
    u = wide(FU2, 10)
    for picks, shift in ((FIRST, 0), (SECOND, 1)):
        k = jnp.full_like(rel, -1)
        for j in range(5):
            k = jnp.where((rel >= 0) & (line == j), 4 * group + picks[j], k)
        met = meets(u, k)
        for j in range(5):
            if shift == 0:
                lo = (0, 128, 96, 64, 32)[j]
                g = d3[:, lo : min(lo + 128, W)]
                g = jnp.concatenate([g, zero[:, : 128 - g.shape[1]]], axis=1) if g.shape[1] < 128 else g
            else:
                if j in (0, 4):
                    continue
                g = jnp.concatenate([zero[:, : 32 * j], d3[:, : 128 - 32 * j]], axis=1)
            total += nn(jnp.where(line == j, met, 0.0).astype(BF), g.astype(BF))
            total += jnp.where((k == 4 * D) & (line == j), colsum(g), 0.0)
    return total


def update_kernel(with_time, params, momentum, ema, sum1, sum0, facts, new_params, new_momentum, new_ema, sums):
    total = facts[0, FL : FL + 1, :]
    for i in range(1, facts.shape[0]):
        total += facts[i, FL : FL + 1, :]
    sums[...] = total
    scale = 1.0 / (LAT * jnp.maximum(total[:, 1:2], 1.0))
    first = sum0[...]
    if with_time:
        first += time_rows(facts, sum0.shape[0])
    for p, g in enumerate((first, sum1[...])):
        g = g * scale
        m = MU * momentum[p] + g
        new_momentum[p] = m
        w = params[p] - LR * (g + MU * m)
        new_params[p] = w
        new_ema[p] = ED * ema[p] + (1.0 - ED) * w


ROWS = 856
SLAB = 864
SOME = 240
REST = SLAB - 3 * SOME


def send(src, dst, sems, i, j, target):
    copy = pltpu.make_async_remote_copy(
        src_ref=src, dst_ref=dst, send_sem=sems[0].at[i], recv_sem=sems[1].at[j],
        device_id={DP: target}, device_id_type=pl.DeviceIdType.MESH,
    )
    copy.start()
    return copy


PIECES = tuple(slice(16 * a, 16 * b) for a, b in ((0, 7), (7, 14), (14, 21), (21, 28), (28, 35), (35, 42), (42, 48), (48, 54)))


def gather_kernel(
    params, step, latents, noise, g0, g1, e, noisy, vec, p1, p2, stats, w1b_out, tw2_out, tw3_out, h0_out, h1_out, a1_out,
    low, slabs, flat, s_ref, w1b, tw2, tw3, h0, h1, a1, w1, win, tv, sh, acc,
    send_sem, recv_sem, keep_sem, slab_sem, out_sem,
):
    low[:, :ROWS, :] = params[...].astype(BF)
    low[:, ROWS:, :] = jnp.zeros((2, SLAB - ROWS, 128), BF)
    me, y = lax.axis_index(DP), lax.axis_index(CH)
    k, x, z = me % 2, (me // 2) % 2, me // 4
    core = {DP: me + 1 - 2 * k}
    side = {DP: me + 2 - 4 * x}
    other = {CH: 1 - y}
    ring = [{DP: (me + 4 * o) % 16} for o in range(4)]
    barrier = pltpu.get_barrier_semaphore()
    for target in [core, side, other] + ring[1:]:
        pl.semaphore_signal(barrier, inc=1, device_id=target, device_id_type=pl.DeviceIdType.MESH)
    pl.semaphore_wait(barrier, 6)
    count = [0]
    started = []

    def push(ref, target):
        i = count[0]
        count[0] += 1
        return [start(ref, ref, i, i, target)]

    def start(src, dst, i, j, target):
        copy = pltpu.make_async_remote_copy(
            src_ref=src, dst_ref=dst, send_sem=send_sem.at[i], recv_sem=recv_sem.at[j],
            device_id=target, device_id_type=pl.DeviceIdType.MESH,
        )
        copy.start()
        started.append(copy)
        return copy

    def push_ring(ref):
        i = count[0]
        count[0] += 3
        return [start(ref, ref, i + o - 1, i + 3 - o, ring[o]) for o in (2, 1, 3)]

    def arrive(copies):
        for copy in copies:
            copy.wait_recv()

    keeps = []
    for p, g in enumerate((g0, g1)):
        keep = pltpu.make_async_copy(low.at[p], g.at[y, z, x, k], keep_sem.at[p])
        keep.start()
        keeps.append(keep)
    work = [(p, g, rows, i % 2) for p, g in enumerate((g0, g1)) for i, rows in enumerate(PIECES)]
    first, second, third, last = {}, {}, {}, []

    def begin(i):
        p, g, rows, _ = work[i]
        if i % len(PIECES) == 0:
            keeps[p].wait()
        first[i] = push_ring(g.at[y, z, x, k, rows])

    def middle(i):
        _, g, rows, turn = work[i]
        arrive(first[i])
        second[i] = push(g.at[y, :, x, k, rows], other if turn else side)
        last.extend(push(g.at[y, :, x, k, rows], core))

    def finish(i):
        _, g, rows, turn = work[i]
        arrive(second[i])
        if turn:
            third[i] = push(g.at[:, :, x, k, rows], side)
            last.extend(push(g.at[1 - y, :, x, k, rows], core))
        else:
            third[i] = push(g.at[y, :, :, k, rows], other)
            last.extend(push(g.at[y, :, 1 - x, k, rows], core))

    def pass_on(i):
        _, g, rows, turn = work[i]
        arrive(third[i])
        last.extend(push(g.at[:, :, 1 - x, k, rows] if turn else g.at[1 - y, :, :, k, rows], core))

    outs = [
        pltpu.make_async_copy(src, dst, out_sem.at[i])
        for i, (src, dst) in enumerate(
            ((w1b, w1b_out), (tw2, tw2_out), (tw3, tw3_out), (h0, h0_out), (h1, h1_out), (a1, a1_out))
        )
    ]
    fetches = [
        pltpu.make_async_copy(g0.at[a, b], slabs.at[a, b], slab_sem.at[4 * a + b]) for a in range(2) for b in range(4)
    ]

    def fetch():
        arrive(last)
        last.clear()
        for copy in fetches:
            copy.start()

    def flat_half(a):
        for copy in fetches[4 * a : 4 * a + 4]:
            copy.wait()
        for t in range(16):
            flat[a, t * ROWS : (t + 1) * ROWS, :] = slabs[a, t // 4, t // 2 % 2, t % 2, :ROWS, :].astype(F32)

    def front():
        take_front(s_ref, win, w1, w1b, vec)
        outs[0].start()

    def times():
        take_time(s_ref, tw2, tw3)
        outs[1].start()
        outs[2].start()

    def both(*steps):
        def one():
            for step in steps:
                step()

        return one

    opening, *rows_of_taps = start_steps(noisy, tv, win, w1, vec, h0, h1, a1, stats, sh, acc)
    todo = [
        fetch,
        both(lambda: flat_half(0), lambda: flat_half(1)),
        lambda: unroll(flat, s_ref, 0, 17),
        lambda: unroll(flat, s_ref, 17, R1 // 400),
        both(front, times),
        both(lambda: time_forward(s_ref, e, tw2, tw3, tv, p1, p2), opening),
        both(outs[3].start, outs[5].start, *rows_of_taps[:2]),
        both(rows_of_taps[2], outs[4].start),
    ]
    ahead = 4
    for i in range(ahead):
        begin(i)
    e[...] = jnp.broadcast_to(time_features(step[...]), (8, D))
    add_noise(step[...], latents, noise, noisy)
    for i in range(len(work) + 2):
        if i < len(work):
            middle(i)
            if i + ahead < len(work):
                begin(i + ahead)
        if 0 <= i - 1 < len(work):
            finish(i - 1)
        if 0 <= i - 3 < len(work):
            pass_on(i - 3)
        if i - 3 >= len(PIECES) - 1:
            todo.pop(0)()
    pass_on(len(work) - 1)
    for step in todo:
        step()
    for copy in outs:
        copy.wait()
    arrive(last)
    for copy in started:
        copy.wait_send()


def gather_weights(*operands):
    hbm, vm = pl.BlockSpec(memory_space=pl.ANY), pl.BlockSpec(memory_space=pltpu.VMEM)
    gathered = sds((2, 4, 2, 2, SLAB, 128), BF)
    large = (sds((3, D, 3 * D), BF), sds((4, 4 * D, D), BF), sds((4 * D, D), BF))
    large += (sds((N, D)), sds((N, D)), sds((N, D), BF))
    small = (sds((8, D)), sds((LAT, N)), sds((8, D)), sds((8, 4 * D)), sds((8, 4 * D)), sds((8, D)))
    dma = pltpu.SemaphoreType.DMA
    return pl.pallas_call(
        gather_kernel,
        out_shape=(gathered, gathered) + small + large,
        in_specs=[vm] * 4,
        out_specs=(hbm, hbm) + (vm,) * len(small) + (hbm,) * len(large),
        scratch_shapes=[
            pltpu.VMEM((2, SLAB, 128), BF),
            pltpu.VMEM(gathered.shape, BF),
            pltpu.VMEM((2, 16 * ROWS, 128), F32),
            pltpu.VMEM((3, 4 * R1 // 5, 128), F32),
            *(pltpu.VMEM(v.shape, v.dtype) for v in large),
            pltpu.VMEM((3, 3 * D, D), BF),
            pltpu.VMEM((36, D), BF),
            pltpu.VMEM((1, D), F32),
            pltpu.VMEM((N + 2 * SIDE, 3 * D), BF),
            pltpu.VMEM((8, D), F32),
            dma((128,)),
            dma((128,)),
            dma((2,)),
            dma((8,)),
            dma((6,)),
        ],
        compiler_params=pltpu.CompilerParams(collective_id=2, has_side_effects=True, vmem_limit_bytes=63 * 2**20),
    )(*operands)


def add_up(*terms):
    total = terms[0].astype(F32)
    for term in terms[1:]:
        total += term.astype(F32)
    return total


def reduce_kernel(
    p1, p0, dtv, tw2_in, tw3_in, p1t, p2t, e, mask, loss, sum1, sum0, all_facts,
    kp1, kp0, tw2, tw3, facts, r1, sa, rx, ta, rz, r1b, sb, rbz, tb, rbx, some, land, fx, timed, send_sem, recv_sem, fsend, frecv, gsend, grecv, lsem,
):
    me = lax.axis_index(DP)
    k, x, z = me % 2, (me // 2) % 2, me // 4
    kept = [
        pltpu.make_async_copy(src, dst, lsem.at[i])
        for i, (src, dst) in enumerate(((p1.at[k], kp1), (p0.at[k], kp0), (tw2_in, tw2), (tw3_in, tw3)))
    ]
    for copy in kept:
        copy.start()
    barrier = pltpu.get_barrier_semaphore()
    for o in range(1, 16):
        pl.semaphore_signal(barrier, inc=1, device_id={DP: (me + o) % 16}, device_id_type=pl.DeviceIdType.MESH)
    pl.semaphore_wait(barrier, 15)
    sems = (send_sem, recv_sem)
    core = me + 1 - 2 * k
    side = me + 2 - 4 * x
    chunks = [p0] + [p1.at[:, :, SOME * i : SOME * (i + 1)] for i in range(3)]
    mine = [kp0] + [kp1.at[:, SOME * i : SOME * (i + 1)] for i in range(3)]
    rest = p1.at[:, :, 3 * SOME :]

    def over_z(src, dst, base):
        return [
            send(src.at[(z + o) % 4], dst.at[3 - o], sems, base + o - 1, base + 3 - o, (me + 4 * o) % 16)
            for o in (2, 1, 3)
        ]

    over_core_b = send(rest.at[1 - k], r1b, sems, 20, 20, core)
    over_core = [send(ref.at[1 - k], r1.at[i], sems, i, i, core) for i, ref in enumerate(chunks)]
    kept[0].wait()
    kept[1].wait()
    over_core_b.wait_recv()
    for m in range(8):
        sb[m // 2, m % 2] = add_up(kp1[m, 3 * SOME :], r1b[m]).astype(BF)
    over_z_b = over_z(sb, rbz, 21)
    over_x = []
    for i, ref in enumerate(mine):
        over_core[i].wait_recv()
        for m in range(8):
            sa[i, m % 2, m // 2] = add_up(ref[m], r1[i, m]).astype(BF)
        over_x.append(send(sa.at[i, 1 - x], rx.at[i], sems, 4 + i, 4 + i, side))
    kept[2].wait()
    kept[3].wait()
    time_back(dtv, tw2, tw3, p1t, p2t, e, mask, loss, facts)
    fsems = (fsend, frecv)
    fx[z, x, k] = facts[...]
    facts_z = [send(facts, fx.at[z, x, k], fsems, o - 1, 3 - o, (me + 4 * o) % 16) for o in (2, 1, 3)]
    along = []
    for i in range(4):
        over_x[i].wait_recv()
        for m in range(4):
            ta[i, m] = add_up(sa[i, x, m], rx[i, m]).astype(BF)
        along.append(over_z(ta.at[i], rz.at[i], 8 + 3 * i))
        if i == 1:
            for copy in facts_z:
                copy.wait_recv()
            facts_x = send(fx.at[:, x, k], fx.at[:, x, k], fsems, 3, 3, side)
        if i == 3:
            facts_x.wait_recv()
            facts_core = send(fx.at[:, :, k], fx.at[:, :, k], fsems, 4, 4, core)
    for copy in over_z_b:
        copy.wait_recv()
    for m in range(2):
        tb[m] = add_up(sb[z, m], rbz[0, m], rbz[1, m], rbz[2, m]).astype(BF)
    over_x_b = send(tb.at[1 - x], rbx, sems, 24, 24, side)

    def done(i):
        for copy in along[i]:
            copy.wait_recv()
        return add_up(ta[i, z], rz[i, 0], rz[i, 1], rz[i, 2])

    facts_core.wait_recv()
    all_facts[...] = fx[...].reshape(16, FACTS, 128)
    timed[...] = time_rows(all_facts, ROWS)
    some[...] = done(0)

    @pl.when(me > 0)
    def _():
        @pl.loop(0, SOME // 8)
        def _(g):
            row = SOME * me + 8 * g
            owner = row // ROWS
            at = pl.multiple_of(row - ROWS * owner, 8)
            pltpu.make_async_remote_copy(
                src_ref=some.at[pl.ds(pl.multiple_of(8 * g, 8), 8)], dst_ref=land.at[pl.ds(at, 8)],
                send_sem=gsend, recv_sem=grecv, device_id={DP: owner}, device_id_type=pl.DeviceIdType.MESH,
            ).start()

    for i in range(3):
        sum1[SOME * i : SOME * (i + 1), :] = done(i + 1)
    over_x_b.wait_recv()
    sum1[3 * SOME :, :] = add_up(tb[x, : ROWS - 3 * SOME], rbx[: ROWS - 3 * SOME])

    def landed(lo, hi):
        part = land.at[lo:hi]
        pltpu.make_async_remote_copy(
            src_ref=part, dst_ref=part, send_sem=gsend, recv_sem=grecv,
            device_id={DP: me}, device_id_type=pl.DeviceIdType.MESH,
        ).wait_recv()
        sum0[lo:hi, :] = land[lo:hi, :] + timed[lo:hi, :]

    @pl.when(me == 0)
    def _():
        landed(SOME, ROWS)
        sum0[:SOME, :] = some[...] + timed[:SOME, :]

    @pl.when((me > 0) & (me < 4))
    def _():
        landed(0, ROWS)

    @pl.when(me == 4)
    def _():
        landed(0, 16 * SOME - 4 * ROWS)
        sum0[16 * SOME - 4 * ROWS :, :] = timed[16 * SOME - 4 * ROWS :, :]

    @pl.when(me > 4)
    def _():
        sum0[...] = timed[...]

    @pl.when(me > 0)
    def _():
        pltpu.make_async_remote_copy(
            src_ref=some, dst_ref=some, send_sem=gsend, recv_sem=grecv,
            device_id={DP: me}, device_id_type=pl.DeviceIdType.MESH,
        ).wait_send()

    for copy in [over_core_b, over_x_b] + over_core + over_z_b + over_x + sum(along, []) + facts_z + [facts_x, facts_core]:
        copy.wait_send()


def sum_over_samples(*operands):
    vm, hbm = pl.BlockSpec(memory_space=pltpu.VMEM), pl.BlockSpec(memory_space=pl.ANY)
    dma = pltpu.SemaphoreType.DMA
    return pl.pallas_call(
        reduce_kernel,
        out_shape=(sds((ROWS, 128)), sds((ROWS, 128)), sds((16, FACTS, 128))),
        in_specs=[hbm, hbm, vm, hbm, hbm] + [vm] * 5,
        out_specs=(vm,) * 3,
        scratch_shapes=[
            pltpu.VMEM((8, SLAB, 128), BF),
            pltpu.VMEM((8, SOME, 128), BF),
            pltpu.VMEM((4, 4 * D, D), BF),
            pltpu.VMEM((4 * D, D), BF),
            pltpu.VMEM((FACTS, 128), F32),
            pltpu.VMEM((4, 8, SOME, 128), BF),
            pltpu.VMEM((4, 2, 4, SOME, 128), BF),
            pltpu.VMEM((4, 4, SOME, 128), BF),
            pltpu.VMEM((4, 4, SOME, 128), BF),
            pltpu.VMEM((4, 3, SOME, 128), BF),
            pltpu.VMEM((8, REST, 128), BF),
            pltpu.VMEM((4, 2, REST, 128), BF),
            pltpu.VMEM((3, 2, REST, 128), BF),
            pltpu.VMEM((2, REST, 128), BF),
            pltpu.VMEM((REST, 128), BF),
            pltpu.VMEM((SOME, 128), F32),
            pltpu.VMEM((ROWS, 128), F32),
            pltpu.VMEM((4, 2, 2, FACTS, 128), F32),
            pltpu.VMEM((ROWS, 128), F32),
            dma((25,)),
            dma((25,)),
            dma((5,)),
            dma((5,)),
            dma,
            dma,
            dma((4,)),
        ],
        compiler_params=pltpu.CompilerParams(
            collective_id=1, has_side_effects=True, vmem_limit_bytes=62 * 2**20
        ),
    )(*operands)


def time_features(steps):
    ladder = lax.broadcasted_iota(jnp.int32, (1, D // 2), 1).astype(F32)
    angles = steps.astype(F32) * jnp.exp(-math.log(10000.0) * ladder / (D // 2))
    return jnp.concatenate([jnp.cos(angles), jnp.sin(angles)], axis=1)


def add_noise(step, latents, noise, noisy):
    shape = (8, 128)
    level = 128 * lax.broadcasted_iota(jnp.int32, shape, 0) + lax.broadcasted_iota(jnp.int32, shape, 1)
    lowest, highest = 0.00085**0.5, 0.012**0.5
    beta = jnp.square(lowest + (highest - lowest) * level.astype(F32) / 999.0)
    logs = jnp.where(level <= step, jnp.log(1.0 - beta), 0.0)
    abar = jnp.exp(jnp.sum(jnp.sum(logs, axis=1, keepdims=True), axis=0, keepdims=True))
    noisy[...] = jnp.sqrt(abar) * latents[...] + jnp.sqrt(1.0 - abar) * noise[...]


def prepare_kernel(step, latents, noise, e, noisy):
    e[...] = jnp.broadcast_to(time_features(step[...]), (8, D))
    add_noise(step[...], latents, noise, noisy)


def shards(params, momentum, ema_params, latents, noise_eps, timesteps, pixel_mask, context):
    c = lax.axis_index(CH)
    d = lax.axis_index(DP)
    n_dp = lax.axis_size(DP)
    rows_dev = params.shape[2]
    rows_all = rows_dev * n_dp
    quick = n_dp == 16 and rows_dev == ROWS
    step, noise = timesteps[:, None], noise_eps[0]
    if quick:
        _, part1, e, noisy, vec0, p1, p2, stats, w1b, tw2, tw3, h0, h1, a1 = gather_weights(
            params[0], step, latents[0], noise
        )
        part1 = part1.reshape(2, 16, SLAB, 128)
    else:
        e, noisy = kcall(prepare_kernel, (sds((8, D)), sds((LAT, N))), (step, latents[0], noise))
        low = params[0].astype(BF)
        part0, part1 = (lax.all_gather(lax.all_gather(low[i], CH, axis=0), DP, axis=1) for i in range(2))

    px = (N, D)
    hx = (HEADS, N, HD)
    sh = (N + 2 * SIDE, 3 * D)
    taps, back = sds((3, 3 * D, D), BF), sds((3, D, 3 * D), BF)
    flat = pltpu.VMEM((2, rows_all, 128), F32)
    unrolled = pltpu.VMEM((3, 4 * R1 // 5, 128), F32)
    units = sds((8, 4 * D))
    if not quick:
        win, w1, w1b, vec0, tw2, tw3, tv, p1, p2 = kcall(
            partial(unpack0_kernel, rows_dev),
            (sds((36, D), BF), taps, back, sds((8, D)), sds((4, 4 * D, D), BF), sds((4 * D, D), BF), sds((1, D)))
            + (units, units),
            (part0, e),
            (flat, unrolled),
        )
        h0, h1, a1, stats = kcall(
            start_kernel,
            (sds(px), sds(px), sds(px, BF), sds((8, D))),
            (noisy, tv, win, w1, vec0),
            (pltpu.VMEM(sh, BF), pltpu.VMEM((8, D), F32)),
        )
    c2, c2b, tr, mats, kvw, vec1, gib, wout, outb = kcall(
        partial(unpack1_kernel, rows_dev),
        (taps, back, sds((4, D, D), BF), sds((16, D, D), BF), sds((2, CTX, D), BF))
        + (sds((24, D)), sds((8, D)), sds((36, D), BF), sds((1, D))),
        (part1,),
        (flat, unrolled, pltpu.VMEM((2, 40, 128), F32)),
    )
    h2, z0, a2, ntr, x1, q, k, v, stats = kcall(
        front_kernel,
        (sds(px),) * 2 + (sds(px, BF),) * 3 + (sds(hx, BF),) * 3 + (sds((8, D)),),
        (h0, h1, stats, c2, tr, vec1),
        (pltpu.VMEM(sh, BF), pltpu.VMEM((8, D), F32)),
        late=(0, 3, 4),
        early=range(8),
    )
    o, lse = kcall(
        attend_kernel, (sds(px, BF), sds((HEADS, 1, N))), (q, k, v), (pltpu.VMEM((D, N), F32),)
    )
    square = (D, W)
    dz1, dh3, dos, loss, gd, ggi, ggo, gkv, dvec, dgib, dwout, dbout = kcall(
        middle_kernel,
        (sds(px), sds(px), sds(hx, BF), sds((1, 1)))
        + (sds((4,) + square, BF), sds((8,) + square, BF), sds((4,) + square, BF), sds((2, CTX, W), BF))
        + (sds((24, D)), sds((8, D)), sds((36, D)), sds((8, 128))),
        (o, z0, h2, context[0], noise, pixel_mask, mats, kvw, vec1, gib, wout, outb),
        [pltpu.VMEM(px, F32)] * 3
        + [pltpu.VMEM(px, BF)] * 4
        + [
            pltpu.VMEM((4, N, D), BF),
            pltpu.VMEM((4, N, D), F32),
            pltpu.VMEM((4, N, D), F32),
            pltpu.VMEM(px, BF),
            pltpu.VMEM(px, BF),
            pltpu.VMEM((HEADS * KEYS, D), BF),
            pltpu.VMEM((HEADS * KEYS, D), BF),
            pltpu.VMEM((N, HEADS * KEYS), F32),
            pltpu.VMEM((N, HEADS * KEYS), BF),
            pltpu.VMEM((8, D), F32),
            pltpu.VMEM((36, N), F32),
        ]
        + [pltpu.VMEM((D, N), BF)] * 4,
        late=(7, 6, 1, 2),
        early=(0, 1, 2, 4, 5, 6, 7),
    )
    dq, dk, dv = kcall(
        attend_back_kernel,
        (sds(px, BF),) * 3,
        (q, k, v, dos, lse),
        (pltpu.VMEM((D, N), F32), pltpu.VMEM(hx, F32), pltpu.VMEM(hx, F32)),
    )
    front = -(-FRONT // (16 * n_dp)) * 16 * n_dp
    lead = (2, 8) if quick else (n_dp,)
    own1, own0, dtv = kcall(
        back_kernel,
        (
            sds(lead + (SLAB if quick else rows_dev, 128), BF),
            sds(lead + (front // n_dp, 128), BF),
            sds((1, D)),
        ),
        (dq, dk, dv, dz1, dh3, z0, h2, h1, h0, stats, w1b, c2b, tr, vec0, vec1, a1, a2, ntr, x1, noisy,
         gd, ggi, ggo, gkv, dvec, dgib, dwout, dbout),
        (
            pltpu.VMEM(px, F32),
            pltpu.VMEM(sh, BF),
            pltpu.VMEM((sh[0], 3 * W), BF),
            pltpu.VMEM((24, D), F32),
            pltpu.VMEM((2, 4 * R1 // 5, 128), F32),
            pltpu.VMEM((7600, 128), F32),
            pltpu.VMEM((2, 40, 128), F32),
        ),
        late=(5, 3, 17, 6, 4, 16, 7, 11, 20, 21, 22, 23, 15, 8, 10),
        early=(0,),
    )
    timed = (dtv, tw2, tw3, p1, p2, e, pixel_mask, loss)
    if quick:
        sum1, sum0, all_facts = sum_over_samples(own1, own0, *timed)
    else:
        facts = kcall(time_back, sds((FACTS, 128)), timed)
        sum1 = lax.psum_scatter(own1, DP, scatter_dimension=0).astype(F32)
        sum0 = lax.all_gather(lax.psum_scatter(own0, DP, scatter_dimension=0), DP, axis=0, tiled=True)
        sum0 = jnp.pad(sum0, ((0, rows_all - front), (0, 0)))
        sum0 = lax.dynamic_slice_in_dim(sum0, d * rows_dev, rows_dev, 0).astype(F32)
        all_facts = lax.all_gather(facts, DP, axis=0)
    state = sds((2, rows_dev, 128))
    new_params, new_momentum, new_ema, sums = kcall(
        partial(update_kernel, not quick),
        (state, state, state, sds((1, 128))),
        (params[0], momentum[0], ema_params[0], sum1, sum0, all_facts),
    )
    return (new_params[None], new_momentum[None], new_ema[None], sums[0, 0], sums[0, 1])


def solution(mesh):
    packed = P(CH, None, DP, None)
    row = P(DP, None, None)
    return jax.shard_map(
        shards,
        mesh=mesh,
        in_specs=(packed, packed, packed, row, row, P(DP), P(DP, None), row),
        out_specs=(packed, packed, packed, P(), P()),
        check_vma=False,
    )
```

```python
import math
from functools import partial

import jax
import jax.numpy as jnp
from jax import lax
from jax.experimental import pallas as pl
from jax.experimental.pallas import tpu as pltpu
from jax.sharding import PartitionSpec as P

D = 320
W = 160
HEADS = 8
HD = 40
CTX = 768
TXT = 77
LAT = 4
SIDE = 32
N = 1024
EPS = 1e-5
LR = 0.2
MU = 0.9
ED = 0.9
CH = "chan"
DP = "dp"
F32 = jnp.float32
BF = jnp.bfloat16
HI = lax.Precision.HIGHEST
SCALE = HD**-0.5
LOG2E = 1.0 / math.log(2.0)

R0 = 4000
U1, U2, U3 = 2920, 4204, 9328
FRONT = 3650
T1, T2, T3 = 3650, 5255, 11660
C2 = 2
PI = 2885
QKV = 3208
SO = 4168
CQ = 4491
CKV = 4811
CO = 6347
GI = 6670
GIB = 9230
GO = 9238
PO = 10519
OUT = 10842
OUTB = 10878
R1 = 13600
VEC0 = (36, 37, 38, 2919)
VEC1 = (0, 1, 2882, 2883, 2884, 3205, 3206, 3207, 4488, 4489, 4490, 6667, 6668, 6669, 10518, 10839, 10840, 10841)
(N2G, N2B, C2B, NTG, NTB, PIB, L1G, L1B, SOB, L2G, L2B, COB, L3G, L3B, GOB, POB, NOG, NOB) = range(18)
MPI, MQ, MK, MV = range(4)
MSO, MCQ, MCO, MPO, MGV, MGG, MGO = 0, 1, 2, 3, 4, 8, 12


class Flow:
    def __init__(self, ins, outs, sems):
        self.ins = {i: pltpu.make_async_copy(src, dst, sems.at[j]) for j, (i, src, dst) in enumerate(ins)}
        n = len(ins)
        self.outs = {i: pltpu.make_async_copy(src, dst, sems.at[n + j]) for j, (i, dst, src) in enumerate(outs)}
        self.waiting = set(self.ins)
        self.going = []
        for copy in self.ins.values():
            copy.start()

    def need(self, *which):
        for i in which:
            self.ins[i].wait()
            self.waiting.discard(i)

    def ready(self, *which):
        for i in which:
            self.outs[i].start()
            self.going.append(i)

    def end(self):
        self.need(*sorted(self.waiting))
        self.ready(*(i for i in self.outs if i not in self.going))
        for copy in self.outs.values():
            copy.wait()


def kcall(body, outs, ins, scratch=(), late=(), early=()):
    vm, hbm = pl.BlockSpec(memory_space=pltpu.VMEM), pl.BlockSpec(memory_space=pl.ANY)
    single = not isinstance(outs, tuple)
    outs = (outs,) if single else outs
    n, m = len(ins), len(outs)
    late, early = tuple(late), tuple(early)
    scratch = list(scratch)
    count = len(scratch)
    if late or early:
        scratch += [pltpu.VMEM(ins[i].shape, ins[i].dtype) for i in late]
        scratch += [pltpu.VMEM(outs[i].shape, outs[i].dtype) for i in early]
        scratch.append(pltpu.SemaphoreType.DMA((len(late) + len(early),)))

    def whole(*refs):
        if not (late or early):
            return body(*refs)
        given, made, rest = list(refs[:n]), list(refs[n : n + m]), refs[n + m :]
        kept = rest[count:-1]
        inward = [(i, given[i], kept[j]) for j, i in enumerate(late)]
        outward = [(i, made[i], kept[len(late) + j]) for j, i in enumerate(early)]
        for i, _, ref in inward:
            given[i] = ref
        for i, _, ref in outward:
            made[i] = ref
        flow = Flow(inward, outward, rest[-1])
        body(flow, *given, *made, *rest[:count])
        flow.end()

    done = pl.pallas_call(
        whole,
        out_shape=outs,
        in_specs=[hbm if i in late else vm for i in range(n)],
        out_specs=tuple(hbm if i in early else vm for i in range(m)),
        scratch_shapes=scratch,
        compiler_params=pltpu.CompilerParams(vmem_limit_bytes=63 * 2**20),
    )(*ins)
    return done[0] if single else done


def sds(shape, dtype=F32):
    return jax.ShapeDtypeStruct(shape, dtype)


def tiles(fn, size=256, total=N):
    for t in range(total // size):
        fn(pl.ds(t * size, size))


def nn(a, b):
    return jnp.dot(a, b, preferred_element_type=F32)


def nt(a, b):
    return lax.dot_general(a, b, (((1,), (1,)), ((), ())), preferred_element_type=F32)


def tn(a, b):
    return lax.dot_general(a, b, (((0,), (0,)), ((), ())), preferred_element_type=F32)


def colsum(v):
    return jnp.sum(v, axis=0, keepdims=True)


def flatten(a_ref, flat, rows):
    for b in range(2):
        for t in range(a_ref.shape[1]):
            flat[b, t * rows : (t + 1) * rows, :] = a_ref[b, t, :rows, :].astype(F32)


def unroll(flat, s_ref, lo_chunk, hi_chunk):
    q = 80

    @pl.loop(lo_chunk, hi_chunk)
    def _(c):
        f = [[flat[b, pl.ds(c * 5 * q + j, q, stride=5), :] for j in range(5)] for b in range(2)]
        for i in range(4):
            row = []
            for b in range(2):
                lo = 32 * i
                first, second = f[b][i], f[b][i + 1]
                row += [first[:, lo:], second[:, : lo + 32]] if lo else [first, second[:, :32]]
            full = jnp.concatenate(row, axis=1)
            for k, (lo, hi) in enumerate(((0, 128), (128, 256), (256, 320))):
                s_ref[k, pl.ds(c * 4 * q + i, q, stride=4), : hi - lo] = full[:, lo:hi]


def get_rows(s_ref, start, count, step=1):
    ds = pl.ds(start, count) if step == 1 else pl.ds(start, count, stride=step)
    return jnp.concatenate([s_ref[0, ds, :], s_ref[1, ds, :], s_ref[2, ds, :64]], axis=1)


def put_taps(s_ref, start, w, back):
    for r in range(3):
        taps = [get_rows(s_ref, start + D * (3 * r + i), D).astype(BF) for i in range(3)]
        for i in range(3):
            w[r, D * i : D * (i + 1), :] = taps[i]
        back[r] = jnp.concatenate(taps[::-1], axis=1)


def unit_row(parts):
    out = [p[:, W * b : W * (b + 1)] for b in range(2) for p in parts]
    return jnp.broadcast_to(jnp.concatenate(out, axis=1), (8, 4 * D))


def unit_parts(row):
    return [
        jnp.concatenate([row[:, W * i : W * (i + 1)], row[:, 640 + W * i : 640 + W * (i + 1)]], axis=1)
        for i in range(4)
    ]


def take_front(s_ref, win, w1, w1b, vec):
    win[...] = get_rows(s_ref, 0, 36).astype(BF)
    put_taps(s_ref, 39, w1, w1b)
    for i, r in enumerate(VEC0):
        vec[i : i + 1, :] = get_rows(s_ref, r, 1)


def take_time(s_ref, tw2, tw3):
    for i in range(4):
        tw2[i] = get_rows(s_ref, U2 + i, 4 * D, 4).astype(BF)
    tw3[...] = get_rows(s_ref, U3, 4 * D).astype(BF)


def time_forward(s_ref, e, tw2, tw3, tv, p1, p2):
    u = e[...].astype(BF)
    p1[...] = unit_row(
        [nn(u, get_rows(s_ref, U1 + i, D, 4).astype(BF))[:1] + get_rows(s_ref, U1 + 4 * D + i, 1) for i in range(4)]
    )
    u = silu(p1[...]).astype(BF)
    p2[...] = unit_row([nn(u, tw2[i])[:1] + get_rows(s_ref, U2 + 16 * D + i, 1) for i in range(4)])
    u = silu(p2[...]).astype(BF)
    tv[...] = nn(u, tw3[...])[:1] + get_rows(s_ref, U3 + 4 * D, 1)


def unpack0_kernel(rows, a_ref, e, win, w1, w1b, vec, tw2, tw3, tv, p1, p2, flat, s_ref):
    flatten(a_ref, flat, rows)
    unroll(flat, s_ref, 0, R1 // 400)
    take_front(s_ref, win, w1, w1b, vec)
    take_time(s_ref, tw2, tw3)
    time_forward(s_ref, e, tw2, tw3, tv, p1, p2)


FE, FU1, FU2, FD1, FD2, FD3, FL = 0, 3, 13, 23, 28, 33, 35
FACTS = 40


def time_back(dtv, tw2, tw3, p1, p2, e, mask, loss, facts):
    g = jnp.broadcast_to(dtv[...], (8, D)).astype(BF)
    d2 = nt(g, tw3[...]) * silu_slope(p2[...])
    total = jnp.zeros((8, 4 * D), F32)
    for i, part in enumerate(unit_parts(d2)):
        total += nt(part.astype(BF), tw2[i])
    d1 = total * silu_slope(p1[...])
    put_facts(facts, e, p1, p2, d1, d2, dtv, mask, loss)


def put_facts(facts, e, p1, p2, d1, d2, dtv, mask, loss):
    first = lax.axis_index(CH) == 0
    facts[...] = jnp.zeros_like(facts)

    def put(at, v):
        for i in range(0, v.shape[1], 128):
            n = min(128, v.shape[1] - i)
            facts[at + i // 128 : at + i // 128 + 1, :n] = v[:1, i : i + n]

    put(FE, e[...].astype(BF).astype(F32))
    put(FU1, silu(p1[...]).astype(BF).astype(F32))
    put(FU2, silu(p2[...]).astype(BF).astype(F32))
    put(FD1, jnp.where(first, d1[:, : 2 * D], d1[:, 2 * D :]))
    put(FD2, jnp.where(first, d2[:, : 2 * D], d2[:, 2 * D :]))
    put(FD3, own(dtv[...]))
    facts[FL : FL + 1, 0:1] = loss[...]
    facts[FL : FL + 1, 1:2] = jnp.sum(mask[...].astype(F32), axis=1, keepdims=True)


def unpack1_kernel(rows, a_ref, c2, c2b, tr, mats, kv, vec, gib, wout, outb, flat, s_ref, o_ref):
    flatten(a_ref, flat, rows)
    unroll(flat, s_ref, 0, R1 // 400)
    put_taps(s_ref, C2, c2, c2b)
    tr[MPI] = get_rows(s_ref, PI, D).astype(BF)
    for m, r in ((MSO, SO), (MCQ, CQ), (MCO, CO), (MPO, PO)):
        mats[m] = get_rows(s_ref, r, D).astype(BF)
    for j in range(3):
        tr[MQ + j] = get_rows(s_ref, QKV + j, D, 3).astype(BF)
    for j in range(8):
        mats[MGV + j] = get_rows(s_ref, GI + j, D, 8).astype(BF)
    for j in range(4):
        for b in range(2):
            mats[MGO + j, b * W : (b + 1) * W, :] = get_rows(s_ref, GO + 640 * b + W * j, W).astype(BF)
    for j in range(2):
        kv[j] = get_rows(s_ref, CKV + j, CTX, 2).astype(BF)
    for i, r in enumerate(VEC1):
        vec[i : i + 1, :] = get_rows(s_ref, r, 1)
    gib[...] = get_rows(s_ref, GIB, 8)
    outb[...] = get_rows(s_ref, OUTB, 1)
    lane = lax.broadcasted_iota(jnp.int32, (W, W), 0)
    col = lax.broadcasted_iota(jnp.int32, (W, W), 1)
    pick = ((lane % 2) * 80 + lane // 2 == col).astype(BF)
    raw = get_rows(s_ref, OUT, 36).astype(BF)
    for b in range(2):
        moved = nn(raw[:, W * b : W * (b + 1)], pick)
        o_ref[0, :36, :] = moved[:, :128]
        o_ref[1, :36, :32] = moved[:, 128:]
        for ch in range(2):
            pieces = []
            for m in range(4):
                ds = pl.ds(m, 9, stride=4)
                both = jnp.concatenate([o_ref[0, ds, :], o_ref[1, ds, :32]], axis=1)
                pieces.append(both[:, 80 * ch : 80 * ch + 80])
            at = (2 * b + ch) * 9
            wout[at : at + 9, :] = jnp.concatenate(pieces, axis=1).astype(BF)


def pixel_col(n, axis):
    shape = (n, 1) if axis == 0 else (1, n)
    return lax.broadcasted_iota(jnp.int32, shape, axis)


def shift_lanes(v, tap):
    r, s = tap // 3 - 1, tap % 3 - 1
    pix = pixel_col(N, 1)
    i, j = pix // SIDE + r, pix % SIDE + s
    ok = (i >= 0) & (i < SIDE) & (j >= 0) & (j < SIDE)
    move = -(r * SIDE + s) % N
    moved = pltpu.roll(v, move, 1) if move else v
    return jnp.where(ok, moved, 0.0)


def put_shifts(ref, v):
    j = pixel_col(N, 0) % SIDE
    left = jnp.where(j == 0, 0.0, pltpu.roll(v, 1, 0)).astype(BF)
    right = jnp.where(j == SIDE - 1, 0.0, pltpu.roll(v, N - 1, 0)).astype(BF)
    ref[SIDE : SIDE + N, :] = jnp.concatenate([left, v.astype(BF), right], axis=1)


def clear_margins(ref):
    zero = jnp.zeros((SIDE, ref.shape[1]), BF)
    ref[:SIDE, :] = zero
    ref[SIDE + N :, :] = zero


def conv_rows(ref, w_ref):
    return sum(nn(ref[SIDE * r : SIDE * r + N, :], w_ref[r]) for r in range(3))


def conv_back_rows(ref, w_ref):
    return sum(nt(ref[SIDE * (2 - r) : SIDE * (2 - r) + N, :], w_ref[r]) for r in range(3))


def group_mean(sums):
    a = lax.broadcasted_iota(jnp.int32, (D, D), 0) // 10
    b = lax.broadcasted_iota(jnp.int32, (D, D), 1) // 10
    pool = jnp.where(a == b, 1.0, 0.0)
    wide = jnp.broadcast_to(sums, (8, D))
    out = jnp.dot(wide, pool, precision=HI, preferred_element_type=F32)
    return out[:1] * (1.0 / (10 * N))


def group_stats(v_ref, acc, sums):
    mean = group_mean(sums)
    acc[0:1, :] = colsum(jnp.square(v_ref[...] - mean))
    return mean, lax.rsqrt(group_mean(acc[0:1, :]) + EPS)


def silu(v):
    return v * jax.nn.sigmoid(v)


def silu_slope(v):
    sig = jax.nn.sigmoid(v)
    return sig * (1.0 + v * (1.0 - sig))


def layer(v):
    mean = jnp.sum(v, axis=1, keepdims=True) * (1.0 / D)
    sq = jnp.sum(v * v, axis=1, keepdims=True) * (1.0 / D)
    inv = lax.rsqrt(sq - mean * mean + EPS)
    return (v - mean) * inv, inv


def layer_back(grad, normed, inv, gain):
    ghat = grad * gain
    m1 = jnp.sum(ghat, axis=1, keepdims=True) * (1.0 / D)
    m2 = jnp.sum(ghat * normed, axis=1, keepdims=True) * (1.0 / D)
    return inv * (ghat - m1 - normed * m2)


def own(v):
    return jnp.where(lax.axis_index(CH) == 0, v[..., :W], v[..., W:])


def head(v, h):
    return v[:, HD * h : HD * (h + 1)]


def group_norm(src, acc, total, stats, at):
    mean, inv = group_stats(src, acc, total)
    stats[at : at + 1, :], stats[at + 1 : at + 2, :] = mean, inv
    return (src[...] - mean) * inv


def start_steps(noisy, tv, win, w1, vec0, h0, h1, a1, stats, sh, acc):
    def first():
        cols = jnp.concatenate([shift_lanes(noisy[...], t) for t in range(9)], axis=0).astype(BF)
        clear_margins(sh)
        stats[...] = jnp.zeros_like(stats)
        h = tn(cols, win[...]) + vec0[0:1, :]
        h0[...] = h
        y = silu(group_norm(h0, acc, colsum(h), stats, 0) * vec0[1:2, :] + vec0[2:3, :])
        put_shifts(sh, y)
        a1[...] = y.astype(BF)

    def taps(r):
        def one():
            part = nn(sh[SIDE * r : SIDE * r + N, :], w1[r])
            if r == 2:
                part += tv[...]
            h1[...] = (h1[...] if r else vec0[3:4, :]) + part

        return one

    return [first, taps(0), taps(1), taps(2)]


def start_kernel(noisy, tv, win, w1, vec0, h0, h1, a1, stats, sh, acc):
    for step in start_steps(noisy, tv, win, w1, vec0, h0, h1, a1, stats, sh, acc):
        step()


def front_kernel(flow, h0, h1, stats_in, c2, tr, vec1, h2, z0, a2, ntr, x1, q, k, v, stats, sh, acc):
    clear_margins(sh)
    stats[...] = stats_in[...]
    y = silu(group_norm(h1, acc, colsum(h1[...]), stats, 2) * vec1[N2G : N2G + 1, :] + vec1[N2B : N2B + 1, :])
    put_shifts(sh, y)
    a2[...] = y.astype(BF)
    flow.ready(2)
    flow.need(0, 3)
    h = h0[...] + conv_rows(sh, c2) + vec1[C2B : C2B + 1, :]
    h2[...] = h
    flow.ready(0)
    n = group_norm(h2, acc, colsum(h), stats, 4)
    n = (n * vec1[NTG : NTG + 1, :] + vec1[NTB : NTB + 1, :]).astype(BF)
    ntr[...] = n
    flow.ready(3)
    flow.need(4)
    z = nn(n, tr[MPI]) + vec1[PIB : PIB + 1, :]
    z0[...] = z
    flow.ready(1)
    normed, _ = layer(z)
    x = (normed * vec1[L1G : L1G + 1, :] + vec1[L1B : L1B + 1, :]).astype(BF)
    x1[...] = x
    flow.ready(4)
    for i, (at, dst) in enumerate(((MQ, q), (MK, k), (MV, v))):
        y = nn(x, tr[at]).astype(BF)
        for hd in range(HEADS):
            dst[hd] = head(y, hd)
        flow.ready(5 + i)


AT = 512


def attend_kernel(q, k, v, o, lse, ot):
    steps = [(h, pl.ds(t * AT, AT)) for h in range(HEADS) for t in range(N // AT)]

    def scores(h, rows):
        return nt(k[h], q[h, rows, :])

    now = scores(*steps[0])
    for i, (h, rows) in enumerate(steps):
        later = scores(*steps[i + 1]) if i + 1 < len(steps) else None
        if i % (N // AT) == 0:
            vt = v[h].astype(F32).T.astype(BF)
        s = now * (SCALE * LOG2E)
        top = jnp.max(s, axis=0, keepdims=True)
        e = jnp.exp2(s - top)
        total = jnp.sum(e, axis=0, keepdims=True)
        lse[h, :, rows] = top + jnp.log(total) * LOG2E
        ot[h * HD : (h + 1) * HD, rows] = nn(vt, (e * (1.0 / total)).astype(BF))
        now = later
    o[...] = ot[...].T.astype(BF)


KEYS = 128


def by_head(v):
    wide = jnp.concatenate([v, jnp.zeros((KEYS - TXT, D), v.dtype)], axis=0)
    col = lax.broadcasted_iota(jnp.int32, (KEYS, D), 1) // HD
    return jnp.concatenate([jnp.where(col == h, wide, 0.0) for h in range(HEADS)], axis=0)


def from_heads(vt):
    row = lax.broadcasted_iota(jnp.int32, (D, KEYS), 0) // HD
    total = jnp.zeros((D, KEYS), F32)
    for h in range(HEADS):
        total += jnp.where(row == h, vt[:, KEYS * h : KEYS * (h + 1)], 0.0)
    return total.T[:TXT]


def transposed(v):
    return v.T


def middle_kernel(
    flow, o, z0, h2, ctx, noise, mask, mats, kvw, vec, gib, wout, outb,
    dz1, dh3, dos, loss, gd, ggi, ggo, gkv, dvec, dgib, dwout, dbout,
    z1, z2, h3, x2, x3, oc, z3b, gl, by_a, by_g, a3, qc, kb, vb, prob, dsc, acc, pt, oct_, x2t, ot, x3t,
):
    def row(i):
        return vec[i : i + 1, :]

    def put(i, v):
        dvec[i : i + 1, :] = v

    flow.need(7)
    kb[...] = by_head(nn(ctx[...], kvw[0])).astype(BF)
    vb[...] = by_head(nn(ctx[...], kvw[1])).astype(BF)
    flow.need(6, 1)
    z = z0[...] + nn(o[...], mats[MSO]) + row(SOB)
    z1[...] = z
    normed, _ = layer(z)
    x = (normed * row(L2G) + row(L2B)).astype(BF)
    x2[...] = x
    qq = nn(x, mats[MCQ]).astype(BF)
    qc[...] = qq
    s = nt(qq, kb[...]) * (SCALE * LOG2E)
    there = lax.broadcasted_iota(jnp.int32, (1, KEYS), 1) < TXT
    for h in range(HEADS):
        at = slice(KEYS * h, KEYS * (h + 1))
        sh = jnp.where(there, s[:, at], -jnp.inf)
        e = jnp.exp2(sh - jnp.max(sh, axis=1, keepdims=True))
        prob[:, at] = e * (1.0 / jnp.sum(e, axis=1, keepdims=True))
    c = nn(prob[...].astype(BF), vb[...]).astype(BF)
    oc[...] = c
    z = z1[...] + nn(c, mats[MCO]) + row(COB)
    z2[...] = z
    normed, _ = layer(z)
    x = (normed * row(L3G) + row(L3B)).astype(BF)
    x3[...] = x
    moving = ((oc, oct_), (x2, x2t), (o, ot), (x3, x3t))
    for j in range(4):
        moving[j][1][...] = transposed(moving[j][0][...])
        a = nn(x, mats[MGV + j]) + gib[j : j + 1, :]
        g = nn(x, mats[MGG + j]) + gib[4 + j : 5 + j, :]
        cdf = 0.5 * (1.0 + lax.erf(g * math.sqrt(0.5)))
        gelu = g * cdf
        by_a[j] = gelu
        by_g[j] = a * (cdf + g * jnp.exp(-0.5 * g * g) * (1.0 / math.sqrt(2.0 * math.pi)))
        y = (a * gelu).astype(BF)
        gl[j] = y
        z = z + nn(y, mats[MGO + j])
    zb = (z + row(GOB)).astype(BF)
    z3b[...] = zb
    flow.need(2)
    h = h2[...] + nn(zb, mats[MPO]) + row(POB)
    h3[...] = h
    mean, inv = group_stats(h3, acc, colsum(h))
    gain, bias = row(NOG), row(NOB)
    a3[...] = silu((h3[...] - mean) * inv * gain + bias).astype(BF)
    taps = nt(wout[...], a3[...])
    for ch in range(LAT):
        pred = jnp.zeros((1, N), F32)
        for t in range(9):
            pred += shift_lanes(taps[9 * ch + t : 9 * ch + t + 1, :], t)
        at = W * (ch // 2) + ch % 2
        err = pred + outb[0:1, at : at + 1] - noise[ch : ch + 1, :]
        weighed = mask[...].astype(F32) * err
        g = 2.0 * weighed
        acc[2 + ch : 3 + ch, 0:1] = jnp.sum(weighed * err, axis=1, keepdims=True)
        dbout[ch : ch + 1, :] = jnp.broadcast_to(jnp.sum(g, axis=1, keepdims=True), (1, 128))
        for t in range(9):
            pt[9 * ch + t : 9 * ch + t + 1, :] = shift_lanes(g, 8 - t)
    loss[...] = acc[2:3, 0:1] + acc[3:4, 0:1] + acc[4:5, 0:1] + acc[5:6, 0:1]

    dvec[...] = jnp.zeros_like(dvec)
    taps = pt[...].astype(BF)
    dwout[...] = nn(taps, a3[...])
    n = (h3[...] - mean) * inv
    g = tn(taps, wout[...]) * silu_slope(n * gain + bias)
    dgain, dbias = colsum(g * n), colsum(g)
    put(NOG, dgain)
    put(NOB, dbias)
    g = inv * (g * gain - group_mean(gain * dbias) - n * group_mean(gain * dgain))
    dh3[...] = g
    flow.ready(1)
    put(POB, colsum(g))
    gd[0] = nn(transposed(z3b[...]), own(g).astype(BF)).astype(BF)
    dz3 = nt(g.astype(BF), mats[MPO])
    z1b = dz3.astype(BF)
    put(GOB, colsum(dz3))
    mine_t = transposed(own(dz3).astype(BF))
    xt = x3t[...]
    dx = jnp.zeros((N, D), F32)
    for j in range(4):
        dgl = nt(z1b, mats[MGO + j])
        ggo[j] = nn(mine_t, gl[j]).T.astype(BF)
        da = dgl * by_a[j]
        dg = dgl * by_g[j]
        dgib[j : j + 1, :] = colsum(da)
        dgib[4 + j : 5 + j, :] = colsum(dg)
        ggi[j] = nn(xt, own(da).astype(BF)).astype(BF)
        ggi[4 + j] = nn(xt, own(dg).astype(BF)).astype(BF)
        dx += nt(da.astype(BF), mats[MGV + j]) + nt(dg.astype(BF), mats[MGG + j])
    flow.ready(5, 6)
    normed, li = layer(z2[...])
    put(L3G, colsum(dx * normed))
    put(L3B, colsum(dx))
    dz = dz3 + layer_back(dx, normed, li, row(L3G))
    z2[...] = dz
    put(COB, colsum(dz))
    gd[1] = nn(oct_[...], own(dz).astype(BF)).astype(BF)
    do = nt(dz.astype(BF), mats[MCO]).astype(BF)
    dp = nt(do, vb[...])
    dot = transposed(do)
    qt = transposed(qc[...])
    gkv[1] = tn(ctx[...], own(from_heads(nn(dot, prob[...].astype(BF)))).astype(BF)).astype(BF)
    for h in range(HEADS):
        at = slice(KEYS * h, KEYS * (h + 1))
        p, d = prob[:, at], dp[:, at]
        dsc[:, at] = (p * (d - jnp.sum(p * d, axis=1, keepdims=True)) * SCALE).astype(BF)
    gkv[0] = tn(ctx[...], own(from_heads(nn(qt, dsc[...]))).astype(BF)).astype(BF)
    flow.ready(7)
    dq = nn(dsc[...], kb[...])
    gd[2] = nn(x2t[...], own(dq).astype(BF)).astype(BF)
    dx = nt(dq.astype(BF), mats[MCQ])
    normed, li = layer(z1[...])
    put(L2G, colsum(dx * normed))
    put(L2B, colsum(dx))
    dz = z2[...] + layer_back(dx, normed, li, row(L2G))
    dz1[...] = dz
    flow.ready(0)
    put(SOB, colsum(dz))
    gd[3] = nn(ot[...], own(dz).astype(BF)).astype(BF)
    do = nt(dz.astype(BF), mats[MSO]).astype(BF)
    for h in range(HEADS):
        dos[h] = head(do, h)


ABT = 256


def attend_back_kernel(q, k, v, do, lse, dq, dk, dv, qt, kacc, vacc):
    steps = [(h, pl.ds(t * ABT, ABT)) for h in range(HEADS) for t in range(N // ABT)]

    def scores(h, rows):
        return nt(k[h], q[h, rows, :]), nt(v[h], do[h, rows, :])

    now = scores(*steps[0])
    for i, (h, rows) in enumerate(steps):
        later = scores(*steps[i + 1]) if i + 1 < len(steps) else None
        s, dp = now
        p = jnp.exp2(s * (SCALE * LOG2E) - lse[h, :, rows])
        ds = (p * (dp - jnp.sum(p * dp, axis=0, keepdims=True)) * SCALE).astype(BF)
        dkt, dvt = nn(ds, q[h, rows, :]), nn(p.astype(BF), do[h, rows, :])
        if i % (N // ABT) == 0:
            kt = k[h].astype(F32).T.astype(BF)
            kacc[h], vacc[h] = dkt, dvt
        else:
            kacc[h] += dkt
            vacc[h] += dvt
        qt[h * HD : (h + 1) * HD, rows] = nn(kt, ds)
        now = later

    dq[...] = qt[...].T.astype(BF)

    def one(rows):
        for acc, dst in ((kacc, dk), (vacc, dv)):
            dst[rows, :] = jnp.concatenate([acc[h, rows, :] for h in range(HEADS)], axis=1).astype(BF)

    tiles(one)


def put_rows(s_ref, start, v, step=1):
    n = v.shape[0]
    ds = pl.ds(start, n) if step == 1 else pl.ds(start, n, stride=step)
    s_ref[0, ds, :] = v[:, :128]
    s_ref[1, ds, :32] = v[:, 128:]


def roll_rows(s_ref, out_ref, lo_chunk, hi_chunk):
    q = 80

    @pl.loop(lo_chunk, hi_chunk)
    def _(c):
        g = []
        for i in range(4):
            ds = pl.ds(c * 4 * q + i, q, stride=4)
            g.append((s_ref[0, ds, :], s_ref[1, ds, :32]))
        base = (c - lo_chunk) * 5 * q
        out_ref[pl.ds(base, q, stride=5), :] = g[0][0]
        for i in range(3):
            lo = 96 - 32 * i
            out_ref[pl.ds(base + i + 1, q, stride=5), :] = jnp.concatenate(
                ([g[i][0][:, 128 - 32 * i :]] if i else []) + [g[i][1], g[i + 1][0][:, :lo]], axis=1
            )
        out_ref[pl.ds(base + 4, q, stride=5), :] = jnp.concatenate([g[3][0][:, 32:], g[3][1]], axis=1)


def by_owner(s_ref, flat, out, total):
    owners, room = math.prod(out.shape[:-2]), out.shape[-2]
    size = room if total < owners * room and len(out.shape) == 3 else min(room, ROWS)
    half = owners // 2 * size
    for lo, hi, first in ((0, min(-(-half // 400), total // 400), 0), (half // 400, total // 400, owners // 2)):
        if hi > lo:
            roll_rows(s_ref, flat, lo, hi)
        at = 400 * max(hi - lo, 0)
        if at < flat.shape[0]:
            flat[at:, :] = jnp.zeros((flat.shape[0] - at, 128), F32)
        for t in range(first, first + owners // 2):
            spot = (t % 2, t // 2) if len(out.shape) == 4 else (t,)
            row = t * size - 400 * lo
            out[(*spot, slice(0, size))] = flat[row : row + size, :].astype(BF)
            if room > size:
                out[(*spot, slice(size, room))] = jnp.zeros((room - size, 128), BF)


def conv_grads(a_ref, g_ref, s_ref, start):
    at = transposed(a_ref[...])
    for r in range(3):
        rows = SIDE * (2 - r)
        three = nn(at, g_ref[rows : rows + N, :])
        for i in range(3):
            put_rows(s_ref, start + D * (3 * r + i), three[:, W * (2 - i) : W * (3 - i)])


def back_kernel(
    flow, dq, dk, dv, dz1, dh3, z0, h2, h1, h0, stats, w1, c2, tr, vec0, vec1, a1, a2, ntr, x1, noisy,
    gd, ggi, ggo, gkv, dvec_in, dgib, dwout, dbout,
    out1, out0, dtv,
    dh, g_ref, go_ref, dvec, s_ref, flat, o_ref,
):
    c = lax.axis_index(CH)
    clear_margins(g_ref)
    clear_margins(go_ref)
    dvec[...] = dvec_in[...]

    def row(i):
        return vec1[i : i + 1, :]

    def put(i, v):
        dvec[i : i + 1, :] = v

    dx = nt(dq[...], tr[MQ]) + nt(dk[...], tr[MK]) + nt(dv[...], tr[MV])
    xt = transposed(x1[...])
    for j, g in enumerate((dq, dk, dv)):
        put_rows(s_ref, QKV + j, nn(xt, own(g[...].astype(F32)).astype(BF)), 3)
    flow.need(5, 3)
    normed, li = layer(z0[...])
    put(L1G, colsum(dx * normed))
    put(L1B, colsum(dx))
    dz = dz1[...] + layer_back(dx, normed, li, row(L1G))
    put(PIB, colsum(dz))
    flow.need(17)
    put_rows(s_ref, PI, tn(ntr[...], own(dz).astype(BF)))
    g = nt(dz.astype(BF), tr[MPI])

    def norm_back(g, n, at, gain):
        dgain, dbias = colsum(g * n), colsum(g)
        back = stats[at + 1 : at + 2, :] * (g * gain - group_mean(gain * dbias) - n * group_mean(gain * dgain))
        return back, dgain, dbias

    def normed_of(src, at):
        return (src[...] - stats[at : at + 1, :]) * stats[at + 1 : at + 2, :]

    flow.need(6, 4)
    g, dgain, dbias = norm_back(g, normed_of(h2, 4), 4, row(NTG))
    put(NTG, dgain)
    put(NTB, dbias)
    g = dh3[...] + g
    dh[...] = g
    put(C2B, colsum(g))
    put_shifts(g_ref, g)
    put_shifts(go_ref, own(g))
    flow.need(16)
    conv_grads(a2, go_ref, s_ref, C2)
    flow.need(7, 11)
    n = normed_of(h1, 2)
    g = conv_back_rows(g_ref, c2) * silu_slope(n * row(N2G) + row(N2B))
    g, dgain, dbias = norm_back(g, n, 2, row(N2G))
    put(N2G, dgain)
    put(N2B, dbias)
    total = colsum(g)
    dtv[...] = total
    put_shifts(g_ref, g)
    put_shifts(go_ref, own(g))

    flow.need(20, 21, 22, 23)
    for i, r in enumerate((PO, CO, CQ, SO)):
        put_rows(s_ref, r, gd[i].astype(F32))
    for j in range(8):
        put_rows(s_ref, GI + j, ggi[j].astype(F32), 8)
    for j in range(4):
        rows = ggo[j].astype(F32)
        for b in range(2):
            put_rows(s_ref, GO + 640 * b + W * j, rows[W * b : W * (b + 1), :])
    for j in range(2):
        put_rows(s_ref, CKV + j, gkv[j].astype(F32), 2)
    for i, r in enumerate(VEC1):
        put_rows(s_ref, r, own(dvec[i : i + 1, :]))
    put_rows(s_ref, GIB, own(dgib[...]))
    wide = jnp.where(c == 0, dwout[:18, :], dwout[18:36, :])
    for ch in range(2):
        for m in range(4):
            o_ref[ch, pl.ds(m, 9, stride=4), :80] = wide[9 * ch : 9 * ch + 9, 80 * m : 80 * m + 80]
    lane = lax.broadcasted_iota(jnp.int32, (80, W), 0)
    col = lax.broadcasted_iota(jnp.int32, (80, W), 1)
    moved = jnp.zeros((36, W), F32)
    for ch in range(2):
        spot = jnp.where(2 * lane + ch == col, 1.0, 0.0)
        moved += jnp.dot(o_ref[ch, :36, :80], spot, precision=HI, preferred_element_type=F32)
    put_rows(s_ref, OUT, moved)
    b0 = jnp.where(c == 0, dbout[0:1, 0:1], dbout[2:3, 0:1])
    b1 = jnp.where(c == 0, dbout[1:2, 0:1], dbout[3:4, 0:1])
    at = lax.broadcasted_iota(jnp.int32, (1, W), 1)
    put_rows(s_ref, OUTB, jnp.where(at == 0, b0, jnp.where(at == 1, b1, 0.0)))
    s_ref[:, OUTB + 1 :, :] = jnp.zeros((2, 4 * R1 // 5 - OUTB - 1, 128), F32)
    by_owner(s_ref, flat, out1, R1)
    flow.ready(0)

    flow.need(15, 8, 10)
    conv_grads(a1, go_ref, s_ref, 39)
    n = normed_of(h0, 0)
    g = conv_back_rows(g_ref, w1) * silu_slope(n * vec0[1:2, :] + vec0[2:3, :])
    g, dgain, dbias = norm_back(g, n, 0, vec0[1:2, :])
    g = dh[...] + g
    cols = jnp.concatenate([shift_lanes(noisy[...], t) for t in range(9)], axis=0).astype(BF)
    put_rows(s_ref, 0, nn(cols, own(g).astype(BF)))
    for r, v in zip(VEC0, (colsum(g), dgain, dbias, total)):
        put_rows(s_ref, r, own(v))
    s_ref[:, 4 * FRONT // 5 : 4 * R0 // 5, :] = jnp.zeros((2, 4 * (R0 - FRONT) // 5, 128), F32)
    by_owner(s_ref, flat, out0, R0)


FIRST = (0, 0, 1, 2, 3)
SECOND = (0, 1, 2, 3, 3)


def time_rows(facts, count):
    row = lax.axis_index(DP) * count + lax.broadcasted_iota(jnp.int32, (count, 1), 0)

    def wide(at, n):
        return jnp.concatenate([facts[:, at + i, :] for i in range(n)], axis=1)

    def meets(u, k):
        spot = jnp.where(k == lax.broadcasted_iota(jnp.int32, (1, u.shape[1]), 1), 1.0, 0.0).astype(BF)
        return nt(spot, u.astype(BF))

    total = jnp.zeros((count, 128), F32)
    for u, at, start, size in ((wide(FE, 3)[:, :D], FD1, T1, D), (wide(FU1, 10), FD2, T2, 4 * D)):
        rel = row - start
        k, line = rel // 5, rel % 5
        met = meets(u, jnp.where(rel < 0, -1, k))
        for j in range(5):
            g = facts[:, at + j, :]
            total += nn(jnp.where(line == j, met, 0.0).astype(BF), g.astype(BF))
            total += jnp.where((rel >= 0) & (k == size) & (line == j), colsum(g), 0.0)
    rel = row - T3
    group, line = rel // 5, rel % 5
    d3 = wide(FD3, 2)[:, :W]
    zero = jnp.zeros((d3.shape[0], 128), F32)
    u = wide(FU2, 10)
    for picks, shift in ((FIRST, 0), (SECOND, 1)):
        k = jnp.full_like(rel, -1)
        for j in range(5):
            k = jnp.where((rel >= 0) & (line == j), 4 * group + picks[j], k)
        met = meets(u, k)
        for j in range(5):
            if shift == 0:
                lo = (0, 128, 96, 64, 32)[j]
                g = d3[:, lo : min(lo + 128, W)]
                g = jnp.concatenate([g, zero[:, : 128 - g.shape[1]]], axis=1) if g.shape[1] < 128 else g
            else:
                if j in (0, 4):
                    continue
                g = jnp.concatenate([zero[:, : 32 * j], d3[:, : 128 - 32 * j]], axis=1)
            total += nn(jnp.where(line == j, met, 0.0).astype(BF), g.astype(BF))
            total += jnp.where((k == 4 * D) & (line == j), colsum(g), 0.0)
    return total


def update_kernel(with_time, params, momentum, ema, sum1, sum0, facts, new_params, new_momentum, new_ema, sums):
    total = facts[0, FL : FL + 1, :]
    for i in range(1, facts.shape[0]):
        total += facts[i, FL : FL + 1, :]
    sums[...] = total
    scale = 1.0 / (LAT * jnp.maximum(total[:, 1:2], 1.0))
    first = sum0[...]
    if with_time:
        first += time_rows(facts, sum0.shape[0])
    for p, g in enumerate((first, sum1[...])):
        g = g * scale
        m = MU * momentum[p] + g
        new_momentum[p] = m
        w = params[p] - LR * (g + MU * m)
        new_params[p] = w
        new_ema[p] = ED * ema[p] + (1.0 - ED) * w


ROWS = 856
SLAB = 864
SOME = 240
REST = SLAB - 3 * SOME


def send(src, dst, sems, i, j, target):
    copy = pltpu.make_async_remote_copy(
        src_ref=src, dst_ref=dst, send_sem=sems[0].at[i], recv_sem=sems[1].at[j],
        device_id={DP: target}, device_id_type=pl.DeviceIdType.MESH,
    )
    copy.start()
    return copy


PIECES = tuple(slice(16 * a, 16 * b) for a, b in ((0, 7), (7, 14), (14, 21), (21, 28), (28, 35), (35, 42), (42, 48), (48, 54)))


def gather_kernel(
    params, step, latents, noise, g0, g1, e, noisy, vec, p1, p2, stats, w1b_out, tw2_out, tw3_out, h0_out, h1_out, a1_out,
    low, slabs, flat, s_ref, w1b, tw2, tw3, h0, h1, a1, w1, win, tv, half1, half2, half3, sh, acc,
    send_sem, recv_sem, keep_sem, slab_sem, out_sem, swap_sem,
):
    low[:, :ROWS, :] = params[...].astype(BF)
    low[:, ROWS:, :] = jnp.zeros((2, SLAB - ROWS, 128), BF)
    me, y = lax.axis_index(DP), lax.axis_index(CH)
    k, x, z = me % 2, (me // 2) % 2, me // 4
    core = {DP: me + 1 - 2 * k}
    side = {DP: me + 2 - 4 * x}
    other = {CH: 1 - y}
    ring = [{DP: (me + 4 * o) % 16} for o in range(4)]
    barrier = pltpu.get_barrier_semaphore()
    for target in [core, side, other] + ring[1:]:
        pl.semaphore_signal(barrier, inc=1, device_id=target, device_id_type=pl.DeviceIdType.MESH)
    pl.semaphore_wait(barrier, 6)
    count = [0]
    started = []

    def push(ref, target):
        i = count[0]
        count[0] += 1
        return [start(ref, ref, i, i, target)]

    def start(src, dst, i, j, target):
        copy = pltpu.make_async_remote_copy(
            src_ref=src, dst_ref=dst, send_sem=send_sem.at[i], recv_sem=recv_sem.at[j],
            device_id=target, device_id_type=pl.DeviceIdType.MESH,
        )
        copy.start()
        started.append(copy)
        return copy

    def push_ring(ref):
        i = count[0]
        count[0] += 3
        return [start(ref, ref, i + o - 1, i + 3 - o, ring[o]) for o in (2, 1, 3)]

    def arrive(copies):
        for copy in copies:
            copy.wait_recv()

    keeps = []
    for p, g in enumerate((g0, g1)):
        keep = pltpu.make_async_copy(low.at[p], g.at[y, z, x, k], keep_sem.at[p])
        keep.start()
        keeps.append(keep)
    work = [(p, g, rows, p * (i % 2)) for p, g in enumerate((g0, g1)) for i, rows in enumerate(PIECES)]
    first, second, third, last = {}, {}, {}, ([], [])

    def begin(i):
        p, g, rows, _ = work[i]
        if i % len(PIECES) == 0:
            keeps[p].wait()
        first[i] = push_ring(g.at[y, z, x, k, rows])

    def middle(i):
        p, g, rows, turn = work[i]
        arrive(first[i])
        second[i] = push(g.at[y, :, x, k, rows], other if turn else side)
        last[p].extend(push(g.at[y, :, x, k, rows], core))

    def finish(i):
        p, g, rows, turn = work[i]
        zs = slice(0, 4 if p else 2)
        arrive(second[i])
        if turn:
            third[i] = push(g.at[:, :, x, k, rows], side)
            last[p].extend(push(g.at[1 - y, :, x, k, rows], core))
        else:
            third[i] = push(g.at[y, zs, :, k, rows], other)
            last[p].extend(push(g.at[y, :, 1 - x, k, rows], core))

    def pass_on(i):
        p, g, rows, turn = work[i]
        zs = slice(0, 4 if p else 2)
        arrive(third[i])
        last[p].extend(push(g.at[:, :, 1 - x, k, rows] if turn else g.at[1 - y, zs, :, k, rows], core))

    outs = [
        pltpu.make_async_copy(src, dst, out_sem.at[i])
        for i, (src, dst) in enumerate(
            ((w1b, w1b_out), (tw2, tw2_out), (tw3, tw3_out), (h0, h0_out), (h1, h1_out), (a1, a1_out))
        )
    ]
    fetches = [
        pltpu.make_async_copy(g0.at[a, b], slabs.at[a, b], slab_sem.at[i])
        for i, (a, b) in enumerate([(y, b) for b in range(4)] + [(1 - y, b) for b in range(2)])
    ]
    slabs[1 - y, 2:4] = jnp.zeros((2,) + slabs.shape[2:], BF)

    def fetch():
        arrive(last[0])
        for copy in fetches:
            copy.start()

    def flat_half(a):
        if a == 0:
            for copy in fetches:
                copy.wait()
        for t in range(16):
            flat[a, t * ROWS : (t + 1) * ROWS, :] = slabs[a, t // 4, t // 2 % 2, t % 2, :ROWS, :].astype(F32)

    def front():
        take_front(s_ref, win, w1, w1b, vec)
        outs[0].start()

    def times():
        for i in range(4):
            tw2[i] = own(get_rows(s_ref, U2 + i, 4 * D, 4)).astype(BF)
        tw3[...] = own(get_rows(s_ref, U3, 4 * D)).astype(BF)
        outs[1].start()
        outs[2].start()

    def swap(i, ref):
        return pltpu.make_async_remote_copy(
            src_ref=ref.at[y], dst_ref=ref.at[y], send_sem=swap_sem.at[i], recv_sem=swap_sem.at[3 + i],
            device_id=other, device_id_type=pl.DeviceIdType.MESH,
        )

    def units(u, w, start, size):
        parts = [nn(u, w(i)) + own(get_rows(s_ref, start + 4 * size + i, 1)) for i in range(4)]
        return jnp.concatenate(parts, axis=1)

    swaps = [swap(0, half1), swap(1, half2), swap(2, half3)]

    def time_one():
        u = e[...].astype(BF)
        half1[y] = units(u, lambda i: own(get_rows(s_ref, U1 + i, D, 4)).astype(BF), U1, D)
        swaps[0].start()

    def time_two():
        swaps[0].wait_recv()
        p1[...] = jnp.concatenate([half1[0], half1[1]], axis=1)
        half2[y] = units(silu(p1[...]).astype(BF), lambda i: tw2[i], U2, 4 * D)
        swaps[1].start()

    def time_three():
        swaps[1].wait_recv()
        p2[...] = jnp.concatenate([half2[0], half2[1]], axis=1)
        half3[y] = nn(silu(p2[...]).astype(BF), tw3[...]) + own(get_rows(s_ref, U3 + 4 * D, 1))
        swaps[2].start()

    def time_last():
        swaps[2].wait_recv()
        tv[...] = jnp.concatenate([half3[0], half3[1]], axis=1)[:1]

    def both(*steps):
        def one():
            for step in steps:
                step()

        return one

    opening, *rows_of_taps = start_steps(noisy, tv, win, w1, vec, h0, h1, a1, stats, sh, acc)
    todo = [
        fetch,
        lambda: flat_half(0),
        lambda: flat_half(1),
        lambda: unroll(flat, s_ref, 0, 9),
        lambda: unroll(flat, s_ref, 9, 18),
        lambda: unroll(flat, s_ref, 18, 27),
        lambda: unroll(flat, s_ref, 27, R1 // 400),
        time_one,
        both(front, times),
        time_two,
        opening,
        both(outs[3].start, outs[5].start, rows_of_taps[0]),
        time_three,
        rows_of_taps[1],
        time_last,
        both(rows_of_taps[2], outs[4].start),
    ]
    ahead = 4
    for i in range(ahead):
        begin(i)
    e[...] = jnp.broadcast_to(time_features(step[...]), (8, D))
    add_noise(step[...], latents, noise, noisy)
    for i in range(len(work) + 2):
        if i < len(work):
            middle(i)
            if i + ahead < len(work):
                begin(i + ahead)
        if i - 3 >= len(PIECES) and todo:
            todo.pop(0)()
        if 0 <= i - 1 < len(work):
            finish(i - 1)
        if 0 <= i - 3 < len(work):
            pass_on(i - 3)
        if i - 3 >= len(PIECES) - 1 and todo:
            todo.pop(0)()
    pass_on(len(work) - 1)
    for step in todo:
        step()
    for copy in outs:
        copy.wait()
    for copy in swaps:
        copy.wait_send()
    arrive(last[1])
    for copy in started:
        copy.wait_send()


def gather_weights(*operands):
    hbm, vm = pl.BlockSpec(memory_space=pl.ANY), pl.BlockSpec(memory_space=pltpu.VMEM)
    gathered = sds((2, 4, 2, 2, SLAB, 128), BF)
    large = (sds((3, D, 3 * D), BF), sds((4, 4 * D, W), BF), sds((4 * D, W), BF))
    large += (sds((N, D)), sds((N, D)), sds((N, D), BF))
    small = (sds((8, D)), sds((LAT, N)), sds((8, D)), sds((8, 4 * D)), sds((8, 4 * D)), sds((8, D)))
    dma = pltpu.SemaphoreType.DMA
    return pl.pallas_call(
        gather_kernel,
        out_shape=(gathered, gathered) + small + large,
        in_specs=[vm] * 4,
        out_specs=(hbm, hbm) + (vm,) * len(small) + (hbm,) * len(large),
        scratch_shapes=[
            pltpu.VMEM((2, SLAB, 128), BF),
            pltpu.VMEM(gathered.shape, BF),
            pltpu.VMEM((2, 16 * ROWS, 128), F32),
            pltpu.VMEM((3, 4 * R1 // 5, 128), F32),
            *(pltpu.VMEM(v.shape, v.dtype) for v in large),
            pltpu.VMEM((3, 3 * D, D), BF),
            pltpu.VMEM((36, D), BF),
            pltpu.VMEM((1, D), F32),
            pltpu.VMEM((2, 8, 2 * D), F32),
            pltpu.VMEM((2, 8, 2 * D), F32),
            pltpu.VMEM((2, 8, W), F32),
            pltpu.VMEM((N + 2 * SIDE, 3 * D), BF),
            pltpu.VMEM((8, D), F32),
            dma((128,)),
            dma((128,)),
            dma((2,)),
            dma((6,)),
            dma((6,)),
            dma((6,)),
        ],
        compiler_params=pltpu.CompilerParams(collective_id=2, has_side_effects=True, vmem_limit_bytes=63 * 2**20),
    )(*operands)


def add_up(*terms):
    total = terms[0].astype(F32)
    for term in terms[1:]:
        total += term.astype(F32)
    return total


def reduce_kernel(
    p1, p0, dtv, tw2_in, tw3_in, p1t, p2t, e, mask, loss, sum1, sum0, all_facts,
    kp1, kp0, tw2, tw3, facts, r1, sa, rx, ta, rz, r1b, sb, rbz, tb, rbx, some, land, fx, timed, send_sem, recv_sem, fsend, frecv, gsend, grecv, lsem, half, ssem,
):
    me = lax.axis_index(DP)
    k, x, z = me % 2, (me // 2) % 2, me // 4
    kept = [
        pltpu.make_async_copy(src, dst, lsem.at[i])
        for i, (src, dst) in enumerate(((p1.at[k], kp1), (p0.at[k], kp0), (tw2_in, tw2), (tw3_in, tw3)))
    ]
    for copy in kept:
        copy.start()
    barrier = pltpu.get_barrier_semaphore()
    for o in range(1, 16):
        pl.semaphore_signal(barrier, inc=1, device_id={DP: (me + o) % 16}, device_id_type=pl.DeviceIdType.MESH)
    y = lax.axis_index(CH)
    pl.semaphore_signal(barrier, inc=1, device_id={CH: 1 - y}, device_id_type=pl.DeviceIdType.MESH)
    pl.semaphore_wait(barrier, 16)
    sems = (send_sem, recv_sem)

    def swap(i):
        copy = pltpu.make_async_remote_copy(
            src_ref=half.at[i, y], dst_ref=half.at[i, y], send_sem=ssem.at[i], recv_sem=ssem.at[2 + i],
            device_id={CH: 1 - y}, device_id_type=pl.DeviceIdType.MESH,
        )
        copy.start()
        return copy

    core = me + 1 - 2 * k
    side = me + 2 - 4 * x
    chunks = [p0] + [p1.at[:, :, SOME * i : SOME * (i + 1)] for i in range(3)]
    mine = [kp0] + [kp1.at[:, SOME * i : SOME * (i + 1)] for i in range(3)]
    rest = p1.at[:, :, 3 * SOME :]

    def over_z(src, dst, base):
        return [
            send(src.at[(z + o) % 4], dst.at[3 - o], sems, base + o - 1, base + 3 - o, (me + 4 * o) % 16)
            for o in (2, 1, 3)
        ]

    over_core_b = send(rest.at[1 - k], r1b, sems, 20, 20, core)
    over_core = [send(ref.at[1 - k], r1.at[i], sems, i, i, core) for i, ref in enumerate(chunks)]
    for copy in kept:
        copy.wait()
    half[0, y] = nt(jnp.broadcast_to(own(dtv[...]), (8, W)).astype(BF), tw3[...])
    swaps = [swap(0)]
    over_core_b.wait_recv()
    for m in range(8):
        sb[m // 2, m % 2] = add_up(kp1[m, 3 * SOME :], r1b[m]).astype(BF)
    over_z_b = over_z(sb, rbz, 21)
    over_x = []
    for i, ref in enumerate(mine):
        over_core[i].wait_recv()
        for m in range(8):
            sa[i, m % 2, m // 2] = add_up(ref[m], r1[i, m]).astype(BF)
        over_x.append(send(sa.at[i, 1 - x], rx.at[i], sems, 4 + i, 4 + i, side))
        if i == 1:
            swaps[0].wait_recv()
            d2 = (half[0, 0] + half[0, 1]) * silu_slope(p2t[...])
            mine2 = jnp.where(y == 0, d2[:, : 2 * D], d2[:, 2 * D :]).astype(BF)
            half[1, y] = sum(nt(mine2[:, W * j : W * (j + 1)], tw2[j]) for j in range(4))
            swaps.append(swap(1))
    swaps[1].wait_recv()
    d1 = (half[1, 0] + half[1, 1]) * silu_slope(p1t[...])
    put_facts(facts, e, p1t, p2t, d1, d2, dtv, mask, loss)
    fsems = (fsend, frecv)
    fx[z, x, k] = facts[...]
    facts_z = [send(facts, fx.at[z, x, k], fsems, o - 1, 3 - o, (me + 4 * o) % 16) for o in (2, 1, 3)]
    along = []
    for i in range(4):
        over_x[i].wait_recv()
        for m in range(4):
            ta[i, m] = add_up(sa[i, x, m], rx[i, m]).astype(BF)
        along.append(over_z(ta.at[i], rz.at[i], 8 + 3 * i))
        if i == 1:
            for copy in facts_z:
                copy.wait_recv()
            facts_x = send(fx.at[:, x, k], fx.at[:, x, k], fsems, 3, 3, side)
        if i == 3:
            facts_x.wait_recv()
            facts_core = send(fx.at[:, :, k], fx.at[:, :, k], fsems, 4, 4, core)
    for copy in over_z_b:
        copy.wait_recv()
    for m in range(2):
        tb[m] = add_up(sb[z, m], rbz[0, m], rbz[1, m], rbz[2, m]).astype(BF)
    over_x_b = send(tb.at[1 - x], rbx, sems, 24, 24, side)

    def done(i):
        for copy in along[i]:
            copy.wait_recv()
        return add_up(ta[i, z], rz[i, 0], rz[i, 1], rz[i, 2])

    facts_core.wait_recv()
    all_facts[...] = fx[...].reshape(16, FACTS, 128)
    timed[...] = time_rows(all_facts, ROWS)
    some[...] = done(0)

    @pl.when(me > 0)
    def _():
        @pl.loop(0, SOME // 8)
        def _(g):
            row = SOME * me + 8 * g
            owner = row // ROWS
            at = pl.multiple_of(row - ROWS * owner, 8)
            pltpu.make_async_remote_copy(
                src_ref=some.at[pl.ds(pl.multiple_of(8 * g, 8), 8)], dst_ref=land.at[pl.ds(at, 8)],
                send_sem=gsend, recv_sem=grecv, device_id={DP: owner}, device_id_type=pl.DeviceIdType.MESH,
            ).start()

    for i in range(3):
        sum1[SOME * i : SOME * (i + 1), :] = done(i + 1)
    over_x_b.wait_recv()
    sum1[3 * SOME :, :] = add_up(tb[x, : ROWS - 3 * SOME], rbx[: ROWS - 3 * SOME])

    def landed(lo, hi):
        part = land.at[lo:hi]
        pltpu.make_async_remote_copy(
            src_ref=part, dst_ref=part, send_sem=gsend, recv_sem=grecv,
            device_id={DP: me}, device_id_type=pl.DeviceIdType.MESH,
        ).wait_recv()
        sum0[lo:hi, :] = land[lo:hi, :] + timed[lo:hi, :]

    @pl.when(me == 0)
    def _():
        landed(SOME, ROWS)
        sum0[:SOME, :] = some[...] + timed[:SOME, :]

    @pl.when((me > 0) & (me < 4))
    def _():
        landed(0, ROWS)

    @pl.when(me == 4)
    def _():
        landed(0, 16 * SOME - 4 * ROWS)
        sum0[16 * SOME - 4 * ROWS :, :] = timed[16 * SOME - 4 * ROWS :, :]

    @pl.when(me > 4)
    def _():
        sum0[...] = timed[...]

    @pl.when(me > 0)
    def _():
        pltpu.make_async_remote_copy(
            src_ref=some, dst_ref=some, send_sem=gsend, recv_sem=grecv,
            device_id={DP: me}, device_id_type=pl.DeviceIdType.MESH,
        ).wait_send()

    for copy in [over_core_b, over_x_b] + over_core + over_z_b + over_x + sum(along, []) + facts_z + [facts_x, facts_core] + swaps:
        copy.wait_send()


def sum_over_samples(*operands):
    vm, hbm = pl.BlockSpec(memory_space=pltpu.VMEM), pl.BlockSpec(memory_space=pl.ANY)
    dma = pltpu.SemaphoreType.DMA
    return pl.pallas_call(
        reduce_kernel,
        out_shape=(sds((ROWS, 128)), sds((ROWS, 128)), sds((16, FACTS, 128))),
        in_specs=[hbm, hbm, vm, hbm, hbm] + [vm] * 5,
        out_specs=(vm,) * 3,
        scratch_shapes=[
            pltpu.VMEM((8, SLAB, 128), BF),
            pltpu.VMEM((8, SOME, 128), BF),
            pltpu.VMEM((4, 4 * D, W), BF),
            pltpu.VMEM((4 * D, W), BF),
            pltpu.VMEM((FACTS, 128), F32),
            pltpu.VMEM((4, 8, SOME, 128), BF),
            pltpu.VMEM((4, 2, 4, SOME, 128), BF),
            pltpu.VMEM((4, 4, SOME, 128), BF),
            pltpu.VMEM((4, 4, SOME, 128), BF),
            pltpu.VMEM((4, 3, SOME, 128), BF),
            pltpu.VMEM((8, REST, 128), BF),
            pltpu.VMEM((4, 2, REST, 128), BF),
            pltpu.VMEM((3, 2, REST, 128), BF),
            pltpu.VMEM((2, REST, 128), BF),
            pltpu.VMEM((REST, 128), BF),
            pltpu.VMEM((SOME, 128), F32),
            pltpu.VMEM((ROWS, 128), F32),
            pltpu.VMEM((4, 2, 2, FACTS, 128), F32),
            pltpu.VMEM((ROWS, 128), F32),
            dma((25,)),
            dma((25,)),
            dma((5,)),
            dma((5,)),
            dma,
            dma,
            dma((4,)),
            pltpu.VMEM((2, 2, 8, 4 * D), F32),
            dma((4,)),
        ],
        compiler_params=pltpu.CompilerParams(
            collective_id=1, has_side_effects=True, vmem_limit_bytes=62 * 2**20
        ),
    )(*operands)


def time_features(steps):
    ladder = lax.broadcasted_iota(jnp.int32, (1, D // 2), 1).astype(F32)
    angles = steps.astype(F32) * jnp.exp(-math.log(10000.0) * ladder / (D // 2))
    return jnp.concatenate([jnp.cos(angles), jnp.sin(angles)], axis=1)


def add_noise(step, latents, noise, noisy):
    shape = (8, 128)
    level = 128 * lax.broadcasted_iota(jnp.int32, shape, 0) + lax.broadcasted_iota(jnp.int32, shape, 1)
    lowest, highest = 0.00085**0.5, 0.012**0.5
    beta = jnp.square(lowest + (highest - lowest) * level.astype(F32) / 999.0)
    logs = jnp.where(level <= step, jnp.log(1.0 - beta), 0.0)
    abar = jnp.exp(jnp.sum(jnp.sum(logs, axis=1, keepdims=True), axis=0, keepdims=True))
    noisy[...] = jnp.sqrt(abar) * latents[...] + jnp.sqrt(1.0 - abar) * noise[...]


def prepare_kernel(step, latents, noise, e, noisy):
    e[...] = jnp.broadcast_to(time_features(step[...]), (8, D))
    add_noise(step[...], latents, noise, noisy)


def shards(params, momentum, ema_params, latents, noise_eps, timesteps, pixel_mask, context):
    c = lax.axis_index(CH)
    d = lax.axis_index(DP)
    n_dp = lax.axis_size(DP)
    rows_dev = params.shape[2]
    rows_all = rows_dev * n_dp
    quick = n_dp == 16 and rows_dev == ROWS
    step, noise = timesteps[:, None], noise_eps[0]
    if quick:
        _, part1, e, noisy, vec0, p1, p2, stats, w1b, tw2, tw3, h0, h1, a1 = gather_weights(
            params[0], step, latents[0], noise
        )
        part1 = part1.reshape(2, 16, SLAB, 128)
    else:
        e, noisy = kcall(prepare_kernel, (sds((8, D)), sds((LAT, N))), (step, latents[0], noise))
        low = params[0].astype(BF)
        part0, part1 = (lax.all_gather(lax.all_gather(low[i], CH, axis=0), DP, axis=1) for i in range(2))

    px = (N, D)
    hx = (HEADS, N, HD)
    sh = (N + 2 * SIDE, 3 * D)
    taps, back = sds((3, 3 * D, D), BF), sds((3, D, 3 * D), BF)
    flat = pltpu.VMEM((2, rows_all, 128), F32)
    unrolled = pltpu.VMEM((3, 4 * R1 // 5, 128), F32)
    units = sds((8, 4 * D))
    if not quick:
        win, w1, w1b, vec0, tw2, tw3, tv, p1, p2 = kcall(
            partial(unpack0_kernel, rows_dev),
            (sds((36, D), BF), taps, back, sds((8, D)), sds((4, 4 * D, D), BF), sds((4 * D, D), BF), sds((1, D)))
            + (units, units),
            (part0, e),
            (flat, unrolled),
        )
        h0, h1, a1, stats = kcall(
            start_kernel,
            (sds(px), sds(px), sds(px, BF), sds((8, D))),
            (noisy, tv, win, w1, vec0),
            (pltpu.VMEM(sh, BF), pltpu.VMEM((8, D), F32)),
        )
    c2, c2b, tr, mats, kvw, vec1, gib, wout, outb = kcall(
        partial(unpack1_kernel, rows_dev),
        (taps, back, sds((4, D, D), BF), sds((16, D, D), BF), sds((2, CTX, D), BF))
        + (sds((24, D)), sds((8, D)), sds((36, D), BF), sds((1, D))),
        (part1,),
        (flat, unrolled, pltpu.VMEM((2, 40, 128), F32)),
    )
    h2, z0, a2, ntr, x1, q, k, v, stats = kcall(
        front_kernel,
        (sds(px),) * 2 + (sds(px, BF),) * 3 + (sds(hx, BF),) * 3 + (sds((8, D)),),
        (h0, h1, stats, c2, tr, vec1),
        (pltpu.VMEM(sh, BF), pltpu.VMEM((8, D), F32)),
        late=(0, 3, 4),
        early=range(8),
    )
    o, lse = kcall(
        attend_kernel, (sds(px, BF), sds((HEADS, 1, N))), (q, k, v), (pltpu.VMEM((D, N), F32),)
    )
    square = (D, W)
    dz1, dh3, dos, loss, gd, ggi, ggo, gkv, dvec, dgib, dwout, dbout = kcall(
        middle_kernel,
        (sds(px), sds(px), sds(hx, BF), sds((1, 1)))
        + (sds((4,) + square, BF), sds((8,) + square, BF), sds((4,) + square, BF), sds((2, CTX, W), BF))
        + (sds((24, D)), sds((8, D)), sds((36, D)), sds((8, 128))),
        (o, z0, h2, context[0], noise, pixel_mask, mats, kvw, vec1, gib, wout, outb),
        [pltpu.VMEM(px, F32)] * 3
        + [pltpu.VMEM(px, BF)] * 4
        + [
            pltpu.VMEM((4, N, D), BF),
            pltpu.VMEM((4, N, D), F32),
            pltpu.VMEM((4, N, D), F32),
            pltpu.VMEM(px, BF),
            pltpu.VMEM(px, BF),
            pltpu.VMEM((HEADS * KEYS, D), BF),
            pltpu.VMEM((HEADS * KEYS, D), BF),
            pltpu.VMEM((N, HEADS * KEYS), F32),
            pltpu.VMEM((N, HEADS * KEYS), BF),
            pltpu.VMEM((8, D), F32),
            pltpu.VMEM((36, N), F32),
        ]
        + [pltpu.VMEM((D, N), BF)] * 4,
        late=(7, 6, 1, 2),
        early=(0, 1, 2, 4, 5, 6, 7),
    )
    dq, dk, dv = kcall(
        attend_back_kernel,
        (sds(px, BF),) * 3,
        (q, k, v, dos, lse),
        (pltpu.VMEM((D, N), F32), pltpu.VMEM(hx, F32), pltpu.VMEM(hx, F32)),
    )
    front = -(-FRONT // (16 * n_dp)) * 16 * n_dp
    lead = (2, 8) if quick else (n_dp,)
    own1, own0, dtv = kcall(
        back_kernel,
        (
            sds(lead + (SLAB if quick else rows_dev, 128), BF),
            sds(lead + (front // n_dp, 128), BF),
            sds((1, D)),
        ),
        (dq, dk, dv, dz1, dh3, z0, h2, h1, h0, stats, w1b, c2b, tr, vec0, vec1, a1, a2, ntr, x1, noisy,
         gd, ggi, ggo, gkv, dvec, dgib, dwout, dbout),
        (
            pltpu.VMEM(px, F32),
            pltpu.VMEM(sh, BF),
            pltpu.VMEM((sh[0], 3 * W), BF),
            pltpu.VMEM((24, D), F32),
            pltpu.VMEM((2, 4 * R1 // 5, 128), F32),
            pltpu.VMEM((7600, 128), F32),
            pltpu.VMEM((2, 40, 128), F32),
        ),
        late=(5, 3, 17, 6, 4, 16, 7, 11, 20, 21, 22, 23, 15, 8, 10),
        early=(0,),
    )
    timed = (dtv, tw2, tw3, p1, p2, e, pixel_mask, loss)
    if quick:
        sum1, sum0, all_facts = sum_over_samples(own1, own0, *timed)
    else:
        facts = kcall(time_back, sds((FACTS, 128)), timed)
        sum1 = lax.psum_scatter(own1, DP, scatter_dimension=0).astype(F32)
        sum0 = lax.all_gather(lax.psum_scatter(own0, DP, scatter_dimension=0), DP, axis=0, tiled=True)
        sum0 = jnp.pad(sum0, ((0, rows_all - front), (0, 0)))
        sum0 = lax.dynamic_slice_in_dim(sum0, d * rows_dev, rows_dev, 0).astype(F32)
        all_facts = lax.all_gather(facts, DP, axis=0)
    state = sds((2, rows_dev, 128))
    new_params, new_momentum, new_ema, sums = kcall(
        partial(update_kernel, not quick),
        (state, state, state, sds((1, 128))),
        (params[0], momentum[0], ema_params[0], sum1, sum0, all_facts),
    )
    return (new_params[None], new_momentum[None], new_ema[None], sums[0, 0], sums[0, 1])


def solution(mesh):
    packed = P(CH, None, DP, None)
    row = P(DP, None, None)
    return jax.shard_map(
        shards,
        mesh=mesh,
        in_specs=(packed, packed, packed, row, row, P(DP), P(DP, None), row),
        out_specs=(packed, packed, packed, P(), P()),
        check_vma=False,
    )
```

```python
import math
from functools import partial

import jax
import jax.numpy as jnp
from jax import lax
from jax.experimental import pallas as pl
from jax.experimental.pallas import tpu as pltpu
from jax.sharding import PartitionSpec as P

D = 320
W = 160
HEADS = 8
HD = 40
CTX = 768
TXT = 77
LAT = 4
SIDE = 32
N = 1024
EPS = 1e-5
LR = 0.2
MU = 0.9
ED = 0.9
CH = "chan"
DP = "dp"
F32 = jnp.float32
BF = jnp.bfloat16
HI = lax.Precision.HIGHEST
SCALE = HD**-0.5
LOG2E = 1.0 / math.log(2.0)

R0 = 4000
U1, U2, U3 = 2920, 4204, 9328
FRONT = 3650
T1, T2, T3 = 3650, 5255, 11660
C2 = 2
PI = 2885
QKV = 3208
SO = 4168
CQ = 4491
CKV = 4811
CO = 6347
GI = 6670
GIB = 9230
GO = 9238
PO = 10519
OUT = 10842
OUTB = 10878
R1 = 13600
VEC0 = (36, 37, 38, 2919)
VEC1 = (0, 1, 2882, 2883, 2884, 3205, 3206, 3207, 4488, 4489, 4490, 6667, 6668, 6669, 10518, 10839, 10840, 10841)
(N2G, N2B, C2B, NTG, NTB, PIB, L1G, L1B, SOB, L2G, L2B, COB, L3G, L3B, GOB, POB, NOG, NOB) = range(18)
MPI, MQ, MK, MV = range(4)
MSO, MCQ, MCO, MPO, MGV, MGG, MGO = 0, 1, 2, 3, 4, 8, 12


class Flow:
    def __init__(self, ins, outs, sems):
        self.ins = {i: pltpu.make_async_copy(src, dst, sems.at[j]) for j, (i, src, dst) in enumerate(ins)}
        n = len(ins)
        self.outs = {i: pltpu.make_async_copy(src, dst, sems.at[n + j]) for j, (i, dst, src) in enumerate(outs)}
        self.waiting = set(self.ins)
        self.going = []
        for copy in self.ins.values():
            copy.start()

    def need(self, *which):
        for i in which:
            self.ins[i].wait()
            self.waiting.discard(i)

    def ready(self, *which):
        for i in which:
            self.outs[i].start()
            self.going.append(i)

    def end(self):
        self.need(*sorted(self.waiting))
        self.ready(*(i for i in self.outs if i not in self.going))
        for copy in self.outs.values():
            copy.wait()


def kcall(body, outs, ins, scratch=(), late=(), early=()):
    vm, hbm = pl.BlockSpec(memory_space=pltpu.VMEM), pl.BlockSpec(memory_space=pl.ANY)
    single = not isinstance(outs, tuple)
    outs = (outs,) if single else outs
    n, m = len(ins), len(outs)
    late, early = tuple(late), tuple(early)
    scratch = list(scratch)
    count = len(scratch)
    if late or early:
        scratch += [pltpu.VMEM(ins[i].shape, ins[i].dtype) for i in late]
        scratch += [pltpu.VMEM(outs[i].shape, outs[i].dtype) for i in early]
        scratch.append(pltpu.SemaphoreType.DMA((len(late) + len(early),)))

    def whole(*refs):
        if not (late or early):
            return body(*refs)
        given, made, rest = list(refs[:n]), list(refs[n : n + m]), refs[n + m :]
        kept = rest[count:-1]
        inward = [(i, given[i], kept[j]) for j, i in enumerate(late)]
        outward = [(i, made[i], kept[len(late) + j]) for j, i in enumerate(early)]
        for i, _, ref in inward:
            given[i] = ref
        for i, _, ref in outward:
            made[i] = ref
        flow = Flow(inward, outward, rest[-1])
        body(flow, *given, *made, *rest[:count])
        flow.end()

    done = pl.pallas_call(
        whole,
        out_shape=outs,
        in_specs=[hbm if i in late else vm for i in range(n)],
        out_specs=tuple(hbm if i in early else vm for i in range(m)),
        scratch_shapes=scratch,
        compiler_params=pltpu.CompilerParams(vmem_limit_bytes=63 * 2**20),
    )(*ins)
    return done[0] if single else done


def sds(shape, dtype=F32):
    return jax.ShapeDtypeStruct(shape, dtype)


def tiles(fn, size=256, total=N):
    for t in range(total // size):
        fn(pl.ds(t * size, size))


def nn(a, b):
    return jnp.dot(a, b, preferred_element_type=F32)


def nt(a, b):
    return lax.dot_general(a, b, (((1,), (1,)), ((), ())), preferred_element_type=F32)


def tn(a, b):
    return lax.dot_general(a, b, (((0,), (0,)), ((), ())), preferred_element_type=F32)


def colsum(v):
    return jnp.sum(v, axis=0, keepdims=True)


def flatten(a_ref, flat, rows):
    for b in range(2):
        for t in range(a_ref.shape[1]):
            flat[b, t * rows : (t + 1) * rows, :] = a_ref[b, t, :rows, :].astype(F32)


def unroll(flat, s_ref, lo_chunk, hi_chunk):
    q = 80

    @pl.loop(lo_chunk, hi_chunk)
    def _(c):
        f = [[flat[b, pl.ds(c * 5 * q + j, q, stride=5), :] for j in range(5)] for b in range(2)]
        for i in range(4):
            row = []
            for b in range(2):
                lo = 32 * i
                first, second = f[b][i], f[b][i + 1]
                row += [first[:, lo:], second[:, : lo + 32]] if lo else [first, second[:, :32]]
            full = jnp.concatenate(row, axis=1)
            for k, (lo, hi) in enumerate(((0, 128), (128, 256), (256, 320))):
                s_ref[k, pl.ds(c * 4 * q + i, q, stride=4), : hi - lo] = full[:, lo:hi]


def get_rows(s_ref, start, count, step=1):
    ds = pl.ds(start, count) if step == 1 else pl.ds(start, count, stride=step)
    return jnp.concatenate([s_ref[0, ds, :], s_ref[1, ds, :], s_ref[2, ds, :64]], axis=1)


def put_taps(s_ref, start, w, back):
    for r in range(3):
        taps = [get_rows(s_ref, start + D * (3 * r + i), D).astype(BF) for i in range(3)]
        for i in range(3):
            w[r, D * i : D * (i + 1), :] = taps[i]
        back[r] = jnp.concatenate(taps[::-1], axis=1)


def unit_row(parts):
    out = [p[:, W * b : W * (b + 1)] for b in range(2) for p in parts]
    return jnp.broadcast_to(jnp.concatenate(out, axis=1), (8, 4 * D))


def unit_parts(row):
    return [
        jnp.concatenate([row[:, W * i : W * (i + 1)], row[:, 640 + W * i : 640 + W * (i + 1)]], axis=1)
        for i in range(4)
    ]


def take_front(s_ref, win, w1, w1b, vec):
    win[...] = get_rows(s_ref, 0, 36).astype(BF)
    put_taps(s_ref, 39, w1, w1b)
    for i, r in enumerate(VEC0):
        vec[i : i + 1, :] = get_rows(s_ref, r, 1)


def take_time(s_ref, tw2, tw3):
    for i in range(4):
        tw2[i] = get_rows(s_ref, U2 + i, 4 * D, 4).astype(BF)
    tw3[...] = get_rows(s_ref, U3, 4 * D).astype(BF)


def time_forward(s_ref, e, tw2, tw3, tv, p1, p2):
    u = e[...].astype(BF)
    p1[...] = unit_row(
        [nn(u, get_rows(s_ref, U1 + i, D, 4).astype(BF))[:1] + get_rows(s_ref, U1 + 4 * D + i, 1) for i in range(4)]
    )
    u = silu(p1[...]).astype(BF)
    p2[...] = unit_row([nn(u, tw2[i])[:1] + get_rows(s_ref, U2 + 16 * D + i, 1) for i in range(4)])
    u = silu(p2[...]).astype(BF)
    tv[...] = nn(u, tw3[...])[:1] + get_rows(s_ref, U3 + 4 * D, 1)


def unpack0_kernel(rows, a_ref, e, win, w1, w1b, vec, tw2, tw3, tv, p1, p2, flat, s_ref):
    flatten(a_ref, flat, rows)
    unroll(flat, s_ref, 0, R1 // 400)
    take_front(s_ref, win, w1, w1b, vec)
    take_time(s_ref, tw2, tw3)
    time_forward(s_ref, e, tw2, tw3, tv, p1, p2)


FE, FU1, FU2, FD1, FD2, FD3, FL = 0, 3, 13, 23, 28, 33, 35
FACTS = 40


def time_back(dtv, tw2, tw3, p1, p2, e, mask, loss, facts):
    g = jnp.broadcast_to(dtv[...], (8, D)).astype(BF)
    d2 = nt(g, tw3[...]) * silu_slope(p2[...])
    total = jnp.zeros((8, 4 * D), F32)
    for i, part in enumerate(unit_parts(d2)):
        total += nt(part.astype(BF), tw2[i])
    d1 = total * silu_slope(p1[...])
    put_facts(facts, e, p1, p2, d1, d2, dtv, mask, loss)


def put_facts(facts, e, p1, p2, d1, d2, dtv, mask, loss):
    first = lax.axis_index(CH) == 0
    facts[...] = jnp.zeros_like(facts)

    def put(at, v):
        for i in range(0, v.shape[1], 128):
            n = min(128, v.shape[1] - i)
            facts[at + i // 128 : at + i // 128 + 1, :n] = v[:1, i : i + n]

    put(FE, e[...].astype(BF).astype(F32))
    put(FU1, silu(p1[...]).astype(BF).astype(F32))
    put(FU2, silu(p2[...]).astype(BF).astype(F32))
    put(FD1, jnp.where(first, d1[:, : 2 * D], d1[:, 2 * D :]))
    put(FD2, jnp.where(first, d2[:, : 2 * D], d2[:, 2 * D :]))
    put(FD3, own(dtv[...]))
    facts[FL : FL + 1, 0:1] = loss[...]
    facts[FL : FL + 1, 1:2] = jnp.sum(mask[...].astype(F32), axis=1, keepdims=True)


def unpack1_kernel(rows, a_ref, c2, c2b, tr, mats, kv, vec, gib, wout, outb, flat, s_ref, o_ref):
    flatten(a_ref, flat, rows)
    unroll(flat, s_ref, 0, R1 // 400)
    put_taps(s_ref, C2, c2, c2b)
    tr[MPI] = get_rows(s_ref, PI, D).astype(BF)
    for m, r in ((MSO, SO), (MCQ, CQ), (MCO, CO), (MPO, PO)):
        mats[m] = get_rows(s_ref, r, D).astype(BF)
    for j in range(3):
        tr[MQ + j] = get_rows(s_ref, QKV + j, D, 3).astype(BF)
    for j in range(8):
        mats[MGV + j] = get_rows(s_ref, GI + j, D, 8).astype(BF)
    for j in range(4):
        for b in range(2):
            mats[MGO + j, b * W : (b + 1) * W, :] = get_rows(s_ref, GO + 640 * b + W * j, W).astype(BF)
    for j in range(2):
        kv[j] = get_rows(s_ref, CKV + j, CTX, 2).astype(BF)
    for i, r in enumerate(VEC1):
        vec[i : i + 1, :] = get_rows(s_ref, r, 1)
    gib[...] = get_rows(s_ref, GIB, 8)
    outb[...] = get_rows(s_ref, OUTB, 1)
    lane = lax.broadcasted_iota(jnp.int32, (W, W), 0)
    col = lax.broadcasted_iota(jnp.int32, (W, W), 1)
    pick = ((lane % 2) * 80 + lane // 2 == col).astype(BF)
    raw = get_rows(s_ref, OUT, 36).astype(BF)
    for b in range(2):
        moved = nn(raw[:, W * b : W * (b + 1)], pick)
        o_ref[0, :36, :] = moved[:, :128]
        o_ref[1, :36, :32] = moved[:, 128:]
        for ch in range(2):
            pieces = []
            for m in range(4):
                ds = pl.ds(m, 9, stride=4)
                both = jnp.concatenate([o_ref[0, ds, :], o_ref[1, ds, :32]], axis=1)
                pieces.append(both[:, 80 * ch : 80 * ch + 80])
            at = (2 * b + ch) * 9
            wout[at : at + 9, :] = jnp.concatenate(pieces, axis=1).astype(BF)


def pixel_col(n, axis):
    shape = (n, 1) if axis == 0 else (1, n)
    return lax.broadcasted_iota(jnp.int32, shape, axis)


def shift_lanes(v, tap):
    r, s = tap // 3 - 1, tap % 3 - 1
    pix = pixel_col(N, 1)
    i, j = pix // SIDE + r, pix % SIDE + s
    ok = (i >= 0) & (i < SIDE) & (j >= 0) & (j < SIDE)
    move = -(r * SIDE + s) % N
    moved = pltpu.roll(v, move, 1) if move else v
    return jnp.where(ok, moved, 0.0)


def put_shifts(ref, v):
    j = pixel_col(N, 0) % SIDE
    left = jnp.where(j == 0, 0.0, pltpu.roll(v, 1, 0)).astype(BF)
    right = jnp.where(j == SIDE - 1, 0.0, pltpu.roll(v, N - 1, 0)).astype(BF)
    ref[SIDE : SIDE + N, :] = jnp.concatenate([left, v.astype(BF), right], axis=1)


def clear_margins(ref):
    zero = jnp.zeros((SIDE, ref.shape[1]), BF)
    ref[:SIDE, :] = zero
    ref[SIDE + N :, :] = zero


def conv_rows(ref, w_ref):
    return sum(nn(ref[SIDE * r : SIDE * r + N, :], w_ref[r]) for r in range(3))


def conv_back_rows(ref, w_ref):
    return sum(nt(ref[SIDE * (2 - r) : SIDE * (2 - r) + N, :], w_ref[r]) for r in range(3))


def group_mean(sums):
    a = lax.broadcasted_iota(jnp.int32, (D, D), 0) // 10
    b = lax.broadcasted_iota(jnp.int32, (D, D), 1) // 10
    pool = jnp.where(a == b, 1.0, 0.0)
    wide = jnp.broadcast_to(sums, (8, D))
    out = jnp.dot(wide, pool, precision=HI, preferred_element_type=F32)
    return out[:1] * (1.0 / (10 * N))


def group_stats(v_ref, acc, sums):
    mean = group_mean(sums)
    acc[0:1, :] = colsum(jnp.square(v_ref[...] - mean))
    return mean, lax.rsqrt(group_mean(acc[0:1, :]) + EPS)


def silu(v):
    return v * jax.nn.sigmoid(v)


def silu_slope(v):
    sig = jax.nn.sigmoid(v)
    return sig * (1.0 + v * (1.0 - sig))


def layer(v):
    mean = jnp.sum(v, axis=1, keepdims=True) * (1.0 / D)
    sq = jnp.sum(v * v, axis=1, keepdims=True) * (1.0 / D)
    inv = lax.rsqrt(sq - mean * mean + EPS)
    return (v - mean) * inv, inv


def layer_back(grad, normed, inv, gain):
    ghat = grad * gain
    m1 = jnp.sum(ghat, axis=1, keepdims=True) * (1.0 / D)
    m2 = jnp.sum(ghat * normed, axis=1, keepdims=True) * (1.0 / D)
    return inv * (ghat - m1 - normed * m2)


def own(v):
    return jnp.where(lax.axis_index(CH) == 0, v[..., :W], v[..., W:])


def head(v, h):
    return v[:, HD * h : HD * (h + 1)]


def group_norm(src, acc, total, stats, at):
    mean, inv = group_stats(src, acc, total)
    stats[at : at + 1, :], stats[at + 1 : at + 2, :] = mean, inv
    return (src[...] - mean) * inv


def start_steps(noisy, tv, win, w1, vec0, h0, h1, a1, stats, sh, acc):
    def first():
        cols = jnp.concatenate([shift_lanes(noisy[...], t) for t in range(9)], axis=0).astype(BF)
        clear_margins(sh)
        stats[...] = jnp.zeros_like(stats)
        h = tn(cols, win[...]) + vec0[0:1, :]
        h0[...] = h
        y = silu(group_norm(h0, acc, colsum(h), stats, 0) * vec0[1:2, :] + vec0[2:3, :])
        put_shifts(sh, y)
        a1[...] = y.astype(BF)

    def taps(r):
        def one():
            part = nn(sh[SIDE * r : SIDE * r + N, :], w1[r])
            if r == 2:
                part += tv[...]
            h1[...] = (h1[...] if r else vec0[3:4, :]) + part

        return one

    return [first, taps(0), taps(1), taps(2)]


def start_kernel(noisy, tv, win, w1, vec0, h0, h1, a1, stats, sh, acc):
    for step in start_steps(noisy, tv, win, w1, vec0, h0, h1, a1, stats, sh, acc):
        step()


def front_kernel(flow, h0, h1, stats_in, c2, tr, vec1, h2, z0, a2, ntr, x1, q, k, v, stats, sh, acc):
    clear_margins(sh)
    stats[...] = stats_in[...]
    y = silu(group_norm(h1, acc, colsum(h1[...]), stats, 2) * vec1[N2G : N2G + 1, :] + vec1[N2B : N2B + 1, :])
    put_shifts(sh, y)
    a2[...] = y.astype(BF)
    flow.ready(2)
    flow.need(0, 3)
    h = h0[...] + conv_rows(sh, c2) + vec1[C2B : C2B + 1, :]
    h2[...] = h
    flow.ready(0)
    n = group_norm(h2, acc, colsum(h), stats, 4)
    n = (n * vec1[NTG : NTG + 1, :] + vec1[NTB : NTB + 1, :]).astype(BF)
    ntr[...] = n
    flow.ready(3)
    flow.need(4)
    z = nn(n, tr[MPI]) + vec1[PIB : PIB + 1, :]
    z0[...] = z
    flow.ready(1)
    normed, _ = layer(z)
    x = (normed * vec1[L1G : L1G + 1, :] + vec1[L1B : L1B + 1, :]).astype(BF)
    x1[...] = x
    flow.ready(4)
    for i, (at, dst) in enumerate(((MQ, q), (MK, k), (MV, v))):
        y = nn(x, tr[at]).astype(BF)
        for hd in range(HEADS):
            dst[hd] = head(y, hd)
        flow.ready(5 + i)


AT = 512


def attend_kernel(q, k, v, o, lse, ot):
    steps = [(h, pl.ds(t * AT, AT)) for h in range(HEADS) for t in range(N // AT)]

    def scores(h, rows):
        return nt(k[h], q[h, rows, :])

    now = scores(*steps[0])
    for i, (h, rows) in enumerate(steps):
        later = scores(*steps[i + 1]) if i + 1 < len(steps) else None
        if i % (N // AT) == 0:
            vt = v[h].astype(F32).T.astype(BF)
        s = now * (SCALE * LOG2E)
        top = jnp.max(s, axis=0, keepdims=True)
        e = jnp.exp2(s - top)
        total = jnp.sum(e, axis=0, keepdims=True)
        lse[h, :, rows] = top + jnp.log(total) * LOG2E
        ot[h * HD : (h + 1) * HD, rows] = nn(vt, (e * (1.0 / total)).astype(BF))
        now = later
    o[...] = ot[...].T.astype(BF)


KEYS = 128


def by_head(v):
    wide = jnp.concatenate([v, jnp.zeros((KEYS - TXT, D), v.dtype)], axis=0)
    col = lax.broadcasted_iota(jnp.int32, (KEYS, D), 1) // HD
    return jnp.concatenate([jnp.where(col == h, wide, 0.0) for h in range(HEADS)], axis=0)


def from_heads(vt):
    row = lax.broadcasted_iota(jnp.int32, (D, KEYS), 0) // HD
    total = jnp.zeros((D, KEYS), F32)
    for h in range(HEADS):
        total += jnp.where(row == h, vt[:, KEYS * h : KEYS * (h + 1)], 0.0)
    return total.T[:TXT]


def transposed(v):
    return v.T


def middle_kernel(
    flow, o, z0, h2, ctx, noise, mask, mats, kvw, vec, gib, wout, outb,
    dz1, dh3, dos, loss, gd, ggi, ggo, gkv, dvec, dgib, dwout, dbout,
    z1, z2, h3, x2, x3, oc, z3b, gl, by_a, by_g, a3, qc, kb, vb, prob, dsc, acc, pt, oct_, x2t, ot, x3t,
):
    def row(i):
        return vec[i : i + 1, :]

    def put(i, v):
        dvec[i : i + 1, :] = v

    flow.need(7)
    kb[...] = by_head(nn(ctx[...], kvw[0])).astype(BF)
    vb[...] = by_head(nn(ctx[...], kvw[1])).astype(BF)
    flow.need(6, 1)
    z = z0[...] + nn(o[...], mats[MSO]) + row(SOB)
    z1[...] = z
    normed, _ = layer(z)
    x = (normed * row(L2G) + row(L2B)).astype(BF)
    x2[...] = x
    qq = nn(x, mats[MCQ]).astype(BF)
    qc[...] = qq
    s = nt(qq, kb[...]) * (SCALE * LOG2E)
    there = lax.broadcasted_iota(jnp.int32, (1, KEYS), 1) < TXT
    for h in range(HEADS):
        at = slice(KEYS * h, KEYS * (h + 1))
        sh = jnp.where(there, s[:, at], -jnp.inf)
        e = jnp.exp2(sh - jnp.max(sh, axis=1, keepdims=True))
        prob[:, at] = e * (1.0 / jnp.sum(e, axis=1, keepdims=True))
    c = nn(prob[...].astype(BF), vb[...]).astype(BF)
    oc[...] = c
    z = z1[...] + nn(c, mats[MCO]) + row(COB)
    z2[...] = z
    normed, _ = layer(z)
    x = (normed * row(L3G) + row(L3B)).astype(BF)
    x3[...] = x
    moving = ((oc, oct_), (x2, x2t), (o, ot), (x3, x3t))
    for j in range(4):
        moving[j][1][...] = transposed(moving[j][0][...])
        a = nn(x, mats[MGV + j]) + gib[j : j + 1, :]
        g = nn(x, mats[MGG + j]) + gib[4 + j : 5 + j, :]
        cdf = 0.5 * (1.0 + lax.erf(g * math.sqrt(0.5)))
        gelu = g * cdf
        by_a[j] = gelu
        by_g[j] = a * (cdf + g * jnp.exp(-0.5 * g * g) * (1.0 / math.sqrt(2.0 * math.pi)))
        y = (a * gelu).astype(BF)
        gl[j] = y
        z = z + nn(y, mats[MGO + j])
    zb = (z + row(GOB)).astype(BF)
    z3b[...] = zb
    flow.need(2)
    h = h2[...] + nn(zb, mats[MPO]) + row(POB)
    h3[...] = h
    mean, inv = group_stats(h3, acc, colsum(h))
    gain, bias = row(NOG), row(NOB)
    a3[...] = silu((h3[...] - mean) * inv * gain + bias).astype(BF)
    taps = nt(wout[...], a3[...])
    for ch in range(LAT):
        pred = jnp.zeros((1, N), F32)
        for t in range(9):
            pred += shift_lanes(taps[9 * ch + t : 9 * ch + t + 1, :], t)
        at = W * (ch // 2) + ch % 2
        err = pred + outb[0:1, at : at + 1] - noise[ch : ch + 1, :]
        weighed = mask[...].astype(F32) * err
        g = 2.0 * weighed
        acc[2 + ch : 3 + ch, 0:1] = jnp.sum(weighed * err, axis=1, keepdims=True)
        dbout[ch : ch + 1, :] = jnp.broadcast_to(jnp.sum(g, axis=1, keepdims=True), (1, 128))
        for t in range(9):
            pt[9 * ch + t : 9 * ch + t + 1, :] = shift_lanes(g, 8 - t)
    loss[...] = acc[2:3, 0:1] + acc[3:4, 0:1] + acc[4:5, 0:1] + acc[5:6, 0:1]

    dvec[...] = jnp.zeros_like(dvec)
    taps = pt[...].astype(BF)
    dwout[...] = nn(taps, a3[...])
    n = (h3[...] - mean) * inv
    g = tn(taps, wout[...]) * silu_slope(n * gain + bias)
    dgain, dbias = colsum(g * n), colsum(g)
    put(NOG, dgain)
    put(NOB, dbias)
    g = inv * (g * gain - group_mean(gain * dbias) - n * group_mean(gain * dgain))
    dh3[...] = g
    flow.ready(1)
    put(POB, colsum(g))
    gd[0] = nn(transposed(z3b[...]), own(g).astype(BF)).astype(BF)
    dz3 = nt(g.astype(BF), mats[MPO])
    z1b = dz3.astype(BF)
    put(GOB, colsum(dz3))
    mine_t = transposed(own(dz3).astype(BF))
    xt = x3t[...]
    dx = jnp.zeros((N, D), F32)
    for j in range(4):
        dgl = nt(z1b, mats[MGO + j])
        ggo[j] = nn(mine_t, gl[j]).T.astype(BF)
        da = dgl * by_a[j]
        dg = dgl * by_g[j]
        dgib[j : j + 1, :] = colsum(da)
        dgib[4 + j : 5 + j, :] = colsum(dg)
        ggi[j] = nn(xt, own(da).astype(BF)).astype(BF)
        ggi[4 + j] = nn(xt, own(dg).astype(BF)).astype(BF)
        dx += nt(da.astype(BF), mats[MGV + j]) + nt(dg.astype(BF), mats[MGG + j])
    flow.ready(5, 6)
    normed, li = layer(z2[...])
    put(L3G, colsum(dx * normed))
    put(L3B, colsum(dx))
    dz = dz3 + layer_back(dx, normed, li, row(L3G))
    z2[...] = dz
    put(COB, colsum(dz))
    gd[1] = nn(oct_[...], own(dz).astype(BF)).astype(BF)
    do = nt(dz.astype(BF), mats[MCO]).astype(BF)
    dp = nt(do, vb[...])
    dot = transposed(do)
    qt = transposed(qc[...])
    gkv[1] = tn(ctx[...], own(from_heads(nn(dot, prob[...].astype(BF)))).astype(BF)).astype(BF)
    for h in range(HEADS):
        at = slice(KEYS * h, KEYS * (h + 1))
        p, d = prob[:, at], dp[:, at]
        dsc[:, at] = (p * (d - jnp.sum(p * d, axis=1, keepdims=True)) * SCALE).astype(BF)
    gkv[0] = tn(ctx[...], own(from_heads(nn(qt, dsc[...]))).astype(BF)).astype(BF)
    flow.ready(7)
    dq = nn(dsc[...], kb[...])
    gd[2] = nn(x2t[...], own(dq).astype(BF)).astype(BF)
    dx = nt(dq.astype(BF), mats[MCQ])
    normed, li = layer(z1[...])
    put(L2G, colsum(dx * normed))
    put(L2B, colsum(dx))
    dz = z2[...] + layer_back(dx, normed, li, row(L2G))
    dz1[...] = dz
    flow.ready(0)
    put(SOB, colsum(dz))
    gd[3] = nn(ot[...], own(dz).astype(BF)).astype(BF)
    do = nt(dz.astype(BF), mats[MSO]).astype(BF)
    for h in range(HEADS):
        dos[h] = head(do, h)


ABT = 256


def attend_back_kernel(q, k, v, do, lse, dq, dk, dv, qt, kacc, vacc):
    steps = [(h, pl.ds(t * ABT, ABT)) for h in range(HEADS) for t in range(N // ABT)]

    def scores(h, rows):
        return nt(k[h], q[h, rows, :]), nt(v[h], do[h, rows, :])

    now = scores(*steps[0])
    for i, (h, rows) in enumerate(steps):
        later = scores(*steps[i + 1]) if i + 1 < len(steps) else None
        s, dp = now
        p = jnp.exp2(s * (SCALE * LOG2E) - lse[h, :, rows])
        ds = (p * (dp - jnp.sum(p * dp, axis=0, keepdims=True)) * SCALE).astype(BF)
        dkt, dvt = nn(ds, q[h, rows, :]), nn(p.astype(BF), do[h, rows, :])
        if i % (N // ABT) == 0:
            kt = k[h].astype(F32).T.astype(BF)
            kacc[h], vacc[h] = dkt, dvt
        else:
            kacc[h] += dkt
            vacc[h] += dvt
        qt[h * HD : (h + 1) * HD, rows] = nn(kt, ds)
        now = later

    dq[...] = qt[...].T.astype(BF)

    def one(rows):
        for acc, dst in ((kacc, dk), (vacc, dv)):
            dst[rows, :] = jnp.concatenate([acc[h, rows, :] for h in range(HEADS)], axis=1).astype(BF)

    tiles(one)


def put_rows(s_ref, start, v, step=1):
    n = v.shape[0]
    ds = pl.ds(start, n) if step == 1 else pl.ds(start, n, stride=step)
    s_ref[0, ds, :] = v[:, :128]
    s_ref[1, ds, :32] = v[:, 128:]


def roll_rows(s_ref, out_ref, lo_chunk, hi_chunk):
    q = 80

    @pl.loop(lo_chunk, hi_chunk)
    def _(c):
        g = []
        for i in range(4):
            ds = pl.ds(c * 4 * q + i, q, stride=4)
            g.append((s_ref[0, ds, :], s_ref[1, ds, :32]))
        base = (c - lo_chunk) * 5 * q
        out_ref[pl.ds(base, q, stride=5), :] = g[0][0]
        for i in range(3):
            lo = 96 - 32 * i
            out_ref[pl.ds(base + i + 1, q, stride=5), :] = jnp.concatenate(
                ([g[i][0][:, 128 - 32 * i :]] if i else []) + [g[i][1], g[i + 1][0][:, :lo]], axis=1
            )
        out_ref[pl.ds(base + 4, q, stride=5), :] = jnp.concatenate([g[3][0][:, 32:], g[3][1]], axis=1)


def by_owner(s_ref, flat, out, total):
    owners, room = math.prod(out.shape[:-2]), out.shape[-2]
    size = room if total < owners * room and len(out.shape) == 3 else min(room, ROWS)
    half = owners // 2 * size
    for lo, hi, first in ((0, min(-(-half // 400), total // 400), 0), (half // 400, total // 400, owners // 2)):
        if hi > lo:
            roll_rows(s_ref, flat, lo, hi)
        at = 400 * max(hi - lo, 0)
        if at < flat.shape[0]:
            flat[at:, :] = jnp.zeros((flat.shape[0] - at, 128), F32)
        for t in range(first, first + owners // 2):
            spot = (t % 2, t // 2) if len(out.shape) == 4 else (t,)
            row = t * size - 400 * lo
            out[(*spot, slice(0, size))] = flat[row : row + size, :].astype(BF)
            if room > size:
                out[(*spot, slice(size, room))] = jnp.zeros((room - size, 128), BF)


def conv_grads(a_ref, g_ref, s_ref, start):
    at = transposed(a_ref[...])
    for r in range(3):
        rows = SIDE * (2 - r)
        three = nn(at, g_ref[rows : rows + N, :])
        for i in range(3):
            put_rows(s_ref, start + D * (3 * r + i), three[:, W * (2 - i) : W * (3 - i)])


def back_kernel(
    flow, dq, dk, dv, dz1, dh3, z0, h2, h1, h0, stats, w1, c2, tr, vec0, vec1, a1, a2, ntr, x1, noisy,
    gd, ggi, ggo, gkv, dvec_in, dgib, dwout, dbout,
    out1, out0, dtv,
    dh, g_ref, go_ref, dvec, s_ref, flat, o_ref,
):
    c = lax.axis_index(CH)
    clear_margins(g_ref)
    clear_margins(go_ref)
    dvec[...] = dvec_in[...]

    def row(i):
        return vec1[i : i + 1, :]

    def put(i, v):
        dvec[i : i + 1, :] = v

    dx = nt(dq[...], tr[MQ]) + nt(dk[...], tr[MK]) + nt(dv[...], tr[MV])
    xt = transposed(x1[...])
    for j, g in enumerate((dq, dk, dv)):
        put_rows(s_ref, QKV + j, nn(xt, own(g[...].astype(F32)).astype(BF)), 3)
    flow.need(5, 3)
    normed, li = layer(z0[...])
    put(L1G, colsum(dx * normed))
    put(L1B, colsum(dx))
    dz = dz1[...] + layer_back(dx, normed, li, row(L1G))
    put(PIB, colsum(dz))
    flow.need(17)
    put_rows(s_ref, PI, tn(ntr[...], own(dz).astype(BF)))
    g = nt(dz.astype(BF), tr[MPI])

    def norm_back(g, n, at, gain):
        dgain, dbias = colsum(g * n), colsum(g)
        back = stats[at + 1 : at + 2, :] * (g * gain - group_mean(gain * dbias) - n * group_mean(gain * dgain))
        return back, dgain, dbias

    def normed_of(src, at):
        return (src[...] - stats[at : at + 1, :]) * stats[at + 1 : at + 2, :]

    flow.need(6, 4)
    g, dgain, dbias = norm_back(g, normed_of(h2, 4), 4, row(NTG))
    put(NTG, dgain)
    put(NTB, dbias)
    g = dh3[...] + g
    dh[...] = g
    put(C2B, colsum(g))
    put_shifts(g_ref, g)
    put_shifts(go_ref, own(g))
    flow.need(16)
    conv_grads(a2, go_ref, s_ref, C2)
    flow.need(7, 11)
    n = normed_of(h1, 2)
    g = conv_back_rows(g_ref, c2) * silu_slope(n * row(N2G) + row(N2B))
    g, dgain, dbias = norm_back(g, n, 2, row(N2G))
    put(N2G, dgain)
    put(N2B, dbias)
    total = colsum(g)
    dtv[...] = total
    put_shifts(g_ref, g)
    put_shifts(go_ref, own(g))

    flow.need(20, 21, 22, 23)
    for i, r in enumerate((PO, CO, CQ, SO)):
        put_rows(s_ref, r, gd[i].astype(F32))
    for j in range(8):
        put_rows(s_ref, GI + j, ggi[j].astype(F32), 8)
    for j in range(4):
        rows = ggo[j].astype(F32)
        for b in range(2):
            put_rows(s_ref, GO + 640 * b + W * j, rows[W * b : W * (b + 1), :])
    for j in range(2):
        put_rows(s_ref, CKV + j, gkv[j].astype(F32), 2)
    for i, r in enumerate(VEC1):
        put_rows(s_ref, r, own(dvec[i : i + 1, :]))
    put_rows(s_ref, GIB, own(dgib[...]))
    wide = jnp.where(c == 0, dwout[:18, :], dwout[18:36, :])
    for ch in range(2):
        for m in range(4):
            o_ref[ch, pl.ds(m, 9, stride=4), :80] = wide[9 * ch : 9 * ch + 9, 80 * m : 80 * m + 80]
    lane = lax.broadcasted_iota(jnp.int32, (80, W), 0)
    col = lax.broadcasted_iota(jnp.int32, (80, W), 1)
    moved = jnp.zeros((36, W), F32)
    for ch in range(2):
        spot = jnp.where(2 * lane + ch == col, 1.0, 0.0)
        moved += jnp.dot(o_ref[ch, :36, :80], spot, precision=HI, preferred_element_type=F32)
    put_rows(s_ref, OUT, moved)
    b0 = jnp.where(c == 0, dbout[0:1, 0:1], dbout[2:3, 0:1])
    b1 = jnp.where(c == 0, dbout[1:2, 0:1], dbout[3:4, 0:1])
    at = lax.broadcasted_iota(jnp.int32, (1, W), 1)
    put_rows(s_ref, OUTB, jnp.where(at == 0, b0, jnp.where(at == 1, b1, 0.0)))
    s_ref[:, OUTB + 1 :, :] = jnp.zeros((2, 4 * R1 // 5 - OUTB - 1, 128), F32)
    by_owner(s_ref, flat, out1, R1)
    flow.ready(0)

    flow.need(15, 8, 10)
    conv_grads(a1, go_ref, s_ref, 39)
    n = normed_of(h0, 0)
    g = conv_back_rows(g_ref, w1) * silu_slope(n * vec0[1:2, :] + vec0[2:3, :])
    g, dgain, dbias = norm_back(g, n, 0, vec0[1:2, :])
    g = dh[...] + g
    cols = jnp.concatenate([shift_lanes(noisy[...], t) for t in range(9)], axis=0).astype(BF)
    put_rows(s_ref, 0, nn(cols, own(g).astype(BF)))
    for r, v in zip(VEC0, (colsum(g), dgain, dbias, total)):
        put_rows(s_ref, r, own(v))
    s_ref[:, 4 * FRONT // 5 : 4 * R0 // 5, :] = jnp.zeros((2, 4 * (R0 - FRONT) // 5, 128), F32)
    by_owner(s_ref, flat, out0, R0)


FIRST = (0, 0, 1, 2, 3)
SECOND = (0, 1, 2, 3, 3)


def time_rows(facts, count):
    row = lax.axis_index(DP) * count + lax.broadcasted_iota(jnp.int32, (count, 1), 0)

    def wide(at, n):
        return jnp.concatenate([facts[:, at + i, :] for i in range(n)], axis=1)

    def meets(u, k):
        spot = jnp.where(k == lax.broadcasted_iota(jnp.int32, (1, u.shape[1]), 1), 1.0, 0.0).astype(BF)
        return nt(spot, u.astype(BF))

    total = jnp.zeros((count, 128), F32)
    for u, at, start, size in ((wide(FE, 3)[:, :D], FD1, T1, D), (wide(FU1, 10), FD2, T2, 4 * D)):
        rel = row - start
        k, line = rel // 5, rel % 5
        met = meets(u, jnp.where(rel < 0, -1, k))
        for j in range(5):
            g = facts[:, at + j, :]
            total += nn(jnp.where(line == j, met, 0.0).astype(BF), g.astype(BF))
            total += jnp.where((rel >= 0) & (k == size) & (line == j), colsum(g), 0.0)
    rel = row - T3
    group, line = rel // 5, rel % 5
    d3 = wide(FD3, 2)[:, :W]
    zero = jnp.zeros((d3.shape[0], 128), F32)
    u = wide(FU2, 10)
    for picks, shift in ((FIRST, 0), (SECOND, 1)):
        k = jnp.full_like(rel, -1)
        for j in range(5):
            k = jnp.where((rel >= 0) & (line == j), 4 * group + picks[j], k)
        met = meets(u, k)
        for j in range(5):
            if shift == 0:
                lo = (0, 128, 96, 64, 32)[j]
                g = d3[:, lo : min(lo + 128, W)]
                g = jnp.concatenate([g, zero[:, : 128 - g.shape[1]]], axis=1) if g.shape[1] < 128 else g
            else:
                if j in (0, 4):
                    continue
                g = jnp.concatenate([zero[:, : 32 * j], d3[:, : 128 - 32 * j]], axis=1)
            total += nn(jnp.where(line == j, met, 0.0).astype(BF), g.astype(BF))
            total += jnp.where((k == 4 * D) & (line == j), colsum(g), 0.0)
    return total


def update_kernel(with_time, params, momentum, ema, sum1, sum0, facts, new_params, new_momentum, new_ema, loss, pixels):
    total = facts[0, FL : FL + 1, :]
    for i in range(1, facts.shape[0]):
        total += facts[i, FL : FL + 1, :]
    loss[...] = total[:, 0:1]
    pixels[...] = total[:, 1:2]
    scale = 1.0 / (LAT * jnp.maximum(total[:, 1:2], 1.0))
    first = sum0[...]
    if with_time:
        first += time_rows(facts, sum0.shape[0])
    for p, g in enumerate((first, sum1[...])):
        g = g * scale
        m = MU * momentum[p] + g
        new_momentum[p] = m
        w = params[p] - LR * (g + MU * m)
        new_params[p] = w
        new_ema[p] = ED * ema[p] + (1.0 - ED) * w


ROWS = 856
SLAB = 864
SOME = 240
REST = SLAB - 3 * SOME


def send(src, dst, sems, i, j, target):
    copy = pltpu.make_async_remote_copy(
        src_ref=src, dst_ref=dst, send_sem=sems[0].at[i], recv_sem=sems[1].at[j],
        device_id={DP: target}, device_id_type=pl.DeviceIdType.MESH,
    )
    copy.start()
    return copy


PIECES = tuple(slice(16 * a, 16 * b) for a, b in ((0, 7), (7, 14), (14, 21), (21, 28), (28, 35), (35, 42), (42, 48), (48, 54)))


def gather_kernel(
    params, step, latents, noise, g0, g1, e, noisy, vec, p1, p2, stats, w1b_out, tw2_out, tw3_out, h0_out, h1_out, a1_out,
    low, slabs, flat, s_ref, w1b, tw2, tw3, h0, h1, a1, w1, win, tv, half1, half2, half3, sh, acc,
    send_sem, recv_sem, keep_sem, slab_sem, out_sem, swap_sem,
):
    low[:, :ROWS, :] = params[...].astype(BF)
    low[:, ROWS:, :] = jnp.zeros((2, SLAB - ROWS, 128), BF)
    me, y = lax.axis_index(DP), lax.axis_index(CH)
    k, x, z = me % 2, (me // 2) % 2, me // 4
    core = {DP: me + 1 - 2 * k}
    side = {DP: me + 2 - 4 * x}
    other = {CH: 1 - y}
    ring = [{DP: (me + 4 * o) % 16} for o in range(4)]
    barrier = pltpu.get_barrier_semaphore()
    for target in [core, side, other] + ring[1:]:
        pl.semaphore_signal(barrier, inc=1, device_id=target, device_id_type=pl.DeviceIdType.MESH)
    pl.semaphore_wait(barrier, 6)
    count = [0]
    started = []

    def push(ref, target):
        i = count[0]
        count[0] += 1
        return [start(ref, ref, i, i, target)]

    def start(src, dst, i, j, target):
        copy = pltpu.make_async_remote_copy(
            src_ref=src, dst_ref=dst, send_sem=send_sem.at[i], recv_sem=recv_sem.at[j],
            device_id=target, device_id_type=pl.DeviceIdType.MESH,
        )
        copy.start()
        started.append(copy)
        return copy

    def push_ring(ref):
        i = count[0]
        count[0] += 3
        return [start(ref, ref, i + o - 1, i + 3 - o, ring[o]) for o in (2, 1, 3)]

    def arrive(copies):
        for copy in copies:
            copy.wait_recv()

    keeps = []
    for p, g in enumerate((g0, g1)):
        keep = pltpu.make_async_copy(low.at[p], g.at[y, z, x, k], keep_sem.at[p])
        keep.start()
        keeps.append(keep)
    work = [(p, g, rows, p * (i % 2)) for p, g in enumerate((g0, g1)) for i, rows in enumerate(PIECES)]
    first, second, third, last = {}, {}, {}, ([], [])

    def begin(i):
        p, g, rows, _ = work[i]
        if i % len(PIECES) == 0:
            keeps[p].wait()
        first[i] = push_ring(g.at[y, z, x, k, rows])

    def middle(i):
        p, g, rows, turn = work[i]
        arrive(first[i])
        second[i] = push(g.at[y, :, x, k, rows], other if turn else side)
        last[p].extend(push(g.at[y, :, x, k, rows], core))

    def finish(i):
        p, g, rows, turn = work[i]
        zs = slice(0, 4 if p else 2)
        arrive(second[i])
        if turn:
            third[i] = push(g.at[:, :, x, k, rows], side)
            last[p].extend(push(g.at[1 - y, :, x, k, rows], core))
        else:
            third[i] = push(g.at[y, zs, :, k, rows], other)
            last[p].extend(push(g.at[y, :, 1 - x, k, rows], core))

    def pass_on(i):
        p, g, rows, turn = work[i]
        zs = slice(0, 4 if p else 2)
        arrive(third[i])
        last[p].extend(push(g.at[:, :, 1 - x, k, rows] if turn else g.at[1 - y, zs, :, k, rows], core))

    outs = [
        pltpu.make_async_copy(src, dst, out_sem.at[i])
        for i, (src, dst) in enumerate(
            ((w1b, w1b_out), (tw2, tw2_out), (tw3, tw3_out), (h0, h0_out), (h1, h1_out), (a1, a1_out))
        )
    ]
    fetches = [
        pltpu.make_async_copy(g0.at[a, b], slabs.at[a, b], slab_sem.at[i])
        for i, (a, b) in enumerate([(y, b) for b in range(4)] + [(1 - y, b) for b in range(2)])
    ]
    slabs[1 - y, 2:4] = jnp.zeros((2,) + slabs.shape[2:], BF)

    def fetch():
        arrive(last[0])
        for copy in fetches:
            copy.start()

    def flat_half(a):
        if a == 0:
            for copy in fetches:
                copy.wait()
        for t in range(16):
            flat[a, t * ROWS : (t + 1) * ROWS, :] = slabs[a, t // 4, t // 2 % 2, t % 2, :ROWS, :].astype(F32)

    def front():
        take_front(s_ref, win, w1, w1b, vec)
        outs[0].start()

    def times():
        for i in range(4):
            tw2[i] = own(get_rows(s_ref, U2 + i, 4 * D, 4)).astype(BF)
        tw3[...] = own(get_rows(s_ref, U3, 4 * D)).astype(BF)
        outs[1].start()
        outs[2].start()

    def swap(i, ref):
        return pltpu.make_async_remote_copy(
            src_ref=ref.at[y], dst_ref=ref.at[y], send_sem=swap_sem.at[i], recv_sem=swap_sem.at[3 + i],
            device_id=other, device_id_type=pl.DeviceIdType.MESH,
        )

    def units(u, w, start, size):
        parts = [nn(u, w(i)) + own(get_rows(s_ref, start + 4 * size + i, 1)) for i in range(4)]
        return jnp.concatenate(parts, axis=1)

    swaps = [swap(0, half1), swap(1, half2), swap(2, half3)]

    def time_one():
        u = e[...].astype(BF)
        half1[y] = units(u, lambda i: own(get_rows(s_ref, U1 + i, D, 4)).astype(BF), U1, D)
        swaps[0].start()

    def time_two():
        swaps[0].wait_recv()
        p1[...] = jnp.concatenate([half1[0], half1[1]], axis=1)
        half2[y] = units(silu(p1[...]).astype(BF), lambda i: tw2[i], U2, 4 * D)
        swaps[1].start()

    def time_three():
        swaps[1].wait_recv()
        p2[...] = jnp.concatenate([half2[0], half2[1]], axis=1)
        half3[y] = nn(silu(p2[...]).astype(BF), tw3[...]) + own(get_rows(s_ref, U3 + 4 * D, 1))
        swaps[2].start()

    def time_last():
        swaps[2].wait_recv()
        tv[...] = jnp.concatenate([half3[0], half3[1]], axis=1)[:1]

    def both(*steps):
        def one():
            for step in steps:
                step()

        return one

    opening, *rows_of_taps = start_steps(noisy, tv, win, w1, vec, h0, h1, a1, stats, sh, acc)
    todo = [
        fetch,
        lambda: flat_half(0),
        lambda: flat_half(1),
        lambda: unroll(flat, s_ref, 0, 9),
        lambda: unroll(flat, s_ref, 9, 18),
        lambda: unroll(flat, s_ref, 18, 27),
        lambda: unroll(flat, s_ref, 27, R1 // 400),
        time_one,
        both(front, times),
        time_two,
        opening,
        both(outs[3].start, outs[5].start, rows_of_taps[0]),
        time_three,
        rows_of_taps[1],
        time_last,
        both(rows_of_taps[2], outs[4].start),
    ]
    ahead = 4
    for i in range(ahead):
        begin(i)
    e[...] = jnp.broadcast_to(time_features(step[...]), (8, D))
    add_noise(step[...], latents, noise, noisy)
    for i in range(len(work) + 2):
        if i < len(work):
            middle(i)
            if i + ahead < len(work):
                begin(i + ahead)
        if i - 3 >= len(PIECES) and todo:
            todo.pop(0)()
        if 0 <= i - 1 < len(work):
            finish(i - 1)
        if 0 <= i - 3 < len(work):
            pass_on(i - 3)
        if i - 3 >= len(PIECES) - 1 and todo:
            todo.pop(0)()
    pass_on(len(work) - 1)
    for step in todo:
        step()
    for copy in outs:
        copy.wait()
    for copy in swaps:
        copy.wait_send()
    arrive(last[1])
    for copy in started:
        copy.wait_send()


def gather_weights(*operands):
    hbm, vm = pl.BlockSpec(memory_space=pl.ANY), pl.BlockSpec(memory_space=pltpu.VMEM)
    gathered = sds((2, 4, 2, 2, SLAB, 128), BF)
    large = (sds((3, D, 3 * D), BF), sds((4, 4 * D, W), BF), sds((4 * D, W), BF))
    large += (sds((N, D)), sds((N, D)), sds((N, D), BF))
    small = (sds((8, D)), sds((LAT, N)), sds((8, D)), sds((8, 4 * D)), sds((8, 4 * D)), sds((8, D)))
    dma = pltpu.SemaphoreType.DMA
    return pl.pallas_call(
        gather_kernel,
        out_shape=(gathered, gathered) + small + large,
        in_specs=[vm] * 4,
        out_specs=(hbm, hbm) + (vm,) * len(small) + (hbm,) * len(large),
        scratch_shapes=[
            pltpu.VMEM((2, SLAB, 128), BF),
            pltpu.VMEM(gathered.shape, BF),
            pltpu.VMEM((2, 16 * ROWS, 128), F32),
            pltpu.VMEM((3, 4 * R1 // 5, 128), F32),
            *(pltpu.VMEM(v.shape, v.dtype) for v in large),
            pltpu.VMEM((3, 3 * D, D), BF),
            pltpu.VMEM((36, D), BF),
            pltpu.VMEM((1, D), F32),
            pltpu.VMEM((2, 8, 2 * D), F32),
            pltpu.VMEM((2, 8, 2 * D), F32),
            pltpu.VMEM((2, 8, W), F32),
            pltpu.VMEM((N + 2 * SIDE, 3 * D), BF),
            pltpu.VMEM((8, D), F32),
            dma((128,)),
            dma((128,)),
            dma((2,)),
            dma((6,)),
            dma((6,)),
            dma((6,)),
        ],
        compiler_params=pltpu.CompilerParams(collective_id=2, has_side_effects=True, vmem_limit_bytes=63 * 2**20),
    )(*operands)


def add_up(*terms):
    total = terms[0].astype(F32)
    for term in terms[1:]:
        total += term.astype(F32)
    return total


def reduce_kernel(
    p1, p0, dtv, tw2_in, tw3_in, p1t, p2t, e, mask, loss, sum1, sum0, all_facts,
    kp1, kp0, tw2, tw3, facts, r1, sa, rx, ta, rz, r1b, sb, rbz, tb, rbx, some, land, fx, timed, send_sem, recv_sem, fsend, frecv, gsend, grecv, lsem, half, ssem,
):
    me = lax.axis_index(DP)
    k, x, z = me % 2, (me // 2) % 2, me // 4
    kept = [
        pltpu.make_async_copy(src, dst, lsem.at[i])
        for i, (src, dst) in enumerate(((p1.at[k], kp1), (p0.at[k], kp0), (tw2_in, tw2), (tw3_in, tw3)))
    ]
    for copy in kept:
        copy.start()
    barrier = pltpu.get_barrier_semaphore()
    for o in range(1, 16):
        pl.semaphore_signal(barrier, inc=1, device_id={DP: (me + o) % 16}, device_id_type=pl.DeviceIdType.MESH)
    y = lax.axis_index(CH)
    pl.semaphore_signal(barrier, inc=1, device_id={CH: 1 - y}, device_id_type=pl.DeviceIdType.MESH)
    pl.semaphore_wait(barrier, 16)
    sems = (send_sem, recv_sem)

    def swap(i):
        copy = pltpu.make_async_remote_copy(
            src_ref=half.at[i, y], dst_ref=half.at[i, y], send_sem=ssem.at[i], recv_sem=ssem.at[2 + i],
            device_id={CH: 1 - y}, device_id_type=pl.DeviceIdType.MESH,
        )
        copy.start()
        return copy

    core = me + 1 - 2 * k
    side = me + 2 - 4 * x
    chunks = [p0] + [p1.at[:, :, SOME * i : SOME * (i + 1)] for i in range(3)]
    mine = [kp0] + [kp1.at[:, SOME * i : SOME * (i + 1)] for i in range(3)]
    rest = p1.at[:, :, 3 * SOME :]

    def over_z(src, dst, base):
        return [
            send(src.at[(z + o) % 4], dst.at[3 - o], sems, base + o - 1, base + 3 - o, (me + 4 * o) % 16)
            for o in (2, 1, 3)
        ]

    over_core_b = send(rest.at[1 - k], r1b, sems, 20, 20, core)
    over_core = [send(ref.at[1 - k], r1.at[i], sems, i, i, core) for i, ref in enumerate(chunks)]
    kept[0].wait()
    kept[1].wait()
    over_core_b.wait_recv()
    for m in range(8):
        sb[m // 2, m % 2] = add_up(kp1[m, 3 * SOME :], r1b[m]).astype(BF)
    over_z_b = over_z(sb, rbz, 21)
    over_x = []
    for i, ref in enumerate(mine):
        over_core[i].wait_recv()
        for m in range(8):
            sa[i, m % 2, m // 2] = add_up(ref[m], r1[i, m]).astype(BF)
        over_x.append(send(sa.at[i, 1 - x], rx.at[i], sems, 4 + i, 4 + i, side))
        if i == 0:
            kept[2].wait()
            kept[3].wait()
            half[0, y] = nt(jnp.broadcast_to(own(dtv[...]), (8, W)).astype(BF), tw3[...])
            swaps = [swap(0)]
        if i == 2:
            swaps[0].wait_recv()
            d2 = (half[0, 0] + half[0, 1]) * silu_slope(p2t[...])
            mine2 = jnp.where(y == 0, d2[:, : 2 * D], d2[:, 2 * D :]).astype(BF)
            half[1, y] = sum(nt(mine2[:, W * j : W * (j + 1)], tw2[j]) for j in range(4))
            swaps.append(swap(1))
    swaps[1].wait_recv()
    d1 = (half[1, 0] + half[1, 1]) * silu_slope(p1t[...])
    put_facts(facts, e, p1t, p2t, d1, d2, dtv, mask, loss)
    fsems = (fsend, frecv)
    fx[z, x, k] = facts[...]
    facts_z = [send(facts, fx.at[z, x, k], fsems, o - 1, 3 - o, (me + 4 * o) % 16) for o in (2, 1, 3)]
    along = []
    for i in range(4):
        over_x[i].wait_recv()
        for m in range(4):
            ta[i, m] = add_up(sa[i, x, m], rx[i, m]).astype(BF)
        along.append(over_z(ta.at[i], rz.at[i], 8 + 3 * i))
        if i == 1:
            for copy in facts_z:
                copy.wait_recv()
            facts_x = send(fx.at[:, x, k], fx.at[:, x, k], fsems, 3, 3, side)
        if i == 3:
            facts_x.wait_recv()
            facts_core = send(fx.at[:, :, k], fx.at[:, :, k], fsems, 4, 4, core)
    for copy in over_z_b:
        copy.wait_recv()
    for m in range(2):
        tb[m] = add_up(sb[z, m], rbz[0, m], rbz[1, m], rbz[2, m]).astype(BF)
    over_x_b = send(tb.at[1 - x], rbx, sems, 24, 24, side)

    def done(i):
        for copy in along[i]:
            copy.wait_recv()
        return add_up(ta[i, z], rz[i, 0], rz[i, 1], rz[i, 2])

    some[...] = done(0)

    @pl.when(me > 0)
    def _():
        @pl.loop(0, SOME // 8)
        def _(g):
            row = SOME * me + 8 * g
            owner = row // ROWS
            at = pl.multiple_of(row - ROWS * owner, 8)
            pltpu.make_async_remote_copy(
                src_ref=some.at[pl.ds(pl.multiple_of(8 * g, 8), 8)], dst_ref=land.at[pl.ds(at, 8)],
                send_sem=gsend, recv_sem=grecv, device_id={DP: owner}, device_id_type=pl.DeviceIdType.MESH,
            ).start()

    facts_core.wait_recv()
    all_facts[...] = fx[...].reshape(16, FACTS, 128)
    timed[...] = time_rows(all_facts, ROWS)
    for i in range(3):
        sum1[SOME * i : SOME * (i + 1), :] = done(i + 1)
    over_x_b.wait_recv()
    sum1[3 * SOME :, :] = add_up(tb[x, : ROWS - 3 * SOME], rbx[: ROWS - 3 * SOME])

    def landed(lo, hi):
        part = land.at[lo:hi]
        pltpu.make_async_remote_copy(
            src_ref=part, dst_ref=part, send_sem=gsend, recv_sem=grecv,
            device_id={DP: me}, device_id_type=pl.DeviceIdType.MESH,
        ).wait_recv()
        sum0[lo:hi, :] = land[lo:hi, :] + timed[lo:hi, :]

    @pl.when(me == 0)
    def _():
        landed(SOME, ROWS)
        sum0[:SOME, :] = some[...] + timed[:SOME, :]

    @pl.when((me > 0) & (me < 4))
    def _():
        landed(0, ROWS)

    @pl.when(me == 4)
    def _():
        landed(0, 16 * SOME - 4 * ROWS)
        sum0[16 * SOME - 4 * ROWS :, :] = timed[16 * SOME - 4 * ROWS :, :]

    @pl.when(me > 4)
    def _():
        sum0[...] = timed[...]

    @pl.when(me > 0)
    def _():
        pltpu.make_async_remote_copy(
            src_ref=some, dst_ref=some, send_sem=gsend, recv_sem=grecv,
            device_id={DP: me}, device_id_type=pl.DeviceIdType.MESH,
        ).wait_send()

    for copy in [over_core_b, over_x_b] + over_core + over_z_b + over_x + sum(along, []) + facts_z + [facts_x, facts_core] + swaps:
        copy.wait_send()


def sum_over_samples(*operands):
    vm, hbm = pl.BlockSpec(memory_space=pltpu.VMEM), pl.BlockSpec(memory_space=pl.ANY)
    dma = pltpu.SemaphoreType.DMA
    return pl.pallas_call(
        reduce_kernel,
        out_shape=(sds((ROWS, 128)), sds((ROWS, 128)), sds((16, FACTS, 128))),
        in_specs=[hbm, hbm, vm, hbm, hbm] + [vm] * 5,
        out_specs=(vm,) * 3,
        scratch_shapes=[
            pltpu.VMEM((8, SLAB, 128), BF),
            pltpu.VMEM((8, SOME, 128), BF),
            pltpu.VMEM((4, 4 * D, W), BF),
            pltpu.VMEM((4 * D, W), BF),
            pltpu.VMEM((FACTS, 128), F32),
            pltpu.VMEM((4, 8, SOME, 128), BF),
            pltpu.VMEM((4, 2, 4, SOME, 128), BF),
            pltpu.VMEM((4, 4, SOME, 128), BF),
            pltpu.VMEM((4, 4, SOME, 128), BF),
            pltpu.VMEM((4, 3, SOME, 128), BF),
            pltpu.VMEM((8, REST, 128), BF),
            pltpu.VMEM((4, 2, REST, 128), BF),
            pltpu.VMEM((3, 2, REST, 128), BF),
            pltpu.VMEM((2, REST, 128), BF),
            pltpu.VMEM((REST, 128), BF),
            pltpu.VMEM((SOME, 128), F32),
            pltpu.VMEM((ROWS, 128), F32),
            pltpu.VMEM((4, 2, 2, FACTS, 128), F32),
            pltpu.VMEM((ROWS, 128), F32),
            dma((25,)),
            dma((25,)),
            dma((5,)),
            dma((5,)),
            dma,
            dma,
            dma((4,)),
            pltpu.VMEM((2, 2, 8, 4 * D), F32),
            dma((4,)),
        ],
        compiler_params=pltpu.CompilerParams(
            collective_id=1, has_side_effects=True, vmem_limit_bytes=62 * 2**20
        ),
    )(*operands)


def time_features(steps):
    ladder = lax.broadcasted_iota(jnp.int32, (1, D // 2), 1).astype(F32)
    angles = steps.astype(F32) * jnp.exp(-math.log(10000.0) * ladder / (D // 2))
    return jnp.concatenate([jnp.cos(angles), jnp.sin(angles)], axis=1)


def add_noise(step, latents, noise, noisy):
    shape = (8, 128)
    level = 128 * lax.broadcasted_iota(jnp.int32, shape, 0) + lax.broadcasted_iota(jnp.int32, shape, 1)
    lowest, highest = 0.00085**0.5, 0.012**0.5
    beta = jnp.square(lowest + (highest - lowest) * level.astype(F32) / 999.0)
    logs = jnp.where(level <= step, jnp.log(1.0 - beta), 0.0)
    abar = jnp.exp(jnp.sum(jnp.sum(logs, axis=1, keepdims=True), axis=0, keepdims=True))
    noisy[...] = jnp.sqrt(abar) * latents[...] + jnp.sqrt(1.0 - abar) * noise[...]


def prepare_kernel(step, latents, noise, e, noisy):
    e[...] = jnp.broadcast_to(time_features(step[...]), (8, D))
    add_noise(step[...], latents, noise, noisy)


def shards(params, momentum, ema_params, latents, noise_eps, timesteps, pixel_mask, context):
    c = lax.axis_index(CH)
    d = lax.axis_index(DP)
    n_dp = lax.axis_size(DP)
    rows_dev = params.shape[2]
    rows_all = rows_dev * n_dp
    quick = n_dp == 16 and rows_dev == ROWS
    step, noise = timesteps[:, None], noise_eps[0]
    if quick:
        _, part1, e, noisy, vec0, p1, p2, stats, w1b, tw2, tw3, h0, h1, a1 = gather_weights(
            params[0], step, latents[0], noise
        )
        part1 = part1.reshape(2, 16, SLAB, 128)
    else:
        e, noisy = kcall(prepare_kernel, (sds((8, D)), sds((LAT, N))), (step, latents[0], noise))
        low = params[0].astype(BF)
        part0, part1 = (lax.all_gather(lax.all_gather(low[i], CH, axis=0), DP, axis=1) for i in range(2))

    px = (N, D)
    hx = (HEADS, N, HD)
    sh = (N + 2 * SIDE, 3 * D)
    taps, back = sds((3, 3 * D, D), BF), sds((3, D, 3 * D), BF)
    flat = pltpu.VMEM((2, rows_all, 128), F32)
    unrolled = pltpu.VMEM((3, 4 * R1 // 5, 128), F32)
    units = sds((8, 4 * D))
    if not quick:
        win, w1, w1b, vec0, tw2, tw3, tv, p1, p2 = kcall(
            partial(unpack0_kernel, rows_dev),
            (sds((36, D), BF), taps, back, sds((8, D)), sds((4, 4 * D, D), BF), sds((4 * D, D), BF), sds((1, D)))
            + (units, units),
            (part0, e),
            (flat, unrolled),
        )
        h0, h1, a1, stats = kcall(
            start_kernel,
            (sds(px), sds(px), sds(px, BF), sds((8, D))),
            (noisy, tv, win, w1, vec0),
            (pltpu.VMEM(sh, BF), pltpu.VMEM((8, D), F32)),
        )
    c2, c2b, tr, mats, kvw, vec1, gib, wout, outb = kcall(
        partial(unpack1_kernel, rows_dev),
        (taps, back, sds((4, D, D), BF), sds((16, D, D), BF), sds((2, CTX, D), BF))
        + (sds((24, D)), sds((8, D)), sds((36, D), BF), sds((1, D))),
        (part1,),
        (flat, unrolled, pltpu.VMEM((2, 40, 128), F32)),
    )
    h2, z0, a2, ntr, x1, q, k, v, stats = kcall(
        front_kernel,
        (sds(px),) * 2 + (sds(px, BF),) * 3 + (sds(hx, BF),) * 3 + (sds((8, D)),),
        (h0, h1, stats, c2, tr, vec1),
        (pltpu.VMEM(sh, BF), pltpu.VMEM((8, D), F32)),
        late=(0, 3, 4),
        early=range(8),
    )
    o, lse = kcall(
        attend_kernel, (sds(px, BF), sds((HEADS, 1, N))), (q, k, v), (pltpu.VMEM((D, N), F32),)
    )
    square = (D, W)
    dz1, dh3, dos, loss, gd, ggi, ggo, gkv, dvec, dgib, dwout, dbout = kcall(
        middle_kernel,
        (sds(px), sds(px), sds(hx, BF), sds((1, 1)))
        + (sds((4,) + square, BF), sds((8,) + square, BF), sds((4,) + square, BF), sds((2, CTX, W), BF))
        + (sds((24, D)), sds((8, D)), sds((36, D)), sds((8, 128))),
        (o, z0, h2, context[0], noise, pixel_mask, mats, kvw, vec1, gib, wout, outb),
        [pltpu.VMEM(px, F32)] * 3
        + [pltpu.VMEM(px, BF)] * 4
        + [
            pltpu.VMEM((4, N, D), BF),
            pltpu.VMEM((4, N, D), F32),
            pltpu.VMEM((4, N, D), F32),
            pltpu.VMEM(px, BF),
            pltpu.VMEM(px, BF),
            pltpu.VMEM((HEADS * KEYS, D), BF),
            pltpu.VMEM((HEADS * KEYS, D), BF),
            pltpu.VMEM((N, HEADS * KEYS), F32),
            pltpu.VMEM((N, HEADS * KEYS), BF),
            pltpu.VMEM((8, D), F32),
            pltpu.VMEM((36, N), F32),
        ]
        + [pltpu.VMEM((D, N), BF)] * 4,
        late=(7, 6, 1, 2),
        early=(0, 1, 2, 4, 5, 6, 7),
    )
    dq, dk, dv = kcall(
        attend_back_kernel,
        (sds(px, BF),) * 3,
        (q, k, v, dos, lse),
        (pltpu.VMEM((D, N), F32), pltpu.VMEM(hx, F32), pltpu.VMEM(hx, F32)),
    )
    front = -(-FRONT // (16 * n_dp)) * 16 * n_dp
    lead = (2, 8) if quick else (n_dp,)
    own1, own0, dtv = kcall(
        back_kernel,
        (
            sds(lead + (SLAB if quick else rows_dev, 128), BF),
            sds(lead + (front // n_dp, 128), BF),
            sds((1, D)),
        ),
        (dq, dk, dv, dz1, dh3, z0, h2, h1, h0, stats, w1b, c2b, tr, vec0, vec1, a1, a2, ntr, x1, noisy,
         gd, ggi, ggo, gkv, dvec, dgib, dwout, dbout),
        (
            pltpu.VMEM(px, F32),
            pltpu.VMEM(sh, BF),
            pltpu.VMEM((sh[0], 3 * W), BF),
            pltpu.VMEM((24, D), F32),
            pltpu.VMEM((2, 4 * R1 // 5, 128), F32),
            pltpu.VMEM((7600, 128), F32),
            pltpu.VMEM((2, 40, 128), F32),
        ),
        late=(5, 3, 17, 6, 4, 16, 7, 11, 20, 21, 22, 23, 15, 8, 10),
        early=(0,),
    )
    timed = (dtv, tw2, tw3, p1, p2, e, pixel_mask, loss)
    if quick:
        sum1, sum0, all_facts = sum_over_samples(own1, own0, *timed)
    else:
        facts = kcall(time_back, sds((FACTS, 128)), timed)
        sum1 = lax.psum_scatter(own1, DP, scatter_dimension=0).astype(F32)
        sum0 = lax.all_gather(lax.psum_scatter(own0, DP, scatter_dimension=0), DP, axis=0, tiled=True)
        sum0 = jnp.pad(sum0, ((0, rows_all - front), (0, 0)))
        sum0 = lax.dynamic_slice_in_dim(sum0, d * rows_dev, rows_dev, 0).astype(F32)
        all_facts = lax.all_gather(facts, DP, axis=0)
    state = sds((2, rows_dev, 128))
    new_params, new_momentum, new_ema, loss, pixels = kcall(
        partial(update_kernel, not quick),
        (state, state, state, sds((1, 1)), sds((1, 1))),
        (params[0], momentum[0], ema_params[0], sum1, sum0, all_facts),
    )
    return (new_params[None], new_momentum[None], new_ema[None], loss.reshape(()), pixels.reshape(()))


def solution(mesh):
    packed = P(CH, None, DP, None)
    row = P(DP, None, None)
    return jax.shard_map(
        shards,
        mesh=mesh,
        in_specs=(packed, packed, packed, row, row, P(DP), P(DP, None), row),
        out_specs=(packed, packed, packed, P(), P()),
        check_vma=False,
    )
```

```python
import math
from functools import partial

import jax
import jax.numpy as jnp
from jax import lax
from jax.experimental import pallas as pl
from jax.experimental.pallas import tpu as pltpu
from jax.sharding import PartitionSpec as P

D = 320
W = 160
HEADS = 8
HD = 40
CTX = 768
TXT = 77
LAT = 4
SIDE = 32
N = 1024
EPS = 1e-5
LR = 0.2
MU = 0.9
ED = 0.9
CH = "chan"
DP = "dp"
F32 = jnp.float32
BF = jnp.bfloat16
HI = lax.Precision.HIGHEST
SCALE = HD**-0.5
LOG2E = 1.0 / math.log(2.0)

R0 = 4000
U1, U2, U3 = 2920, 4204, 9328
FRONT = 3650
T1, T2, T3 = 3650, 5255, 11660
C2 = 2
PI = 2885
QKV = 3208
SO = 4168
CQ = 4491
CKV = 4811
CO = 6347
GI = 6670
GIB = 9230
GO = 9238
PO = 10519
OUT = 10842
OUTB = 10878
R1 = 13600
VEC0 = (36, 37, 38, 2919)
VEC1 = (0, 1, 2882, 2883, 2884, 3205, 3206, 3207, 4488, 4489, 4490, 6667, 6668, 6669, 10518, 10839, 10840, 10841)
(N2G, N2B, C2B, NTG, NTB, PIB, L1G, L1B, SOB, L2G, L2B, COB, L3G, L3B, GOB, POB, NOG, NOB) = range(18)
MPI, MQ, MK, MV = range(4)
MSO, MCQ, MCO, MPO, MGV, MGG, MGO = 0, 1, 2, 3, 4, 8, 12


class Flow:
    def __init__(self, ins, outs, sems):
        self.ins = {i: pltpu.make_async_copy(src, dst, sems.at[j]) for j, (i, src, dst) in enumerate(ins)}
        n = len(ins)
        self.outs = {i: pltpu.make_async_copy(src, dst, sems.at[n + j]) for j, (i, dst, src) in enumerate(outs)}
        self.waiting = set(self.ins)
        self.going = []
        for copy in self.ins.values():
            copy.start()

    def need(self, *which):
        for i in which:
            self.ins[i].wait()
            self.waiting.discard(i)

    def ready(self, *which):
        for i in which:
            self.outs[i].start()
            self.going.append(i)

    def end(self):
        self.need(*sorted(self.waiting))
        self.ready(*(i for i in self.outs if i not in self.going))
        for copy in self.outs.values():
            copy.wait()


def kcall(body, outs, ins, scratch=(), late=(), early=()):
    vm, hbm = pl.BlockSpec(memory_space=pltpu.VMEM), pl.BlockSpec(memory_space=pl.ANY)
    single = not isinstance(outs, tuple)
    outs = (outs,) if single else outs
    n, m = len(ins), len(outs)
    late, early = tuple(late), tuple(early)
    scratch = list(scratch)
    count = len(scratch)
    if late or early:
        scratch += [pltpu.VMEM(ins[i].shape, ins[i].dtype) for i in late]
        scratch += [pltpu.VMEM(outs[i].shape, outs[i].dtype) for i in early]
        scratch.append(pltpu.SemaphoreType.DMA((len(late) + len(early),)))

    def whole(*refs):
        if not (late or early):
            return body(*refs)
        given, made, rest = list(refs[:n]), list(refs[n : n + m]), refs[n + m :]
        kept = rest[count:-1]
        inward = [(i, given[i], kept[j]) for j, i in enumerate(late)]
        outward = [(i, made[i], kept[len(late) + j]) for j, i in enumerate(early)]
        for i, _, ref in inward:
            given[i] = ref
        for i, _, ref in outward:
            made[i] = ref
        flow = Flow(inward, outward, rest[-1])
        body(flow, *given, *made, *rest[:count])
        flow.end()

    done = pl.pallas_call(
        whole,
        out_shape=outs,
        in_specs=[hbm if i in late else vm for i in range(n)],
        out_specs=tuple(hbm if i in early else vm for i in range(m)),
        scratch_shapes=scratch,
        compiler_params=pltpu.CompilerParams(vmem_limit_bytes=63 * 2**20),
    )(*ins)
    return done[0] if single else done


def sds(shape, dtype=F32):
    return jax.ShapeDtypeStruct(shape, dtype)


def tiles(fn, size=256, total=N):
    for t in range(total // size):
        fn(pl.ds(t * size, size))


def nn(a, b):
    return jnp.dot(a, b, preferred_element_type=F32)


def nt(a, b):
    return lax.dot_general(a, b, (((1,), (1,)), ((), ())), preferred_element_type=F32)


def tn(a, b):
    return lax.dot_general(a, b, (((0,), (0,)), ((), ())), preferred_element_type=F32)


def colsum(v):
    return jnp.sum(v, axis=0, keepdims=True)


def flatten(a_ref, flat, rows):
    for b in range(2):
        for t in range(a_ref.shape[1]):
            flat[b, t * rows : (t + 1) * rows, :] = a_ref[b, t, :rows, :].astype(F32)


def unroll(flat, s_ref, lo_chunk, hi_chunk):
    q = 80

    @pl.loop(lo_chunk, hi_chunk)
    def _(c):
        f = [[flat[b, pl.ds(c * 5 * q + j, q, stride=5), :] for j in range(5)] for b in range(2)]
        for i in range(4):
            row = []
            for b in range(2):
                lo = 32 * i
                first, second = f[b][i], f[b][i + 1]
                row += [first[:, lo:], second[:, : lo + 32]] if lo else [first, second[:, :32]]
            full = jnp.concatenate(row, axis=1)
            for k, (lo, hi) in enumerate(((0, 128), (128, 256), (256, 320))):
                s_ref[k, pl.ds(c * 4 * q + i, q, stride=4), : hi - lo] = full[:, lo:hi]


def get_rows(s_ref, start, count, step=1):
    ds = pl.ds(start, count) if step == 1 else pl.ds(start, count, stride=step)
    return jnp.concatenate([s_ref[0, ds, :], s_ref[1, ds, :], s_ref[2, ds, :64]], axis=1)


def put_taps(s_ref, start, w, back):
    for r in range(3):
        taps = [get_rows(s_ref, start + D * (3 * r + i), D).astype(BF) for i in range(3)]
        for i in range(3):
            w[r, D * i : D * (i + 1), :] = taps[i]
        back[r] = jnp.concatenate(taps[::-1], axis=1)


def unit_row(parts):
    out = [p[:, W * b : W * (b + 1)] for b in range(2) for p in parts]
    return jnp.broadcast_to(jnp.concatenate(out, axis=1), (8, 4 * D))


def unit_parts(row):
    return [
        jnp.concatenate([row[:, W * i : W * (i + 1)], row[:, 640 + W * i : 640 + W * (i + 1)]], axis=1)
        for i in range(4)
    ]


def take_front(s_ref, win, w1, w1b, vec):
    win[...] = get_rows(s_ref, 0, 36).astype(BF)
    put_taps(s_ref, 39, w1, w1b)
    for i, r in enumerate(VEC0):
        vec[i : i + 1, :] = get_rows(s_ref, r, 1)


def take_time(s_ref, tw2, tw3):
    for i in range(4):
        tw2[i] = get_rows(s_ref, U2 + i, 4 * D, 4).astype(BF)
    tw3[...] = get_rows(s_ref, U3, 4 * D).astype(BF)


def time_forward(s_ref, e, tw2, tw3, tv, p1, p2):
    u = e[...].astype(BF)
    p1[...] = unit_row(
        [nn(u, get_rows(s_ref, U1 + i, D, 4).astype(BF))[:1] + get_rows(s_ref, U1 + 4 * D + i, 1) for i in range(4)]
    )
    u = silu(p1[...]).astype(BF)
    p2[...] = unit_row([nn(u, tw2[i])[:1] + get_rows(s_ref, U2 + 16 * D + i, 1) for i in range(4)])
    u = silu(p2[...]).astype(BF)
    tv[...] = nn(u, tw3[...])[:1] + get_rows(s_ref, U3 + 4 * D, 1)


def unpack0_kernel(rows, a_ref, e, win, w1, w1b, vec, tw2, tw3, tv, p1, p2, flat, s_ref):
    flatten(a_ref, flat, rows)
    unroll(flat, s_ref, 0, R1 // 400)
    take_front(s_ref, win, w1, w1b, vec)
    take_time(s_ref, tw2, tw3)
    time_forward(s_ref, e, tw2, tw3, tv, p1, p2)


FE, FU1, FU2, FD1, FD2, FD3, FL = 0, 3, 13, 23, 28, 33, 35
FACTS = 40


def time_back(dtv, tw2, tw3, p1, p2, e, mask, loss, facts):
    g = jnp.broadcast_to(dtv[...], (8, D)).astype(BF)
    d2 = nt(g, tw3[...]) * silu_slope(p2[...])
    total = jnp.zeros((8, 4 * D), F32)
    for i, part in enumerate(unit_parts(d2)):
        total += nt(part.astype(BF), tw2[i])
    d1 = total * silu_slope(p1[...])
    put_facts(facts, e, p1, p2, d1, d2, dtv, mask, loss)


def put_facts(facts, e, p1, p2, d1, d2, dtv, mask, loss):
    first = lax.axis_index(CH) == 0
    facts[...] = jnp.zeros_like(facts)

    def put(at, v):
        for i in range(0, v.shape[1], 128):
            n = min(128, v.shape[1] - i)
            facts[at + i // 128 : at + i // 128 + 1, :n] = v[:1, i : i + n]

    put(FE, e[...].astype(BF).astype(F32))
    put(FU1, silu(p1[...]).astype(BF).astype(F32))
    put(FU2, silu(p2[...]).astype(BF).astype(F32))
    put(FD1, jnp.where(first, d1[:, : 2 * D], d1[:, 2 * D :]))
    put(FD2, jnp.where(first, d2[:, : 2 * D], d2[:, 2 * D :]))
    put(FD3, own(dtv[...]))
    facts[FL : FL + 1, 0:1] = loss[...]
    facts[FL : FL + 1, 1:2] = jnp.sum(mask[...].astype(F32), axis=1, keepdims=True)


def unpack1_kernel(rows, a_ref, c2, c2b, tr, mats, kv, vec, gib, wout, outb, flat, s_ref, o_ref):
    flatten(a_ref, flat, rows)
    unroll(flat, s_ref, 0, R1 // 400)
    put_taps(s_ref, C2, c2, c2b)
    tr[MPI] = get_rows(s_ref, PI, D).astype(BF)
    for m, r in ((MSO, SO), (MCQ, CQ), (MCO, CO), (MPO, PO)):
        mats[m] = get_rows(s_ref, r, D).astype(BF)
    for j in range(3):
        tr[MQ + j] = get_rows(s_ref, QKV + j, D, 3).astype(BF)
    for j in range(8):
        mats[MGV + j] = get_rows(s_ref, GI + j, D, 8).astype(BF)
    for j in range(4):
        for b in range(2):
            mats[MGO + j, b * W : (b + 1) * W, :] = get_rows(s_ref, GO + 640 * b + W * j, W).astype(BF)
    for j in range(2):
        kv[j] = get_rows(s_ref, CKV + j, CTX, 2).astype(BF)
    for i, r in enumerate(VEC1):
        vec[i : i + 1, :] = get_rows(s_ref, r, 1)
    gib[...] = get_rows(s_ref, GIB, 8)
    outb[...] = get_rows(s_ref, OUTB, 1)
    lane = lax.broadcasted_iota(jnp.int32, (W, W), 0)
    col = lax.broadcasted_iota(jnp.int32, (W, W), 1)
    pick = ((lane % 2) * 80 + lane // 2 == col).astype(BF)
    raw = get_rows(s_ref, OUT, 36).astype(BF)
    for b in range(2):
        moved = nn(raw[:, W * b : W * (b + 1)], pick)
        o_ref[0, :36, :] = moved[:, :128]
        o_ref[1, :36, :32] = moved[:, 128:]
        for ch in range(2):
            pieces = []
            for m in range(4):
                ds = pl.ds(m, 9, stride=4)
                both = jnp.concatenate([o_ref[0, ds, :], o_ref[1, ds, :32]], axis=1)
                pieces.append(both[:, 80 * ch : 80 * ch + 80])
            at = (2 * b + ch) * 9
            wout[at : at + 9, :] = jnp.concatenate(pieces, axis=1).astype(BF)


def pixel_col(n, axis):
    shape = (n, 1) if axis == 0 else (1, n)
    return lax.broadcasted_iota(jnp.int32, shape, axis)


def shift_lanes(v, tap):
    r, s = tap // 3 - 1, tap % 3 - 1
    pix = pixel_col(N, 1)
    i, j = pix // SIDE + r, pix % SIDE + s
    ok = (i >= 0) & (i < SIDE) & (j >= 0) & (j < SIDE)
    move = -(r * SIDE + s) % N
    moved = pltpu.roll(v, move, 1) if move else v
    return jnp.where(ok, moved, 0.0)


def put_shifts(ref, v):
    j = pixel_col(N, 0) % SIDE
    left = jnp.where(j == 0, 0.0, pltpu.roll(v, 1, 0)).astype(BF)
    right = jnp.where(j == SIDE - 1, 0.0, pltpu.roll(v, N - 1, 0)).astype(BF)
    ref[SIDE : SIDE + N, :] = jnp.concatenate([left, v.astype(BF), right], axis=1)


def clear_margins(ref):
    zero = jnp.zeros((SIDE, ref.shape[1]), BF)
    ref[:SIDE, :] = zero
    ref[SIDE + N :, :] = zero


def conv_rows(ref, w_ref):
    return sum(nn(ref[SIDE * r : SIDE * r + N, :], w_ref[r]) for r in range(3))


def conv_back_rows(ref, w_ref):
    return sum(nt(ref[SIDE * (2 - r) : SIDE * (2 - r) + N, :], w_ref[r]) for r in range(3))


def group_mean(sums):
    a = lax.broadcasted_iota(jnp.int32, (D, D), 0) // 10
    b = lax.broadcasted_iota(jnp.int32, (D, D), 1) // 10
    pool = jnp.where(a == b, 1.0, 0.0)
    wide = jnp.broadcast_to(sums, (8, D))
    out = jnp.dot(wide, pool, precision=HI, preferred_element_type=F32)
    return out[:1] * (1.0 / (10 * N))


def group_stats(v_ref, acc, sums):
    mean = group_mean(sums)
    acc[0:1, :] = colsum(jnp.square(v_ref[...] - mean))
    return mean, lax.rsqrt(group_mean(acc[0:1, :]) + EPS)


def silu(v):
    return v * jax.nn.sigmoid(v)


def silu_slope(v):
    sig = jax.nn.sigmoid(v)
    return sig * (1.0 + v * (1.0 - sig))


def layer(v):
    mean = jnp.sum(v, axis=1, keepdims=True) * (1.0 / D)
    sq = jnp.sum(v * v, axis=1, keepdims=True) * (1.0 / D)
    inv = lax.rsqrt(sq - mean * mean + EPS)
    return (v - mean) * inv, inv


def layer_back(grad, normed, inv, gain):
    ghat = grad * gain
    m1 = jnp.sum(ghat, axis=1, keepdims=True) * (1.0 / D)
    m2 = jnp.sum(ghat * normed, axis=1, keepdims=True) * (1.0 / D)
    return inv * (ghat - m1 - normed * m2)


def own(v):
    return jnp.where(lax.axis_index(CH) == 0, v[..., :W], v[..., W:])


def head(v, h):
    return v[:, HD * h : HD * (h + 1)]


def group_norm(src, acc, total, stats, at):
    mean, inv = group_stats(src, acc, total)
    stats[at : at + 1, :], stats[at + 1 : at + 2, :] = mean, inv
    return (src[...] - mean) * inv


def start_steps(noisy, tv, win, w1, vec0, h0, h1, a1, stats, sh, acc):
    def first():
        cols = jnp.concatenate([shift_lanes(noisy[...], t) for t in range(9)], axis=0).astype(BF)
        clear_margins(sh)
        stats[...] = jnp.zeros_like(stats)
        h = tn(cols, win[...]) + vec0[0:1, :]
        h0[...] = h
        y = silu(group_norm(h0, acc, colsum(h), stats, 0) * vec0[1:2, :] + vec0[2:3, :])
        put_shifts(sh, y)
        a1[...] = y.astype(BF)

    def taps(r):
        def one():
            part = nn(sh[SIDE * r : SIDE * r + N, :], w1[r])
            if r == 2:
                part += tv[...]
            h1[...] = (h1[...] if r else vec0[3:4, :]) + part

        return one

    return [first, taps(0), taps(1), taps(2)]


def start_kernel(noisy, tv, win, w1, vec0, h0, h1, a1, stats, sh, acc):
    for step in start_steps(noisy, tv, win, w1, vec0, h0, h1, a1, stats, sh, acc):
        step()


def front_kernel(flow, h0, h1, stats_in, c2, tr, vec1, h2, z0, a2, ntr, x1, q, k, v, stats, sh, acc):
    clear_margins(sh)
    stats[...] = stats_in[...]
    y = silu(group_norm(h1, acc, colsum(h1[...]), stats, 2) * vec1[N2G : N2G + 1, :] + vec1[N2B : N2B + 1, :])
    put_shifts(sh, y)
    a2[...] = y.astype(BF)
    flow.ready(2)
    flow.need(0, 3)
    h = h0[...] + conv_rows(sh, c2) + vec1[C2B : C2B + 1, :]
    h2[...] = h
    flow.ready(0)
    n = group_norm(h2, acc, colsum(h), stats, 4)
    n = (n * vec1[NTG : NTG + 1, :] + vec1[NTB : NTB + 1, :]).astype(BF)
    ntr[...] = n
    flow.ready(3)
    flow.need(4)
    z = nn(n, tr[MPI]) + vec1[PIB : PIB + 1, :]
    z0[...] = z
    flow.ready(1)
    normed, _ = layer(z)
    x = (normed * vec1[L1G : L1G + 1, :] + vec1[L1B : L1B + 1, :]).astype(BF)
    x1[...] = x
    flow.ready(4)
    for i, (at, dst) in enumerate(((MQ, q), (MK, k), (MV, v))):
        y = nn(x, tr[at]).astype(BF)
        for hd in range(HEADS):
            dst[hd] = head(y, hd)
        flow.ready(5 + i)


AT = 512


def attend_kernel(q, k, v, o, lse, ot):
    steps = [(h, pl.ds(t * AT, AT)) for h in range(HEADS) for t in range(N // AT)]

    def scores(h, rows):
        return nt(k[h], q[h, rows, :])

    now = scores(*steps[0])
    for i, (h, rows) in enumerate(steps):
        later = scores(*steps[i + 1]) if i + 1 < len(steps) else None
        if i % (N // AT) == 0:
            vt = v[h].astype(F32).T.astype(BF)
        s = now * (SCALE * LOG2E)
        top = jnp.max(s, axis=0, keepdims=True)
        e = jnp.exp2(s - top)
        total = jnp.sum(e, axis=0, keepdims=True)
        lse[h, :, rows] = top + jnp.log(total) * LOG2E
        ot[h * HD : (h + 1) * HD, rows] = nn(vt, (e * (1.0 / total)).astype(BF))
        now = later
    o[...] = ot[...].T.astype(BF)


KEYS = 128


def by_head(v):
    wide = jnp.concatenate([v, jnp.zeros((KEYS - TXT, D), v.dtype)], axis=0)
    col = lax.broadcasted_iota(jnp.int32, (KEYS, D), 1) // HD
    return jnp.concatenate([jnp.where(col == h, wide, 0.0) for h in range(HEADS)], axis=0)


def from_heads(vt):
    row = lax.broadcasted_iota(jnp.int32, (D, KEYS), 0) // HD
    total = jnp.zeros((D, KEYS), F32)
    for h in range(HEADS):
        total += jnp.where(row == h, vt[:, KEYS * h : KEYS * (h + 1)], 0.0)
    return total.T[:TXT]


def transposed(v):
    return v.T


def middle_kernel(
    flow, o, z0, h2, ctx, noise, mask, mats, kvw, vec, gib, wout, outb,
    dz1, dh3, dos, loss, gd, ggi, ggo, gkv, dvec, dgib, dwout, dbout,
    z1, z2, h3, x2, x3, oc, z3b, gl, by_a, by_g, a3, qc, kb, vb, prob, dsc, acc, pt, oct_, x2t, ot, x3t,
):
    def row(i):
        return vec[i : i + 1, :]

    def put(i, v):
        dvec[i : i + 1, :] = v

    flow.need(7)
    kb[...] = by_head(nn(ctx[...], kvw[0])).astype(BF)
    vb[...] = by_head(nn(ctx[...], kvw[1])).astype(BF)
    flow.need(6, 1)
    z = z0[...] + nn(o[...], mats[MSO]) + row(SOB)
    z1[...] = z
    normed, _ = layer(z)
    x = (normed * row(L2G) + row(L2B)).astype(BF)
    x2[...] = x
    qq = nn(x, mats[MCQ]).astype(BF)
    qc[...] = qq
    s = nt(qq, kb[...]) * (SCALE * LOG2E)
    there = lax.broadcasted_iota(jnp.int32, (1, KEYS), 1) < TXT
    for h in range(HEADS):
        at = slice(KEYS * h, KEYS * (h + 1))
        sh = jnp.where(there, s[:, at], -jnp.inf)
        e = jnp.exp2(sh - jnp.max(sh, axis=1, keepdims=True))
        prob[:, at] = e * (1.0 / jnp.sum(e, axis=1, keepdims=True))
    c = nn(prob[...].astype(BF), vb[...]).astype(BF)
    oc[...] = c
    z = z1[...] + nn(c, mats[MCO]) + row(COB)
    z2[...] = z
    normed, _ = layer(z)
    x = (normed * row(L3G) + row(L3B)).astype(BF)
    x3[...] = x
    moving = ((oc, oct_), (x2, x2t), (o, ot), (x3, x3t))
    for j in range(4):
        moving[j][1][...] = transposed(moving[j][0][...])
        a = nn(x, mats[MGV + j]) + gib[j : j + 1, :]
        g = nn(x, mats[MGG + j]) + gib[4 + j : 5 + j, :]
        cdf = 0.5 * (1.0 + lax.erf(g * math.sqrt(0.5)))
        gelu = g * cdf
        by_a[j] = gelu
        by_g[j] = a * (cdf + g * jnp.exp(-0.5 * g * g) * (1.0 / math.sqrt(2.0 * math.pi)))
        y = (a * gelu).astype(BF)
        gl[j] = y
        z = z + nn(y, mats[MGO + j])
    zb = (z + row(GOB)).astype(BF)
    z3b[...] = zb
    flow.need(2)
    h = h2[...] + nn(zb, mats[MPO]) + row(POB)
    h3[...] = h
    mean, inv = group_stats(h3, acc, colsum(h))
    gain, bias = row(NOG), row(NOB)
    a3[...] = silu((h3[...] - mean) * inv * gain + bias).astype(BF)
    taps = nt(wout[...], a3[...])
    for ch in range(LAT):
        pred = jnp.zeros((1, N), F32)
        for t in range(9):
            pred += shift_lanes(taps[9 * ch + t : 9 * ch + t + 1, :], t)
        at = W * (ch // 2) + ch % 2
        err = pred + outb[0:1, at : at + 1] - noise[ch : ch + 1, :]
        weighed = mask[...].astype(F32) * err
        g = 2.0 * weighed
        acc[2 + ch : 3 + ch, 0:1] = jnp.sum(weighed * err, axis=1, keepdims=True)
        dbout[ch : ch + 1, :] = jnp.broadcast_to(jnp.sum(g, axis=1, keepdims=True), (1, 128))
        for t in range(9):
            pt[9 * ch + t : 9 * ch + t + 1, :] = shift_lanes(g, 8 - t)
    loss[...] = acc[2:3, 0:1] + acc[3:4, 0:1] + acc[4:5, 0:1] + acc[5:6, 0:1]

    dvec[...] = jnp.zeros_like(dvec)
    taps = pt[...].astype(BF)
    dwout[...] = nn(taps, a3[...])
    n = (h3[...] - mean) * inv
    g = tn(taps, wout[...]) * silu_slope(n * gain + bias)
    dgain, dbias = colsum(g * n), colsum(g)
    put(NOG, dgain)
    put(NOB, dbias)
    g = inv * (g * gain - group_mean(gain * dbias) - n * group_mean(gain * dgain))
    dh3[...] = g
    flow.ready(1)
    put(POB, colsum(g))
    gd[0] = nn(transposed(z3b[...]), own(g).astype(BF)).astype(BF)
    dz3 = nt(g.astype(BF), mats[MPO])
    z1b = dz3.astype(BF)
    put(GOB, colsum(dz3))
    mine_t = transposed(own(dz3).astype(BF))
    xt = x3t[...]
    dx = jnp.zeros((N, D), F32)
    for j in range(4):
        dgl = nt(z1b, mats[MGO + j])
        ggo[j] = nn(mine_t, gl[j]).T.astype(BF)
        da = dgl * by_a[j]
        dg = dgl * by_g[j]
        dgib[j : j + 1, :] = colsum(da)
        dgib[4 + j : 5 + j, :] = colsum(dg)
        ggi[j] = nn(xt, own(da).astype(BF)).astype(BF)
        ggi[4 + j] = nn(xt, own(dg).astype(BF)).astype(BF)
        dx += nt(da.astype(BF), mats[MGV + j]) + nt(dg.astype(BF), mats[MGG + j])
    flow.ready(5, 6)
    normed, li = layer(z2[...])
    put(L3G, colsum(dx * normed))
    put(L3B, colsum(dx))
    dz = dz3 + layer_back(dx, normed, li, row(L3G))
    z2[...] = dz
    put(COB, colsum(dz))
    gd[1] = nn(oct_[...], own(dz).astype(BF)).astype(BF)
    do = nt(dz.astype(BF), mats[MCO]).astype(BF)
    dp = nt(do, vb[...])
    dot = transposed(do)
    qt = transposed(qc[...])
    gkv[1] = tn(ctx[...], own(from_heads(nn(dot, prob[...].astype(BF)))).astype(BF)).astype(BF)
    for h in range(HEADS):
        at = slice(KEYS * h, KEYS * (h + 1))
        p, d = prob[:, at], dp[:, at]
        dsc[:, at] = (p * (d - jnp.sum(p * d, axis=1, keepdims=True)) * SCALE).astype(BF)
    gkv[0] = tn(ctx[...], own(from_heads(nn(qt, dsc[...]))).astype(BF)).astype(BF)
    flow.ready(7)
    dq = nn(dsc[...], kb[...])
    gd[2] = nn(x2t[...], own(dq).astype(BF)).astype(BF)
    dx = nt(dq.astype(BF), mats[MCQ])
    normed, li = layer(z1[...])
    put(L2G, colsum(dx * normed))
    put(L2B, colsum(dx))
    dz = z2[...] + layer_back(dx, normed, li, row(L2G))
    dz1[...] = dz
    flow.ready(0)
    put(SOB, colsum(dz))
    gd[3] = nn(ot[...], own(dz).astype(BF)).astype(BF)
    do = nt(dz.astype(BF), mats[MSO]).astype(BF)
    for h in range(HEADS):
        dos[h] = head(do, h)


ABT = 256


def attend_back_kernel(q, k, v, do, lse, dq, dk, dv, qt, kacc, vacc):
    steps = [(h, pl.ds(t * ABT, ABT)) for h in range(HEADS) for t in range(N // ABT)]

    def scores(h, rows):
        return nt(k[h], q[h, rows, :]), nt(v[h], do[h, rows, :])

    now = scores(*steps[0])
    for i, (h, rows) in enumerate(steps):
        later = scores(*steps[i + 1]) if i + 1 < len(steps) else None
        s, dp = now
        p = jnp.exp2(s * (SCALE * LOG2E) - lse[h, :, rows])
        ds = (p * (dp - jnp.sum(p * dp, axis=0, keepdims=True)) * SCALE).astype(BF)
        dkt, dvt = nn(ds, q[h, rows, :]), nn(p.astype(BF), do[h, rows, :])
        if i % (N // ABT) == 0:
            kt = k[h].astype(F32).T.astype(BF)
            kacc[h], vacc[h] = dkt, dvt
        else:
            kacc[h] += dkt
            vacc[h] += dvt
        qt[h * HD : (h + 1) * HD, rows] = nn(kt, ds)
        now = later

    dq[...] = qt[...].T.astype(BF)

    def one(rows):
        for acc, dst in ((kacc, dk), (vacc, dv)):
            dst[rows, :] = jnp.concatenate([acc[h, rows, :] for h in range(HEADS)], axis=1).astype(BF)

    tiles(one)


def put_rows(s_ref, start, v, step=1):
    n = v.shape[0]
    ds = pl.ds(start, n) if step == 1 else pl.ds(start, n, stride=step)
    s_ref[0, ds, :] = v[:, :128]
    s_ref[1, ds, :32] = v[:, 128:]


def roll_rows(s_ref, out_ref, lo_chunk, hi_chunk):
    q = 80

    @pl.loop(lo_chunk, hi_chunk)
    def _(c):
        g = []
        for i in range(4):
            ds = pl.ds(c * 4 * q + i, q, stride=4)
            g.append((s_ref[0, ds, :], s_ref[1, ds, :32]))
        base = (c - lo_chunk) * 5 * q
        out_ref[pl.ds(base, q, stride=5), :] = g[0][0]
        for i in range(3):
            lo = 96 - 32 * i
            out_ref[pl.ds(base + i + 1, q, stride=5), :] = jnp.concatenate(
                ([g[i][0][:, 128 - 32 * i :]] if i else []) + [g[i][1], g[i + 1][0][:, :lo]], axis=1
            )
        out_ref[pl.ds(base + 4, q, stride=5), :] = jnp.concatenate([g[3][0][:, 32:], g[3][1]], axis=1)


def by_owner(s_ref, flat, out, total):
    owners, room = math.prod(out.shape[:-2]), out.shape[-2]
    size = room if total < owners * room and len(out.shape) == 3 else min(room, ROWS)
    half = owners // 2 * size
    for lo, hi, first in ((0, min(-(-half // 400), total // 400), 0), (half // 400, total // 400, owners // 2)):
        if hi > lo:
            roll_rows(s_ref, flat, lo, hi)
        at = 400 * max(hi - lo, 0)
        if at < flat.shape[0]:
            flat[at:, :] = jnp.zeros((flat.shape[0] - at, 128), F32)
        for t in range(first, first + owners // 2):
            spot = (t % 2, t // 2) if len(out.shape) == 4 else (t,)
            row = t * size - 400 * lo
            out[(*spot, slice(0, size))] = flat[row : row + size, :].astype(BF)
            if room > size:
                out[(*spot, slice(size, room))] = jnp.zeros((room - size, 128), BF)


def conv_grads(a_ref, g_ref, s_ref, start):
    at = transposed(a_ref[...])
    for r in range(3):
        rows = SIDE * (2 - r)
        three = nn(at, g_ref[rows : rows + N, :])
        for i in range(3):
            put_rows(s_ref, start + D * (3 * r + i), three[:, W * (2 - i) : W * (3 - i)])


def back_kernel(
    flow, dq, dk, dv, dz1, dh3, z0, h2, h1, h0, stats, w1, c2, tr, vec0, vec1, a1, a2, ntr, x1, noisy,
    gd, ggi, ggo, gkv, dvec_in, dgib, dwout, dbout,
    out1, out0, dtv,
    dh, g_ref, go_ref, dvec, s_ref, flat, o_ref,
):
    c = lax.axis_index(CH)
    clear_margins(g_ref)
    clear_margins(go_ref)
    dvec[...] = dvec_in[...]

    def row(i):
        return vec1[i : i + 1, :]

    def put(i, v):
        dvec[i : i + 1, :] = v

    dx = nt(dq[...], tr[MQ]) + nt(dk[...], tr[MK]) + nt(dv[...], tr[MV])
    xt = transposed(x1[...])
    for j, g in enumerate((dq, dk, dv)):
        put_rows(s_ref, QKV + j, nn(xt, own(g[...].astype(F32)).astype(BF)), 3)
    flow.need(5, 3)
    normed, li = layer(z0[...])
    put(L1G, colsum(dx * normed))
    put(L1B, colsum(dx))
    dz = dz1[...] + layer_back(dx, normed, li, row(L1G))
    put(PIB, colsum(dz))
    flow.need(17)
    put_rows(s_ref, PI, tn(ntr[...], own(dz).astype(BF)))
    g = nt(dz.astype(BF), tr[MPI])

    def norm_back(g, n, at, gain):
        dgain, dbias = colsum(g * n), colsum(g)
        back = stats[at + 1 : at + 2, :] * (g * gain - group_mean(gain * dbias) - n * group_mean(gain * dgain))
        return back, dgain, dbias

    def normed_of(src, at):
        return (src[...] - stats[at : at + 1, :]) * stats[at + 1 : at + 2, :]

    flow.need(6, 4)
    g, dgain, dbias = norm_back(g, normed_of(h2, 4), 4, row(NTG))
    put(NTG, dgain)
    put(NTB, dbias)
    g = dh3[...] + g
    dh[...] = g
    put(C2B, colsum(g))
    put_shifts(g_ref, g)
    put_shifts(go_ref, own(g))
    flow.need(16)
    conv_grads(a2, go_ref, s_ref, C2)
    flow.need(7, 11)
    n = normed_of(h1, 2)
    g = conv_back_rows(g_ref, c2) * silu_slope(n * row(N2G) + row(N2B))
    g, dgain, dbias = norm_back(g, n, 2, row(N2G))
    put(N2G, dgain)
    put(N2B, dbias)
    total = colsum(g)
    dtv[...] = total
    put_shifts(g_ref, g)
    put_shifts(go_ref, own(g))

    flow.need(20, 21, 22, 23)
    for i, r in enumerate((PO, CO, CQ, SO)):
        put_rows(s_ref, r, gd[i].astype(F32))
    for j in range(8):
        put_rows(s_ref, GI + j, ggi[j].astype(F32), 8)
    for j in range(4):
        rows = ggo[j].astype(F32)
        for b in range(2):
            put_rows(s_ref, GO + 640 * b + W * j, rows[W * b : W * (b + 1), :])
    for j in range(2):
        put_rows(s_ref, CKV + j, gkv[j].astype(F32), 2)
    for i, r in enumerate(VEC1):
        put_rows(s_ref, r, own(dvec[i : i + 1, :]))
    put_rows(s_ref, GIB, own(dgib[...]))
    wide = jnp.where(c == 0, dwout[:18, :], dwout[18:36, :])
    for ch in range(2):
        for m in range(4):
            o_ref[ch, pl.ds(m, 9, stride=4), :80] = wide[9 * ch : 9 * ch + 9, 80 * m : 80 * m + 80]
    lane = lax.broadcasted_iota(jnp.int32, (80, W), 0)
    col = lax.broadcasted_iota(jnp.int32, (80, W), 1)
    moved = jnp.zeros((36, W), F32)
    for ch in range(2):
        spot = jnp.where(2 * lane + ch == col, 1.0, 0.0)
        moved += jnp.dot(o_ref[ch, :36, :80], spot, precision=HI, preferred_element_type=F32)
    put_rows(s_ref, OUT, moved)
    b0 = jnp.where(c == 0, dbout[0:1, 0:1], dbout[2:3, 0:1])
    b1 = jnp.where(c == 0, dbout[1:2, 0:1], dbout[3:4, 0:1])
    at = lax.broadcasted_iota(jnp.int32, (1, W), 1)
    put_rows(s_ref, OUTB, jnp.where(at == 0, b0, jnp.where(at == 1, b1, 0.0)))
    s_ref[:, OUTB + 1 :, :] = jnp.zeros((2, 4 * R1 // 5 - OUTB - 1, 128), F32)
    by_owner(s_ref, flat, out1, R1)
    flow.ready(0)

    flow.need(15, 8, 10)
    conv_grads(a1, go_ref, s_ref, 39)
    n = normed_of(h0, 0)
    g = conv_back_rows(g_ref, w1) * silu_slope(n * vec0[1:2, :] + vec0[2:3, :])
    g, dgain, dbias = norm_back(g, n, 0, vec0[1:2, :])
    g = dh[...] + g
    cols = jnp.concatenate([shift_lanes(noisy[...], t) for t in range(9)], axis=0).astype(BF)
    put_rows(s_ref, 0, nn(cols, own(g).astype(BF)))
    for r, v in zip(VEC0, (colsum(g), dgain, dbias, total)):
        put_rows(s_ref, r, own(v))
    s_ref[:, 4 * FRONT // 5 : 4 * R0 // 5, :] = jnp.zeros((2, 4 * (R0 - FRONT) // 5, 128), F32)
    by_owner(s_ref, flat, out0, R0)


FIRST = (0, 0, 1, 2, 3)
SECOND = (0, 1, 2, 3, 3)


def time_rows(facts, count):
    row = lax.axis_index(DP) * count + lax.broadcasted_iota(jnp.int32, (count, 1), 0)

    def wide(at, n):
        return jnp.concatenate([facts[:, at + i, :] for i in range(n)], axis=1)

    def meets(u, k):
        spot = jnp.where(k == lax.broadcasted_iota(jnp.int32, (1, u.shape[1]), 1), 1.0, 0.0).astype(BF)
        return nt(spot, u.astype(BF))

    total = jnp.zeros((count, 128), F32)
    for u, at, start, size in ((wide(FE, 3)[:, :D], FD1, T1, D), (wide(FU1, 10), FD2, T2, 4 * D)):
        rel = row - start
        k, line = rel // 5, rel % 5
        met = meets(u, jnp.where(rel < 0, -1, k))
        for j in range(5):
            g = facts[:, at + j, :]
            total += nn(jnp.where(line == j, met, 0.0).astype(BF), g.astype(BF))
            total += jnp.where((rel >= 0) & (k == size) & (line == j), colsum(g), 0.0)
    rel = row - T3
    group, line = rel // 5, rel % 5
    d3 = wide(FD3, 2)[:, :W]
    zero = jnp.zeros((d3.shape[0], 128), F32)
    u = wide(FU2, 10)
    for picks, shift in ((FIRST, 0), (SECOND, 1)):
        k = jnp.full_like(rel, -1)
        for j in range(5):
            k = jnp.where((rel >= 0) & (line == j), 4 * group + picks[j], k)
        met = meets(u, k)
        for j in range(5):
            if shift == 0:
                lo = (0, 128, 96, 64, 32)[j]
                g = d3[:, lo : min(lo + 128, W)]
                g = jnp.concatenate([g, zero[:, : 128 - g.shape[1]]], axis=1) if g.shape[1] < 128 else g
            else:
                if j in (0, 4):
                    continue
                g = jnp.concatenate([zero[:, : 32 * j], d3[:, : 128 - 32 * j]], axis=1)
            total += nn(jnp.where(line == j, met, 0.0).astype(BF), g.astype(BF))
            total += jnp.where((k == 4 * D) & (line == j), colsum(g), 0.0)
    return total


def update_kernel(with_time, params, momentum, ema, sum1, sum0, facts, new_params, new_momentum, new_ema, loss, pixels):
    total = facts[0, FL : FL + 1, :]
    for i in range(1, facts.shape[0]):
        total += facts[i, FL : FL + 1, :]
    loss[...] = total[:, 0:1]
    pixels[...] = total[:, 1:2]
    scale = 1.0 / (LAT * jnp.maximum(total[:, 1:2], 1.0))
    first = sum0[...]
    if with_time:
        first += time_rows(facts, sum0.shape[0])
    for p, g in enumerate((first, sum1[...])):
        g = g * scale
        m = MU * momentum[p] + g
        new_momentum[p] = m
        w = params[p] - LR * (g + MU * m)
        new_params[p] = w
        new_ema[p] = ED * ema[p] + (1.0 - ED) * w


ROWS = 856
SLAB = 864
SOME = 240
REST = SLAB - 3 * SOME


def send(src, dst, sems, i, j, target):
    copy = pltpu.make_async_remote_copy(
        src_ref=src, dst_ref=dst, send_sem=sems[0].at[i], recv_sem=sems[1].at[j],
        device_id={DP: target}, device_id_type=pl.DeviceIdType.MESH,
    )
    copy.start()
    return copy


PIECES = tuple(slice(16 * a, 16 * b) for a, b in ((0, 7), (7, 14), (14, 21), (21, 28), (28, 35), (35, 42), (42, 48), (48, 54)))


def gather_kernel(
    params, step, latents, noise, g0, g1, e, noisy, vec, p1, p2, stats, w1b_out, tw2_out, tw3_out, h0_out, h1_out, a1_out,
    low, slabs, flat, s_ref, w1b, tw2, tw3, h0, h1, a1, w1, win, tv, half1, half2, half3, sh, acc,
    send_sem, recv_sem, keep_sem, slab_sem, out_sem, swap_sem,
):
    low[:, :ROWS, :] = params[...].astype(BF)
    low[:, ROWS:, :] = jnp.zeros((2, SLAB - ROWS, 128), BF)
    me, y = lax.axis_index(DP), lax.axis_index(CH)
    k, x, z = me % 2, (me // 2) % 2, me // 4
    core = {DP: me + 1 - 2 * k}
    side = {DP: me + 2 - 4 * x}
    other = {CH: 1 - y}
    ring = [{DP: (me + 4 * o) % 16} for o in range(4)]
    barrier = pltpu.get_barrier_semaphore()
    for target in [core, side, other] + ring[1:]:
        pl.semaphore_signal(barrier, inc=1, device_id=target, device_id_type=pl.DeviceIdType.MESH)
    pl.semaphore_wait(barrier, 6)
    count = [0]
    started = []

    def push(ref, target):
        i = count[0]
        count[0] += 1
        return [start(ref, ref, i, i, target)]

    def start(src, dst, i, j, target):
        copy = pltpu.make_async_remote_copy(
            src_ref=src, dst_ref=dst, send_sem=send_sem.at[i], recv_sem=recv_sem.at[j],
            device_id=target, device_id_type=pl.DeviceIdType.MESH,
        )
        copy.start()
        started.append(copy)
        return copy

    def push_ring(ref):
        i = count[0]
        count[0] += 3
        return [start(ref, ref, i + o - 1, i + 3 - o, ring[o]) for o in (2, 1, 3)]

    def arrive(copies):
        for copy in copies:
            copy.wait_recv()

    keeps = []
    for p, g in enumerate((g0, g1)):
        keep = pltpu.make_async_copy(low.at[p], g.at[y, z, x, k], keep_sem.at[p])
        keep.start()
        keeps.append(keep)
    work = [(p, g, rows, p * (i % 2)) for p, g in enumerate((g0, g1)) for i, rows in enumerate(PIECES)]
    first, second, third, last = {}, {}, {}, ([], [])

    def begin(i):
        p, g, rows, _ = work[i]
        if i % len(PIECES) == 0:
            keeps[p].wait()
        first[i] = push_ring(g.at[y, z, x, k, rows])

    def middle(i):
        p, g, rows, turn = work[i]
        arrive(first[i])
        second[i] = push(g.at[y, :, x, k, rows], other if turn else side)
        last[p].extend(push(g.at[y, :, x, k, rows], core))

    def finish(i):
        p, g, rows, turn = work[i]
        zs = slice(0, 4 if p else 2)
        arrive(second[i])
        if turn:
            third[i] = push(g.at[:, :, x, k, rows], side)
            last[p].extend(push(g.at[1 - y, :, x, k, rows], core))
        else:
            third[i] = push(g.at[y, zs, :, k, rows], other)
            last[p].extend(push(g.at[y, :, 1 - x, k, rows], core))

    def pass_on(i):
        p, g, rows, turn = work[i]
        zs = slice(0, 4 if p else 2)
        arrive(third[i])
        last[p].extend(push(g.at[:, :, 1 - x, k, rows] if turn else g.at[1 - y, zs, :, k, rows], core))

    outs = [
        pltpu.make_async_copy(src, dst, out_sem.at[i])
        for i, (src, dst) in enumerate(
            ((w1b, w1b_out), (tw2, tw2_out), (tw3, tw3_out), (h0, h0_out), (h1, h1_out), (a1, a1_out))
        )
    ]
    fetches = [
        pltpu.make_async_copy(g0.at[a, b], slabs.at[a, b], slab_sem.at[i])
        for i, (a, b) in enumerate([(y, b) for b in range(4)] + [(1 - y, b) for b in range(2)])
    ]
    slabs[1 - y, 2:4] = jnp.zeros((2,) + slabs.shape[2:], BF)

    def fetch():
        arrive(last[0])
        for copy in fetches:
            copy.start()

    def flat_half(a):
        if a == 0:
            for copy in fetches:
                copy.wait()
        for t in range(16):
            flat[a, t * ROWS : (t + 1) * ROWS, :] = slabs[a, t // 4, t // 2 % 2, t % 2, :ROWS, :].astype(F32)

    def front():
        take_front(s_ref, win, w1, w1b, vec)
        outs[0].start()

    def times():
        for i in range(4):
            tw2[i] = own(get_rows(s_ref, U2 + i, 4 * D, 4)).astype(BF)
        tw3[...] = own(get_rows(s_ref, U3, 4 * D)).astype(BF)
        outs[1].start()
        outs[2].start()

    def swap(i, ref):
        return pltpu.make_async_remote_copy(
            src_ref=ref.at[y], dst_ref=ref.at[y], send_sem=swap_sem.at[i], recv_sem=swap_sem.at[3 + i],
            device_id=other, device_id_type=pl.DeviceIdType.MESH,
        )

    def units(u, w, start, size):
        parts = [nn(u, w(i)) + own(get_rows(s_ref, start + 4 * size + i, 1)) for i in range(4)]
        return jnp.concatenate(parts, axis=1)

    swaps = [swap(0, half1), swap(1, half2), swap(2, half3)]

    def time_one():
        u = e[...].astype(BF)
        half1[y] = units(u, lambda i: own(get_rows(s_ref, U1 + i, D, 4)).astype(BF), U1, D)
        swaps[0].start()

    def time_two():
        swaps[0].wait_recv()
        p1[...] = jnp.concatenate([half1[0], half1[1]], axis=1)
        half2[y] = units(silu(p1[...]).astype(BF), lambda i: tw2[i], U2, 4 * D)
        swaps[1].start()

    def time_three():
        swaps[1].wait_recv()
        p2[...] = jnp.concatenate([half2[0], half2[1]], axis=1)
        half3[y] = nn(silu(p2[...]).astype(BF), tw3[...]) + own(get_rows(s_ref, U3 + 4 * D, 1))
        swaps[2].start()

    def time_last():
        swaps[2].wait_recv()
        tv[...] = jnp.concatenate([half3[0], half3[1]], axis=1)[:1]

    def both(*steps):
        def one():
            for step in steps:
                step()

        return one

    opening, *rows_of_taps = start_steps(noisy, tv, win, w1, vec, h0, h1, a1, stats, sh, acc)
    todo = [
        fetch,
        lambda: flat_half(0),
        lambda: flat_half(1),
        lambda: unroll(flat, s_ref, 0, 9),
        lambda: unroll(flat, s_ref, 9, 18),
        lambda: unroll(flat, s_ref, 18, 27),
        lambda: unroll(flat, s_ref, 27, R1 // 400),
        time_one,
        both(front, times),
        time_two,
        opening,
        both(outs[3].start, outs[5].start, rows_of_taps[0]),
        time_three,
        rows_of_taps[1],
        time_last,
        both(rows_of_taps[2], outs[4].start),
    ]
    ahead = 2
    for i in range(ahead):
        begin(i)
    e[...] = jnp.broadcast_to(time_features(step[...]), (8, D))
    add_noise(step[...], latents, noise, noisy)
    for i in range(len(work) + 2):
        if i < len(work):
            middle(i)
            if i + ahead < len(work):
                begin(i + ahead)
        if i - 3 >= len(PIECES) and todo:
            todo.pop(0)()
        if 0 <= i - 1 < len(work):
            finish(i - 1)
        if 0 <= i - 3 < len(work):
            pass_on(i - 3)
        if i - 3 >= len(PIECES) - 1 and todo:
            todo.pop(0)()
    pass_on(len(work) - 1)
    for step in todo:
        step()
    for copy in outs:
        copy.wait()
    for copy in swaps:
        copy.wait_send()
    arrive(last[1])
    for copy in started:
        copy.wait_send()


def gather_weights(*operands):
    hbm, vm = pl.BlockSpec(memory_space=pl.ANY), pl.BlockSpec(memory_space=pltpu.VMEM)
    gathered = sds((2, 4, 2, 2, SLAB, 128), BF)
    large = (sds((3, D, 3 * D), BF), sds((4, 4 * D, W), BF), sds((4 * D, W), BF))
    large += (sds((N, D)), sds((N, D)), sds((N, D), BF))
    small = (sds((8, D)), sds((LAT, N)), sds((8, D)), sds((8, 4 * D)), sds((8, 4 * D)), sds((8, D)))
    dma = pltpu.SemaphoreType.DMA
    return pl.pallas_call(
        gather_kernel,
        out_shape=(gathered, gathered) + small + large,
        in_specs=[vm] * 4,
        out_specs=(hbm, hbm) + (vm,) * len(small) + (hbm,) * len(large),
        scratch_shapes=[
            pltpu.VMEM((2, SLAB, 128), BF),
            pltpu.VMEM(gathered.shape, BF),
            pltpu.VMEM((2, 16 * ROWS, 128), F32),
            pltpu.VMEM((3, 4 * R1 // 5, 128), F32),
            *(pltpu.VMEM(v.shape, v.dtype) for v in large),
            pltpu.VMEM((3, 3 * D, D), BF),
            pltpu.VMEM((36, D), BF),
            pltpu.VMEM((1, D), F32),
            pltpu.VMEM((2, 8, 2 * D), F32),
            pltpu.VMEM((2, 8, 2 * D), F32),
            pltpu.VMEM((2, 8, W), F32),
            pltpu.VMEM((N + 2 * SIDE, 3 * D), BF),
            pltpu.VMEM((8, D), F32),
            dma((128,)),
            dma((128,)),
            dma((2,)),
            dma((6,)),
            dma((6,)),
            dma((6,)),
        ],
        compiler_params=pltpu.CompilerParams(collective_id=2, has_side_effects=True, vmem_limit_bytes=63 * 2**20),
    )(*operands)


def add_up(*terms):
    total = terms[0].astype(F32)
    for term in terms[1:]:
        total += term.astype(F32)
    return total


def reduce_kernel(
    p1, p0, dtv, tw2_in, tw3_in, p1t, p2t, e, mask, loss, sum1, sum0, all_facts,
    kp1, kp0, tw2, tw3, facts, r1, sa, rx, ta, rz, r1b, sb, rbz, tb, rbx, some, land, fx, timed, send_sem, recv_sem, fsend, frecv, gsend, grecv, lsem, half, ssem,
):
    me = lax.axis_index(DP)
    k, x, z = me % 2, (me // 2) % 2, me // 4
    kept = [
        pltpu.make_async_copy(src, dst, lsem.at[i])
        for i, (src, dst) in enumerate(((p1.at[k], kp1), (p0.at[k], kp0), (tw2_in, tw2), (tw3_in, tw3)))
    ]
    for copy in kept:
        copy.start()
    barrier = pltpu.get_barrier_semaphore()
    for o in range(1, 16):
        pl.semaphore_signal(barrier, inc=1, device_id={DP: (me + o) % 16}, device_id_type=pl.DeviceIdType.MESH)
    y = lax.axis_index(CH)
    pl.semaphore_signal(barrier, inc=1, device_id={CH: 1 - y}, device_id_type=pl.DeviceIdType.MESH)
    pl.semaphore_wait(barrier, 16)
    sems = (send_sem, recv_sem)

    def swap(i):
        copy = pltpu.make_async_remote_copy(
            src_ref=half.at[i, y], dst_ref=half.at[i, y], send_sem=ssem.at[i], recv_sem=ssem.at[2 + i],
            device_id={CH: 1 - y}, device_id_type=pl.DeviceIdType.MESH,
        )
        copy.start()
        return copy

    core = me + 1 - 2 * k
    side = me + 2 - 4 * x
    chunks = [p0] + [p1.at[:, :, SOME * i : SOME * (i + 1)] for i in range(3)]
    mine = [kp0] + [kp1.at[:, SOME * i : SOME * (i + 1)] for i in range(3)]
    rest = p1.at[:, :, 3 * SOME :]

    def over_z(src, dst, base):
        return [
            send(src.at[(z + o) % 4], dst.at[3 - o], sems, base + o - 1, base + 3 - o, (me + 4 * o) % 16)
            for o in (2, 1, 3)
        ]

    over_core_b = send(rest.at[1 - k], r1b, sems, 20, 20, core)
    over_core = [send(ref.at[1 - k], r1.at[i], sems, i, i, core) for i, ref in enumerate(chunks)]
    kept[0].wait()
    kept[1].wait()
    over_core_b.wait_recv()
    for m in range(8):
        sb[m // 2, m % 2] = add_up(kp1[m, 3 * SOME :], r1b[m]).astype(BF)
    over_z_b = over_z(sb, rbz, 21)
    over_x = []
    for i, ref in enumerate(mine):
        over_core[i].wait_recv()
        for m in range(8):
            sa[i, m % 2, m // 2] = add_up(ref[m], r1[i, m]).astype(BF)
        over_x.append(send(sa.at[i, 1 - x], rx.at[i], sems, 4 + i, 4 + i, side))
        if i == 0:
            kept[2].wait()
            kept[3].wait()
            half[0, y] = nt(jnp.broadcast_to(own(dtv[...]), (8, W)).astype(BF), tw3[...])
            swaps = [swap(0)]
        if i == 2:
            swaps[0].wait_recv()
            d2 = (half[0, 0] + half[0, 1]) * silu_slope(p2t[...])
            mine2 = jnp.where(y == 0, d2[:, : 2 * D], d2[:, 2 * D :]).astype(BF)
            half[1, y] = sum(nt(mine2[:, W * j : W * (j + 1)], tw2[j]) for j in range(4))
            swaps.append(swap(1))
    swaps[1].wait_recv()
    d1 = (half[1, 0] + half[1, 1]) * silu_slope(p1t[...])
    put_facts(facts, e, p1t, p2t, d1, d2, dtv, mask, loss)
    fsems = (fsend, frecv)
    fx[z, x, k] = facts[...]
    facts_z = [send(facts, fx.at[z, x, k], fsems, o - 1, 3 - o, (me + 4 * o) % 16) for o in (2, 1, 3)]
    along = []
    for i in range(4):
        over_x[i].wait_recv()
        for m in range(4):
            ta[i, m] = add_up(sa[i, x, m], rx[i, m]).astype(BF)
        along.append(over_z(ta.at[i], rz.at[i], 8 + 3 * i))
        if i == 1:
            for copy in facts_z:
                copy.wait_recv()
            facts_x = send(fx.at[:, x, k], fx.at[:, x, k], fsems, 3, 3, side)
        if i == 3:
            facts_x.wait_recv()
            facts_core = send(fx.at[:, :, k], fx.at[:, :, k], fsems, 4, 4, core)
    for copy in over_z_b:
        copy.wait_recv()
    for m in range(2):
        tb[m] = add_up(sb[z, m], rbz[0, m], rbz[1, m], rbz[2, m]).astype(BF)
    over_x_b = send(tb.at[1 - x], rbx, sems, 24, 24, side)

    def done(i):
        for copy in along[i]:
            copy.wait_recv()
        return add_up(ta[i, z], rz[i, 0], rz[i, 1], rz[i, 2])

    some[...] = done(0)

    @pl.when(me > 0)
    def _():
        @pl.loop(0, SOME // 8)
        def _(g):
            row = SOME * me + 8 * g
            owner = row // ROWS
            at = pl.multiple_of(row - ROWS * owner, 8)
            pltpu.make_async_remote_copy(
                src_ref=some.at[pl.ds(pl.multiple_of(8 * g, 8), 8)], dst_ref=land.at[pl.ds(at, 8)],
                send_sem=gsend, recv_sem=grecv, device_id={DP: owner}, device_id_type=pl.DeviceIdType.MESH,
            ).start()

    facts_core.wait_recv()
    all_facts[...] = fx[...].reshape(16, FACTS, 128)
    timed[...] = time_rows(all_facts, ROWS)
    for i in range(3):
        sum1[SOME * i : SOME * (i + 1), :] = done(i + 1)
    over_x_b.wait_recv()
    sum1[3 * SOME :, :] = add_up(tb[x, : ROWS - 3 * SOME], rbx[: ROWS - 3 * SOME])

    def landed(lo, hi):
        part = land.at[lo:hi]
        pltpu.make_async_remote_copy(
            src_ref=part, dst_ref=part, send_sem=gsend, recv_sem=grecv,
            device_id={DP: me}, device_id_type=pl.DeviceIdType.MESH,
        ).wait_recv()
        sum0[lo:hi, :] = land[lo:hi, :] + timed[lo:hi, :]

    @pl.when(me == 0)
    def _():
        landed(SOME, ROWS)
        sum0[:SOME, :] = some[...] + timed[:SOME, :]

    @pl.when((me > 0) & (me < 4))
    def _():
        landed(0, ROWS)

    @pl.when(me == 4)
    def _():
        landed(0, 16 * SOME - 4 * ROWS)
        sum0[16 * SOME - 4 * ROWS :, :] = timed[16 * SOME - 4 * ROWS :, :]

    @pl.when(me > 4)
    def _():
        sum0[...] = timed[...]

    @pl.when(me > 0)
    def _():
        pltpu.make_async_remote_copy(
            src_ref=some, dst_ref=some, send_sem=gsend, recv_sem=grecv,
            device_id={DP: me}, device_id_type=pl.DeviceIdType.MESH,
        ).wait_send()

    for copy in [over_core_b, over_x_b] + over_core + over_z_b + over_x + sum(along, []) + facts_z + [facts_x, facts_core] + swaps:
        copy.wait_send()


def sum_over_samples(*operands):
    vm, hbm = pl.BlockSpec(memory_space=pltpu.VMEM), pl.BlockSpec(memory_space=pl.ANY)
    dma = pltpu.SemaphoreType.DMA
    return pl.pallas_call(
        reduce_kernel,
        out_shape=(sds((ROWS, 128)), sds((ROWS, 128)), sds((16, FACTS, 128))),
        in_specs=[hbm, hbm, vm, hbm, hbm] + [vm] * 5,
        out_specs=(vm,) * 3,
        scratch_shapes=[
            pltpu.VMEM((8, SLAB, 128), BF),
            pltpu.VMEM((8, SOME, 128), BF),
            pltpu.VMEM((4, 4 * D, W), BF),
            pltpu.VMEM((4 * D, W), BF),
            pltpu.VMEM((FACTS, 128), F32),
            pltpu.VMEM((4, 8, SOME, 128), BF),
            pltpu.VMEM((4, 2, 4, SOME, 128), BF),
            pltpu.VMEM((4, 4, SOME, 128), BF),
            pltpu.VMEM((4, 4, SOME, 128), BF),
            pltpu.VMEM((4, 3, SOME, 128), BF),
            pltpu.VMEM((8, REST, 128), BF),
            pltpu.VMEM((4, 2, REST, 128), BF),
            pltpu.VMEM((3, 2, REST, 128), BF),
            pltpu.VMEM((2, REST, 128), BF),
            pltpu.VMEM((REST, 128), BF),
            pltpu.VMEM((SOME, 128), F32),
            pltpu.VMEM((ROWS, 128), F32),
            pltpu.VMEM((4, 2, 2, FACTS, 128), F32),
            pltpu.VMEM((ROWS, 128), F32),
            dma((25,)),
            dma((25,)),
            dma((5,)),
            dma((5,)),
            dma,
            dma,
            dma((4,)),
            pltpu.VMEM((2, 2, 8, 4 * D), F32),
            dma((4,)),
        ],
        compiler_params=pltpu.CompilerParams(
            collective_id=1, has_side_effects=True, vmem_limit_bytes=62 * 2**20
        ),
    )(*operands)


def time_features(steps):
    ladder = lax.broadcasted_iota(jnp.int32, (1, D // 2), 1).astype(F32)
    angles = steps.astype(F32) * jnp.exp(-math.log(10000.0) * ladder / (D // 2))
    return jnp.concatenate([jnp.cos(angles), jnp.sin(angles)], axis=1)


def add_noise(step, latents, noise, noisy):
    shape = (8, 128)
    level = 128 * lax.broadcasted_iota(jnp.int32, shape, 0) + lax.broadcasted_iota(jnp.int32, shape, 1)
    lowest, highest = 0.00085**0.5, 0.012**0.5
    beta = jnp.square(lowest + (highest - lowest) * level.astype(F32) / 999.0)
    logs = jnp.where(level <= step, jnp.log(1.0 - beta), 0.0)
    abar = jnp.exp(jnp.sum(jnp.sum(logs, axis=1, keepdims=True), axis=0, keepdims=True))
    noisy[...] = jnp.sqrt(abar) * latents[...] + jnp.sqrt(1.0 - abar) * noise[...]


def prepare_kernel(step, latents, noise, e, noisy):
    e[...] = jnp.broadcast_to(time_features(step[...]), (8, D))
    add_noise(step[...], latents, noise, noisy)


def shards(params, momentum, ema_params, latents, noise_eps, timesteps, pixel_mask, context):
    c = lax.axis_index(CH)
    d = lax.axis_index(DP)
    n_dp = lax.axis_size(DP)
    rows_dev = params.shape[2]
    rows_all = rows_dev * n_dp
    quick = n_dp == 16 and rows_dev == ROWS
    step, noise = timesteps[:, None], noise_eps[0]
    if quick:
        _, part1, e, noisy, vec0, p1, p2, stats, w1b, tw2, tw3, h0, h1, a1 = gather_weights(
            params[0], step, latents[0], noise
        )
        part1 = part1.reshape(2, 16, SLAB, 128)
    else:
        e, noisy = kcall(prepare_kernel, (sds((8, D)), sds((LAT, N))), (step, latents[0], noise))
        low = params[0].astype(BF)
        part0, part1 = (lax.all_gather(lax.all_gather(low[i], CH, axis=0), DP, axis=1) for i in range(2))

    px = (N, D)
    hx = (HEADS, N, HD)
    sh = (N + 2 * SIDE, 3 * D)
    taps, back = sds((3, 3 * D, D), BF), sds((3, D, 3 * D), BF)
    flat = pltpu.VMEM((2, rows_all, 128), F32)
    unrolled = pltpu.VMEM((3, 4 * R1 // 5, 128), F32)
    units = sds((8, 4 * D))
    if not quick:
        win, w1, w1b, vec0, tw2, tw3, tv, p1, p2 = kcall(
            partial(unpack0_kernel, rows_dev),
            (sds((36, D), BF), taps, back, sds((8, D)), sds((4, 4 * D, D), BF), sds((4 * D, D), BF), sds((1, D)))
            + (units, units),
            (part0, e),
            (flat, unrolled),
        )
        h0, h1, a1, stats = kcall(
            start_kernel,
            (sds(px), sds(px), sds(px, BF), sds((8, D))),
            (noisy, tv, win, w1, vec0),
            (pltpu.VMEM(sh, BF), pltpu.VMEM((8, D), F32)),
        )
    c2, c2b, tr, mats, kvw, vec1, gib, wout, outb = kcall(
        partial(unpack1_kernel, rows_dev),
        (taps, back, sds((4, D, D), BF), sds((16, D, D), BF), sds((2, CTX, D), BF))
        + (sds((24, D)), sds((8, D)), sds((36, D), BF), sds((1, D))),
        (part1,),
        (flat, unrolled, pltpu.VMEM((2, 40, 128), F32)),
    )
    h2, z0, a2, ntr, x1, q, k, v, stats = kcall(
        front_kernel,
        (sds(px),) * 2 + (sds(px, BF),) * 3 + (sds(hx, BF),) * 3 + (sds((8, D)),),
        (h0, h1, stats, c2, tr, vec1),
        (pltpu.VMEM(sh, BF), pltpu.VMEM((8, D), F32)),
        late=(0, 3, 4),
        early=range(8),
    )
    o, lse = kcall(
        attend_kernel, (sds(px, BF), sds((HEADS, 1, N))), (q, k, v), (pltpu.VMEM((D, N), F32),)
    )
    square = (D, W)
    dz1, dh3, dos, loss, gd, ggi, ggo, gkv, dvec, dgib, dwout, dbout = kcall(
        middle_kernel,
        (sds(px), sds(px), sds(hx, BF), sds((1, 1)))
        + (sds((4,) + square, BF), sds((8,) + square, BF), sds((4,) + square, BF), sds((2, CTX, W), BF))
        + (sds((24, D)), sds((8, D)), sds((36, D)), sds((8, 128))),
        (o, z0, h2, context[0], noise, pixel_mask, mats, kvw, vec1, gib, wout, outb),
        [pltpu.VMEM(px, F32)] * 3
        + [pltpu.VMEM(px, BF)] * 4
        + [
            pltpu.VMEM((4, N, D), BF),
            pltpu.VMEM((4, N, D), F32),
            pltpu.VMEM((4, N, D), F32),
            pltpu.VMEM(px, BF),
            pltpu.VMEM(px, BF),
            pltpu.VMEM((HEADS * KEYS, D), BF),
            pltpu.VMEM((HEADS * KEYS, D), BF),
            pltpu.VMEM((N, HEADS * KEYS), F32),
            pltpu.VMEM((N, HEADS * KEYS), BF),
            pltpu.VMEM((8, D), F32),
            pltpu.VMEM((36, N), F32),
        ]
        + [pltpu.VMEM((D, N), BF)] * 4,
        late=(7, 6, 1, 2),
        early=(0, 1, 2, 4, 5, 6, 7),
    )
    dq, dk, dv = kcall(
        attend_back_kernel,
        (sds(px, BF),) * 3,
        (q, k, v, dos, lse),
        (pltpu.VMEM((D, N), F32), pltpu.VMEM(hx, F32), pltpu.VMEM(hx, F32)),
    )
    front = -(-FRONT // (16 * n_dp)) * 16 * n_dp
    lead = (2, 8) if quick else (n_dp,)
    own1, own0, dtv = kcall(
        back_kernel,
        (
            sds(lead + (SLAB if quick else rows_dev, 128), BF),
            sds(lead + (front // n_dp, 128), BF),
            sds((1, D)),
        ),
        (dq, dk, dv, dz1, dh3, z0, h2, h1, h0, stats, w1b, c2b, tr, vec0, vec1, a1, a2, ntr, x1, noisy,
         gd, ggi, ggo, gkv, dvec, dgib, dwout, dbout),
        (
            pltpu.VMEM(px, F32),
            pltpu.VMEM(sh, BF),
            pltpu.VMEM((sh[0], 3 * W), BF),
            pltpu.VMEM((24, D), F32),
            pltpu.VMEM((2, 4 * R1 // 5, 128), F32),
            pltpu.VMEM((7600, 128), F32),
            pltpu.VMEM((2, 40, 128), F32),
        ),
        late=(5, 3, 17, 6, 4, 16, 7, 11, 20, 21, 22, 23, 15, 8, 10),
        early=(0,),
    )
    timed = (dtv, tw2, tw3, p1, p2, e, pixel_mask, loss)
    if quick:
        sum1, sum0, all_facts = sum_over_samples(own1, own0, *timed)
    else:
        facts = kcall(time_back, sds((FACTS, 128)), timed)
        sum1 = lax.psum_scatter(own1, DP, scatter_dimension=0).astype(F32)
        sum0 = lax.all_gather(lax.psum_scatter(own0, DP, scatter_dimension=0), DP, axis=0, tiled=True)
        sum0 = jnp.pad(sum0, ((0, rows_all - front), (0, 0)))
        sum0 = lax.dynamic_slice_in_dim(sum0, d * rows_dev, rows_dev, 0).astype(F32)
        all_facts = lax.all_gather(facts, DP, axis=0)
    state = sds((2, rows_dev, 128))
    new_params, new_momentum, new_ema, loss, pixels = kcall(
        partial(update_kernel, not quick),
        (state, state, state, sds((1, 1)), sds((1, 1))),
        (params[0], momentum[0], ema_params[0], sum1, sum0, all_facts),
    )
    return (new_params[None], new_momentum[None], new_ema[None], loss.reshape(()), pixels.reshape(()))


def solution(mesh):
    packed = P(CH, None, DP, None)
    row = P(DP, None, None)
    return jax.shard_map(
        shards,
        mesh=mesh,
        in_specs=(packed, packed, packed, row, row, P(DP), P(DP, None), row),
        out_specs=(packed, packed, packed, P(), P()),
        check_vma=False,
    )
```
